32 devices in a mesh: blk: 16 (over z, y, core), tm: 2 (over x).
Axes of the slice: x: 2, y: 2, z: 4, core: 2. Of those that a mesh axis runs over, the one named last changes fastest.
Arguments:
- waveforms: bfloat16 [480, 16384], P(None, ('blk', 'tm')), may hold values from -60 to 60
- templates: bfloat16 [16, 480, 256], P('blk'), may hold values from -6 to 6
- station_mask: int32 [16, 160], P('blk'), may hold values 0 or 1
- channel_order: int32 [480], replicated, may hold values from 0 to 479, each once
Outputs:
- detection: float32 [16, 16384], P(None, ('blk', 'tm'))
The draws below stay inside these ranges and needn't reach their ends.
Inputs may be any that keep to these rules, and one draw needn't show every extreme that they name: `channel_order`: each of 0 to 479 appears once.
All inputs are finite; a program needn't handle non-finite values. No bound on the sum of `station_mask` on one device may be relied on, other than what follows from the above.
Results may differ from the reference program's by a relative error of at most 0.0003.
Values may be sent and summed in bfloat16 or wider, within the bound.
No kernel may reach another device: no remote copies, remote signals or barrier semaphores. Data moves between devices by JAX's collectives and lax.ppermute only.
A program may use at most 64 MiB of HBM per device.

```python
import jax
import jax.numpy as jnp
from jax import lax

STATIONS = 160
CHANNELS = 480
TPL_LEN = 256
SLAB = 512
TEMPLATES = 16
TIME = 16384


def draw_waveforms(key, part):
    noise_key = jax.random.fold_in(key, 101)
    level_key = jax.random.fold_in(key, 202)
    gain_key = jax.random.fold_in(key, 303)
    level_count = TIME // 8 + 1
    levels = jnp.exp(1.5 * jax.random.uniform(level_key, (level_count,), jnp.float32, -1.0, 1.0))
    envelope = jnp.repeat(levels, 8)[:TIME]
    gains = jnp.exp(1.2 * jax.random.uniform(gain_key, (CHANNELS, 1), jnp.float32, -1.0, 1.0))
    noise = jnp.clip(jax.random.normal(noise_key, (CHANNELS, TIME), jnp.float32), -4.0, 4.0)
    return (noise * envelope[None, :] * gains).astype(jnp.bfloat16)


def set_ends(values, stream_key, smallest, high):
    longest = values.shape.index(max(values.shape))
    spots = []
    for shift in (0, 1):
        where = [jax.random.randint(jax.random.fold_in(stream_key, axis), (), 0, length) for axis, length in enumerate(values.shape)]
        where[longest] = (where[longest] + shift) % values.shape[longest]
        spots.append(tuple(where))
    return values.at[spots[0]].set(smallest).at[spots[1]].set(high)


def block_levels(rng, dims, pieces, low, high):
    loudness, own = 1.0, jax.random.fold_in(rng, 6)
    for dim, blocks in pieces:
        steps = jnp.exp(jax.random.uniform(jax.random.fold_in(own, dim), (blocks,), jnp.float32, low / len(pieces), high / len(pieces)))
        loudness = loudness * jnp.repeat(steps, dims[dim] // blocks).reshape([-1 if axis == dim else 1 for axis in range(len(dims))])
    return loudness


def gaussian(own_key, shape, width, most, cuts=(), kind=jnp.bfloat16):
    array = jax.random.normal(own_key, shape, jnp.float32) * width
    if len(cuts) > 0:
        array = block_levels(own_key, shape, cuts, -0.22, 0.18) * array
    return jnp.clip(array, min=-most, max=most).astype(kind)


def setup_inputs(seed: int = 0) -> dict:
    key_list = jax.random.split(jax.random.key(seed), 5)
    waveforms = draw_waveforms(jax.random.fold_in(key_list[4], 71), 0)
    templates = gaussian(key_list[1], (TEMPLATES, CHANNELS, TPL_LEN), 1.0, 6.0, ((0, 16),))
    station_mask = set_ends((jax.random.randint(key_list[2], (TEMPLATES, STATIONS), 0, 4) < 3).astype(jnp.int32), jax.random.fold_in(key_list[2], 1), 0, 1)
    channel_order = jax.random.permutation(key_list[3], CHANNELS).astype(jnp.int32)
    return dict(waveforms=waveforms, templates=templates, station_mask=station_mask, channel_order=channel_order)


EPSILON = 1e-05

def station_table(station_mask, channel_order):
    station_of = channel_order // 3
    onehot = (jnp.arange(STATIONS, dtype=jnp.int32)[:, None] == station_of[None, :]).astype(jnp.float32)
    return jnp.dot(station_mask.astype(jnp.float32), onehot, precision=lax.Precision.HIGHEST)

def window_sums(squares, window_len):
    running = squares
    window = 1
    while window < window_len:
        columns = running.shape[1]
        running = running[:, :columns - window] + running[:, window:]
        window = window * 2
    return running

def correlate(masked_row, extended, slab_len, window_len):
    products = lax.dot_general(masked_row, extended, (((0,), (0,)), ((), ())), preferred_element_type=jnp.float32)
    columns = extended.shape[1]
    flattened = jnp.concatenate([products.reshape(-1), jnp.zeros((window_len,), jnp.float32)])
    skewed = flattened.reshape(window_len, columns + 1)[:, :slab_len]
    return lax.optimization_barrier(jnp.sum(skewed, axis=0))

def reference(waveforms, templates, station_mask, channel_order):
    channel_mask = station_table(station_mask, channel_order)
    masked = templates * channel_mask.astype(jnp.bfloat16)[:, :, None]
    tpl_norm = jnp.sqrt(lax.optimization_barrier(jnp.sum(masked.astype(jnp.float32) ** 2, axis=(1, 2))) + EPSILON)
    live = lax.optimization_barrier(jnp.sum(channel_mask, axis=1))
    row_scale = jnp.sqrt(TPL_LEN * live) / tpl_norm
    padded = jnp.pad(waveforms, ((0, 0), (0, TPL_LEN - 1)))
    block_count = TIME // SLAB

    def one_block(block_index):
        begin = (block_index * SLAB).astype(jnp.int32)
        extended = lax.dynamic_slice_in_dim(padded, begin, SLAB + TPL_LEN - 1, 1)
        energy = window_sums(extended.astype(jnp.float32) ** 2, TPL_LEN)
        window_energy = jnp.dot(channel_mask, energy, precision=lax.Precision.HIGHEST)
        dots = lax.map(lambda masked_row: correlate(masked_row, extended, SLAB, TPL_LEN), masked)
        return dots * row_scale[:, None] / jnp.sqrt(window_energy + EPSILON)
    blocks = lax.map(one_block, jnp.arange(block_count, dtype=jnp.int32))
    return jnp.transpose(blocks, (1, 0, 2)).reshape(TEMPLATES, TIME)
```

```python
import functools

import jax
import jax.numpy as jnp
from jax import lax
from jax.experimental import pallas as pl
from jax.experimental.pallas import tpu as pltpu
from jax.sharding import PartitionSpec as P

EPSILON = 1e-05
LANES = 128
INNER = 4
FINE = 16
VMEM_BYTES = 40 * 1024 * 1024

BF16 = jnp.bfloat16
F32 = jnp.float32


def call(kernel, out_shape, scratch=(), flops=0, bytes_accessed=0):
    return pl.pallas_call(
        kernel,
        out_shape=out_shape,
        scratch_shapes=list(scratch),
        compiler_params=pltpu.CompilerParams(vmem_limit_bytes=VMEM_BYTES),
        cost_estimate=pl.CostEstimate(
            flops=flops, bytes_accessed=bytes_accessed, transcendentals=0
        ),
    )


def one_hot(order_row, station_count):
    columns = order_row.shape[1]
    first = 3 * lax.broadcasted_iota(jnp.int32, (station_count, columns), 0)
    hit = (order_row >= first) & (order_row < first + 3)
    return jnp.where(hit, 1.0, 0.0).astype(BF16)


def template_kernel(tm_count, tpl_ref, flag_ref, order_ref, *refs):
    outs, meta_ref = refs[:INNER], refs[INNER]
    tpl_pad, order_pad, turned = refs[INNER + 1 :]
    channels, window = tpl_ref.shape[1:]
    stations = flag_ref.shape[1]
    padded = tpl_pad.shape[0]
    part = LANES // tm_count
    tpl_pad[channels:, :] = jnp.zeros((padded - channels, window), BF16)
    tpl_pad[:channels, :] = tpl_ref[0]
    order_pad[...] = jnp.full((1, padded), -1, jnp.int32)
    order_pad[:, :channels] = order_ref[...]
    flags = jnp.broadcast_to(flag_ref[...].astype(F32), (8, stations))
    mask = jnp.dot(
        flags.astype(BF16), one_hot(order_pad[...], stations), preferred_element_type=F32
    )
    masked = tpl_pad[...].T * mask[:1].astype(BF16)
    turned[...] = masked
    wide = masked.astype(F32)
    norm = jnp.sqrt(jnp.sum(wide * wide, keepdims=True) + EPSILON)
    live = jnp.sum(mask[:1], keepdims=True)
    meta_ref[...] = jnp.broadcast_to(jnp.sqrt(window * live) / norm, meta_ref.shape)
    meta_ref[:, :stations] = flags[:1]
    my_inner = lax.rem(lax.axis_index("blk"), INNER)
    my_tm = lax.axis_index("tm")
    spot = lax.broadcasted_iota(jnp.int32, (FINE, LANES), 1) // part
    for flip in range(INNER):
        start = pl.multiple_of((my_inner ^ flip) * LANES, LANES)
        for step in range(window // (FINE * tm_count)):
            tile = jnp.zeros((FINE, LANES), F32)
            for within in range(tm_count):
                row = FINE * (step * tm_count + within)
                chunk = turned[row : row + FINE, pl.ds(start, LANES)].astype(F32)
                turn = lax.rem(part * (within - my_tm) + LANES, LANES)
                tile = jnp.where(spot == within, pltpu.roll(chunk, turn, 1), tile)
            outs[flip][FINE * step : FINE * (step + 1), :] = tile.astype(BF16)


def wave_kernel(group, tm_count, wave_ref, *refs):
    outs, wave_pad = refs[:group], refs[group]
    channels, slab = wave_ref.shape
    padded = wave_pad.shape[0]
    part = padded // group
    wave_pad[channels:, :] = jnp.zeros((padded - channels, slab), BF16)
    wave_pad[:channels, :] = wave_ref[...]
    me = lax.rem(lax.axis_index("blk"), INNER) * tm_count + lax.axis_index("tm")
    for flip in range(group):
        start = pl.multiple_of((me ^ flip) * part, part)
        outs[flip][...] = wave_pad[pl.ds(start, part), :]


def head_kernel(group, tm_count, *refs):
    parts, out_ref = refs[:group], refs[group]
    me = lax.rem(lax.axis_index("blk"), INNER) * tm_count + lax.axis_index("tm")
    for flip in range(group):

        @pl.when(me == flip)
        def _():
            out_ref[...] = parts[flip][:, : out_ref.shape[1]]


def shift_kernel(group, tm_count, *refs):
    parts, halo_ref, out_ref, joined = refs[:group], refs[group], refs[group + 1], refs[group + 2]
    part, slab = parts[0].shape
    me = lax.rem(lax.axis_index("blk"), INNER) * tm_count + lax.axis_index("tm")
    for flip in range(group):
        start = pl.multiple_of((me ^ flip) * slab, slab)
        joined[:, pl.ds(start, slab)] = parts[flip][...].astype(F32)
    joined[:, group * slab :] = halo_ref[...].astype(F32)
    columns = joined.shape[1]
    for copy in range(LANES // FINE):
        rows = slice(copy * part, (copy + 1) * part)
        if copy == 0:
            out_ref[rows, :] = joined[...].astype(BF16)
        else:
            out_ref[rows, :] = pltpu.roll(joined[...], columns - FINE * copy, 1).astype(BF16)


def dots_kernel(group, tm_count, *refs):
    count = lax.axis_size("blk")
    tpls, shifts, outs = refs[:count], refs[count], refs[count + 1 : count + 1 + group]
    left, products, gathered = refs[count + 1 + group :]
    my_blk = lax.axis_index("blk")
    me = lax.rem(my_blk, INNER) * tm_count + lax.axis_index("tm")
    per_half = left.shape[2] // LANES
    for flip in range(count):
        row = pl.multiple_of((my_blk ^ flip) * FINE, FINE)
        for step in range(2 * per_half):
            lane = (step % per_half) * LANES
            left[step // per_half, pl.ds(row, FINE), lane : lane + LANES] = tpls[flip][
                FINE * step : FINE * (step + 1), :
            ]
    slab = gathered.shape[2]
    tiles = products.shape[0]
    span = (tiles - 1) * LANES
    per_block = span // slab

    def block(index, carry):
        start = pl.multiple_of(index * span, span)
        product = jnp.dot(
            left[0], shifts[:, pl.ds(start, span + LANES)], preferred_element_type=F32
        ) + jnp.dot(
            left[1],
            shifts[:, pl.ds(pl.multiple_of(start + LANES, LANES), span + LANES)],
            preferred_element_type=F32,
        )
        for tile in range(tiles):
            products[tile] = product[:, tile * LANES : (tile + 1) * LANES]

        def fine_rows(fine):
            return jnp.concatenate(
                [products[tile, pl.ds(fine, count, stride=FINE), :] for tile in range(tiles)],
                axis=1,
            )

        total = fine_rows(FINE - 1)
        for fine in reversed(range(FINE - 1)):
            total = fine_rows(fine) + pltpu.roll(total, span + LANES - 1, 1)
        for piece in range(per_block):
            gathered[index * per_block + piece] = total[:, piece * slab : (piece + 1) * slab]
        return carry

    lax.fori_loop(0, group // per_block, block, 0)
    for flip in range(group):
        outs[flip][...] = gathered[me ^ flip]


def power_kernel(wave_ref, meta_ref, order_ref, out_ref, head_ref):
    stations = meta_ref.shape[1]
    mask = jnp.dot(
        meta_ref[...].astype(BF16), one_hot(order_ref[...], stations), preferred_element_type=F32
    ).astype(BF16)
    wave = wave_ref[...].astype(F32)
    squares = wave * wave
    high = squares.astype(BF16)
    low = (squares - high.astype(F32)).astype(BF16)
    power = jnp.dot(mask, high, preferred_element_type=F32) + jnp.dot(
        mask, low, preferred_element_type=F32
    )
    out_ref[...] = power
    head_ref[...] = power[:, : head_ref.shape[1]]


def factor_kernel(power_ref, halo_ref, scale_ref, out_ref, joined):
    slab, window = power_ref.shape[1], halo_ref.shape[1]
    joined[:, :slab] = power_ref[...]
    joined[:, slab:] = halo_ref[...]
    running = joined[...]
    columns = running.shape[1]
    width = 1
    while width < window:
        running = running + pltpu.roll(running, columns - width, 1)
        width *= 2
    out_ref[...] = scale_ref[:, :1] / jnp.sqrt(running[:, :slab] + EPSILON)


def finish_kernel(*refs):
    parts, factor_ref, out_ref = refs[:-2], refs[-2], refs[-1]
    total = parts[0][...]
    for part in parts[1:]:
        total = total + part[...]
    out_ref[...] = total * factor_ref[...]


def on_device(waveforms, templates, station_mask, channel_order):
    channels, slab = waveforms.shape
    rows, _, window = templates.shape
    stations = station_mask.shape[1]
    blk_count, tm_count = lax.axis_size("blk"), lax.axis_size("tm")
    assert rows == 1 and LANES % tm_count == 0
    group = INNER * tm_count
    padded = INNER * LANES
    part = padded // group
    chunk = group * slab
    span = 2 * slab
    both = ("blk", "tm")
    sds = jax.ShapeDtypeStruct
    order_row = channel_order[None, :]

    *tpl_parts, meta = call(
        functools.partial(template_kernel, tm_count),
        [sds((window * part // LANES, LANES), BF16)] * INNER + [sds((1, 2 * LANES), F32)],
        [
            pltpu.VMEM((padded, window), BF16),
            pltpu.VMEM((1, padded), jnp.int32),
            pltpu.VMEM((window, padded), BF16),
        ],
        bytes_accessed=channels * window * 2,
    )(templates, station_mask, order_row)
    tpls = [tpl_parts[0]]
    for flip in range(1, blk_count):
        route = [(b, b ^ flip) for b in range(blk_count)]
        tpls.append(lax.ppermute(tpl_parts[flip % INNER], "blk", route))

    wave_parts = call(
        functools.partial(wave_kernel, group, tm_count),
        [sds((part, slab), BF16)] * group,
        [pltpu.VMEM((padded, slab), BF16)],
        bytes_accessed=channels * slab * 4,
    )(waveforms)
    total = blk_count * tm_count
    routes = [[(i, i ^ flip) for i in range(total)] for flip in range(group)]
    waves = [wave_parts[0]]
    for flip in range(1, group):
        waves.append(lax.ppermute(wave_parts[flip], both, routes[flip]))

    meta_all = lax.all_gather(meta, "blk", axis=0, tiled=True)
    power, power_head = call(
        power_kernel,
        [sds((blk_count, slab), F32), sds((blk_count, window), F32)],
        flops=4 * blk_count * channels * slab,
        bytes_accessed=channels * slab * 2,
    )(waveforms, meta_all[:, :stations], order_row)
    power_halo = lax.ppermute(power_head, both, [(i, i - 1) for i in range(1, total)])
    factor = call(
        factor_kernel,
        sds((blk_count, slab), F32),
        [pltpu.VMEM((blk_count, slab + window), F32)],
        bytes_accessed=blk_count * slab * 8,
    )(power, power_halo, meta_all[:, stations:])

    head = call(
        functools.partial(head_kernel, group, tm_count),
        sds((part, window), BF16),
        bytes_accessed=chunk * part * 2,
    )(*waves)
    halo = lax.ppermute(head, "blk", [(b, b - INNER) for b in range(INNER, blk_count)])
    copies = LANES // FINE
    shifts = call(
        functools.partial(shift_kernel, group, tm_count),
        sds((copies * part, chunk + window), BF16),
        [pltpu.VMEM((part, chunk + window), F32)],
        bytes_accessed=chunk * part * 2 * (copies + 1),
    )(*waves, halo)

    partials = call(
        functools.partial(dots_kernel, group, tm_count),
        [sds((blk_count, slab), F32)] * group,
        [
            pltpu.VMEM((2, blk_count * FINE, copies * part), BF16),
            pltpu.VMEM((span // LANES + 1, blk_count * FINE, LANES), F32),
            pltpu.VMEM((group, blk_count, slab), F32),
        ],
        flops=2 * blk_count * window * part * chunk,
        bytes_accessed=copies * part * chunk * 2,
    )(*tpls, shifts)
    sums = [partials[0]]
    for flip in range(1, group):
        sums.append(lax.ppermute(partials[flip], both, routes[flip]))
    return call(
        finish_kernel, sds((blk_count, slab), F32), bytes_accessed=blk_count * slab * 4 * (group + 2)
    )(*sums, factor)


def solution(mesh):
    placed = (P(None, ("blk", "tm")), P("blk", None, None), P("blk", None), P())
    return jax.shard_map(
        on_device, mesh=mesh, in_specs=placed, out_specs=P(None, ("blk", "tm")), check_vma=False
    )
```

```python
import functools

import jax
import jax.numpy as jnp
from jax import lax
from jax.experimental import pallas as pl
from jax.experimental.pallas import tpu as pltpu
from jax.sharding import PartitionSpec as P

EPSILON = 1e-05
LANES = 128
INNER = 4
FINE = 16
VMEM_BYTES = 40 * 1024 * 1024

BF16 = jnp.bfloat16
F32 = jnp.float32


def call(kernel, out_shape, scratch=(), flops=0, bytes_accessed=0):
    return pl.pallas_call(
        kernel,
        out_shape=out_shape,
        scratch_shapes=list(scratch),
        compiler_params=pltpu.CompilerParams(vmem_limit_bytes=VMEM_BYTES),
        cost_estimate=pl.CostEstimate(
            flops=flops, bytes_accessed=bytes_accessed, transcendentals=0
        ),
    )


def one_hot(order_row, station_count):
    columns = order_row.shape[1]
    first = 3 * lax.broadcasted_iota(jnp.int32, (station_count, columns), 0)
    hit = (order_row >= first) & (order_row < first + 3)
    return jnp.where(hit, 1.0, 0.0).astype(BF16)


def template_kernel(tm_count, tpl_ref, flag_ref, order_ref, *refs):
    out_ref, tpl_pad, order_pad, turned = refs
    channels, window = tpl_ref.shape[1:]
    stations = flag_ref.shape[1]
    padded = tpl_pad.shape[0]
    part = LANES // tm_count
    tpl_pad[channels:, :] = jnp.zeros((padded - channels, window), BF16)
    tpl_pad[:channels, :] = tpl_ref[0]
    order_pad[...] = jnp.full((1, padded), -1, jnp.int32)
    order_pad[:, :channels] = order_ref[...]
    flags = jnp.broadcast_to(flag_ref[...].astype(F32), (8, stations))
    mask = jnp.dot(
        flags.astype(BF16), one_hot(order_pad[...], stations), preferred_element_type=F32
    )
    masked = tpl_pad[...].T * mask[:1].astype(BF16)
    turned[...] = masked
    wide = masked.astype(F32)
    norm = jnp.sqrt(jnp.sum(wide * wide, keepdims=True) + EPSILON)
    live = jnp.sum(mask[:1], keepdims=True)
    rest = jnp.broadcast_to(jnp.sqrt(window * live) / norm, (1, LANES))
    extra = [jnp.zeros((1, LANES), F32)] * FINE
    for piece in range(3):
        extra[piece] = rest.astype(BF16).astype(F32)
        rest = rest - extra[piece]
    wide_flags = jnp.concatenate(
        [flags[:1], jnp.zeros((1, -stations % LANES), F32)], axis=1
    )
    for piece in range(wide_flags.shape[1] // LANES):
        extra[3 + piece] = wide_flags[:, piece * LANES : (piece + 1) * LANES]
    extra = jnp.concatenate(extra, axis=0).astype(BF16)
    my_tm = lax.axis_index("tm")
    spot = lax.broadcasted_iota(jnp.int32, (FINE, LANES), 1) // part
    for member in range(INNER):
        start = member * LANES
        pieces = []
        for step in range(window // (FINE * tm_count)):
            tile = jnp.zeros((FINE, LANES), F32)
            for within in range(tm_count):
                row = FINE * (step * tm_count + within)
                chunk = turned[row : row + FINE, start : start + LANES].astype(F32)
                turn = lax.rem(part * (within - my_tm) + LANES, LANES)
                tile = jnp.where(spot == within, pltpu.roll(chunk, turn, 1), tile)
            pieces.append(tile.astype(BF16))
        payload = jnp.concatenate(pieces + [extra], axis=0)
        for target in range(member, out_ref.shape[0], INNER):
            out_ref[target] = payload


def shift_kernel(waves_ref, halo_ref, out_ref, joined):
    group, part, slab = waves_ref.shape
    for member in range(group):
        joined[:, member * slab : (member + 1) * slab] = waves_ref[member].astype(F32)
    joined[:, group * slab :] = halo_ref[...].astype(F32)
    columns = joined.shape[1]
    for copy in range(LANES // FINE):
        rows = slice(copy * part, (copy + 1) * part)
        if copy == 0:
            out_ref[rows, :] = joined[...].astype(BF16)
        else:
            out_ref[rows, :] = pltpu.roll(joined[...], columns - FINE * copy, 1).astype(BF16)


def dots_kernel(tpls, shifts, out_ref, left, products):
    count = tpls.shape[0]
    group, _, slab = out_ref.shape
    per_half = left.shape[2] // LANES
    for template in range(count):
        row = template * FINE
        for step in range(2 * per_half):
            lane = (step % per_half) * LANES
            left[step // per_half, row : row + FINE, lane : lane + LANES] = tpls[
                template, FINE * step : FINE * (step + 1), :
            ]
    tiles = products.shape[0]
    span = (tiles - 1) * LANES
    per_block = span // slab

    def block(index, carry):
        start = pl.multiple_of(index * span, span)
        product = jnp.dot(
            left[0], shifts[:, pl.ds(start, span + LANES)], preferred_element_type=F32
        ) + jnp.dot(
            left[1],
            shifts[:, pl.ds(pl.multiple_of(start + LANES, LANES), span + LANES)],
            preferred_element_type=F32,
        )
        for tile in range(tiles):
            products[tile] = product[:, tile * LANES : (tile + 1) * LANES]

        def fine_rows(fine):
            return jnp.concatenate(
                [products[tile, pl.ds(fine, count, stride=FINE), :] for tile in range(tiles)],
                axis=1,
            )

        total = fine_rows(FINE - 1)
        for fine in reversed(range(FINE - 1)):
            total = fine_rows(fine) + pltpu.roll(total, span + LANES - 1, 1)
        for piece in range(per_block):
            out_ref[index * per_block + piece] = total[:, piece * slab : (piece + 1) * slab]
        return carry

    lax.fori_loop(0, group // per_block, block, 0)


def power_kernel(stations, wave_ref, tpls_ref, order_ref, out_ref, head_ref, scale_ref):
    extra = tpls_ref[:, tpls_ref.shape[1] - FINE :, :].astype(F32)
    scale_ref[...] = extra[:, 0, :] + extra[:, 1, :] + extra[:, 2, :]
    tiles = -(-stations // LANES)
    flags = jnp.concatenate([extra[:, 3 + tile, :] for tile in range(tiles)], axis=1)
    mask = jnp.dot(
        flags.astype(BF16),
        one_hot(order_ref[...], tiles * LANES),
        preferred_element_type=F32,
    ).astype(BF16)
    wave = wave_ref[...].astype(F32)
    squares = wave * wave
    high = squares.astype(BF16)
    low = (squares - high.astype(F32)).astype(BF16)
    power = jnp.dot(mask, high, preferred_element_type=F32) + jnp.dot(
        mask, low, preferred_element_type=F32
    )
    out_ref[...] = power
    head_ref[...] = power[:, : head_ref.shape[1]]


def factor_kernel(power_ref, halo_ref, scale_ref, out_ref, joined):
    slab, window = power_ref.shape[1], halo_ref.shape[1]
    joined[:, :slab] = power_ref[...]
    joined[:, slab:] = halo_ref[...]
    running = joined[...]
    columns = running.shape[1]
    width = 1
    while width < window:
        running = running + pltpu.roll(running, columns - width, 1)
        width *= 2
    out_ref[...] = scale_ref[:, :1] / jnp.sqrt(running[:, :slab] + EPSILON)


def finish_kernel(parts_ref, factor_ref, out_ref):
    out_ref[...] = jnp.sum(parts_ref[...], axis=0) * factor_ref[...]


def on_device(waveforms, templates, station_mask, channel_order):
    channels, slab = waveforms.shape
    rows, _, window = templates.shape
    stations = station_mask.shape[1]
    outer_count, tm_count = lax.axis_size("outer"), lax.axis_size("tm")
    blk_count = outer_count * INNER
    assert rows == 1 and LANES % tm_count == 0
    group = INNER * tm_count
    padded = INNER * LANES
    part = padded // group
    chunk = group * slab
    span = 2 * slab
    blk, members, every = ("outer", "inner"), ("inner", "tm"), ("outer", "inner", "tm")
    sds = jax.ShapeDtypeStruct
    order_row = channel_order[None, :]

    payload = call(
        functools.partial(template_kernel, tm_count),
        sds((blk_count, window * part // LANES + FINE, LANES), BF16),
        [
            pltpu.VMEM((padded, window), BF16),
            pltpu.VMEM((1, padded), jnp.int32),
            pltpu.VMEM((window, padded), BF16),
        ],
        bytes_accessed=channels * window * 2,
    )(templates, station_mask, order_row)
    tpls = lax.all_to_all(payload, blk, 0, 0, tiled=True)

    wave_parts = jnp.pad(waveforms, ((0, padded - channels), (0, 0)))
    waves = lax.all_to_all(wave_parts.reshape(group, part, slab), members, 0, 0, tiled=True)
    halo = lax.ppermute(
        waves[0, :, :window], "outer", [(b, b - 1) for b in range(1, outer_count)]
    )
    copies = LANES // FINE
    shifts = call(
        shift_kernel,
        sds((copies * part, chunk + window), BF16),
        [pltpu.VMEM((part, chunk + window), F32)],
        bytes_accessed=chunk * part * 2 * (copies + 1),
    )(waves, halo)

    power, power_head, scale = call(
        functools.partial(power_kernel, stations),
        [
            sds((blk_count, slab), F32),
            sds((blk_count, window), F32),
            sds((blk_count, LANES), F32),
        ],
        flops=4 * blk_count * channels * slab,
        bytes_accessed=channels * slab * 2,
    )(waveforms, tpls, order_row)
    total = blk_count * tm_count
    power_halo = lax.ppermute(power_head, every, [(i, i - 1) for i in range(1, total)])
    factor = call(
        factor_kernel,
        sds((blk_count, slab), F32),
        [pltpu.VMEM((blk_count, slab + window), F32)],
        bytes_accessed=blk_count * slab * 8,
    )(power, power_halo, scale)

    partials = call(
        dots_kernel,
        sds((group, blk_count, slab), F32),
        [
            pltpu.VMEM((2, blk_count * FINE, copies * part), BF16),
            pltpu.VMEM((span // LANES + 1, blk_count * FINE, LANES), F32),
        ],
        flops=2 * blk_count * window * part * chunk,
        bytes_accessed=copies * part * chunk * 2,
    )(tpls, shifts)
    sums = lax.all_to_all(partials, members, 0, 0, tiled=True)
    return call(
        finish_kernel, sds((blk_count, slab), F32), bytes_accessed=blk_count * slab * 4 * (group + 2)
    )(sums, factor)


def solution(mesh):
    blk_count, tm_count = mesh.devices.shape
    shape = (blk_count // INNER, INNER, tm_count)
    mesh = jax.sharding.Mesh(mesh.devices.reshape(shape), ("outer", "inner", "tm"))
    blk, every = ("outer", "inner"), ("outer", "inner", "tm")
    placed = (P(None, every), P(blk, None, None), P(blk, None), P())
    return jax.shard_map(
        on_device, mesh=mesh, in_specs=placed, out_specs=P(None, every), check_vma=False
    )
```

```python
import functools

import jax
import jax.numpy as jnp
from jax import lax
from jax.experimental import pallas as pl
from jax.experimental.pallas import tpu as pltpu
from jax.sharding import PartitionSpec as P

EPSILON = 1e-05
LANES = 128
INNER = 4
FINE = 16
VMEM_BYTES = 40 * 1024 * 1024

BF16 = jnp.bfloat16
F32 = jnp.float32


HBM = pl.BlockSpec(memory_space=pltpu.HBM)
VMEM = pl.BlockSpec(memory_space=pltpu.VMEM)
AFTER = pl.BlockSpec(memory_space=pl.ANY)


def call(kernel, in_specs, out_shape, scratch=(), flops=0, bytes_accessed=0):
    return pl.pallas_call(
        kernel,
        in_specs=in_specs,
        out_specs=jax.tree.map(lambda _: VMEM, out_shape),
        out_shape=out_shape,
        scratch_shapes=list(scratch),
        compiler_params=pltpu.CompilerParams(vmem_limit_bytes=VMEM_BYTES),
        cost_estimate=pl.CostEstimate(
            flops=flops, bytes_accessed=bytes_accessed, transcendentals=0
        ),
    )


def one_hot(order_row, station_count):
    columns = order_row.shape[1]
    first = 3 * lax.broadcasted_iota(jnp.int32, (station_count, columns), 0)
    hit = (order_row >= first) & (order_row < first + 3)
    return jnp.where(hit, 1.0, 0.0).astype(BF16)


def template_kernel(tm_count, tpl_hbm, flag_hbm, order_hbm, out_ref, *scratch):
    tpl_pad, flag_ref, order_ref, order_pad, turned, sems = scratch
    channels, window = tpl_hbm.shape[1:]
    copies = [
        pltpu.make_async_copy(flag_hbm, flag_ref, sems.at[0]),
        pltpu.make_async_copy(order_hbm, order_ref, sems.at[1]),
        pltpu.make_async_copy(tpl_hbm.at[0], tpl_pad.at[pl.ds(0, channels)], sems.at[2]),
    ]
    for copy in copies:
        copy.start()
    stations = flag_ref.shape[1]
    padded = tpl_pad.shape[0]
    part = LANES // tm_count
    tpl_pad[channels:, :] = jnp.zeros((padded - channels, window), BF16)
    order_pad[...] = jnp.full((1, padded), -1, jnp.int32)
    copies[0].wait()
    copies[1].wait()
    order_pad[:, :channels] = order_ref[...]
    flags = jnp.broadcast_to(flag_ref[...].astype(F32), (8, stations))
    mask = jnp.dot(
        flags.astype(BF16), one_hot(order_pad[...], stations), preferred_element_type=F32
    )
    copies[2].wait()
    masked = tpl_pad[...].T * mask[:1].astype(BF16)
    turned[...] = masked
    wide = masked.astype(F32)
    norm = jnp.sqrt(jnp.sum(wide * wide, keepdims=True) + EPSILON)
    live = jnp.sum(mask[:1], keepdims=True)
    rest = jnp.broadcast_to(jnp.sqrt(window * live) / norm, (1, LANES))
    extra = [jnp.zeros((1, LANES), F32)] * FINE
    for piece in range(3):
        extra[piece] = rest.astype(BF16).astype(F32)
        rest = rest - extra[piece]
    wide_flags = jnp.concatenate(
        [flags[:1], jnp.zeros((1, -stations % LANES), F32)], axis=1
    )
    for piece in range(wide_flags.shape[1] // LANES):
        extra[3 + piece] = wide_flags[:, piece * LANES : (piece + 1) * LANES]
    extra = jnp.concatenate(extra, axis=0).astype(BF16)
    my_tm = lax.axis_index("tm")
    spot = lax.broadcasted_iota(jnp.int32, (FINE, LANES), 1) // part
    for member in range(INNER):
        start = member * LANES
        pieces = []
        for step in range(window // (FINE * tm_count)):
            tile = jnp.zeros((FINE, LANES), F32)
            for within in range(tm_count):
                row = FINE * (step * tm_count + within)
                chunk = turned[row : row + FINE, start : start + LANES].astype(F32)
                turn = lax.rem(part * (within - my_tm) + LANES, LANES)
                tile = jnp.where(spot == within, pltpu.roll(chunk, turn, 1), tile)
            pieces.append(tile.astype(BF16))
        payload = jnp.concatenate(pieces + [extra], axis=0)
        for target in range(member, out_ref.shape[0], INNER):
            out_ref[target] = payload


def wave_kernel(wave_hbm, after, out_ref, sem):
    del after
    channels, slab = wave_hbm.shape
    copy = pltpu.make_async_copy(wave_hbm, out_ref.at[pl.ds(0, channels)], sem)
    copy.start()
    out_ref[channels:, :] = jnp.zeros((out_ref.shape[0] - channels, slab), BF16)
    copy.wait()


def shift_kernel(waves_ref, halo_ref, out_ref, joined):
    group, part, slab = waves_ref.shape
    for member in range(group):
        joined[:, member * slab : (member + 1) * slab] = waves_ref[member].astype(F32)
    joined[:, group * slab :] = halo_ref[...].astype(F32)
    columns = joined.shape[1]
    for copy in range(LANES // FINE):
        rows = slice(copy * part, (copy + 1) * part)
        if copy == 0:
            out_ref[rows, :] = joined[...].astype(BF16)
        else:
            out_ref[rows, :] = pltpu.roll(joined[...], columns - FINE * copy, 1).astype(BF16)


def dots_kernel(tpls, shifts, after, out_ref, left, products):
    del after
    count = tpls.shape[0]
    group, _, slab = out_ref.shape
    per_half = left.shape[2] // LANES
    for template in range(count):
        row = template * FINE
        for step in range(2 * per_half):
            lane = (step % per_half) * LANES
            left[step // per_half, row : row + FINE, lane : lane + LANES] = tpls[
                template, FINE * step : FINE * (step + 1), :
            ]
    tiles = products.shape[0]
    span = (tiles - 1) * LANES
    per_block = span // slab

    def block(index, carry):
        start = pl.multiple_of(index * span, span)
        product = jnp.dot(
            left[0], shifts[:, pl.ds(start, span + LANES)], preferred_element_type=F32
        ) + jnp.dot(
            left[1],
            shifts[:, pl.ds(pl.multiple_of(start + LANES, LANES), span + LANES)],
            preferred_element_type=F32,
        )
        for tile in range(tiles):
            products[tile] = product[:, tile * LANES : (tile + 1) * LANES]

        def fine_rows(fine):
            return jnp.concatenate(
                [products[tile, pl.ds(fine, count, stride=FINE), :] for tile in range(tiles)],
                axis=1,
            )

        total = fine_rows(FINE - 1)
        for fine in reversed(range(FINE - 1)):
            total = fine_rows(fine) + pltpu.roll(total, span + LANES - 1, 1)
        for piece in range(per_block):
            out_ref[index * per_block + piece] = total[:, piece * slab : (piece + 1) * slab]
        return carry

    lax.fori_loop(0, group // per_block, block, 0)


def power_kernel(stations, wave_ref, tpls_ref, order_ref, out_ref, head_ref, scale_ref):
    extra = tpls_ref[:, tpls_ref.shape[1] - FINE :, :].astype(F32)
    scale_ref[...] = extra[:, 0, :] + extra[:, 1, :] + extra[:, 2, :]
    tiles = -(-stations // LANES)
    flags = jnp.concatenate([extra[:, 3 + tile, :] for tile in range(tiles)], axis=1)
    mask = jnp.dot(
        flags.astype(BF16),
        one_hot(order_ref[...], tiles * LANES),
        preferred_element_type=F32,
    ).astype(BF16)
    wave = wave_ref[...].astype(F32)
    squares = wave * wave
    high = squares.astype(BF16)
    low = (squares - high.astype(F32)).astype(BF16)
    power = jnp.dot(mask, high, preferred_element_type=F32) + jnp.dot(
        mask, low, preferred_element_type=F32
    )
    out_ref[...] = power
    head_ref[...] = power[:, : head_ref.shape[1]]


def factor_kernel(power_ref, halo_ref, scale_ref, after, out_ref, joined):
    del after
    slab, window = power_ref.shape[1], halo_ref.shape[1]
    joined[:, :slab] = power_ref[...]
    joined[:, slab:] = halo_ref[...]
    running = joined[...]
    columns = running.shape[1]
    width = 1
    while width < window:
        running = running + pltpu.roll(running, columns - width, 1)
        width *= 2
    out_ref[...] = scale_ref[:, :1] / jnp.sqrt(running[:, :slab] + EPSILON)


def finish_kernel(parts_ref, factor_ref, out_ref):
    out_ref[...] = jnp.sum(parts_ref[...], axis=0) * factor_ref[...]


def on_device(waveforms, templates, station_mask, channel_order):
    channels, slab = waveforms.shape
    rows, _, window = templates.shape
    stations = station_mask.shape[1]
    outer_count, tm_count = lax.axis_size("outer"), lax.axis_size("tm")
    blk_count = outer_count * INNER
    assert rows == 1 and LANES % tm_count == 0
    group = INNER * tm_count
    padded = INNER * LANES
    part = padded // group
    chunk = group * slab
    span = 2 * slab
    blk, members, every = ("outer", "inner"), ("inner", "tm"), ("outer", "inner", "tm")
    sds = jax.ShapeDtypeStruct
    order_row = channel_order[None, :]

    payload = call(
        functools.partial(template_kernel, tm_count),
        [HBM] * 3,
        sds((blk_count, window * part // LANES + FINE, LANES), BF16),
        [
            pltpu.VMEM((padded, window), BF16),
            pltpu.VMEM((1, stations), jnp.int32),
            pltpu.VMEM((1, channels), jnp.int32),
            pltpu.VMEM((1, padded), jnp.int32),
            pltpu.VMEM((window, padded), BF16),
            pltpu.SemaphoreType.DMA((3,)),
        ],
        bytes_accessed=channels * window * 2,
    )(templates, station_mask, order_row)
    tpls = lax.all_to_all(payload, blk, 0, 0, tiled=True)

    wave_parts = call(
        wave_kernel,
        [HBM, AFTER],
        sds((padded, slab), BF16),
        [pltpu.SemaphoreType.DMA],
        bytes_accessed=channels * slab * 2,
    )(waveforms, payload)
    waves = lax.all_to_all(wave_parts.reshape(group, part, slab), members, 0, 0, tiled=True)
    halo = lax.ppermute(
        waves[0, :, :window], "outer", [(b, b - 1) for b in range(1, outer_count)]
    )
    copies = LANES // FINE
    shifts = call(
        shift_kernel,
        [VMEM] * 2,
        sds((copies * part, chunk + window), BF16),
        [pltpu.VMEM((part, chunk + window), F32)],
        bytes_accessed=chunk * part * 2 * (copies + 1),
    )(waves, halo)

    power, power_head, scale = call(
        functools.partial(power_kernel, stations),
        [VMEM] * 3,
        [
            sds((blk_count, slab), F32),
            sds((blk_count, window), F32),
            sds((blk_count, LANES), F32),
        ],
        flops=4 * blk_count * channels * slab,
        bytes_accessed=channels * slab * 2,
    )(waveforms, tpls, order_row)
    total = blk_count * tm_count
    power_halo = lax.ppermute(power_head, every, [(i, i - 1) for i in range(1, total)])
    partials = call(
        dots_kernel,
        [VMEM, VMEM, AFTER],
        sds((group, blk_count, slab), F32),
        [
            pltpu.VMEM((2, blk_count * FINE, copies * part), BF16),
            pltpu.VMEM((span // LANES + 1, blk_count * FINE, LANES), F32),
        ],
        flops=2 * blk_count * window * part * chunk,
        bytes_accessed=copies * part * chunk * 2,
    )(tpls, shifts, power_head)
    sums = lax.all_to_all(partials, members, 0, 0, tiled=True)
    factor = call(
        factor_kernel,
        [VMEM] * 3 + [AFTER],
        sds((blk_count, slab), F32),
        [pltpu.VMEM((blk_count, slab + window), F32)],
        bytes_accessed=blk_count * slab * 8,
    )(power, power_halo, scale, partials)
    return call(
        finish_kernel,
        [VMEM] * 2,
        sds((blk_count, slab), F32),
        bytes_accessed=blk_count * slab * 4 * (group + 2),
    )(sums, factor)


def solution(mesh):
    blk_count, tm_count = mesh.devices.shape
    shape = (blk_count // INNER, INNER, tm_count)
    mesh = jax.sharding.Mesh(mesh.devices.reshape(shape), ("outer", "inner", "tm"))
    blk, every = ("outer", "inner"), ("outer", "inner", "tm")
    placed = (P(None, every), P(blk, None, None), P(blk, None), P())
    return jax.shard_map(
        on_device, mesh=mesh, in_specs=placed, out_specs=P(None, every), check_vma=False
    )
```

```python
import functools

import jax
import jax.numpy as jnp
from jax import lax
from jax.experimental import pallas as pl
from jax.experimental.pallas import tpu as pltpu
from jax.sharding import PartitionSpec as P

EPSILON = 1e-05
LANES = 128
INNER = 4
META = 16
FINE = 16
MIB = 1024 * 1024

BF16 = jnp.bfloat16
F32 = jnp.float32


HBM = pl.BlockSpec(memory_space=pltpu.HBM)
VMEM = pl.BlockSpec(memory_space=pltpu.VMEM)
AFTER = pl.BlockSpec(memory_space=pl.ANY)


def call(kernel, in_specs, out_shape, scratch=(), flops=0, bytes_accessed=0, vmem=24):
    return pl.pallas_call(
        kernel,
        in_specs=in_specs,
        out_specs=jax.tree.map(lambda _: VMEM, out_shape),
        out_shape=out_shape,
        scratch_shapes=list(scratch),
        compiler_params=pltpu.CompilerParams(vmem_limit_bytes=vmem * MIB),
        cost_estimate=pl.CostEstimate(
            flops=flops, bytes_accessed=bytes_accessed, transcendentals=0
        ),
    )


def one_hot(order_row, station_count):
    columns = order_row.shape[1]
    first = 3 * lax.broadcasted_iota(jnp.int32, (station_count, columns), 0)
    hit = (order_row >= first) & (order_row < first + 3)
    return jnp.where(hit, 1.0, 0.0).astype(BF16)


def side_major(inner):
    return (inner % 2) * (INNER // 2) + inner // 2


def prologue_kernel(tm_count, tpl_hbm, flag_hbm, order_hbm, wave_hbm, *refs):
    out_ref, send_ref, keep_ref = refs[:3]
    tpl_pad, flag_ref, order_ref, order_pad, wave_pad, turned, sems = refs[3:]
    channels, window = tpl_hbm.shape[1:]
    copies = [
        pltpu.make_async_copy(flag_hbm, flag_ref, sems.at[0]),
        pltpu.make_async_copy(order_hbm, order_ref, sems.at[1]),
        pltpu.make_async_copy(tpl_hbm.at[0], tpl_pad.at[pl.ds(0, channels)], sems.at[2]),
        pltpu.make_async_copy(wave_hbm, wave_pad.at[pl.ds(0, channels)], sems.at[3]),
    ]
    for copy in copies:
        copy.start()
    stations = flag_ref.shape[1]
    padded = tpl_pad.shape[0]
    part = LANES // tm_count
    wave_pad[channels:, :] = jnp.zeros((padded - channels, wave_pad.shape[1]), BF16)
    tpl_pad[channels:, :] = jnp.zeros((padded - channels, window), BF16)
    order_pad[...] = jnp.full((1, padded), -1, jnp.int32)
    copies[0].wait()
    copies[1].wait()
    order_pad[:, :channels] = order_ref[...]
    flags = jnp.broadcast_to(flag_ref[...].astype(F32), (8, stations))
    mask = jnp.dot(
        flags.astype(BF16), one_hot(order_pad[...], stations), preferred_element_type=F32
    )
    copies[2].wait()
    masked = tpl_pad[...].T * mask[:1].astype(BF16)
    turned[...] = masked
    wide = masked.astype(F32)
    norm = jnp.sqrt(jnp.sum(wide * wide, keepdims=True) + EPSILON)
    live = jnp.sum(mask[:1], keepdims=True)
    rest = jnp.broadcast_to(jnp.sqrt(window * live) / norm, (1, LANES))
    extra = [jnp.zeros((1, LANES), F32)] * META
    for piece in range(3):
        extra[piece] = rest.astype(BF16).astype(F32)
        rest = rest - extra[piece]
    wide_flags = jnp.concatenate(
        [flags[:1], jnp.zeros((1, -stations % LANES), F32)], axis=1
    )
    for piece in range(wide_flags.shape[1] // LANES):
        extra[3 + piece] = wide_flags[:, piece * LANES : (piece + 1) * LANES]
    extra = jnp.concatenate(extra, axis=0).astype(BF16)
    my_tm = lax.axis_index("tm")
    spot = lax.broadcasted_iota(jnp.int32, (FINE, LANES), 1) // part
    for member in range(INNER):
        start = side_major(member) * LANES
        pieces = []
        for step in range(window // (FINE * tm_count)):
            tile = jnp.zeros((FINE, LANES), F32)
            for within in range(tm_count):
                row = FINE * (step * tm_count + within)
                chunk = turned[row : row + FINE, start : start + LANES].astype(F32)
                turn = lax.rem(part * (within - my_tm) + LANES, LANES)
                tile = jnp.where(spot == within, pltpu.roll(chunk, turn, 1), tile)
            pieces.append(tile.astype(BF16))
        payload = jnp.concatenate(pieces + [extra], axis=0)
        for target in range(member, out_ref.shape[0], INNER):
            out_ref[target] = payload
    copies[3].wait()
    core = lax.rem(lax.axis_index("inner"), 2)
    half = padded // 2
    keep_ref[...] = wave_pad[pl.ds(pl.multiple_of(core * half, half), half), :]
    send_ref[...] = wave_pad[pl.ds(pl.multiple_of((1 - core) * half, half), half), :]


def split_kernel(tm_count, keep_ref, got_ref, *outs):
    my_inner = lax.axis_index("inner")
    core = lax.rem(my_inner, 2)
    me = lax.div(my_inner, 2) * tm_count + lax.axis_index("tm")
    part = outs[0].shape[1]
    for flip, out_ref in enumerate(outs):
        rows = pl.ds(pl.multiple_of((me ^ flip) * part, part), part)
        out_ref[core] = keep_ref[rows, :]
        out_ref[1 - core] = got_ref[rows, :]


def join_kernel(tm_count, *refs):
    parts, out_ref, head_ref = refs[:-2], refs[-2], refs[-1]
    me = lax.div(lax.axis_index("inner"), 2) * tm_count + lax.axis_index("tm")
    slab = parts[0].shape[2]
    for flip, part in enumerate(parts):
        other = me ^ flip
        y, tm = lax.div(other, tm_count), lax.rem(other, tm_count)
        for core in range(2):
            place = (y * 2 + core) * tm_count + tm
            out_ref[:, pl.ds(pl.multiple_of(place * slab, slab), slab)] = part[core]
    head_ref[...] = out_ref[:, : head_ref.shape[1]]


def correlate(tpls, samples, out_ref, first, left, shifts, products):
    count = tpls.shape[0]
    slab = out_ref.shape[2]
    part, columns = samples.shape
    copies = shifts.shape[0] // part
    for copy in range(copies):
        turned = samples if copy == 0 else pltpu.roll(samples, columns - FINE * copy, 1)
        shifts[copy * part : (copy + 1) * part, :] = turned
    parts, _, depth = left.shape
    steps = depth // LANES
    for template in range(count):
        row = template * FINE
        for step in range(parts * steps):
            lane = (step % steps) * LANES
            left[step // steps, row : row + FINE, lane : lane + LANES] = tpls[
                template, FINE * step : FINE * (step + 1), :
            ]
    tiles = products.shape[0]
    span = (tiles - 1) * LANES
    per_block = span // slab

    def block(index, carry):
        start = pl.multiple_of(index * span, span)
        product = None
        for piece in range(parts):
            here = pl.ds(pl.multiple_of(start + piece * copies * FINE, LANES), span + LANES)
            term = jnp.dot(left[piece], shifts[:, here], preferred_element_type=F32)
            product = term if product is None else product + term
        for tile in range(tiles):
            products[tile] = product[:, tile * LANES : (tile + 1) * LANES]

        def fine_rows(fine):
            return jnp.concatenate(
                [products[tile, pl.ds(fine, count, stride=FINE), :] for tile in range(tiles)],
                axis=1,
            )

        total = fine_rows(FINE - 1)
        for fine in reversed(range(FINE - 1)):
            total = fine_rows(fine) + pltpu.roll(total, span + LANES - 1, 1)
        for piece in range(per_block):
            out_ref[first + index * per_block + piece] = total[:, piece * slab : (piece + 1) * slab]
        return carry

    blocks = (columns - 2 * LANES) // span
    lax.fori_loop(0, blocks, block, 0)


def first_dots_kernel(tpls, samples_ref, out_ref, left, shifts, products):
    columns = shifts.shape[1]
    correlate(tpls, samples_ref[:, :columns], out_ref, 0, left, shifts, products)


def last_dots_kernel(tpls, samples_ref, halo_ref, done_ref, after, out_ref, *scratch):
    del after
    rest = samples_ref.shape[1] + halo_ref.shape[1] - scratch[1].shape[1]
    samples = jnp.concatenate([samples_ref[:, rest:], halo_ref[...]], axis=1)
    first = done_ref.shape[0]
    out_ref[:first] = done_ref[...]
    correlate(tpls, samples, out_ref, first, *scratch)


def power_kernel(stations, wave_ref, tpls_ref, order_ref, out_ref, head_ref, scale_ref):
    extra = tpls_ref[:, tpls_ref.shape[1] - META :, :].astype(F32)
    scale_ref[...] = extra[:, 0, :] + extra[:, 1, :] + extra[:, 2, :]
    tiles = -(-stations // LANES)
    flags = jnp.concatenate([extra[:, 3 + tile, :] for tile in range(tiles)], axis=1)
    mask = jnp.dot(
        flags.astype(BF16),
        one_hot(order_ref[...], tiles * LANES),
        preferred_element_type=F32,
    ).astype(BF16)
    wave = wave_ref[...].astype(F32)
    squares = wave * wave
    high = squares.astype(BF16)
    low = (squares - high.astype(F32)).astype(BF16)
    power = jnp.dot(mask, high, preferred_element_type=F32) + jnp.dot(
        mask, low, preferred_element_type=F32
    )
    out_ref[...] = power
    head_ref[...] = power[:, : head_ref.shape[1]]


def factor_kernel(power_ref, halo_ref, scale_ref, after, out_ref, joined):
    del after
    slab, window = power_ref.shape[1], halo_ref.shape[1]
    joined[:, :slab] = power_ref[...]
    joined[:, slab:] = halo_ref[...]
    running = joined[...]
    columns = running.shape[1]
    width = 1
    while width < window:
        running = running + pltpu.roll(running, columns - width, 1)
        width *= 2
    out_ref[...] = scale_ref[:, :1] / jnp.sqrt(running[:, :slab] + EPSILON)


def finish_kernel(parts_ref, factor_ref, out_ref):
    out_ref[...] = jnp.sum(parts_ref[...], axis=0) * factor_ref[...]


def on_device(waveforms, templates, station_mask, channel_order):
    channels, slab = waveforms.shape
    rows, _, window = templates.shape
    stations = station_mask.shape[1]
    outer_count, tm_count = lax.axis_size("outer"), lax.axis_size("tm")
    blk_count = outer_count * INNER
    assert rows == 1 and LANES % tm_count == 0
    group = INNER * tm_count
    padded = INNER * LANES
    part = padded // group
    chunk = group * slab
    span = 2 * slab
    total = blk_count * tm_count
    blk, members, every = ("outer", "inner"), ("inner", "tm"), ("outer", "inner", "tm")
    sds = jax.ShapeDtypeStruct
    order_row = channel_order[None, :]

    payload, send, keep = call(
        functools.partial(prologue_kernel, tm_count),
        [HBM] * 4,
        [
            sds((blk_count, window * part // LANES + META, LANES), BF16),
            sds((padded // 2, slab), BF16),
            sds((padded // 2, slab), BF16),
        ],
        [
            pltpu.VMEM((padded, window), BF16),
            pltpu.VMEM((1, stations), jnp.int32),
            pltpu.VMEM((1, channels), jnp.int32),
            pltpu.VMEM((1, padded), jnp.int32),
            pltpu.VMEM((padded, slab), BF16),
            pltpu.VMEM((window, padded), BF16),
            pltpu.SemaphoreType.DMA((4,)),
        ],
        bytes_accessed=channels * (window + slab) * 2,
        vmem=60,
    )(templates, station_mask, order_row, waveforms)
    tpls = lax.all_to_all(payload, blk, 0, 0, tiled=True)

    got = lax.ppermute(send, "inner", [(b, b ^ 1) for b in range(INNER)])
    half = group // 2
    parts = call(
        functools.partial(split_kernel, tm_count),
        [VMEM] * 2,
        [sds((2, part, slab), BF16)] * half,
        bytes_accessed=padded * slab * 2,
    )(keep, got)
    waves = [parts[0]]
    for flip in range(1, half):
        y, tm = flip // tm_count, flip % tm_count
        route = [(i, i ^ (2 * tm_count * y + tm)) for i in range(total)]
        waves.append(lax.ppermute(parts[flip], every, route))
    samples, head = call(
        functools.partial(join_kernel, tm_count),
        [VMEM] * half,
        [sds((part, chunk), BF16), sds((part, window), BF16)],
        bytes_accessed=part * chunk * 4,
    )(*waves)
    halo = lax.ppermute(head, "outer", [(b, b - 1) for b in range(1, outer_count)])

    power, power_head, scale = call(
        functools.partial(power_kernel, stations),
        [VMEM] * 3,
        [
            sds((blk_count, slab), F32),
            sds((blk_count, window), F32),
            sds((blk_count, LANES), F32),
        ],
        flops=4 * blk_count * channels * slab,
        bytes_accessed=channels * slab * 2,
    )(waveforms, tpls, order_row)
    power_halo = lax.ppermute(power_head, every, [(i, i - 1) for i in range(1, total)])

    copies = max(LANES // FINE, tm_count)
    coarse = window // FINE

    def scratch(columns):
        return [
            pltpu.VMEM((coarse // copies, blk_count * FINE, copies * part), BF16),
            pltpu.VMEM((copies * part, columns), BF16),
            pltpu.VMEM((span // LANES + 1, blk_count * FINE, LANES), F32),
        ]

    blocks = group // 2
    work = 2 * blk_count * window * part * span
    partials = call(
        first_dots_kernel,
        [VMEM] * 2,
        sds((2 * (blocks - 1), blk_count, slab), F32),
        scratch((blocks - 1) * span + window),
        flops=work * (blocks - 1),
        bytes_accessed=part * chunk * 2,
    )(tpls, samples)
    partials = call(
        last_dots_kernel,
        [VMEM] * 4 + [AFTER],
        sds((group, blk_count, slab), F32),
        scratch(span + window),
        flops=work,
        bytes_accessed=part * chunk * 2,
    )(tpls, samples, halo, partials, power_halo)
    sums = lax.all_to_all(partials, members, 0, 0, tiled=True)
    factor = call(
        factor_kernel,
        [VMEM] * 3 + [AFTER],
        sds((blk_count, slab), F32),
        [pltpu.VMEM((blk_count, slab + window), F32)],
        bytes_accessed=blk_count * slab * 8,
    )(power, power_halo, scale, partials)
    return call(
        finish_kernel,
        [VMEM] * 2,
        sds((blk_count, slab), F32),
        bytes_accessed=blk_count * slab * 4 * (group + 2),
    )(sums, factor)


def solution(mesh):
    blk_count, tm_count = mesh.devices.shape
    shape = (blk_count // INNER, INNER, tm_count)
    mesh = jax.sharding.Mesh(mesh.devices.reshape(shape), ("outer", "inner", "tm"))
    blk, every = ("outer", "inner"), ("outer", "inner", "tm")
    placed = (P(None, every), P(blk, None, None), P(blk, None), P())
    return jax.shard_map(
        on_device, mesh=mesh, in_specs=placed, out_specs=P(None, every), check_vma=False
    )
```

```python
import functools

import jax
import jax.numpy as jnp
from jax import lax
from jax.experimental import pallas as pl
from jax.experimental.pallas import tpu as pltpu
from jax.sharding import PartitionSpec as P

EPSILON = 1e-05
LANES = 128
INNER = 4
META = 16
FINE = 16
MIB = 1024 * 1024

BF16 = jnp.bfloat16
F32 = jnp.float32


HBM = pl.BlockSpec(memory_space=pltpu.HBM)
VMEM = pl.BlockSpec(memory_space=pltpu.VMEM)
AFTER = pl.BlockSpec(memory_space=pl.ANY)


def call(kernel, in_specs, out_shape, scratch=(), flops=0, bytes_accessed=0, vmem=24):
    return pl.pallas_call(
        kernel,
        in_specs=in_specs,
        out_specs=jax.tree.map(lambda _: VMEM, out_shape),
        out_shape=out_shape,
        scratch_shapes=list(scratch),
        compiler_params=pltpu.CompilerParams(vmem_limit_bytes=vmem * MIB),
        cost_estimate=pl.CostEstimate(
            flops=flops, bytes_accessed=bytes_accessed, transcendentals=0
        ),
    )


def one_hot(order_row, station_count):
    columns = order_row.shape[1]
    first = 3 * lax.broadcasted_iota(jnp.int32, (station_count, columns), 0)
    hit = (order_row >= first) & (order_row < first + 3)
    return jnp.where(hit, 1.0, 0.0).astype(BF16)


def side_major(inner):
    return (inner % 2) * (INNER // 2) + inner // 2


def prologue_kernel(tm_count, tpl_hbm, flag_hbm, order_hbm, wave_hbm, *refs):
    out_ref, send_ref, keep_ref = refs[:3]
    tpl_pad, flag_ref, order_ref, order_pad, wave_pad, turned, sems = refs[3:]
    channels, window = tpl_hbm.shape[1:]
    copies = [
        pltpu.make_async_copy(flag_hbm, flag_ref, sems.at[0]),
        pltpu.make_async_copy(order_hbm, order_ref, sems.at[1]),
        pltpu.make_async_copy(tpl_hbm.at[0], tpl_pad.at[pl.ds(0, channels)], sems.at[2]),
        pltpu.make_async_copy(wave_hbm, wave_pad.at[pl.ds(0, channels)], sems.at[3]),
    ]
    for copy in copies:
        copy.start()
    stations = flag_ref.shape[1]
    padded = tpl_pad.shape[0]
    part = LANES // tm_count
    wave_pad[channels:, :] = jnp.zeros((padded - channels, wave_pad.shape[1]), BF16)
    tpl_pad[channels:, :] = jnp.zeros((padded - channels, window), BF16)
    order_pad[...] = jnp.full((1, padded), -1, jnp.int32)
    copies[0].wait()
    copies[1].wait()
    order_pad[:, :channels] = order_ref[...]
    flags = jnp.broadcast_to(flag_ref[...].astype(F32), (8, stations))
    mask = jnp.dot(
        flags.astype(BF16), one_hot(order_pad[...], stations), preferred_element_type=F32
    )
    copies[2].wait()
    masked = tpl_pad[...].T * mask[:1].astype(BF16)
    turned[...] = masked
    wide = masked.astype(F32)
    norm = jnp.sqrt(jnp.sum(wide * wide, keepdims=True) + EPSILON)
    live = jnp.sum(mask[:1], keepdims=True)
    rest = jnp.broadcast_to(jnp.sqrt(window * live) / norm, (1, LANES))
    extra = [jnp.zeros((1, LANES), F32)] * META
    for piece in range(3):
        extra[piece] = rest.astype(BF16).astype(F32)
        rest = rest - extra[piece]
    wide_flags = jnp.concatenate(
        [flags[:1], jnp.zeros((1, -stations % LANES), F32)], axis=1
    )
    for piece in range(wide_flags.shape[1] // LANES):
        extra[3 + piece] = wide_flags[:, piece * LANES : (piece + 1) * LANES]
    extra = jnp.concatenate(extra, axis=0).astype(BF16)
    my_tm = lax.axis_index("tm")
    spot = lax.broadcasted_iota(jnp.int32, (FINE, LANES), 1) // part
    for member in range(INNER):
        start = side_major(member) * LANES
        pieces = []
        for step in range(window // (FINE * tm_count)):
            tile = jnp.zeros((FINE, LANES), F32)
            for within in range(tm_count):
                row = FINE * (step * tm_count + within)
                chunk = turned[row : row + FINE, start : start + LANES].astype(F32)
                turn = lax.rem(part * (within - my_tm) + LANES, LANES)
                tile = jnp.where(spot == within, pltpu.roll(chunk, turn, 1), tile)
            pieces.append(tile.astype(BF16))
        payload = jnp.concatenate(pieces + [extra], axis=0)
        for target in range(member, out_ref.shape[0], INNER):
            out_ref[target] = payload
    copies[3].wait()
    core = lax.rem(lax.axis_index("inner"), 2)
    half = padded // 2
    keep_ref[...] = wave_pad[pl.ds(pl.multiple_of(core * half, half), half), :]
    send_ref[...] = wave_pad[pl.ds(pl.multiple_of((1 - core) * half, half), half), :]


def split_kernel(tm_count, keep_ref, got_ref, *outs):
    my_inner = lax.axis_index("inner")
    core = lax.rem(my_inner, 2)
    me = lax.div(my_inner, 2) * tm_count + lax.axis_index("tm")
    part = outs[0].shape[1]
    for flip, out_ref in enumerate(outs):
        rows = pl.ds(pl.multiple_of((me ^ flip) * part, part), part)
        out_ref[core] = keep_ref[rows, :]
        out_ref[1 - core] = got_ref[rows, :]


def join_kernel(tm_count, *refs):
    parts, out_ref, head_ref = refs[:-2], refs[-2], refs[-1]
    me = lax.div(lax.axis_index("inner"), 2) * tm_count + lax.axis_index("tm")
    slab = parts[0].shape[2]
    for flip, part in enumerate(parts):
        other = me ^ flip
        y, tm = lax.div(other, tm_count), lax.rem(other, tm_count)
        for core in range(2):
            place = (y * 2 + core) * tm_count + tm
            out_ref[:, pl.ds(pl.multiple_of(place * slab, slab), slab)] = part[core]
    head_ref[...] = out_ref[:, : head_ref.shape[1]]


def correlate(tpls, samples, out_ref, first, left, shifts, products):
    count = tpls.shape[0]
    slab = out_ref.shape[2]
    part, columns = samples.shape
    copies = shifts.shape[0] // part
    for copy in range(copies):
        turned = samples if copy == 0 else pltpu.roll(samples, columns - FINE * copy, 1)
        shifts[copy * part : (copy + 1) * part, :] = turned
    parts, _, depth = left.shape
    steps = depth // LANES
    for template in range(count):
        row = template * FINE
        for step in range(parts * steps):
            lane = (step % steps) * LANES
            left[step // steps, row : row + FINE, lane : lane + LANES] = tpls[
                template, FINE * step : FINE * (step + 1), :
            ]
    tiles = products.shape[0]
    span = (tiles - 1) * LANES
    per_block = span // slab

    def block(index, carry):
        start = pl.multiple_of(index * span, span)
        product = None
        for piece in range(parts):
            here = pl.ds(pl.multiple_of(start + piece * copies * FINE, LANES), span + LANES)
            term = jnp.dot(left[piece], shifts[:, here], preferred_element_type=F32)
            product = term if product is None else product + term
        for tile in range(tiles):
            products[tile] = product[:, tile * LANES : (tile + 1) * LANES]

        def fine_rows(fine):
            return jnp.concatenate(
                [products[tile, pl.ds(fine, count, stride=FINE), :] for tile in range(tiles)],
                axis=1,
            )

        total = fine_rows(FINE - 1)
        for fine in reversed(range(FINE - 1)):
            total = fine_rows(fine) + pltpu.roll(total, span + LANES - 1, 1)
        for piece in range(per_block):
            out_ref[first + index * per_block + piece] = total[:, piece * slab : (piece + 1) * slab]
        return carry

    blocks = (columns - 2 * LANES) // span
    lax.fori_loop(0, blocks, block, 0)


def first_dots_kernel(tpls, samples_ref, out_ref, left, shifts, products):
    columns = shifts.shape[1]
    correlate(tpls, samples_ref[:, :columns], out_ref, 0, left, shifts, products)


def last_dots_kernel(tpls, samples_ref, halo_ref, done_ref, after, *refs):
    del after
    keep_ref, send_ref, out_ref = refs[:3]
    scratch = refs[3:]
    rest = samples_ref.shape[1] + halo_ref.shape[1] - scratch[1].shape[1]
    samples = jnp.concatenate([samples_ref[:, rest:], halo_ref[...]], axis=1)
    first = done_ref.shape[0]
    out_ref[:first] = done_ref[...]
    correlate(tpls, samples, out_ref, first, *scratch)
    core = lax.rem(lax.axis_index("inner"), 2)
    half = keep_ref.shape[0]
    run = half // 2
    for y in range(2):
        for tm in range(run):
            keep_ref[y * run + tm] = out_ref[(2 * y + core) * run + tm]
            send_ref[y * run + tm] = out_ref[(2 * y + 1 - core) * run + tm]


def add_kernel(tm_count, keep_ref, got_ref, *outs):
    me = lax.div(lax.axis_index("inner"), 2) * tm_count + lax.axis_index("tm")
    for flip, out_ref in enumerate(outs):
        out_ref[...] = keep_ref[me ^ flip] + got_ref[me ^ flip]


def power_kernel(stations, wave_ref, tpls_ref, order_ref, out_ref, head_ref, scale_ref):
    extra = tpls_ref[:, tpls_ref.shape[1] - META :, :].astype(F32)
    scale_ref[...] = extra[:, 0, :] + extra[:, 1, :] + extra[:, 2, :]
    tiles = -(-stations // LANES)
    flags = jnp.concatenate([extra[:, 3 + tile, :] for tile in range(tiles)], axis=1)
    mask = jnp.dot(
        flags.astype(BF16),
        one_hot(order_ref[...], tiles * LANES),
        preferred_element_type=F32,
    ).astype(BF16)
    wave = wave_ref[...].astype(F32)
    squares = wave * wave
    high = squares.astype(BF16)
    low = (squares - high.astype(F32)).astype(BF16)
    power = jnp.dot(mask, high, preferred_element_type=F32) + jnp.dot(
        mask, low, preferred_element_type=F32
    )
    out_ref[...] = power
    head_ref[...] = power[:, : head_ref.shape[1]]


def factor_kernel(power_ref, halo_ref, scale_ref, after, out_ref, joined):
    del after
    slab, window = power_ref.shape[1], halo_ref.shape[1]
    joined[:, :slab] = power_ref[...]
    joined[:, slab:] = halo_ref[...]
    running = joined[...]
    columns = running.shape[1]
    width = 1
    while width < window:
        running = running + pltpu.roll(running, columns - width, 1)
        width *= 2
    out_ref[...] = scale_ref[:, :1] / jnp.sqrt(running[:, :slab] + EPSILON)


def finish_kernel(*refs):
    parts, factor_ref, out_ref = refs[:-2], refs[-2], refs[-1]
    total = parts[0][...]
    for part in parts[1:]:
        total = total + part[...]
    out_ref[...] = total * factor_ref[...]


def on_device(waveforms, templates, station_mask, channel_order):
    channels, slab = waveforms.shape
    rows, _, window = templates.shape
    stations = station_mask.shape[1]
    outer_count, tm_count = lax.axis_size("outer"), lax.axis_size("tm")
    blk_count = outer_count * INNER
    assert rows == 1 and LANES % tm_count == 0
    group = INNER * tm_count
    padded = INNER * LANES
    part = padded // group
    chunk = group * slab
    span = 2 * slab
    total = blk_count * tm_count
    blk, every = ("outer", "inner"), ("outer", "inner", "tm")
    sds = jax.ShapeDtypeStruct
    order_row = channel_order[None, :]

    payload, send, keep = call(
        functools.partial(prologue_kernel, tm_count),
        [HBM] * 4,
        [
            sds((blk_count, window * part // LANES + META, LANES), BF16),
            sds((padded // 2, slab), BF16),
            sds((padded // 2, slab), BF16),
        ],
        [
            pltpu.VMEM((padded, window), BF16),
            pltpu.VMEM((1, stations), jnp.int32),
            pltpu.VMEM((1, channels), jnp.int32),
            pltpu.VMEM((1, padded), jnp.int32),
            pltpu.VMEM((padded, slab), BF16),
            pltpu.VMEM((window, padded), BF16),
            pltpu.SemaphoreType.DMA((4,)),
        ],
        bytes_accessed=channels * (window + slab) * 2,
        vmem=60,
    )(templates, station_mask, order_row, waveforms)
    tpls = lax.all_to_all(payload, blk, 0, 0, tiled=True)

    got = lax.ppermute(send, "inner", [(b, b ^ 1) for b in range(INNER)])
    half = group // 2
    parts = call(
        functools.partial(split_kernel, tm_count),
        [VMEM] * 2,
        [sds((2, part, slab), BF16)] * half,
        bytes_accessed=padded * slab * 2,
    )(keep, got)

    def swap(part, flip):
        y, tm = flip // tm_count, flip % tm_count
        route = [(i, i ^ (2 * tm_count * y + tm)) for i in range(total)]
        return lax.ppermute(part, every, route)

    waves = [parts[0]] + [swap(parts[flip], flip) for flip in range(1, half)]
    samples, head = call(
        functools.partial(join_kernel, tm_count),
        [VMEM] * half,
        [sds((part, chunk), BF16), sds((part, window), BF16)],
        bytes_accessed=part * chunk * 4,
    )(*waves)
    halo = lax.ppermute(head, "outer", [(b, b - 1) for b in range(1, outer_count)])

    power, power_head, scale = call(
        functools.partial(power_kernel, stations),
        [VMEM] * 3,
        [
            sds((blk_count, slab), F32),
            sds((blk_count, window), F32),
            sds((blk_count, LANES), F32),
        ],
        flops=4 * blk_count * channels * slab,
        bytes_accessed=channels * slab * 2,
    )(waveforms, tpls, order_row)
    power_halo = lax.ppermute(power_head, every, [(i, i - 1) for i in range(1, total)])

    copies = max(LANES // FINE, tm_count)
    coarse = window // FINE

    def scratch(columns):
        return [
            pltpu.VMEM((coarse // copies, blk_count * FINE, copies * part), BF16),
            pltpu.VMEM((copies * part, columns), BF16),
            pltpu.VMEM((span // LANES + 1, blk_count * FINE, LANES), F32),
        ]

    blocks = group // 2
    work = 2 * blk_count * window * part * span
    partials = call(
        first_dots_kernel,
        [VMEM] * 2,
        sds((2 * (blocks - 1), blk_count, slab), F32),
        scratch((blocks - 1) * span + window),
        flops=work * (blocks - 1),
        bytes_accessed=part * chunk * 2,
    )(tpls, samples)
    keep, send = call(
        last_dots_kernel,
        [VMEM] * 4 + [AFTER],
        [sds((half, blk_count, slab), F32)] * 2,
        [pltpu.VMEM((group, blk_count, slab), F32)] + scratch(span + window),
        flops=work,
        bytes_accessed=part * chunk * 2,
    )(tpls, samples, halo, partials, power_halo)
    got = lax.ppermute(send, "inner", [(b, b ^ 1) for b in range(INNER)])
    factor = call(
        factor_kernel,
        [VMEM] * 3 + [AFTER],
        sds((blk_count, slab), F32),
        [pltpu.VMEM((blk_count, slab + window), F32)],
        bytes_accessed=blk_count * slab * 8,
    )(power, power_halo, scale, send)
    sums = call(
        functools.partial(add_kernel, tm_count),
        [VMEM] * 2,
        [sds((blk_count, slab), F32)] * half,
        bytes_accessed=blk_count * slab * 12 * half,
    )(keep, got)
    sums = [sums[0]] + [swap(sums[flip], flip) for flip in range(1, half)]
    return call(
        finish_kernel,
        [VMEM] * (half + 1),
        sds((blk_count, slab), F32),
        bytes_accessed=blk_count * slab * 4 * (half + 2),
    )(*sums, factor)


def solution(mesh):
    blk_count, tm_count = mesh.devices.shape
    shape = (blk_count // INNER, INNER, tm_count)
    mesh = jax.sharding.Mesh(mesh.devices.reshape(shape), ("outer", "inner", "tm"))
    blk, every = ("outer", "inner"), ("outer", "inner", "tm")
    placed = (P(None, every), P(blk, None, None), P(blk, None), P())
    return jax.shard_map(
        on_device, mesh=mesh, in_specs=placed, out_specs=P(None, every), check_vma=False
    )
```

```python
import functools

import jax
import jax.numpy as jnp
from jax import lax
from jax.experimental import pallas as pl
from jax.experimental.pallas import tpu as pltpu
from jax.sharding import PartitionSpec as P

EPSILON = 1e-05
LANES = 128
INNER = 4
META = 16
FINE = 16
MIB = 1024 * 1024

BF16 = jnp.bfloat16
F32 = jnp.float32


HBM = pl.BlockSpec(memory_space=pltpu.HBM)
VMEM = pl.BlockSpec(memory_space=pltpu.VMEM)
AFTER = pl.BlockSpec(memory_space=pl.ANY)


def call(kernel, in_specs, out_shape, scratch=(), flops=0, bytes_accessed=0, vmem=24):
    return pl.pallas_call(
        kernel,
        in_specs=in_specs,
        out_specs=jax.tree.map(lambda _: VMEM, out_shape),
        out_shape=out_shape,
        scratch_shapes=list(scratch),
        compiler_params=pltpu.CompilerParams(vmem_limit_bytes=vmem * MIB),
        cost_estimate=pl.CostEstimate(
            flops=flops, bytes_accessed=bytes_accessed, transcendentals=0
        ),
    )


def one_hot(order_row, station_count):
    columns = order_row.shape[1]
    first = 3 * lax.broadcasted_iota(jnp.int32, (station_count, columns), 0)
    hit = (order_row >= first) & (order_row < first + 3)
    return jnp.where(hit, 1.0, 0.0).astype(BF16)


def side_major(inner):
    return lax.rem(inner, 2) * (INNER // 2) + lax.div(inner, 2)


def prologue_kernel(tm_count, tpl_hbm, flag_hbm, order_hbm, wave_hbm, *refs):
    outs, send_ref, keep_ref = refs[:INNER], refs[INNER], refs[INNER + 1]
    tpl_pad, flag_ref, order_ref, order_pad, wave_pad, turned, sems = refs[INNER + 2 :]
    channels, window = tpl_hbm.shape[1:]
    copies = [
        pltpu.make_async_copy(flag_hbm, flag_ref, sems.at[0]),
        pltpu.make_async_copy(order_hbm, order_ref, sems.at[1]),
        pltpu.make_async_copy(tpl_hbm.at[0], tpl_pad.at[pl.ds(0, channels)], sems.at[2]),
        pltpu.make_async_copy(wave_hbm, wave_pad.at[pl.ds(0, channels)], sems.at[3]),
    ]
    for copy in copies:
        copy.start()
    stations = flag_ref.shape[1]
    padded = tpl_pad.shape[0]
    part = LANES // tm_count
    wave_pad[channels:, :] = jnp.zeros((padded - channels, wave_pad.shape[1]), BF16)
    tpl_pad[channels:, :] = jnp.zeros((padded - channels, window), BF16)
    order_pad[...] = jnp.full((1, padded), -1, jnp.int32)
    copies[0].wait()
    copies[1].wait()
    order_pad[:, :channels] = order_ref[...]
    flags = jnp.broadcast_to(flag_ref[...].astype(F32), (8, stations))
    mask = jnp.dot(
        flags.astype(BF16), one_hot(order_pad[...], stations), preferred_element_type=F32
    )
    copies[2].wait()
    masked = tpl_pad[...].T * mask[:1].astype(BF16)
    turned[...] = masked
    wide = masked.astype(F32)
    norm = jnp.sqrt(jnp.sum(wide * wide, keepdims=True) + EPSILON)
    live = jnp.sum(mask[:1], keepdims=True)
    rest = jnp.broadcast_to(jnp.sqrt(window * live) / norm, (1, LANES))
    extra = [jnp.zeros((1, LANES), F32)] * META
    for piece in range(3):
        extra[piece] = rest.astype(BF16).astype(F32)
        rest = rest - extra[piece]
    wide_flags = jnp.concatenate(
        [flags[:1], jnp.zeros((1, -stations % LANES), F32)], axis=1
    )
    for piece in range(wide_flags.shape[1] // LANES):
        extra[3 + piece] = wide_flags[:, piece * LANES : (piece + 1) * LANES]
    extra = jnp.concatenate(extra, axis=0).astype(BF16)
    my_tm = lax.axis_index("tm")
    spot = lax.broadcasted_iota(jnp.int32, (FINE, LANES), 1) // part
    inner = lax.axis_index("inner")
    for flip in range(INNER):
        start = pl.multiple_of(side_major(inner ^ flip) * LANES, LANES)
        for step in range(window // (FINE * tm_count)):
            tile = jnp.zeros((FINE, LANES), F32)
            for within in range(tm_count):
                row = FINE * (step * tm_count + within)
                chunk = turned[row : row + FINE, pl.ds(start, LANES)].astype(F32)
                turn = lax.rem(part * (within - my_tm) + LANES, LANES)
                tile = jnp.where(spot == within, pltpu.roll(chunk, turn, 1), tile)
            outs[flip][FINE * step : FINE * (step + 1), :] = tile.astype(BF16)
        outs[flip][window * part // LANES :, :] = extra
    copies[3].wait()
    core = lax.rem(inner, 2)
    half = padded // 2
    keep_ref[...] = wave_pad[pl.ds(pl.multiple_of(core * half, half), half), :]
    send_ref[...] = wave_pad[pl.ds(pl.multiple_of((1 - core) * half, half), half), :]


def pack_kernel(*refs):
    parts, out_ref = refs[:-1], refs[-1]
    inner = lax.axis_index("inner")
    for flip, part in enumerate(parts):
        out_ref[inner ^ flip] = part[...]


def split_kernel(tm_count, keep_ref, got_ref, *outs):
    my_inner = lax.axis_index("inner")
    core = lax.rem(my_inner, 2)
    me = lax.div(my_inner, 2) * tm_count + lax.axis_index("tm")
    part = outs[0].shape[1]
    for flip, out_ref in enumerate(outs):
        rows = pl.ds(pl.multiple_of((me ^ flip) * part, part), part)
        out_ref[core] = keep_ref[rows, :]
        out_ref[1 - core] = got_ref[rows, :]


def join_kernel(tm_count, *refs):
    parts, out_ref, head_ref = refs[:-2], refs[-2], refs[-1]
    me = lax.div(lax.axis_index("inner"), 2) * tm_count + lax.axis_index("tm")
    slab = parts[0].shape[2]
    for flip, part in enumerate(parts):
        other = me ^ flip
        y, tm = lax.div(other, tm_count), lax.rem(other, tm_count)
        for core in range(2):
            place = (y * 2 + core) * tm_count + tm
            out_ref[:, pl.ds(pl.multiple_of(place * slab, slab), slab)] = part[core]
    head_ref[...] = out_ref[:, : head_ref.shape[1]]


def correlate(tpls, samples, out_ref, first, left, shifts, products):
    slab = out_ref.shape[2]
    part, columns = samples.shape
    depth = left.shape[1]
    copies = LANES // FINE
    usable = columns - 2 * LANES
    for copy in range(depth // part):
        tile, turn = copy // copies * LANES, copy % copies * FINE
        turned = samples if turn == 0 else pltpu.roll(samples, columns - turn, 1)
        shifts[copy * part : (copy + 1) * part, :] = turned[:, tile : tile + usable + LANES]
    steps = depth // LANES
    outer = lax.axis_index("outer")
    for flip, pack in enumerate(tpls):
        for inner in range(INNER):
            row = pl.multiple_of(((outer ^ flip) * INNER + inner) * FINE, FINE)
            for step in range(steps):
                left[pl.ds(row, FINE), step * LANES : (step + 1) * LANES] = pack[
                    inner, FINE * step : FINE * (step + 1), :
                ]
    count = len(tpls) * INNER
    tiles = products.shape[0]
    span = (tiles - 1) * LANES
    per_block = span // slab

    def block(index, carry):
        start = pl.multiple_of(index * span, span)
        for tile in range(0, tiles, 2):
            width = min(2, tiles - tile)
            here = pl.ds(pl.multiple_of(start + tile * LANES, LANES), width * LANES)
            product = jnp.dot(left[...], shifts[:, here], preferred_element_type=F32)
            for piece in range(width):
                products[tile + piece] = product[:, piece * LANES : (piece + 1) * LANES]

        def fine_rows(fine):
            return jnp.concatenate(
                [products[tile, pl.ds(fine, count, stride=FINE), :] for tile in range(tiles)],
                axis=1,
            )

        total = fine_rows(FINE - 1)
        for fine in reversed(range(FINE - 1)):
            total = fine_rows(fine) + pltpu.roll(total, span + LANES - 1, 1)
        for piece in range(per_block):
            out_ref[first + index * per_block + piece] = total[:, piece * slab : (piece + 1) * slab]
        return carry

    lax.fori_loop(0, usable // span, block, 0)


def first_dots_kernel(count, *refs):
    tpls, samples_ref, out_ref, scratch = refs[:count], refs[count], refs[count + 1], refs[count + 2 :]
    columns = scratch[1].shape[1] + LANES
    correlate(tpls, samples_ref[:, :columns], out_ref, 0, *scratch)


def last_dots_kernel(count, *refs):
    tpls, (samples_ref, halo_ref, done_ref, _) = refs[:count], refs[count : count + 4]
    keep_ref, send_ref, out_ref = refs[count + 4 : count + 7]
    scratch = refs[count + 7 :]
    rest = samples_ref.shape[1] + halo_ref.shape[1] - scratch[1].shape[1] - LANES
    samples = jnp.concatenate([samples_ref[:, rest:], halo_ref[...]], axis=1)
    first = done_ref.shape[0]
    out_ref[:first] = done_ref[...]
    correlate(tpls, samples, out_ref, first, *scratch)
    core = lax.rem(lax.axis_index("inner"), 2)
    half = keep_ref.shape[0]
    run = half // 2
    for y in range(2):
        for tm in range(run):
            keep_ref[y * run + tm] = out_ref[(2 * y + core) * run + tm]
            send_ref[y * run + tm] = out_ref[(2 * y + 1 - core) * run + tm]


def add_kernel(tm_count, keep_ref, got_ref, *outs):
    me = lax.div(lax.axis_index("inner"), 2) * tm_count + lax.axis_index("tm")
    for flip, out_ref in enumerate(outs):
        out_ref[...] = keep_ref[me ^ flip] + got_ref[me ^ flip]


def power_kernel(stations, wave_ref, order_ref, *refs):
    tpls, (out_ref, head_ref, scale_ref, gathered) = refs[:-4], refs[-4:]
    outer = lax.axis_index("outer")
    for flip, pack in enumerate(tpls):
        place = pl.ds((outer ^ flip) * INNER, INNER)
        gathered[place] = pack[:, pack.shape[1] - META :, :].astype(F32)
    extra = gathered[...]
    scale_ref[...] = extra[:, 0, :] + extra[:, 1, :] + extra[:, 2, :]
    tiles = -(-stations // LANES)
    flags = jnp.concatenate([extra[:, 3 + tile, :] for tile in range(tiles)], axis=1)
    mask = jnp.dot(
        flags.astype(BF16),
        one_hot(order_ref[...], tiles * LANES),
        preferred_element_type=F32,
    ).astype(BF16)
    wave = wave_ref[...].astype(F32)
    squares = wave * wave
    high = squares.astype(BF16)
    low = (squares - high.astype(F32)).astype(BF16)
    power = jnp.dot(mask, high, preferred_element_type=F32) + jnp.dot(
        mask, low, preferred_element_type=F32
    )
    out_ref[...] = power
    head_ref[...] = power[:, : head_ref.shape[1]]


def factor_kernel(power_ref, halo_ref, scale_ref, after, out_ref, joined):
    del after
    slab, window = power_ref.shape[1], halo_ref.shape[1]
    joined[:, :slab] = power_ref[...]
    joined[:, slab:] = halo_ref[...]
    running = joined[...]
    columns = running.shape[1]
    width = 1
    while width < window:
        running = running + pltpu.roll(running, columns - width, 1)
        width *= 2
    out_ref[...] = scale_ref[:, :1] / jnp.sqrt(running[:, :slab] + EPSILON)


def finish_kernel(*refs):
    parts, factor_ref, out_ref = refs[:-2], refs[-2], refs[-1]
    total = parts[0][...]
    for part in parts[1:]:
        total = total + part[...]
    out_ref[...] = total * factor_ref[...]


def on_device(waveforms, templates, station_mask, channel_order):
    channels, slab = waveforms.shape
    group_rows, _, window = templates.shape
    stations = station_mask.shape[1]
    outer_count, tm_count = lax.axis_size("outer"), lax.axis_size("tm")
    blk_count = outer_count * INNER
    assert group_rows == 1 and LANES % tm_count == 0
    group = INNER * tm_count
    padded = INNER * LANES
    part = padded // group
    chunk = group * slab
    span = 2 * slab
    total = blk_count * tm_count
    every = ("outer", "inner", "tm")
    sds = jax.ShapeDtypeStruct
    order_row = channel_order[None, :]

    rows = window * part // LANES + META
    *pieces, send, keep = call(
        functools.partial(prologue_kernel, tm_count),
        [HBM] * 4,
        [
            *[sds((rows, LANES), BF16)] * INNER,
            sds((padded // 2, slab), BF16),
            sds((padded // 2, slab), BF16),
        ],
        [
            pltpu.VMEM((padded, window), BF16),
            pltpu.VMEM((1, stations), jnp.int32),
            pltpu.VMEM((1, channels), jnp.int32),
            pltpu.VMEM((1, padded), jnp.int32),
            pltpu.VMEM((padded, slab), BF16),
            pltpu.VMEM((window, padded), BF16),
            pltpu.SemaphoreType.DMA((4,)),
        ],
        bytes_accessed=channels * (window + slab) * 2,
        vmem=60,
    )(templates, station_mask, order_row, waveforms)

    plane = [pieces[0]] + [
        lax.ppermute(pieces[flip], "inner", [(b, b ^ flip) for b in range(INNER)])
        for flip in range(1, INNER)
    ]
    pack = call(pack_kernel, [VMEM] * INNER, sds((INNER, rows, LANES), BF16))(*plane)
    tpls = [pack] + [
        lax.ppermute(pack, "outer", [(b, b ^ flip) for b in range(outer_count)])
        for flip in range(1, outer_count)
    ]

    got = lax.ppermute(send, "inner", [(b, b ^ 1) for b in range(INNER)])
    half = group // 2
    parts = call(
        functools.partial(split_kernel, tm_count),
        [VMEM] * 2,
        [sds((2, part, slab), BF16)] * half,
        bytes_accessed=padded * slab * 2,
    )(keep, got)

    def swap(part, flip):
        y, tm = flip // tm_count, flip % tm_count
        route = [(i, i ^ (2 * tm_count * y + tm)) for i in range(total)]
        return lax.ppermute(part, every, route)

    waves = [parts[0]] + [swap(parts[flip], flip) for flip in range(1, half)]
    samples, head = call(
        functools.partial(join_kernel, tm_count),
        [VMEM] * half,
        [sds((part, chunk), BF16), sds((part, window), BF16)],
        bytes_accessed=part * chunk * 4,
    )(*waves)
    halo = lax.ppermute(head, "outer", [(b, b - 1) for b in range(1, outer_count)])

    power, power_head, scale = call(
        functools.partial(power_kernel, stations),
        [VMEM] * (outer_count + 2),
        [
            sds((blk_count, slab), F32),
            sds((blk_count, window), F32),
            sds((blk_count, LANES), F32),
        ],
        [pltpu.VMEM((blk_count, META, LANES), F32)],
        flops=4 * blk_count * channels * slab,
        bytes_accessed=channels * slab * 2,
    )(waveforms, order_row, *tpls)
    power_halo = lax.ppermute(power_head, every, [(i, i - 1) for i in range(1, total)])

    depth = window // FINE * part

    def scratch(columns):
        return [
            pltpu.VMEM((blk_count * FINE, depth), BF16),
            pltpu.VMEM((depth, columns + LANES), BF16),
            pltpu.VMEM((span // LANES + 1, blk_count * FINE, LANES), F32),
        ]

    blocks = group // 2
    work = 2 * blk_count * window * part * span
    partials = call(
        functools.partial(first_dots_kernel, outer_count),
        [VMEM] * (outer_count + 1),
        sds((2 * (blocks - 1), blk_count, slab), F32),
        scratch((blocks - 1) * span),
        flops=work * (blocks - 1),
        bytes_accessed=part * chunk * 2,
    )(*tpls, samples)
    keep, send = call(
        functools.partial(last_dots_kernel, outer_count),
        [VMEM] * (outer_count + 3) + [AFTER],
        [sds((half, blk_count, slab), F32)] * 2,
        [pltpu.VMEM((group, blk_count, slab), F32)] + scratch(span),
        flops=work,
        bytes_accessed=part * chunk * 2,
    )(*tpls, samples, halo, partials, power_halo)
    got = lax.ppermute(send, "inner", [(b, b ^ 1) for b in range(INNER)])
    factor = call(
        factor_kernel,
        [VMEM] * 3 + [AFTER],
        sds((blk_count, slab), F32),
        [pltpu.VMEM((blk_count, slab + window), F32)],
        bytes_accessed=blk_count * slab * 8,
    )(power, power_halo, scale, send)
    sums = call(
        functools.partial(add_kernel, tm_count),
        [VMEM] * 2,
        [sds((blk_count, slab), F32)] * half,
        bytes_accessed=blk_count * slab * 12 * half,
    )(keep, got)
    sums = [sums[0]] + [swap(sums[flip], flip) for flip in range(1, half)]
    return call(
        finish_kernel,
        [VMEM] * (half + 1),
        sds((blk_count, slab), F32),
        bytes_accessed=blk_count * slab * 4 * (half + 2),
    )(*sums, factor)


def solution(mesh):
    blk_count, tm_count = mesh.devices.shape
    shape = (blk_count // INNER, INNER, tm_count)
    mesh = jax.sharding.Mesh(mesh.devices.reshape(shape), ("outer", "inner", "tm"))
    blk, every = ("outer", "inner"), ("outer", "inner", "tm")
    placed = (P(None, every), P(blk, None, None), P(blk, None), P())
    return jax.shard_map(
        on_device, mesh=mesh, in_specs=placed, out_specs=P(None, every), check_vma=False
    )
```

```python
import functools

import jax
import jax.numpy as jnp
from jax import lax
from jax.experimental import pallas as pl
from jax.experimental.pallas import tpu as pltpu
from jax.sharding import PartitionSpec as P

EPSILON = 1e-05
LANES = 128
INNER = 4
META = 16
FINE = 16
MIB = 1024 * 1024

BF16 = jnp.bfloat16
F32 = jnp.float32


HBM = pl.BlockSpec(memory_space=pltpu.HBM)
VMEM = pl.BlockSpec(memory_space=pltpu.VMEM)


def call(kernel, in_specs, out_shape, scratch=(), flops=0, bytes_accessed=0, vmem=24):
    return pl.pallas_call(
        kernel,
        in_specs=in_specs,
        out_specs=jax.tree.map(lambda _: VMEM, out_shape),
        out_shape=out_shape,
        scratch_shapes=list(scratch),
        compiler_params=pltpu.CompilerParams(vmem_limit_bytes=vmem * MIB),
        cost_estimate=pl.CostEstimate(
            flops=flops, bytes_accessed=bytes_accessed, transcendentals=0
        ),
    )


def one_hot(order_row, station_count):
    columns = order_row.shape[1]
    first = 3 * lax.broadcasted_iota(jnp.int32, (station_count, columns), 0)
    hit = (order_row >= first) & (order_row < first + 3)
    return jnp.where(hit, 1.0, 0.0).astype(BF16)


def side_major(inner):
    return lax.rem(inner, 2) * (INNER // 2) + lax.div(inner, 2)


def prologue_kernel(tm_count, tpl_hbm, flag_hbm, order_hbm, wave_hbm, *refs):
    out_ref, send_ref, keep_ref = refs[:3]
    tpl_pad, flag_ref, order_ref, order_pad, wave_pad, turned, sems = refs[3:]
    channels, window = tpl_hbm.shape[1:]
    copies = [
        pltpu.make_async_copy(flag_hbm, flag_ref, sems.at[0]),
        pltpu.make_async_copy(order_hbm, order_ref, sems.at[1]),
        pltpu.make_async_copy(tpl_hbm.at[0], tpl_pad.at[pl.ds(0, channels)], sems.at[2]),
        pltpu.make_async_copy(wave_hbm, wave_pad.at[pl.ds(0, channels)], sems.at[3]),
    ]
    for copy in copies:
        copy.start()
    stations = flag_ref.shape[1]
    padded = tpl_pad.shape[0]
    part = LANES // tm_count
    wave_pad[channels:, :] = jnp.zeros((padded - channels, wave_pad.shape[1]), BF16)
    tpl_pad[channels:, :] = jnp.zeros((padded - channels, window), BF16)
    order_pad[...] = jnp.full((1, padded), -1, jnp.int32)
    copies[0].wait()
    copies[1].wait()
    order_pad[:, :channels] = order_ref[...]
    flags = jnp.broadcast_to(flag_ref[...].astype(F32), (8, stations))
    mask = jnp.dot(
        flags.astype(BF16), one_hot(order_pad[...], stations), preferred_element_type=F32
    )
    copies[2].wait()
    masked = tpl_pad[...].T * mask[:1].astype(BF16)
    turned[...] = masked
    wide = masked.astype(F32)
    norm = jnp.sqrt(jnp.sum(wide * wide, keepdims=True) + EPSILON)
    live = jnp.sum(mask[:1], keepdims=True)
    rest = jnp.broadcast_to(jnp.sqrt(window * live) / norm, (1, LANES))
    extra = [jnp.zeros((1, LANES), F32)] * META
    for piece in range(3):
        extra[piece] = rest.astype(BF16).astype(F32)
        rest = rest - extra[piece]
    wide_flags = jnp.concatenate(
        [flags[:1], jnp.zeros((1, -stations % LANES), F32)], axis=1
    )
    for piece in range(wide_flags.shape[1] // LANES):
        extra[3 + piece] = wide_flags[:, piece * LANES : (piece + 1) * LANES]
    extra = jnp.concatenate(extra, axis=0).astype(BF16)
    my_tm = lax.axis_index("tm")
    spot = lax.broadcasted_iota(jnp.int32, (FINE, LANES), 1) // part
    for member in range(INNER):
        start = (member % 2 * (INNER // 2) + member // 2) * LANES
        pieces = []
        for step in range(window // (FINE * tm_count)):
            tile = jnp.zeros((FINE, LANES), F32)
            for within in range(tm_count):
                row = FINE * (step * tm_count + within)
                chunk = turned[row : row + FINE, start : start + LANES].astype(F32)
                turn = lax.rem(part * (within - my_tm) + LANES, LANES)
                tile = jnp.where(spot == within, pltpu.roll(chunk, turn, 1), tile)
            pieces.append(tile.astype(BF16))
        payload = jnp.concatenate(pieces + [extra], axis=0)
        for target in range(member, out_ref.shape[0], INNER):
            out_ref[target] = payload
    copies[3].wait()
    core = lax.rem(lax.axis_index("inner"), 2)
    half = padded // 2
    keep_ref[...] = wave_pad[pl.ds(pl.multiple_of(core * half, half), half), :]
    send_ref[...] = wave_pad[pl.ds(pl.multiple_of((1 - core) * half, half), half), :]


def split_kernel(tm_count, keep_ref, got_ref, *outs):
    my_inner = lax.axis_index("inner")
    core = lax.rem(my_inner, 2)
    me = lax.div(my_inner, 2) * tm_count + lax.axis_index("tm")
    part = outs[0].shape[1]
    for flip, out_ref in enumerate(outs):
        rows = pl.ds(pl.multiple_of((me ^ flip) * part, part), part)
        out_ref[core] = keep_ref[rows, :]
        out_ref[1 - core] = got_ref[rows, :]


def join_kernel(tm_count, *refs):
    parts, out_ref, head_ref = refs[:-2], refs[-2], refs[-1]
    me = lax.div(lax.axis_index("inner"), 2) * tm_count + lax.axis_index("tm")
    slab = parts[0].shape[2]
    for flip, part in enumerate(parts):
        other = me ^ flip
        y, tm = lax.div(other, tm_count), lax.rem(other, tm_count)
        for core in range(2):
            place = (y * 2 + core) * tm_count + tm
            out_ref[:, pl.ds(pl.multiple_of(place * slab, slab), slab)] = part[core]
    head_ref[...] = out_ref[:, : head_ref.shape[1]]


def correlate(tpls, samples, out_ref, first, left, shifts, products):
    slab = out_ref.shape[2]
    part, columns = samples.shape
    size, depth = left.shape
    copies = LANES // FINE
    usable = columns - 2 * LANES
    for copy in range(depth // part):
        tile, turn = copy // copies * LANES, copy % copies * FINE
        turned = samples if turn == 0 else pltpu.roll(samples, columns - turn, 1)
        shifts[copy * part : (copy + 1) * part, :] = turned[:, tile : tile + usable + LANES]
    count = tpls.shape[0]
    row = lax.broadcasted_iota(jnp.int32, (size, size), 0)
    column = lax.broadcasted_iota(jnp.int32, (size, size), 1)
    source = lax.rem(row, count) * FINE + lax.div(row, count)
    order = jnp.where(column == source, 1.0, 0.0).astype(BF16)
    for step in range(depth // LANES):
        rows = tpls[:, FINE * step : FINE * (step + 1), :].reshape(size, LANES)
        left[:, step * LANES : (step + 1) * LANES] = jnp.dot(
            order, rows, preferred_element_type=F32
        ).astype(BF16)
    tiles = products.shape[1] // LANES
    span = (tiles - 1) * LANES
    per_block = span // slab

    def block(index, carry):
        start = pl.multiple_of(index * span, span)
        for tile in range(0, tiles, 2):
            width = min(2, tiles - tile) * LANES
            here = pl.ds(pl.multiple_of(start + tile * LANES, LANES), width)
            products[:, tile * LANES : tile * LANES + width] = jnp.dot(
                left[...], shifts[:, here], preferred_element_type=F32
            )
        total = products[(FINE - 1) * count :, :]
        for fine in reversed(range(FINE - 1)):
            total = products[fine * count : (fine + 1) * count, :] + pltpu.roll(
                total, span + LANES - 1, 1
            )
        for piece in range(per_block):
            out_ref[first + index * per_block + piece] = total[:, piece * slab : (piece + 1) * slab]
        return carry

    lax.fori_loop(0, usable // span, block, 0)


def first_dots_kernel(tpls, samples_ref, out_ref, left, shifts, products):
    columns = shifts.shape[1] + LANES
    correlate(tpls, samples_ref[:, :columns], out_ref, 0, left, shifts, products)


def last_dots_kernel(tpls, samples_ref, halo_ref, mask_ref, done_ref, *refs):
    keep_ref, send_ref, out_ref = refs[:3]
    scratch = refs[3:]
    first, slab = done_ref.shape[0], done_ref.shape[2]
    half = keep_ref.shape[0]
    run = half // 2
    core = lax.rem(lax.axis_index("inner"), 2)

    def powers(member, out):
        start = (member + 1) * slab
        if start < samples_ref.shape[1]:
            wave = samples_ref[:, start : start + halo_ref.shape[1]]
        else:
            wave = halo_ref[...]
        out[...] = masked_squares(mask_ref[...], wave)

    for y in range(2):
        for side in range(2):
            for tm in range(run):
                member = (2 * y + side) * run + tm
                for owner, out in ((core, keep_ref), (1 - core, send_ref)):

                    @pl.when(owner == side)
                    def _():
                        powers(member, out.at[y * run + tm, :, pl.ds(slab, halo_ref.shape[1])])

    rest = samples_ref.shape[1] + halo_ref.shape[1] - scratch[1].shape[1] - LANES
    samples = jnp.concatenate([samples_ref[:, rest:], halo_ref[...]], axis=1)
    out_ref[:first] = done_ref[...]
    correlate(tpls, samples, out_ref, first, *scratch)
    for y in range(2):
        for tm in range(run):
            keep_ref[y * run + tm, :, :slab] = out_ref[(2 * y + core) * run + tm]
            send_ref[y * run + tm, :, :slab] = out_ref[(2 * y + 1 - core) * run + tm]


def add_kernel(tm_count, keep_ref, got_ref, *outs):
    me = lax.div(lax.axis_index("inner"), 2) * tm_count + lax.axis_index("tm")
    for flip, out_ref in enumerate(outs):
        out_ref[...] = keep_ref[me ^ flip] + got_ref[me ^ flip]


def masked_squares(mask, wave):
    wave = wave.astype(F32)
    squares = wave * wave
    high = squares.astype(BF16)
    low = (squares - high.astype(F32)).astype(BF16)
    return jnp.dot(mask, high, preferred_element_type=F32) + jnp.dot(
        mask, low, preferred_element_type=F32
    )


def power_kernel(stations, tm_count, wave_ref, tpls_ref, order_ref, *refs):
    out_ref, scale_ref, mask_ref, order_pad = refs
    extra = tpls_ref[:, tpls_ref.shape[1] - META :, :].astype(F32)
    scale_ref[...] = extra[:, 0, :] + extra[:, 1, :] + extra[:, 2, :]
    tiles = -(-stations // LANES)
    flags = jnp.concatenate([extra[:, 3 + tile, :] for tile in range(tiles)], axis=1)
    channels = wave_ref.shape[0]
    padded = order_pad.shape[1]
    order_pad[...] = jnp.full((1, padded), -1, jnp.int32)
    order_pad[:, :channels] = order_ref[...]
    mask = jnp.dot(
        flags.astype(BF16),
        one_hot(order_pad[...], tiles * LANES),
        preferred_element_type=F32,
    )
    out_ref[...] = masked_squares(mask[:, :channels].astype(BF16), wave_ref[...])
    part = LANES // tm_count
    mine = side_major(lax.axis_index("inner")) * LANES + lax.axis_index("tm") * part
    mask_ref[...] = pltpu.roll(mask, lax.rem(padded - mine, padded), 1)[:, :part].astype(BF16)


def finish_kernel(*refs):
    parts, (power_ref, scale_ref, out_ref, joined) = refs[:-4], refs[-4:]
    slab = power_ref.shape[1]
    total = parts[0][...]
    for part in parts[1:]:
        total = total + part[...]
    joined[:, :slab] = power_ref[...]
    joined[:, slab:] = total[:, slab:]
    running = joined[...]
    columns = running.shape[1]
    width = 1
    while width < columns - slab:
        running = running + pltpu.roll(running, columns - width, 1)
        width *= 2
    out_ref[...] = total[:, :slab] * (scale_ref[:, :1] / jnp.sqrt(running[:, :slab] + EPSILON))


def on_device(waveforms, templates, station_mask, channel_order):
    channels, slab = waveforms.shape
    rows, _, window = templates.shape
    stations = station_mask.shape[1]
    outer_count, tm_count = lax.axis_size("outer"), lax.axis_size("tm")
    blk_count = outer_count * INNER
    assert rows == 1 and LANES % tm_count == 0
    group = INNER * tm_count
    padded = INNER * LANES
    part = padded // group
    chunk = group * slab
    span = 2 * slab
    total = blk_count * tm_count
    blk, every = ("outer", "inner"), ("outer", "inner", "tm")
    sds = jax.ShapeDtypeStruct
    order_row = channel_order[None, :]

    payload, send, keep = call(
        functools.partial(prologue_kernel, tm_count),
        [HBM] * 4,
        [
            sds((blk_count, window * part // LANES + META, LANES), BF16),
            sds((padded // 2, slab), BF16),
            sds((padded // 2, slab), BF16),
        ],
        [
            pltpu.VMEM((padded, window), BF16),
            pltpu.VMEM((1, stations), jnp.int32),
            pltpu.VMEM((1, channels), jnp.int32),
            pltpu.VMEM((1, padded), jnp.int32),
            pltpu.VMEM((padded, slab), BF16),
            pltpu.VMEM((window, padded), BF16),
            pltpu.SemaphoreType.DMA((4,)),
        ],
        bytes_accessed=channels * (window + slab) * 2,
        vmem=60,
    )(templates, station_mask, order_row, waveforms)
    tpls = lax.all_to_all(payload, blk, 0, 0, tiled=True)

    got = lax.ppermute(send, "inner", [(b, b ^ 1) for b in range(INNER)])
    half = group // 2
    parts = call(
        functools.partial(split_kernel, tm_count),
        [VMEM] * 2,
        [sds((2, part, slab), BF16)] * half,
        bytes_accessed=padded * slab * 2,
    )(keep, got)

    def swap(part, flip):
        y, tm = flip // tm_count, flip % tm_count
        route = [(i, i ^ (2 * tm_count * y + tm)) for i in range(total)]
        return lax.ppermute(part, every, route)

    waves = [parts[0]] + [swap(parts[flip], flip) for flip in range(1, half)]
    samples, head = call(
        functools.partial(join_kernel, tm_count),
        [VMEM] * half,
        [sds((part, chunk), BF16), sds((part, window), BF16)],
        bytes_accessed=part * chunk * 4,
    )(*waves)
    halo = lax.ppermute(head, "outer", [(b, b - 1) for b in range(1, outer_count)])

    power, scale, mask = call(
        functools.partial(power_kernel, stations, tm_count),
        [VMEM] * 3,
        [
            sds((blk_count, slab), F32),
            sds((blk_count, LANES), F32),
            sds((blk_count, part), BF16),
        ],
        [pltpu.VMEM((1, padded), jnp.int32)],
        flops=4 * blk_count * channels * slab,
        bytes_accessed=channels * slab * 2,
    )(waveforms, tpls, order_row)

    depth = window // FINE * part

    def scratch(columns):
        return [
            pltpu.VMEM((blk_count * FINE, depth), BF16),
            pltpu.VMEM((depth, columns + LANES), BF16),
            pltpu.VMEM((blk_count * FINE, span + LANES), F32),
        ]

    blocks = group // 2
    work = 2 * blk_count * window * part * span
    partials = call(
        first_dots_kernel,
        [VMEM] * 2,
        sds((2 * (blocks - 1), blk_count, slab), F32),
        scratch((blocks - 1) * span),
        flops=work * (blocks - 1),
        bytes_accessed=part * chunk * 2,
    )(tpls, samples)
    keep, send = call(
        last_dots_kernel,
        [VMEM] * 5,
        [sds((half, blk_count, slab + window), F32)] * 2,
        [pltpu.VMEM((group, blk_count, slab), F32)] + scratch(span),
        flops=work,
        bytes_accessed=part * chunk * 2,
    )(tpls, samples, halo, mask, partials)
    got = lax.ppermute(send, "inner", [(b, b ^ 1) for b in range(INNER)])
    sums = call(
        functools.partial(add_kernel, tm_count),
        [VMEM] * 2,
        [sds((blk_count, slab + window), F32)] * half,
        bytes_accessed=blk_count * slab * 12 * half,
    )(keep, got)
    sums = [sums[0]] + [swap(sums[flip], flip) for flip in range(1, half)]
    return call(
        finish_kernel,
        [VMEM] * (half + 2),
        sds((blk_count, slab), F32),
        [pltpu.VMEM((blk_count, slab + window), F32)],
        bytes_accessed=blk_count * slab * 4 * (half + 2),
    )(*sums, power, scale)


def solution(mesh):
    blk_count, tm_count = mesh.devices.shape
    shape = (blk_count // INNER, INNER, tm_count)
    mesh = jax.sharding.Mesh(mesh.devices.reshape(shape), ("outer", "inner", "tm"))
    blk, every = ("outer", "inner"), ("outer", "inner", "tm")
    placed = (P(None, every), P(blk, None, None), P(blk, None), P())
    return jax.shard_map(
        on_device, mesh=mesh, in_specs=placed, out_specs=P(None, every), check_vma=False
    )
```

```python
import functools

import jax
import jax.numpy as jnp
from jax import lax
from jax.experimental import pallas as pl
from jax.experimental.pallas import tpu as pltpu
from jax.sharding import PartitionSpec as P

EPSILON = 1e-05
LANES = 128
INNER = 4
META = 16
FINE = 16
MIB = 1024 * 1024

BF16 = jnp.bfloat16
F32 = jnp.float32


HBM = pl.BlockSpec(memory_space=pltpu.HBM)
VMEM = pl.BlockSpec(memory_space=pltpu.VMEM)


def call(kernel, in_specs, out_shape, scratch=(), flops=0, bytes_accessed=0, vmem=24):
    return pl.pallas_call(
        kernel,
        in_specs=in_specs,
        out_specs=jax.tree.map(lambda _: VMEM, out_shape),
        out_shape=out_shape,
        scratch_shapes=list(scratch),
        compiler_params=pltpu.CompilerParams(vmem_limit_bytes=vmem * MIB),
        cost_estimate=pl.CostEstimate(
            flops=flops, bytes_accessed=bytes_accessed, transcendentals=0
        ),
    )


def one_hot(order_row, station_count):
    columns = order_row.shape[1]
    first = 3 * lax.broadcasted_iota(jnp.int32, (station_count, columns), 0)
    hit = (order_row >= first) & (order_row < first + 3)
    return jnp.where(hit, 1.0, 0.0).astype(BF16)


def side_major(inner):
    return lax.rem(inner, 2) * (INNER // 2) + lax.div(inner, 2)


def prologue_kernel(tm_count, tpl_hbm, flag_hbm, order_hbm, wave_hbm, *refs):
    out_ref, send_ref, keep_ref = refs[:3]
    tpl_pad, flag_ref, order_ref, order_pad, wave_pad, turned, sems = refs[3:]
    channels, window = tpl_hbm.shape[1:]
    copies = [
        pltpu.make_async_copy(flag_hbm, flag_ref, sems.at[0]),
        pltpu.make_async_copy(order_hbm, order_ref, sems.at[1]),
        pltpu.make_async_copy(tpl_hbm.at[0], tpl_pad.at[pl.ds(0, channels)], sems.at[2]),
        pltpu.make_async_copy(wave_hbm, wave_pad.at[pl.ds(0, channels)], sems.at[3]),
    ]
    for copy in copies:
        copy.start()
    stations = flag_ref.shape[1]
    padded = tpl_pad.shape[0]
    part = LANES // tm_count
    wave_pad[channels:, :] = jnp.zeros((padded - channels, wave_pad.shape[1]), BF16)
    tpl_pad[channels:, :] = jnp.zeros((padded - channels, window), BF16)
    order_pad[...] = jnp.full((1, padded), -1, jnp.int32)
    copies[0].wait()
    copies[1].wait()
    order_pad[:, :channels] = order_ref[...]
    flags = jnp.broadcast_to(flag_ref[...].astype(F32), (8, stations))
    mask = jnp.dot(
        flags.astype(BF16), one_hot(order_pad[...], stations), preferred_element_type=F32
    )
    copies[2].wait()
    masked = tpl_pad[...].T * mask[:1].astype(BF16)
    turned[...] = masked
    wide = masked.astype(F32)
    norm = jnp.sqrt(jnp.sum(wide * wide, keepdims=True) + EPSILON)
    live = jnp.sum(mask[:1], keepdims=True)
    rest = jnp.broadcast_to(jnp.sqrt(window * live) / norm, (1, LANES))
    extra = [jnp.zeros((1, LANES), F32)] * META
    for piece in range(3):
        extra[piece] = rest.astype(BF16).astype(F32)
        rest = rest - extra[piece]
    wide_flags = jnp.concatenate(
        [flags[:1], jnp.zeros((1, -stations % LANES), F32)], axis=1
    )
    for piece in range(wide_flags.shape[1] // LANES):
        extra[3 + piece] = wide_flags[:, piece * LANES : (piece + 1) * LANES]
    extra = jnp.concatenate(extra, axis=0).astype(BF16)
    my_tm = lax.axis_index("tm")
    spot = lax.broadcasted_iota(jnp.int32, (FINE, LANES), 1) // part
    for member in range(INNER):
        start = (member % 2 * (INNER // 2) + member // 2) * LANES
        pieces = []
        for step in range(window // (FINE * tm_count)):
            tile = jnp.zeros((FINE, LANES), F32)
            for within in range(tm_count):
                row = FINE * (step * tm_count + within)
                chunk = turned[row : row + FINE, start : start + LANES].astype(F32)
                turn = lax.rem(part * (within - my_tm) + LANES, LANES)
                tile = jnp.where(spot == within, pltpu.roll(chunk, turn, 1), tile)
            pieces.append(tile.astype(BF16))
        payload = jnp.concatenate(pieces + [extra], axis=0)
        for target in range(member, out_ref.shape[0], INNER):
            out_ref[target] = payload
    copies[3].wait()
    core = lax.rem(lax.axis_index("inner"), 2)
    half = padded // 2
    keep_ref[...] = wave_pad[pl.ds(pl.multiple_of(core * half, half), half), :]
    send_ref[...] = wave_pad[pl.ds(pl.multiple_of((1 - core) * half, half), half), :]


def split_kernel(tm_count, keep_ref, got_ref, *outs):
    my_inner = lax.axis_index("inner")
    core = lax.rem(my_inner, 2)
    me = lax.div(my_inner, 2) * tm_count + lax.axis_index("tm")
    part = outs[0].shape[1]
    for flip, out_ref in enumerate(outs):
        rows = pl.ds(pl.multiple_of((me ^ flip) * part, part), part)
        out_ref[core] = keep_ref[rows, :]
        out_ref[1 - core] = got_ref[rows, :]


def join_kernel(tm_count, *refs):
    parts, out_ref, head_ref = refs[:-2], refs[-2], refs[-1]
    me = lax.div(lax.axis_index("inner"), 2) * tm_count + lax.axis_index("tm")
    slab = parts[0].shape[2]
    for flip, part in enumerate(parts):
        other = me ^ flip
        y, tm = lax.div(other, tm_count), lax.rem(other, tm_count)
        for core in range(2):
            place = (y * 2 + core) * tm_count + tm
            out_ref[:, pl.ds(pl.multiple_of(place * slab, slab), slab)] = part[core]
    head_ref[...] = out_ref[:, : head_ref.shape[1]]


def correlate(tpls, samples, out_ref, first, left, shifts, products):
    slab = out_ref.shape[2]
    part, columns = samples.shape
    size, depth = left.shape
    copies = LANES // FINE
    usable = columns - 2 * LANES
    for copy in range(depth // part):
        tile, turn = copy // copies * LANES, copy % copies * FINE
        turned = samples if turn == 0 else pltpu.roll(samples, columns - turn, 1)
        shifts[copy * part : (copy + 1) * part, :] = turned[:, tile : tile + usable + LANES]
    count = tpls.shape[0]
    row = lax.broadcasted_iota(jnp.int32, (size, size), 0)
    column = lax.broadcasted_iota(jnp.int32, (size, size), 1)
    source = lax.rem(row, count) * FINE + lax.div(row, count)
    order = jnp.where(column == source, 1.0, 0.0).astype(BF16)
    for step in range(depth // LANES):
        rows = tpls[:, FINE * step : FINE * (step + 1), :].reshape(size, LANES)
        left[:, step * LANES : (step + 1) * LANES] = jnp.dot(
            order, rows, preferred_element_type=F32
        ).astype(BF16)
    tiles = products.shape[2] // LANES
    span = (tiles - 1) * LANES
    per_block = span // slab
    blocks = usable // span

    def multiply(index, slot):
        start = pl.multiple_of(index * span, span)
        for tile in range(0, tiles, 2):
            width = min(2, tiles - tile) * LANES
            here = pl.ds(pl.multiple_of(start + tile * LANES, LANES), width)
            products[slot, :, tile * LANES : tile * LANES + width] = jnp.dot(
                left[...], shifts[:, here], preferred_element_type=F32
            )

    def gather(index, slot):
        def tree(first, number):
            if number == 1:
                return products[slot, first * count : (first + 1) * count, :]
            half = number // 2
            later = pltpu.roll(tree(first + half, half), span + LANES - half, 1)
            return tree(first, half) + later

        total = tree(0, FINE)
        for piece in range(per_block):
            out_ref[first + index * per_block + piece] = total[:, piece * slab : (piece + 1) * slab]

    multiply(0, 0)
    if blocks <= 4:
        for index in range(1, blocks):
            multiply(index, index % 2)
            gather(index - 1, (index - 1) % 2)
    else:

        def step(index, carry):
            multiply(index, lax.rem(index, 2))
            gather(index - 1, lax.rem(index + 1, 2))
            return carry

        lax.fori_loop(1, blocks, step, 0)
    gather(blocks - 1, (blocks - 1) % 2)


def first_dots_kernel(tpls, samples_ref, out_ref, left, shifts, products):
    columns = shifts.shape[1] + LANES
    correlate(tpls, samples_ref[:, :columns], out_ref, 0, left, shifts, products)


def last_dots_kernel(tpls, samples_ref, halo_ref, mask_ref, done_ref, *refs):
    keep_ref, send_ref, out_ref, edges = refs[:4]
    scratch = refs[4:]
    first, slab = done_ref.shape[0], done_ref.shape[2]
    group = edges.shape[0]
    window = halo_ref.shape[1]
    after = [samples_ref[:, (m + 1) * slab : (m + 1) * slab + window] for m in range(group - 1)]
    squares = masked_squares(mask_ref[...], jnp.concatenate(after + [halo_ref[...]], axis=1))
    column = lax.broadcasted_iota(jnp.int32, squares.shape, 1) % window
    reach = 1
    while reach < window:
        earlier = pltpu.roll(squares, reach, 1)
        squares = squares + jnp.where(column >= reach, earlier, 0.0)
        reach *= 2
    squares = jnp.where(column >= 1, pltpu.roll(squares, 1, 1), 0.0)
    for member in range(group):
        edges[member] = squares[:, member * window : (member + 1) * window]
    rest = samples_ref.shape[1] + window - scratch[1].shape[1] - LANES
    samples = jnp.concatenate([samples_ref[:, rest:], halo_ref[...]], axis=1)
    out_ref[:first] = done_ref[...]
    correlate(tpls, samples, out_ref, first, *scratch)
    core = lax.rem(lax.axis_index("inner"), 2)
    run = keep_ref.shape[0] // 2
    for y in range(2):
        for tm in range(run):
            for ref, side in ((keep_ref, core), (send_ref, 1 - core)):
                member = (2 * y + side) * run + tm
                ref[y * run + tm, :, :slab] = out_ref[member]
                ref[y * run + tm, :, slab:] = edges[member]


def add_kernel(tm_count, keep_ref, got_ref, *outs):
    me = lax.div(lax.axis_index("inner"), 2) * tm_count + lax.axis_index("tm")
    for flip, out_ref in enumerate(outs):
        out_ref[...] = keep_ref[me ^ flip] + got_ref[me ^ flip]


def masked_squares(mask, wave):
    wave = wave.astype(F32)
    squares = wave * wave
    high = squares.astype(BF16)
    low = (squares - high.astype(F32)).astype(BF16)
    return jnp.dot(mask, high, preferred_element_type=F32) + jnp.dot(
        mask, low, preferred_element_type=F32
    )


def power_kernel(stations, window, tm_count, wave_ref, tpls_ref, order_ref, *refs):
    out_ref, scale_ref, mask_ref, order_pad = refs
    extra = tpls_ref[:, tpls_ref.shape[1] - META :, :].astype(F32)
    scale_ref[...] = extra[:, 0, :] + extra[:, 1, :] + extra[:, 2, :]
    tiles = -(-stations // LANES)
    flags = jnp.concatenate([extra[:, 3 + tile, :] for tile in range(tiles)], axis=1)
    channels = wave_ref.shape[0]
    padded = order_pad.shape[1]
    order_pad[...] = jnp.full((1, padded), -1, jnp.int32)
    order_pad[:, :channels] = order_ref[...]
    mask = jnp.dot(
        flags.astype(BF16),
        one_hot(order_pad[...], tiles * LANES),
        preferred_element_type=F32,
    )
    power = masked_squares(mask[:, :channels].astype(BF16), wave_ref[...])
    columns = power.shape[1]
    column = lax.broadcasted_iota(jnp.int32, power.shape, 1)
    reach = 1
    while reach < window:
        later = pltpu.roll(power, columns - reach, 1)
        power = power + jnp.where(column < columns - reach, later, 0.0)
        reach *= 2
    out_ref[...] = power
    part = LANES // tm_count
    mine = side_major(lax.axis_index("inner")) * LANES + lax.axis_index("tm") * part
    mask_ref[...] = pltpu.roll(mask, lax.rem(padded - mine, padded), 1)[:, :part].astype(BF16)


def finish_kernel(*refs):
    parts, (power_ref, scale_ref, out_ref) = refs[:-3], refs[-3:]
    slab = power_ref.shape[1]
    total = parts[0][...]
    for part in parts[1:]:
        total = total + part[...]
    dots, edge = total[:, :slab], total[:, slab:]
    inside = slab - edge.shape[1]
    energy = jnp.concatenate(
        [power_ref[:, :inside], power_ref[:, inside:] + edge], axis=1
    )
    out_ref[...] = dots * (scale_ref[:, :1] / jnp.sqrt(energy + EPSILON))


def on_device(waveforms, templates, station_mask, channel_order):
    channels, slab = waveforms.shape
    rows, _, window = templates.shape
    stations = station_mask.shape[1]
    outer_count, tm_count = lax.axis_size("outer"), lax.axis_size("tm")
    blk_count = outer_count * INNER
    assert rows == 1 and LANES % tm_count == 0
    group = INNER * tm_count
    padded = INNER * LANES
    part = padded // group
    chunk = group * slab
    span = 2 * slab
    total = blk_count * tm_count
    blk, every = ("outer", "inner"), ("outer", "inner", "tm")
    sds = jax.ShapeDtypeStruct
    order_row = channel_order[None, :]

    payload, send, keep = call(
        functools.partial(prologue_kernel, tm_count),
        [HBM] * 4,
        [
            sds((blk_count, window * part // LANES + META, LANES), BF16),
            sds((padded // 2, slab), BF16),
            sds((padded // 2, slab), BF16),
        ],
        [
            pltpu.VMEM((padded, window), BF16),
            pltpu.VMEM((1, stations), jnp.int32),
            pltpu.VMEM((1, channels), jnp.int32),
            pltpu.VMEM((1, padded), jnp.int32),
            pltpu.VMEM((padded, slab), BF16),
            pltpu.VMEM((window, padded), BF16),
            pltpu.SemaphoreType.DMA((4,)),
        ],
        bytes_accessed=channels * (window + slab) * 2,
        vmem=60,
    )(templates, station_mask, order_row, waveforms)
    tpls = lax.all_to_all(payload, blk, 0, 0, tiled=True)

    got = lax.ppermute(send, "inner", [(b, b ^ 1) for b in range(INNER)])
    half = group // 2
    parts = call(
        functools.partial(split_kernel, tm_count),
        [VMEM] * 2,
        [sds((2, part, slab), BF16)] * half,
        bytes_accessed=padded * slab * 2,
    )(keep, got)

    def swap(part, flip):
        y, tm = flip // tm_count, flip % tm_count
        route = [(i, i ^ (2 * tm_count * y + tm)) for i in range(total)]
        return lax.ppermute(part, every, route)

    waves = [parts[0]] + [swap(parts[flip], flip) for flip in range(1, half)]
    samples, head = call(
        functools.partial(join_kernel, tm_count),
        [VMEM] * half,
        [sds((part, chunk), BF16), sds((part, window), BF16)],
        bytes_accessed=part * chunk * 4,
    )(*waves)
    halo = lax.ppermute(head, "outer", [(b, b - 1) for b in range(1, outer_count)])

    power, scale, mask = call(
        functools.partial(power_kernel, stations, window, tm_count),
        [VMEM] * 3,
        [
            sds((blk_count, slab), F32),
            sds((blk_count, LANES), F32),
            sds((blk_count, part), BF16),
        ],
        [pltpu.VMEM((1, padded), jnp.int32)],
        flops=4 * blk_count * channels * slab,
        bytes_accessed=channels * slab * 2,
    )(waveforms, tpls, order_row)

    depth = window // FINE * part

    def scratch(columns):
        return [
            pltpu.VMEM((blk_count * FINE, depth), BF16),
            pltpu.VMEM((depth, columns + LANES), BF16),
            pltpu.VMEM((2, blk_count * FINE, span + LANES), F32),
        ]

    blocks = group // 2
    work = 2 * blk_count * window * part * span
    partials = call(
        first_dots_kernel,
        [VMEM] * 2,
        sds((2 * (blocks - 1), blk_count, slab), F32),
        scratch((blocks - 1) * span),
        flops=work * (blocks - 1),
        bytes_accessed=part * chunk * 2,
    )(tpls, samples)
    keep, send = call(
        last_dots_kernel,
        [VMEM] * 5,
        [sds((half, blk_count, slab + window), F32)] * 2,
        [
            pltpu.VMEM((group, blk_count, slab), F32),
            pltpu.VMEM((group, blk_count, window), F32),
        ]
        + scratch(span),
        flops=work,
        bytes_accessed=part * chunk * 2,
    )(tpls, samples, halo, mask, partials)
    got = lax.ppermute(send, "inner", [(b, b ^ 1) for b in range(INNER)])
    sums = call(
        functools.partial(add_kernel, tm_count),
        [VMEM] * 2,
        [sds((blk_count, slab + window), F32)] * half,
        bytes_accessed=blk_count * slab * 12 * half,
    )(keep, got)
    sums = [sums[0]] + [swap(sums[flip], flip) for flip in range(1, half)]
    return call(
        finish_kernel,
        [VMEM] * (half + 2),
        sds((blk_count, slab), F32),
        bytes_accessed=blk_count * slab * 4 * (half + 2),
    )(*sums, power, scale)


def solution(mesh):
    blk_count, tm_count = mesh.devices.shape
    shape = (blk_count // INNER, INNER, tm_count)
    mesh = jax.sharding.Mesh(mesh.devices.reshape(shape), ("outer", "inner", "tm"))
    blk, every = ("outer", "inner"), ("outer", "inner", "tm")
    placed = (P(None, every), P(blk, None, None), P(blk, None), P())
    return jax.shard_map(
        on_device, mesh=mesh, in_specs=placed, out_specs=P(None, every), check_vma=False
    )
```

```python
import functools

import jax
import jax.numpy as jnp
from jax import lax
from jax.experimental import pallas as pl
from jax.experimental.pallas import tpu as pltpu
from jax.sharding import PartitionSpec as P

EPSILON = 1e-05
LANES = 128
INNER = 4
FINE = 16
MIB = 1024 * 1024

BF16 = jnp.bfloat16
F32 = jnp.float32


HBM = pl.BlockSpec(memory_space=pltpu.HBM)
VMEM = pl.BlockSpec(memory_space=pltpu.VMEM)
AFTER = pl.BlockSpec(memory_space=pl.ANY)


def call(kernel, in_specs, out_shape, scratch=(), flops=0, bytes_accessed=0, vmem=24):
    return pl.pallas_call(
        kernel,
        in_specs=in_specs,
        out_specs=jax.tree.map(lambda _: VMEM, out_shape),
        out_shape=out_shape,
        scratch_shapes=list(scratch),
        compiler_params=pltpu.CompilerParams(vmem_limit_bytes=vmem * MIB),
        cost_estimate=pl.CostEstimate(
            flops=flops, bytes_accessed=bytes_accessed, transcendentals=0
        ),
    )


def one_hot(order_row, station_count):
    columns = order_row.shape[1]
    first = 3 * lax.broadcasted_iota(jnp.int32, (station_count, columns), 0)
    hit = (order_row >= first) & (order_row < first + 3)
    return jnp.where(hit, 1.0, 0.0).astype(BF16)


def side_major(inner):
    return lax.rem(inner, 2) * (INNER // 2) + lax.div(inner, 2)


def regroup(channels, padded, part, transposed):
    real = part * channels // padded
    shape = (channels, padded) if transposed else (padded, channels)
    channel = lax.broadcasted_iota(jnp.int32, shape, 0 if transposed else 1)
    place = lax.broadcasted_iota(jnp.int32, shape, 1 if transposed else 0)
    within = place % part
    hit = (channel == lax.div(place, part) * real + within) & (within < real)
    return jnp.where(hit, 1.0, 0.0).astype(BF16)


def spare_lanes(part, real):
    slots = LANES // part * (part - real)
    slot = lax.broadcasted_iota(jnp.int32, (8, LANES), 0)
    lane = lax.broadcasted_iota(jnp.int32, (8, LANES), 1)
    home = lax.div(slot, part - real) * part + real + lax.rem(slot, part - real)
    return jnp.where((lane == home) & (slot < slots), 1.0, 0.0).astype(BF16)


def sample_kernel(part, wave_hbm, send_ref, keep_ref, wave_ref, grouped, sem):
    copy = pltpu.make_async_copy(wave_hbm, wave_ref, sem)
    copy.start()
    padded = grouped.shape[0]
    order = regroup(wave_ref.shape[0], padded, part, False)
    copy.wait()
    grouped[...] = jnp.dot(order, wave_ref[...], preferred_element_type=F32).astype(BF16)
    core = lax.rem(lax.axis_index("inner"), 2)
    half = padded // 2
    keep_ref[...] = grouped[pl.ds(pl.multiple_of(core * half, half), half), :]
    send_ref[...] = grouped[pl.ds(pl.multiple_of((1 - core) * half, half), half), :]


def template_kernel(tm_count, tpl_hbm, flag_hbm, order_hbm, after, out_ref, *scratch):
    del after
    tpl_ref, flag_ref, order_ref, turned, sems = scratch
    channels, window = tpl_hbm.shape[1:]
    copies = [
        pltpu.make_async_copy(flag_hbm, flag_ref, sems.at[0]),
        pltpu.make_async_copy(order_hbm, order_ref, sems.at[1]),
        pltpu.make_async_copy(tpl_hbm.at[0], tpl_ref, sems.at[2]),
    ]
    for copy in copies:
        copy.start()
    stations = flag_ref.shape[1]
    padded = turned.shape[1]
    part = LANES // tm_count
    rows = out_ref.shape[1]
    groups = regroup(channels, padded, part, True)
    copies[0].wait()
    copies[1].wait()
    flags = jnp.broadcast_to(flag_ref[...].astype(F32), (8, stations))
    mask = jnp.dot(
        flags.astype(BF16), one_hot(order_ref[...], stations), preferred_element_type=F32
    )
    live = jnp.sum(mask[:1], keepdims=True)
    mask = jnp.dot(mask.astype(BF16), groups, preferred_element_type=F32)[:1]
    copies[2].wait()
    masked = mask * lax.dot_general(
        tpl_ref[...], groups, (((0,), (0,)), ((), ())), preferred_element_type=F32
    )
    turned[...] = masked
    norm = jnp.sqrt(jnp.sum(masked * masked, keepdims=True) + EPSILON)
    rest = jnp.broadcast_to(jnp.sqrt(window * live) / norm, (1, rows))
    row = lax.broadcasted_iota(jnp.int32, (1, rows), 1)
    scale = jnp.zeros((1, rows), F32)
    for piece in range(3):
        now = rest.astype(BF16).astype(F32)
        scale = jnp.where(row == piece, now, scale)
        rest = rest - now
    slots = -(-stations // rows)
    wide = flags[:1]
    if stations % rows:
        wide = jnp.concatenate([wide, jnp.zeros((1, rows - stations % rows), F32)], axis=1)
    meta = [wide[:, slot * rows : (slot + 1) * rows] for slot in range(slots)] + [scale]
    meta = jnp.concatenate(meta + [jnp.zeros((8 - len(meta), rows), F32)], axis=0)
    meta = lax.dot_general(
        meta.astype(BF16),
        spare_lanes(part, part * channels // padded),
        (((0,), (0,)), ((), ())),
        preferred_element_type=F32,
    )
    my_tm = lax.axis_index("tm")
    spot = lax.broadcasted_iota(jnp.int32, (FINE, LANES), 1) // part
    for member in range(INNER):
        start = (member % 2 * (INNER // 2) + member // 2) * LANES
        pieces = []
        for step in range(window // (FINE * tm_count)):
            tile = jnp.zeros((FINE, LANES), F32)
            for within in range(tm_count):
                row = FINE * (step * tm_count + within)
                chunk = turned[row : row + FINE, start : start + LANES]
                turn = lax.rem(part * (within - my_tm) + LANES, LANES)
                tile = jnp.where(spot == within, pltpu.roll(chunk, turn, 1), tile)
            pieces.append(tile)
        payload = (jnp.concatenate(pieces, axis=0) + meta).astype(BF16)
        for target in range(member, out_ref.shape[0], INNER):
            out_ref[target] = payload


def split_kernel(tm_count, keep_ref, got_ref, *outs):
    my_inner = lax.axis_index("inner")
    core = lax.rem(my_inner, 2)
    me = lax.div(my_inner, 2) * tm_count + lax.axis_index("tm")
    part = outs[0].shape[1]
    for flip, out_ref in enumerate(outs):
        rows = pl.ds(pl.multiple_of((me ^ flip) * part, part), part)
        out_ref[core] = keep_ref[rows, :]
        out_ref[1 - core] = got_ref[rows, :]


def join_kernel(tm_count, *refs):
    parts, out_ref, head_ref = refs[:-2], refs[-2], refs[-1]
    me = lax.div(lax.axis_index("inner"), 2) * tm_count + lax.axis_index("tm")
    slab = parts[0].shape[2]
    for flip, part in enumerate(parts):
        other = me ^ flip
        y, tm = lax.div(other, tm_count), lax.rem(other, tm_count)
        for core in range(2):
            place = (y * 2 + core) * tm_count + tm
            out_ref[:, pl.ds(pl.multiple_of(place * slab, slab), slab)] = part[core]
    head_ref[...] = out_ref[:, : head_ref.shape[1]]


def correlate(tpls, samples, out_ref, first, left, shifts, products):
    slab = out_ref.shape[2]
    part, columns = samples.shape
    size, depth = left.shape
    copies = LANES // FINE
    usable = columns - 2 * LANES
    for copy in range(depth // part):
        tile, turn = copy // copies * LANES, copy % copies * FINE
        turned = samples if turn == 0 else pltpu.roll(samples, columns - turn, 1)
        shifts[copy * part : (copy + 1) * part, :] = turned[:, tile : tile + usable + LANES]
    count = tpls.shape[0]
    row = lax.broadcasted_iota(jnp.int32, (size, size), 0)
    column = lax.broadcasted_iota(jnp.int32, (size, size), 1)
    source = lax.rem(row, count) * FINE + lax.div(row, count)
    order = jnp.where(column == source, 1.0, 0.0).astype(BF16)
    for step in range(depth // LANES):
        rows = tpls[:, FINE * step : FINE * (step + 1), :].reshape(size, LANES)
        left[:, step * LANES : (step + 1) * LANES] = jnp.dot(
            order, rows, preferred_element_type=F32
        ).astype(BF16)
    tiles = products.shape[2] // LANES
    span = (tiles - 1) * LANES
    per_block = span // slab
    blocks = usable // span

    def multiply(index, slot):
        start = pl.multiple_of(index * span, span)
        for tile in range(0, tiles, 2):
            width = min(2, tiles - tile) * LANES
            here = pl.ds(pl.multiple_of(start + tile * LANES, LANES), width)
            products[slot, :, tile * LANES : tile * LANES + width] = jnp.dot(
                left[...], shifts[:, here], preferred_element_type=F32
            )

    def gather(index, slot):
        def tree(first, number):
            if number == 1:
                return products[slot, first * count : (first + 1) * count, :]
            half = number // 2
            later = pltpu.roll(tree(first + half, half), span + LANES - half, 1)
            return tree(first, half) + later

        total = tree(0, FINE)
        for piece in range(per_block):
            out_ref[first + index * per_block + piece] = total[:, piece * slab : (piece + 1) * slab]

    multiply(0, 0)
    if blocks <= 4:
        for index in range(1, blocks):
            multiply(index, index % 2)
            gather(index - 1, (index - 1) % 2)
    else:

        def step(index, carry):
            multiply(index, lax.rem(index, 2))
            gather(index - 1, lax.rem(index + 1, 2))
            return carry

        lax.fori_loop(1, blocks, step, 0)
    gather(blocks - 1, (blocks - 1) % 2)


def first_dots_kernel(tpls, samples_ref, out_ref, left, shifts, products):
    columns = shifts.shape[1] + LANES
    correlate(tpls, samples_ref[:, :columns], out_ref, 0, left, shifts, products)


def last_dots_kernel(tpls, samples_ref, halo_ref, mask_ref, done_ref, *refs):
    keep_ref, send_ref, out_ref, edges = refs[:4]
    scratch = refs[4:]
    first, slab = done_ref.shape[0], done_ref.shape[2]
    group = edges.shape[0]
    window = halo_ref.shape[1]
    after = [samples_ref[:, (m + 1) * slab : (m + 1) * slab + window] for m in range(group - 1)]
    squares = masked_squares(mask_ref[...], jnp.concatenate(after + [halo_ref[...]], axis=1))
    column = lax.broadcasted_iota(jnp.int32, squares.shape, 1) % window
    reach = 1
    while reach < window:
        earlier = pltpu.roll(squares, reach, 1)
        squares = squares + jnp.where(column >= reach, earlier, 0.0)
        reach *= 2
    squares = jnp.where(column >= 1, pltpu.roll(squares, 1, 1), 0.0)
    for member in range(group):
        edges[member] = squares[:, member * window : (member + 1) * window]
    rest = samples_ref.shape[1] + window - scratch[1].shape[1] - LANES
    samples = jnp.concatenate([samples_ref[:, rest:], halo_ref[...]], axis=1)
    out_ref[:first] = done_ref[...]
    correlate(tpls, samples, out_ref, first, *scratch)
    core = lax.rem(lax.axis_index("inner"), 2)
    run = keep_ref.shape[0] // 2
    for y in range(2):
        for tm in range(run):
            for ref, side in ((keep_ref, core), (send_ref, 1 - core)):
                member = (2 * y + side) * run + tm
                ref[y * run + tm, :, :slab] = out_ref[member]
                ref[y * run + tm, :, slab:] = edges[member]


def add_kernel(tm_count, keep_ref, got_ref, *outs):
    me = lax.div(lax.axis_index("inner"), 2) * tm_count + lax.axis_index("tm")
    for flip, out_ref in enumerate(outs):
        out_ref[...] = keep_ref[me ^ flip] + got_ref[me ^ flip]


def masked_squares(mask, wave):
    wave = wave.astype(F32)
    squares = wave * wave
    high = squares.astype(BF16)
    low = (squares - high.astype(F32)).astype(BF16)
    return jnp.dot(mask, high, preferred_element_type=F32) + jnp.dot(
        mask, low, preferred_element_type=F32
    )


def power_kernel(stations, window, tm_count, wave_ref, tpls_ref, order_ref, *refs):
    out_ref, scale_ref, mask_ref = refs
    count, rows, _ = tpls_ref.shape
    channels = wave_ref.shape[0]
    padded = INNER * LANES
    part = LANES // tm_count
    meta = lax.dot_general(
        spare_lanes(part, part * channels // padded),
        tpls_ref[...].reshape(count * rows, LANES),
        (((1,), (1,)), ((), ())),
        preferred_element_type=F32,
    )
    slots = -(-stations // rows)

    def read(slot):
        return jnp.concatenate(
            [meta[slot : slot + 1, t * rows : (t + 1) * rows] for t in range(count)], axis=0
        )

    scale = jnp.sum(read(slots)[:, :3], axis=1, keepdims=True)
    scale_ref[...] = jnp.broadcast_to(scale, scale_ref.shape)
    flags = jnp.concatenate([read(slot) for slot in range(slots)], axis=1)[:, :stations]
    mask = jnp.dot(
        flags.astype(BF16), one_hot(order_ref[...], stations), preferred_element_type=F32
    ).astype(BF16)
    power = masked_squares(mask, wave_ref[...])
    columns = power.shape[1]
    column = lax.broadcasted_iota(jnp.int32, power.shape, 1)
    reach = 1
    while reach < window:
        later = pltpu.roll(power, columns - reach, 1)
        power = power + jnp.where(column < columns - reach, later, 0.0)
        reach *= 2
    out_ref[...] = power
    mask = jnp.dot(
        mask, regroup(channels, padded, part, True), preferred_element_type=F32
    )
    mine = side_major(lax.axis_index("inner")) * LANES + lax.axis_index("tm") * part
    mask_ref[...] = pltpu.roll(mask, lax.rem(padded - mine, padded), 1)[:, :part].astype(BF16)


def finish_kernel(*refs):
    parts, (power_ref, scale_ref, out_ref) = refs[:-3], refs[-3:]
    slab = power_ref.shape[1]
    total = parts[0][...]
    for part in parts[1:]:
        total = total + part[...]
    dots, edge = total[:, :slab], total[:, slab:]
    inside = slab - edge.shape[1]
    energy = jnp.concatenate(
        [power_ref[:, :inside], power_ref[:, inside:] + edge], axis=1
    )
    out_ref[...] = dots * (scale_ref[:, :1] / jnp.sqrt(energy + EPSILON))


def on_device(waveforms, templates, station_mask, channel_order):
    channels, slab = waveforms.shape
    rows, _, window = templates.shape
    stations = station_mask.shape[1]
    outer_count, tm_count = lax.axis_size("outer"), lax.axis_size("tm")
    blk_count = outer_count * INNER
    assert rows == 1 and LANES % tm_count == 0
    group = INNER * tm_count
    padded = INNER * LANES
    part = padded // group
    chunk = group * slab
    span = 2 * slab
    total = blk_count * tm_count
    blk, every = ("outer", "inner"), ("outer", "inner", "tm")
    sds = jax.ShapeDtypeStruct
    order_row = channel_order[None, :]

    send, keep = call(
        functools.partial(sample_kernel, part),
        [HBM],
        [sds((padded // 2, slab), BF16)] * 2,
        [
            pltpu.VMEM((channels, slab), BF16),
            pltpu.VMEM((padded, slab), BF16),
            pltpu.SemaphoreType.DMA,
        ],
        bytes_accessed=channels * slab * 2,
        vmem=60,
    )(waveforms)
    payload = call(
        functools.partial(template_kernel, tm_count),
        [HBM] * 3 + [AFTER],
        sds((blk_count, window * part // LANES, LANES), BF16),
        [
            pltpu.VMEM((channels, window), BF16),
            pltpu.VMEM((1, stations), jnp.int32),
            pltpu.VMEM((1, channels), jnp.int32),
            pltpu.VMEM((window, padded), F32),
            pltpu.SemaphoreType.DMA((3,)),
        ],
        bytes_accessed=channels * window * 2,
        vmem=60,
    )(templates, station_mask, order_row, keep)
    tpls = lax.all_to_all(payload, blk, 0, 0, tiled=True)

    got = lax.ppermute(send, "inner", [(b, b ^ 1) for b in range(INNER)])
    half = group // 2
    parts = call(
        functools.partial(split_kernel, tm_count),
        [VMEM] * 2,
        [sds((2, part, slab), BF16)] * half,
        bytes_accessed=padded * slab * 2,
    )(keep, got)

    def swap(part, flip):
        y, tm = flip // tm_count, flip % tm_count
        route = [(i, i ^ (2 * tm_count * y + tm)) for i in range(total)]
        return lax.ppermute(part, every, route)

    waves = [parts[0]] + [swap(parts[flip], flip) for flip in range(1, half)]
    samples, head = call(
        functools.partial(join_kernel, tm_count),
        [VMEM] * half,
        [sds((part, chunk), BF16), sds((part, window), BF16)],
        bytes_accessed=part * chunk * 4,
    )(*waves)
    halo = lax.ppermute(head, "outer", [(b, b - 1) for b in range(1, outer_count)])

    power, scale, mask = call(
        functools.partial(power_kernel, stations, window, tm_count),
        [VMEM] * 3,
        [
            sds((blk_count, slab), F32),
            sds((blk_count, LANES), F32),
            sds((blk_count, part), BF16),
        ],
        flops=4 * blk_count * channels * slab,
        bytes_accessed=channels * slab * 2,
    )(waveforms, tpls, order_row)

    depth = window // FINE * part

    def scratch(columns):
        return [
            pltpu.VMEM((blk_count * FINE, depth), BF16),
            pltpu.VMEM((depth, columns + LANES), BF16),
            pltpu.VMEM((2, blk_count * FINE, span + LANES), F32),
        ]

    blocks = group // 2
    work = 2 * blk_count * window * part * span
    partials = call(
        first_dots_kernel,
        [VMEM] * 2,
        sds((2 * (blocks - 1), blk_count, slab), F32),
        scratch((blocks - 1) * span),
        flops=work * (blocks - 1),
        bytes_accessed=part * chunk * 2,
    )(tpls, samples)
    keep, send = call(
        last_dots_kernel,
        [VMEM] * 5,
        [sds((half, blk_count, slab + window), F32)] * 2,
        [
            pltpu.VMEM((group, blk_count, slab), F32),
            pltpu.VMEM((group, blk_count, window), F32),
        ]
        + scratch(span),
        flops=work,
        bytes_accessed=part * chunk * 2,
    )(tpls, samples, halo, mask, partials)
    got = lax.ppermute(send, "inner", [(b, b ^ 1) for b in range(INNER)])
    sums = call(
        functools.partial(add_kernel, tm_count),
        [VMEM] * 2,
        [sds((blk_count, slab + window), F32)] * half,
        bytes_accessed=blk_count * slab * 12 * half,
    )(keep, got)
    sums = [sums[0]] + [swap(sums[flip], flip) for flip in range(1, half)]
    return call(
        finish_kernel,
        [VMEM] * (half + 2),
        sds((blk_count, slab), F32),
        bytes_accessed=blk_count * slab * 4 * (half + 2),
    )(*sums, power, scale)


def solution(mesh):
    blk_count, tm_count = mesh.devices.shape
    shape = (blk_count // INNER, INNER, tm_count)
    mesh = jax.sharding.Mesh(mesh.devices.reshape(shape), ("outer", "inner", "tm"))
    blk, every = ("outer", "inner"), ("outer", "inner", "tm")
    placed = (P(None, every), P(blk, None, None), P(blk, None), P())
    return jax.shard_map(
        on_device, mesh=mesh, in_specs=placed, out_specs=P(None, every), check_vma=False
    )
```

```python
import functools

import jax
import jax.numpy as jnp
from jax import lax
from jax.experimental import pallas as pl
from jax.experimental.pallas import tpu as pltpu
from jax.sharding import PartitionSpec as P

EPSILON = 1e-05
LANES = 128
INNER = 4
FINE = 16
MIB = 1024 * 1024

BF16 = jnp.bfloat16
F32 = jnp.float32


HBM = pl.BlockSpec(memory_space=pltpu.HBM)
VMEM = pl.BlockSpec(memory_space=pltpu.VMEM)
AFTER = pl.BlockSpec(memory_space=pl.ANY)


def call(kernel, in_specs, out_shape, scratch=(), flops=0, bytes_accessed=0, vmem=24):
    return pl.pallas_call(
        kernel,
        in_specs=in_specs,
        out_specs=jax.tree.map(lambda _: VMEM, out_shape),
        out_shape=out_shape,
        scratch_shapes=list(scratch),
        compiler_params=pltpu.CompilerParams(vmem_limit_bytes=vmem * MIB),
        cost_estimate=pl.CostEstimate(
            flops=flops, bytes_accessed=bytes_accessed, transcendentals=0
        ),
    )


def one_hot(order_row, station_count):
    columns = order_row.shape[1]
    first = 3 * lax.broadcasted_iota(jnp.int32, (station_count, columns), 0)
    hit = (order_row >= first) & (order_row < first + 3)
    return jnp.where(hit, 1.0, 0.0).astype(BF16)


def side_major(inner):
    return lax.rem(inner, 2) * (INNER // 2) + lax.div(inner, 2)


def regroup(channels, padded, part, transposed):
    real = part * channels // padded
    shape = (channels, padded) if transposed else (padded, channels)
    channel = lax.broadcasted_iota(jnp.int32, shape, 0 if transposed else 1)
    place = lax.broadcasted_iota(jnp.int32, shape, 1 if transposed else 0)
    within = place % part
    hit = (channel == lax.div(place, part) * real + within) & (within < real)
    return jnp.where(hit, 1.0, 0.0).astype(BF16)


def spare_lanes(part, real):
    slots = LANES // part * (part - real)
    slot = lax.broadcasted_iota(jnp.int32, (8, LANES), 0)
    lane = lax.broadcasted_iota(jnp.int32, (8, LANES), 1)
    home = lax.div(slot, part - real) * part + real + lax.rem(slot, part - real)
    return jnp.where((lane == home) & (slot < slots), 1.0, 0.0).astype(BF16)


def prologue_kernel(tm_count, wave_hbm, tpl_hbm, flag_hbm, order_hbm, *refs):
    send_ref, samples_ref, tpls_ref = refs[:3]
    wave_ref, grouped, tpl_ref, flag_ref, order_ref, turned, sems = refs[3:]
    channels, window = tpl_hbm.shape[1:]
    copies = [
        pltpu.make_async_copy(flag_hbm, flag_ref, sems.at[0]),
        pltpu.make_async_copy(order_hbm, order_ref, sems.at[1]),
        pltpu.make_async_copy(tpl_hbm.at[0], tpl_ref, sems.at[2]),
        pltpu.make_async_copy(wave_hbm, wave_ref, sems.at[3]),
    ]
    for copy in copies:
        copy.start()
    stations = flag_ref.shape[1]
    padded = turned.shape[1]
    part = LANES // tm_count
    rows = tpls_ref.shape[1]
    groups = regroup(channels, padded, part, True)
    order = regroup(channels, padded, part, False)
    copies[0].wait()
    copies[1].wait()
    flags = jnp.broadcast_to(flag_ref[...].astype(F32), (8, stations))
    mask = jnp.dot(
        flags.astype(BF16), one_hot(order_ref[...], stations), preferred_element_type=F32
    )
    live = jnp.sum(mask[:1], keepdims=True)
    mask = jnp.dot(mask.astype(BF16), groups, preferred_element_type=F32)[:1]
    copies[2].wait()
    masked = mask * lax.dot_general(
        tpl_ref[...], groups, (((0,), (0,)), ((), ())), preferred_element_type=F32
    )
    turned[...] = masked
    norm = jnp.sqrt(jnp.sum(masked * masked, keepdims=True) + EPSILON)
    rest = jnp.broadcast_to(jnp.sqrt(window * live) / norm, (1, rows))
    row = lax.broadcasted_iota(jnp.int32, (1, rows), 1)
    scale = jnp.zeros((1, rows), F32)
    for piece in range(3):
        now = rest.astype(BF16).astype(F32)
        scale = jnp.where(row == piece, now, scale)
        rest = rest - now
    slots = -(-stations // rows)
    wide = flags[:1]
    if stations % rows:
        wide = jnp.concatenate([wide, jnp.zeros((1, rows - stations % rows), F32)], axis=1)
    meta = [wide[:, slot * rows : (slot + 1) * rows] for slot in range(slots)] + [scale]
    meta = jnp.concatenate(meta + [jnp.zeros((8 - len(meta), rows), F32)], axis=0)
    meta = lax.dot_general(
        meta.astype(BF16),
        spare_lanes(part, part * channels // padded),
        (((0,), (0,)), ((), ())),
        preferred_element_type=F32,
    )
    my_tm = lax.axis_index("tm")
    my_core = lax.rem(lax.axis_index("inner"), 2)
    first = send_ref.shape[0] - 2 * rows
    spot = lax.broadcasted_iota(jnp.int32, (FINE, LANES), 1) // part
    for member in range(INNER):
        start = (member % 2 * (INNER // 2) + member // 2) * LANES
        pieces = []
        for step in range(window // (FINE * tm_count)):
            tile = jnp.zeros((FINE, LANES), F32)
            for within in range(tm_count):
                row = FINE * (step * tm_count + within)
                chunk = turned[row : row + FINE, start : start + LANES]
                turn = lax.rem(part * (within - my_tm) + LANES, LANES)
                tile = jnp.where(spot == within, pltpu.roll(chunk, turn, 1), tile)
            pieces.append(tile)
        payload = (jnp.concatenate(pieces, axis=0) + meta).astype(BF16)
        y, core = member // 2, member % 2

        @pl.when(core == my_core)
        def _():
            tpls_ref[y] = payload

        @pl.when(core != my_core)
        def _():
            send_ref[first + y * rows : first + (y + 1) * rows, :] = payload

    copies[3].wait()
    grouped[...] = jnp.dot(order, wave_ref[...], preferred_element_type=F32).astype(BF16)
    half = padded // 2
    samples_ref[...] = grouped[pl.ds(pl.multiple_of(my_core * half, half), half), :]
    theirs = pl.ds(pl.multiple_of((1 - my_core) * half, half), half)
    for tile in range(first // half):
        columns = slice(tile * LANES, (tile + 1) * LANES)
        send_ref[tile * half : (tile + 1) * half, :] = grouped[theirs, columns]


def plane_kernel(tpls_ref, got_ref, keep_ref, send_ref):
    y, core = lax.div(lax.axis_index("inner"), 2), lax.rem(lax.axis_index("inner"), 2)
    rows = tpls_ref.shape[1]
    first = got_ref.shape[0] - 2 * rows
    for side in range(2):
        got = got_ref[first + side * rows : first + (side + 1) * rows, :]

        @pl.when(side == y)
        def _():
            keep_ref[core] = tpls_ref[side]
            keep_ref[1 - core] = got

        @pl.when(side != y)
        def _():
            send_ref[core] = tpls_ref[side]
            send_ref[1 - core] = got


def pack_kernel(keep_ref, got_ref, out_ref):
    y = lax.div(lax.axis_index("inner"), 2)
    for core in range(2):
        out_ref[2 * y + core] = keep_ref[core]
        out_ref[2 * (1 - y) + core] = got_ref[core]


def split_kernel(tm_count, keep_ref, got_ref, *outs):
    my_inner = lax.axis_index("inner")
    core = lax.rem(my_inner, 2)
    me = lax.div(my_inner, 2) * tm_count + lax.axis_index("tm")
    part = outs[0].shape[1]
    half, slab = keep_ref.shape
    for flip, out_ref in enumerate(outs):
        start = (me ^ flip) * part
        out_ref[core] = keep_ref[pl.ds(pl.multiple_of(start, part), part), :]
        for tile in range(slab // LANES):
            rows = pl.ds(pl.multiple_of(tile * half + start, part), part)
            out_ref[1 - core, :, tile * LANES : (tile + 1) * LANES] = got_ref[rows, :]


def join_kernel(tm_count, *refs):
    parts, out_ref, head_ref = refs[:-2], refs[-2], refs[-1]
    me = lax.div(lax.axis_index("inner"), 2) * tm_count + lax.axis_index("tm")
    slab = parts[0].shape[2]
    for flip, part in enumerate(parts):
        other = me ^ flip
        y, tm = lax.div(other, tm_count), lax.rem(other, tm_count)
        for core in range(2):
            place = (y * 2 + core) * tm_count + tm
            out_ref[:, pl.ds(pl.multiple_of(place * slab, slab), slab)] = part[core]
    head_ref[...] = out_ref[:, : head_ref.shape[1]]


def arrival(template):
    outer = lax.div(template, INNER) ^ lax.axis_index("outer")
    return outer * INNER + lax.rem(template, INNER)


def correlate(tpls, samples, out_ref, first, left, shifts, products):
    slab = out_ref.shape[2]
    part, columns = samples.shape
    size, depth = left.shape
    copies = LANES // FINE
    usable = columns - 2 * LANES
    for copy in range(depth // part):
        tile, turn = copy // copies * LANES, copy % copies * FINE
        turned = samples if turn == 0 else pltpu.roll(samples, columns - turn, 1)
        shifts[copy * part : (copy + 1) * part, :] = turned[:, tile : tile + usable + LANES]
    count = len(tpls) * INNER
    row = lax.broadcasted_iota(jnp.int32, (size, size), 0)
    column = lax.broadcasted_iota(jnp.int32, (size, size), 1)
    source = arrival(lax.rem(row, count)) * FINE + lax.div(row, count)
    order = jnp.where(column == source, 1.0, 0.0).astype(BF16)
    for step in range(depth // LANES):
        rows = [
            pack[:, FINE * step : FINE * (step + 1), :].reshape(INNER * FINE, LANES)
            for pack in tpls
        ]
        left[:, step * LANES : (step + 1) * LANES] = jnp.dot(
            order, jnp.concatenate(rows, axis=0), preferred_element_type=F32
        ).astype(BF16)
    tiles = products.shape[2] // LANES
    span = (tiles - 1) * LANES
    per_block = span // slab
    blocks = usable // span

    def multiply(index, slot):
        start = pl.multiple_of(index * span, span)
        for tile in range(0, tiles, 2):
            width = min(2, tiles - tile) * LANES
            here = pl.ds(pl.multiple_of(start + tile * LANES, LANES), width)
            products[slot, :, tile * LANES : tile * LANES + width] = jnp.dot(
                left[...], shifts[:, here], preferred_element_type=F32
            )

    def gather(index, slot):
        def tree(first, number):
            if number == 1:
                return products[slot, first * count : (first + 1) * count, :]
            half = number // 2
            later = pltpu.roll(tree(first + half, half), span + LANES - half, 1)
            return tree(first, half) + later

        total = tree(0, FINE)
        for piece in range(per_block):
            out_ref[first + index * per_block + piece] = total[:, piece * slab : (piece + 1) * slab]

    multiply(0, 0)
    if blocks <= 4:
        for index in range(1, blocks):
            multiply(index, index % 2)
            gather(index - 1, (index - 1) % 2)
    else:

        def step(index, carry):
            multiply(index, lax.rem(index, 2))
            gather(index - 1, lax.rem(index + 1, 2))
            return carry

        lax.fori_loop(1, blocks, step, 0)
    gather(blocks - 1, (blocks - 1) % 2)


def first_dots_kernel(*refs):
    tpls, (samples_ref, out_ref, left, shifts, products) = refs[:-5], refs[-5:]
    columns = shifts.shape[1] + LANES
    correlate(tpls, samples_ref[:, :columns], out_ref, 0, left, shifts, products)


def last_dots_kernel(*refs):
    tpls, (samples_ref, halo_ref, mask_ref, done_ref) = refs[:-11], refs[-11:-7]
    (keep_ref, send_ref), (out_ref, edges, *scratch) = refs[-7:-5], refs[-5:]
    first, slab = done_ref.shape[0], done_ref.shape[2]
    group = edges.shape[0]
    window = halo_ref.shape[1]
    after = [samples_ref[:, (m + 1) * slab : (m + 1) * slab + window] for m in range(group - 1)]
    squares = masked_squares(mask_ref[...], jnp.concatenate(after + [halo_ref[...]], axis=1))
    column = lax.broadcasted_iota(jnp.int32, squares.shape, 1) % window
    reach = 1
    while reach < window:
        earlier = pltpu.roll(squares, reach, 1)
        squares = squares + jnp.where(column >= reach, earlier, 0.0)
        reach *= 2
    squares = jnp.where(column >= 1, pltpu.roll(squares, 1, 1), 0.0)
    for member in range(group):
        edges[member] = squares[:, member * window : (member + 1) * window]
    rest = samples_ref.shape[1] + window - scratch[1].shape[1] - LANES
    samples = jnp.concatenate([samples_ref[:, rest:], halo_ref[...]], axis=1)
    out_ref[:first] = done_ref[...]
    correlate(tpls, samples, out_ref, first, *scratch)
    core = lax.rem(lax.axis_index("inner"), 2)
    run = keep_ref.shape[0] // 2
    for y in range(2):
        for tm in range(run):
            for ref, side in ((keep_ref, core), (send_ref, 1 - core)):
                member = (2 * y + side) * run + tm
                ref[y * run + tm, :, :slab] = out_ref[member]
                ref[y * run + tm, :, slab:] = edges[member]


def add_kernel(tm_count, keep_ref, got_ref, *outs):
    me = lax.div(lax.axis_index("inner"), 2) * tm_count + lax.axis_index("tm")
    for flip, out_ref in enumerate(outs):
        out_ref[...] = keep_ref[me ^ flip] + got_ref[me ^ flip]


def masked_squares(mask, wave):
    wave = wave.astype(F32)
    squares = wave * wave
    high = squares.astype(BF16)
    low = (squares - high.astype(F32)).astype(BF16)
    return jnp.dot(mask, high, preferred_element_type=F32) + jnp.dot(
        mask, low, preferred_element_type=F32
    )


def mask_kernel(stations, channels, tm_count, *refs):
    tpls, (order_ref, scale_ref, mask_ref, part_ref) = refs[:-4], refs[-4:]
    rows = tpls[0].shape[1]
    count = len(tpls) * INNER
    padded = INNER * LANES
    part = LANES // tm_count
    meta = lax.dot_general(
        spare_lanes(part, part * channels // padded),
        jnp.concatenate([pack[...].reshape(INNER * rows, LANES) for pack in tpls], axis=0),
        (((1,), (1,)), ((), ())),
        preferred_element_type=F32,
    )
    template = lax.broadcasted_iota(jnp.int32, (count, count), 0)
    place = lax.broadcasted_iota(jnp.int32, (count, count), 1)
    sort = jnp.where(place == arrival(template), 1.0, 0.0).astype(BF16)
    slots = -(-stations // rows)

    def read(slot):
        return jnp.concatenate(
            [meta[slot : slot + 1, t * rows : (t + 1) * rows] for t in range(count)], axis=0
        )

    values = jnp.concatenate([read(slot) for slot in range(slots + 1)], axis=1)
    values = jnp.dot(sort, values.astype(BF16), preferred_element_type=F32)
    start = slots * rows
    scale = jnp.sum(values[:, start : start + 3], axis=1, keepdims=True)
    scale_ref[...] = jnp.broadcast_to(scale, scale_ref.shape)
    mask = jnp.dot(
        values[:, :stations].astype(BF16),
        one_hot(order_ref[...], stations),
        preferred_element_type=F32,
    ).astype(BF16)
    mask_ref[...] = mask
    grouped = jnp.dot(mask, regroup(channels, padded, part, True), preferred_element_type=F32)
    mine = side_major(lax.axis_index("inner")) * LANES + lax.axis_index("tm") * part
    part_ref[...] = pltpu.roll(grouped, lax.rem(padded - mine, padded), 1)[:, :part].astype(BF16)


def power_kernel(window, wave_ref, mask_ref, after, out_ref):
    del after
    power = masked_squares(mask_ref[...], wave_ref[...])
    columns = power.shape[1]
    column = lax.broadcasted_iota(jnp.int32, power.shape, 1)
    reach = 1
    while reach < window:
        later = pltpu.roll(power, columns - reach, 1)
        power = power + jnp.where(column < columns - reach, later, 0.0)
        reach *= 2
    out_ref[...] = power


def finish_kernel(*refs):
    parts, (power_ref, scale_ref, out_ref) = refs[:-3], refs[-3:]
    slab = power_ref.shape[1]
    total = parts[0][...]
    for part in parts[1:]:
        total = total + part[...]
    dots, edge = total[:, :slab], total[:, slab:]
    inside = slab - edge.shape[1]
    energy = jnp.concatenate(
        [power_ref[:, :inside], power_ref[:, inside:] + edge], axis=1
    )
    out_ref[...] = dots * (scale_ref[:, :1] / jnp.sqrt(energy + EPSILON))


def on_device(waveforms, templates, station_mask, channel_order):
    channels, slab = waveforms.shape
    rows, _, window = templates.shape
    stations = station_mask.shape[1]
    outer_count, tm_count = lax.axis_size("outer"), lax.axis_size("tm")
    blk_count = outer_count * INNER
    assert rows == 1 and LANES % tm_count == 0
    group = INNER * tm_count
    padded = INNER * LANES
    part = padded // group
    chunk = group * slab
    span = 2 * slab
    total = blk_count * tm_count
    blk, every = ("outer", "inner"), ("outer", "inner", "tm")
    sds = jax.ShapeDtypeStruct
    order_row = channel_order[None, :]

    rows = window * part // LANES
    send, keep, pieces = call(
        functools.partial(prologue_kernel, tm_count),
        [HBM] * 4,
        [
            sds((padded // 2 * slab // LANES + 2 * rows, LANES), BF16),
            sds((padded // 2, slab), BF16),
            sds((2, rows, LANES), BF16),
        ],
        [
            pltpu.VMEM((channels, slab), BF16),
            pltpu.VMEM((padded, slab), BF16),
            pltpu.VMEM((channels, window), BF16),
            pltpu.VMEM((1, stations), jnp.int32),
            pltpu.VMEM((1, channels), jnp.int32),
            pltpu.VMEM((window, padded), F32),
            pltpu.SemaphoreType.DMA((4,)),
        ],
        bytes_accessed=channels * (window + slab) * 2,
        vmem=60,
    )(waveforms, templates, station_mask, order_row)

    got = lax.ppermute(send, "inner", [(b, b ^ 1) for b in range(INNER)])

    ours, theirs = call(
        plane_kernel, [VMEM] * 2, [sds((2, rows, LANES), BF16)] * 2, bytes_accessed=rows * LANES * 8
    )(pieces, got)
    others = lax.ppermute(theirs, "inner", [(b, b ^ 2) for b in range(INNER)])
    pack = call(pack_kernel, [VMEM] * 2, sds((INNER, rows, LANES), BF16))(ours, others)
    tpls = [pack] + [
        lax.ppermute(pack, "outer", [(b, b ^ flip) for b in range(outer_count)])
        for flip in range(1, outer_count)
    ]

    half = group // 2
    parts = call(
        functools.partial(split_kernel, tm_count),
        [VMEM] * 2,
        [sds((2, part, slab), BF16)] * half,
        bytes_accessed=padded * slab * 2,
    )(keep, got)

    def swap(part, flip):
        y, tm = flip // tm_count, flip % tm_count
        route = [(i, i ^ (2 * tm_count * y + tm)) for i in range(total)]
        return lax.ppermute(part, every, route)

    waves = [parts[0]] + [swap(parts[flip], flip) for flip in range(1, half)]
    samples, head = call(
        functools.partial(join_kernel, tm_count),
        [VMEM] * half,
        [sds((part, chunk), BF16), sds((part, window), BF16)],
        bytes_accessed=part * chunk * 4,
    )(*waves)
    halo = lax.ppermute(head, "outer", [(b, b - 1) for b in range(1, outer_count)])

    scale, mask, mask_part = call(
        functools.partial(mask_kernel, stations, channels, tm_count),
        [VMEM] * (outer_count + 1),
        [
            sds((blk_count, LANES), F32),
            sds((blk_count, channels), BF16),
            sds((blk_count, part), BF16),
        ],
        bytes_accessed=blk_count * rows * LANES * 2,
    )(*tpls, order_row)

    depth = window // FINE * part

    def scratch(columns):
        return [
            pltpu.VMEM((blk_count * FINE, depth), BF16),
            pltpu.VMEM((depth, columns + LANES), BF16),
            pltpu.VMEM((2, blk_count * FINE, span + LANES), F32),
        ]

    blocks = group // 2
    work = 2 * blk_count * window * part * span
    partials = call(
        first_dots_kernel,
        [VMEM] * (outer_count + 1),
        sds((2 * (blocks - 1), blk_count, slab), F32),
        scratch((blocks - 1) * span),
        flops=work * (blocks - 1),
        bytes_accessed=part * chunk * 2,
    )(*tpls, samples)
    keep, send = call(
        last_dots_kernel,
        [VMEM] * (outer_count + 4),
        [sds((half, blk_count, slab + window), F32)] * 2,
        [
            pltpu.VMEM((group, blk_count, slab), F32),
            pltpu.VMEM((group, blk_count, window), F32),
        ]
        + scratch(span),
        flops=work,
        bytes_accessed=part * chunk * 2,
    )(*tpls, samples, halo, mask_part, partials)
    got = lax.ppermute(send, "inner", [(b, b ^ 1) for b in range(INNER)])
    power = call(
        functools.partial(power_kernel, window),
        [VMEM, VMEM, AFTER],
        sds((blk_count, slab), F32),
        flops=4 * blk_count * channels * slab,
        bytes_accessed=channels * slab * 2,
    )(waveforms, mask, send)
    sums = call(
        functools.partial(add_kernel, tm_count),
        [VMEM] * 2,
        [sds((blk_count, slab + window), F32)] * half,
        bytes_accessed=blk_count * slab * 12 * half,
    )(keep, got)
    sums = [sums[0]] + [swap(sums[flip], flip) for flip in range(1, half)]
    return call(
        finish_kernel,
        [VMEM] * (half + 2),
        sds((blk_count, slab), F32),
        bytes_accessed=blk_count * slab * 4 * (half + 2),
    )(*sums, power, scale)


def solution(mesh):
    blk_count, tm_count = mesh.devices.shape
    shape = (blk_count // INNER, INNER, tm_count)
    mesh = jax.sharding.Mesh(mesh.devices.reshape(shape), ("outer", "inner", "tm"))
    blk, every = ("outer", "inner"), ("outer", "inner", "tm")
    placed = (P(None, every), P(blk, None, None), P(blk, None), P())
    return jax.shard_map(
        on_device, mesh=mesh, in_specs=placed, out_specs=P(None, every), check_vma=False
    )
```

```python
import functools

import jax
import jax.numpy as jnp
from jax import lax
from jax.experimental import pallas as pl
from jax.experimental.pallas import tpu as pltpu
from jax.sharding import PartitionSpec as P

EPSILON = 1e-05
LANES = 128
INNER = 4
FINE = 16
MIB = 1024 * 1024

BF16 = jnp.bfloat16
F32 = jnp.float32


HBM = pl.BlockSpec(memory_space=pltpu.HBM)
VMEM = pl.BlockSpec(memory_space=pltpu.VMEM)
AFTER = pl.BlockSpec(memory_space=pl.ANY)


def call(kernel, in_specs, out_shape, scratch=(), flops=0, bytes_accessed=0, vmem=24):
    return pl.pallas_call(
        kernel,
        in_specs=in_specs,
        out_specs=jax.tree.map(lambda _: VMEM, out_shape),
        out_shape=out_shape,
        scratch_shapes=list(scratch),
        compiler_params=pltpu.CompilerParams(vmem_limit_bytes=vmem * MIB),
        cost_estimate=pl.CostEstimate(
            flops=flops, bytes_accessed=bytes_accessed, transcendentals=0
        ),
    )


def one_hot(order_row, station_count):
    columns = order_row.shape[1]
    first = 3 * lax.broadcasted_iota(jnp.int32, (station_count, columns), 0)
    hit = (order_row >= first) & (order_row < first + 3)
    return jnp.where(hit, 1.0, 0.0).astype(BF16)


def side_major(inner):
    return lax.rem(inner, 2) * (INNER // 2) + lax.div(inner, 2)


def place_of(real, part):
    base = real // FINE * FINE
    return base, real - base


def regroup_rows(source, target, part):
    channels, width = source.shape
    groups = target.shape[0] // part
    real = channels // groups
    base, extra = place_of(real, part)
    rest = source[groups * base :, :].astype(F32)
    fill = jnp.zeros((part - real, width), F32)
    for group in range(groups):
        if base:
            run = source[group * base : (group + 1) * base, :]
            target[group * part : group * part + base, :] = run
        piece = [rest[group * extra : (group + 1) * extra], fill]
        target[group * part + base : (group + 1) * part, :] = jnp.concatenate(
            piece, axis=0
        ).astype(BF16)


def regroup(channels, padded, part):
    groups = padded // part
    real = channels // groups
    base, extra = place_of(real, part)
    channel = lax.broadcasted_iota(jnp.int32, (channels, padded), 0)
    place = lax.broadcasted_iota(jnp.int32, (1, padded), 1)
    group, within = place >> (part.bit_length() - 1), place & (part - 1)
    rest = groups * base + extra * group + within - base
    source = jnp.where(within < base, base * group + within, rest)
    source = jnp.where(within < real, source, -1)
    return jnp.where(channel == source, 1.0, 0.0).astype(BF16)


def spare_lanes(part, real):
    slots = LANES // part * (part - real)
    slot = lax.broadcasted_iota(jnp.int32, (8, LANES), 0)
    lane = lax.broadcasted_iota(jnp.int32, (8, LANES), 1)
    spare = part - real
    home = lax.div(slot, spare) * part + real + lax.rem(slot, spare)
    return jnp.where((lane == home) & (slot < slots), 1.0, 0.0).astype(BF16)


def prologue_kernel(tm_count, wave_hbm, tpl_hbm, flag_hbm, order_hbm, *refs):
    send_ref, samples_ref, tpls_ref = refs[:3]
    wave_ref, grouped, tpl_ref, tpl_grouped, flag_ref, order_ref, turned, sems = refs[3:]
    channels, window = tpl_hbm.shape[1:]
    copies = [
        pltpu.make_async_copy(flag_hbm, flag_ref, sems.at[0]),
        pltpu.make_async_copy(order_hbm, order_ref, sems.at[1]),
        pltpu.make_async_copy(tpl_hbm.at[0], tpl_ref, sems.at[2]),
        pltpu.make_async_copy(wave_hbm, wave_ref, sems.at[3]),
    ]
    for copy in copies:
        copy.start()
    stations = flag_ref.shape[1]
    padded = turned.shape[1]
    part = LANES // tm_count
    rows = tpls_ref.shape[1]
    groups = regroup(channels, padded, part)
    copies[0].wait()
    copies[1].wait()
    flags = jnp.broadcast_to(flag_ref[...].astype(F32), (8, stations))
    mask = jnp.dot(
        flags.astype(BF16), one_hot(order_ref[...], stations), preferred_element_type=F32
    )
    live = jnp.sum(mask[:1], keepdims=True)
    mask = jnp.dot(mask.astype(BF16), groups, preferred_element_type=F32)[:1]
    copies[2].wait()
    regroup_rows(tpl_ref, tpl_grouped, part)
    masked = tpl_grouped[...].T.astype(F32) * mask
    turned[...] = masked
    norm = jnp.sqrt(jnp.sum(masked * masked, keepdims=True) + EPSILON)
    rest = jnp.broadcast_to(jnp.sqrt(window * live) / norm, (1, rows))
    row = lax.broadcasted_iota(jnp.int32, (1, rows), 1)
    scale = jnp.zeros((1, rows), F32)
    for piece in range(3):
        now = rest.astype(BF16).astype(F32)
        scale = jnp.where(row == piece, now, scale)
        rest = rest - now
    slots = -(-stations // rows)
    wide = flags[:1]
    if stations % rows:
        wide = jnp.concatenate([wide, jnp.zeros((1, rows - stations % rows), F32)], axis=1)
    meta = [wide[:, slot * rows : (slot + 1) * rows] for slot in range(slots)] + [scale]
    meta = jnp.concatenate(meta + [jnp.zeros((8 - len(meta), rows), F32)], axis=0)
    meta = lax.dot_general(
        meta.astype(BF16),
        spare_lanes(part, part * channels // padded),
        (((0,), (0,)), ((), ())),
        preferred_element_type=F32,
    )
    my_tm = lax.axis_index("tm")
    my_core = lax.rem(lax.axis_index("inner"), 2)
    first = send_ref.shape[0] - 2 * rows
    spot = lax.broadcasted_iota(jnp.int32, (FINE, LANES), 1) >> (part.bit_length() - 1)
    for member in range(INNER):
        start = (member % 2 * (INNER // 2) + member // 2) * LANES
        pieces = []
        for step in range(window // (FINE * tm_count)):
            tile = jnp.zeros((FINE, LANES), F32)
            for within in range(tm_count):
                row = FINE * (step * tm_count + within)
                chunk = turned[row : row + FINE, start : start + LANES]
                turn = lax.rem(part * (within - my_tm) + LANES, LANES)
                tile = jnp.where(spot == within, pltpu.roll(chunk, turn, 1), tile)
            pieces.append(tile)
        payload = (jnp.concatenate(pieces, axis=0) + meta).astype(BF16)
        y, core = member // 2, member % 2

        @pl.when(core == my_core)
        def _():
            tpls_ref[y] = payload

        @pl.when(core != my_core)
        def _():
            send_ref[first + y * rows : first + (y + 1) * rows, :] = payload

    copies[3].wait()
    regroup_rows(wave_ref, grouped, part)
    half = padded // 2
    samples_ref[...] = grouped[pl.ds(pl.multiple_of(my_core * half, half), half), :]
    theirs = pl.ds(pl.multiple_of((1 - my_core) * half, half), half)
    for tile in range(first // half):
        columns = slice(tile * LANES, (tile + 1) * LANES)
        send_ref[tile * half : (tile + 1) * half, :] = grouped[theirs, columns]


def plane_kernel(tpls_ref, got_ref, keep_ref, send_ref):
    y, core = lax.div(lax.axis_index("inner"), 2), lax.rem(lax.axis_index("inner"), 2)
    rows = tpls_ref.shape[1]
    first = got_ref.shape[0] - 2 * rows
    for side in range(2):
        got = got_ref[first + side * rows : first + (side + 1) * rows, :]

        @pl.when(side == y)
        def _():
            keep_ref[core] = tpls_ref[side]
            keep_ref[1 - core] = got

        @pl.when(side != y)
        def _():
            send_ref[core] = tpls_ref[side]
            send_ref[1 - core] = got


def pack_kernel(keep_ref, got_ref, out_ref):
    y = lax.div(lax.axis_index("inner"), 2)
    for core in range(2):
        out_ref[2 * y + core] = keep_ref[core]
        out_ref[2 * (1 - y) + core] = got_ref[core]


def split_kernel(tm_count, flips, keep_ref, got_ref, after, *outs):
    del after
    my_inner = lax.axis_index("inner")
    core = lax.rem(my_inner, 2)
    me = lax.div(my_inner, 2) * tm_count + lax.axis_index("tm")
    part = outs[0].shape[1]
    half, slab = keep_ref.shape
    for flip, out_ref in zip(flips, outs):
        start = (me ^ flip) * part
        out_ref[core] = keep_ref[pl.ds(pl.multiple_of(start, part), part), :]
        for tile in range(slab // LANES):
            rows = pl.ds(pl.multiple_of(tile * half + start, part), part)
            out_ref[1 - core, :, tile * LANES : (tile + 1) * LANES] = got_ref[rows, :]


def join_kernel(tm_count, *refs):
    parts, out_ref, head_ref = refs[:-2], refs[-2], refs[-1]
    me = lax.div(lax.axis_index("inner"), 2) * tm_count + lax.axis_index("tm")
    slab = parts[0].shape[2]
    for flip, part in enumerate(parts):
        other = me ^ flip
        y, tm = lax.div(other, tm_count), lax.rem(other, tm_count)
        for core in range(2):
            place = (y * 2 + core) * tm_count + tm
            out_ref[:, pl.ds(pl.multiple_of(place * slab, slab), slab)] = part[core]
    head_ref[...] = out_ref[:, : head_ref.shape[1]]


def arrival(template):
    return template ^ (lax.axis_index("outer") * INNER)


def correlate(tpls, samples, out_ref, first, left, shifts, products):
    slab = out_ref.shape[2]
    part, columns = samples.shape
    size, depth = left.shape
    copies = LANES // FINE
    usable = columns - 2 * LANES
    for copy in range(depth // part):
        tile, turn = copy // copies * LANES, copy % copies * FINE
        turned = samples if turn == 0 else pltpu.roll(samples, columns - turn, 1)
        shifts[copy * part : (copy + 1) * part, :] = turned[:, tile : tile + usable + LANES]
    count = len(tpls) * INNER
    row = lax.broadcasted_iota(jnp.int32, (size, size), 0)
    column = lax.broadcasted_iota(jnp.int32, (size, size), 1)
    shift = count.bit_length() - 1
    source = arrival(row & (count - 1)) * FINE + (row >> shift)
    order = jnp.where(column == source, 1.0, 0.0).astype(BF16)
    for step in range(depth // LANES):
        rows = [
            pack[:, FINE * step : FINE * (step + 1), :].reshape(INNER * FINE, LANES)
            for pack in tpls
        ]
        left[:, step * LANES : (step + 1) * LANES] = jnp.dot(
            order, jnp.concatenate(rows, axis=0), preferred_element_type=F32
        ).astype(BF16)
    tiles = products.shape[2] // LANES
    span = (tiles - 1) * LANES
    per_block = span // slab
    blocks = usable // span

    def multiply(index, slot):
        start = pl.multiple_of(index * span, span)
        for tile in range(0, tiles, 2):
            width = min(2, tiles - tile) * LANES
            here = pl.ds(pl.multiple_of(start + tile * LANES, LANES), width)
            products[slot, :, tile * LANES : tile * LANES + width] = jnp.dot(
                left[...], shifts[:, here], preferred_element_type=F32
            )

    def gather(index, slot):
        def tree(first, number):
            if number == 1:
                return products[slot, first * count : (first + 1) * count, :]
            half = number // 2
            later = pltpu.roll(tree(first + half, half), span + LANES - half, 1)
            return tree(first, half) + later

        total = tree(0, FINE)
        for piece in range(per_block):
            out_ref[first + index * per_block + piece] = total[:, piece * slab : (piece + 1) * slab]

    multiply(0, 0)
    if blocks <= 4:
        for index in range(1, blocks):
            multiply(index, index % 2)
            gather(index - 1, (index - 1) % 2)
    else:

        def step(index, carry):
            multiply(index, lax.rem(index, 2))
            gather(index - 1, lax.rem(index + 1, 2))
            return carry

        lax.fori_loop(1, blocks, step, 0)
    gather(blocks - 1, (blocks - 1) % 2)


def first_dots_kernel(*refs):
    tpls, (samples_ref, out_ref, left, shifts, products) = refs[:-5], refs[-5:]
    columns = shifts.shape[1] + LANES
    correlate(tpls, samples_ref[:, :columns], out_ref, 0, left, shifts, products)


def last_dots_kernel(*refs):
    tpls, (samples_ref, halo_ref, mask_ref, done_ref) = refs[:-11], refs[-11:-7]
    (keep_ref, send_ref), (out_ref, edges, *scratch) = refs[-7:-5], refs[-5:]
    first, slab = done_ref.shape[0], done_ref.shape[2]
    group = edges.shape[0]
    window = halo_ref.shape[1]
    after = [samples_ref[:, (m + 1) * slab : (m + 1) * slab + window] for m in range(group - 1)]
    squares = masked_squares(mask_ref[...], jnp.concatenate(after + [halo_ref[...]], axis=1))
    column = lax.broadcasted_iota(jnp.int32, squares.shape, 1) & (window - 1)
    reach = 1
    while reach < window:
        earlier = pltpu.roll(squares, reach, 1)
        squares = squares + jnp.where(column >= reach, earlier, 0.0)
        reach *= 2
    squares = jnp.where(column >= 1, pltpu.roll(squares, 1, 1), 0.0)
    for member in range(group):
        edges[member] = squares[:, member * window : (member + 1) * window]
    rest = samples_ref.shape[1] + window - scratch[1].shape[1] - LANES
    samples = jnp.concatenate([samples_ref[:, rest:], halo_ref[...]], axis=1)
    out_ref[:first] = done_ref[...]
    correlate(tpls, samples, out_ref, first, *scratch)
    core = lax.rem(lax.axis_index("inner"), 2)
    run = keep_ref.shape[0] // 2
    for y in range(2):
        for tm in range(run):
            for ref, side in ((keep_ref, core), (send_ref, 1 - core)):
                member = (2 * y + side) * run + tm
                ref[y * run + tm, :, :slab] = out_ref[member]
                ref[y * run + tm, :, slab:] = edges[member]


def add_kernel(tm_count, keep_ref, got_ref, *outs):
    me = lax.div(lax.axis_index("inner"), 2) * tm_count + lax.axis_index("tm")
    for flip, out_ref in enumerate(outs):
        out_ref[...] = keep_ref[me ^ flip] + got_ref[me ^ flip]


def masked_squares(mask, wave):
    wave = wave.astype(F32)
    squares = wave * wave
    high = squares.astype(BF16)
    low = (squares - high.astype(F32)).astype(BF16)
    return jnp.dot(mask, high, preferred_element_type=F32) + jnp.dot(
        mask, low, preferred_element_type=F32
    )


def mask_kernel(stations, channels, tm_count, *refs):
    tpls, (order_ref, scale_ref, mask_ref, part_ref) = refs[:-4], refs[-4:]
    rows = tpls[0].shape[1]
    count = len(tpls) * INNER
    padded = INNER * LANES
    part = LANES // tm_count
    meta = lax.dot_general(
        spare_lanes(part, part * channels // padded),
        jnp.concatenate([pack[...].reshape(INNER * rows, LANES) for pack in tpls], axis=0),
        (((1,), (1,)), ((), ())),
        preferred_element_type=F32,
    )
    template = lax.broadcasted_iota(jnp.int32, (count, count), 0)
    place = lax.broadcasted_iota(jnp.int32, (count, count), 1)
    sort = jnp.where(place == arrival(template), 1.0, 0.0).astype(BF16)
    slots = -(-stations // rows)

    def read(slot):
        return jnp.concatenate(
            [meta[slot : slot + 1, t * rows : (t + 1) * rows] for t in range(count)], axis=0
        )

    values = jnp.concatenate([read(slot) for slot in range(slots + 1)], axis=1)
    values = jnp.dot(sort, values.astype(BF16), preferred_element_type=F32)
    start = slots * rows
    scale = jnp.sum(values[:, start : start + 3], axis=1, keepdims=True)
    scale_ref[...] = jnp.broadcast_to(scale, scale_ref.shape)
    mask = jnp.dot(
        values[:, :stations].astype(BF16),
        one_hot(order_ref[...], stations),
        preferred_element_type=F32,
    ).astype(BF16)
    mask_ref[...] = mask
    grouped = jnp.dot(mask, regroup(channels, padded, part), preferred_element_type=F32)
    mine = side_major(lax.axis_index("inner")) * LANES + lax.axis_index("tm") * part
    part_ref[...] = pltpu.roll(grouped, lax.rem(padded - mine, padded), 1)[:, :part].astype(BF16)


def power_kernel(window, wave_ref, mask_ref, after, out_ref):
    del after
    power = masked_squares(mask_ref[...], wave_ref[...])
    columns = power.shape[1]
    column = lax.broadcasted_iota(jnp.int32, power.shape, 1)
    reach = 1
    while reach < window:
        later = pltpu.roll(power, columns - reach, 1)
        power = power + jnp.where(column < columns - reach, later, 0.0)
        reach *= 2
    out_ref[...] = power


def finish_kernel(*refs):
    parts, (power_ref, scale_ref, out_ref) = refs[:-3], refs[-3:]
    slab = power_ref.shape[1]
    total = parts[0][...]
    for part in parts[1:]:
        total = total + part[...]
    dots, edge = total[:, :slab], total[:, slab:]
    inside = slab - edge.shape[1]
    energy = jnp.concatenate(
        [power_ref[:, :inside], power_ref[:, inside:] + edge], axis=1
    )
    out_ref[...] = dots * (scale_ref[:, :1] / jnp.sqrt(energy + EPSILON))


def on_device(waveforms, templates, station_mask, channel_order):
    channels, slab = waveforms.shape
    rows, _, window = templates.shape
    stations = station_mask.shape[1]
    outer_count, tm_count = lax.axis_size("outer"), lax.axis_size("tm")
    blk_count = outer_count * INNER
    assert rows == 1 and LANES % tm_count == 0
    group = INNER * tm_count
    padded = INNER * LANES
    part = padded // group
    chunk = group * slab
    span = 2 * slab
    total = blk_count * tm_count
    blk, every = ("outer", "inner"), ("outer", "inner", "tm")
    sds = jax.ShapeDtypeStruct
    order_row = channel_order[None, :]

    rows = window * part // LANES
    held = [
        pltpu.with_memory_space_constraint(x, pltpu.HBM)
        for x in (waveforms, templates, station_mask, order_row)
    ]
    send, keep, pieces = call(
        functools.partial(prologue_kernel, tm_count),
        [HBM] * 4,
        [
            sds((padded // 2 * slab // LANES + 2 * rows, LANES), BF16),
            sds((padded // 2, slab), BF16),
            sds((2, rows, LANES), BF16),
        ],
        [
            pltpu.VMEM((channels, slab), BF16),
            pltpu.VMEM((padded, slab), BF16),
            pltpu.VMEM((channels, window), BF16),
            pltpu.VMEM((padded, window), BF16),
            pltpu.VMEM((1, stations), jnp.int32),
            pltpu.VMEM((1, channels), jnp.int32),
            pltpu.VMEM((window, padded), F32),
            pltpu.SemaphoreType.DMA((4,)),
        ],
        bytes_accessed=channels * (window + slab) * 2,
    )(*held)

    got = lax.ppermute(send, "inner", [(b, b ^ 1) for b in range(INNER)])

    ours, theirs = call(
        plane_kernel, [VMEM] * 2, [sds((2, rows, LANES), BF16)] * 2, bytes_accessed=rows * LANES * 8
    )(pieces, got)
    others = lax.ppermute(theirs, "inner", [(b, b ^ 2) for b in range(INNER)])
    pack = call(pack_kernel, [VMEM] * 2, sds((INNER, rows, LANES), BF16))(ours, others)
    tpls = [pack] + [
        lax.ppermute(pack, "outer", [(b, b ^ flip) for b in range(outer_count)])
        for flip in range(1, outer_count)
    ]

    half = group // 2
    def split(flips, after):
        return call(
            functools.partial(split_kernel, tm_count, flips),
            [VMEM, VMEM, AFTER],
            [sds((2, part, slab), BF16)] * len(flips),
            bytes_accessed=padded * slab * 2,
        )(keep, got, after)

    parts = split(range(tm_count), theirs) + split(range(tm_count, half), pack)

    def swap(part, flip):
        y, tm = flip // tm_count, flip % tm_count
        route = [(i, i ^ (2 * tm_count * y + tm)) for i in range(total)]
        return lax.ppermute(part, every, route)

    waves = [parts[0]] + [swap(parts[flip], flip) for flip in range(1, half)]
    samples, head = call(
        functools.partial(join_kernel, tm_count),
        [VMEM] * half,
        [sds((part, chunk), BF16), sds((part, window), BF16)],
        bytes_accessed=part * chunk * 4,
    )(*waves)
    halo = lax.ppermute(head, "outer", [(b, b - 1) for b in range(1, outer_count)])

    scale, mask, mask_part = call(
        functools.partial(mask_kernel, stations, channels, tm_count),
        [VMEM] * (outer_count + 1),
        [
            sds((blk_count, LANES), F32),
            sds((blk_count, channels), BF16),
            sds((blk_count, part), BF16),
        ],
        bytes_accessed=blk_count * rows * LANES * 2,
    )(*tpls, order_row)

    depth = window // FINE * part

    def scratch(columns):
        return [
            pltpu.VMEM((blk_count * FINE, depth), BF16),
            pltpu.VMEM((depth, columns + LANES), BF16),
            pltpu.VMEM((2, blk_count * FINE, span + LANES), F32),
        ]

    blocks = group // 2
    work = 2 * blk_count * window * part * span
    partials = call(
        first_dots_kernel,
        [VMEM] * (outer_count + 1),
        sds((2 * (blocks - 1), blk_count, slab), F32),
        scratch((blocks - 1) * span),
        flops=work * (blocks - 1),
        bytes_accessed=part * chunk * 2,
    )(*tpls, samples)
    keep, send = call(
        last_dots_kernel,
        [VMEM] * (outer_count + 4),
        [sds((half, blk_count, slab + window), F32)] * 2,
        [
            pltpu.VMEM((group, blk_count, slab), F32),
            pltpu.VMEM((group, blk_count, window), F32),
        ]
        + scratch(span),
        flops=work,
        bytes_accessed=part * chunk * 2,
    )(*tpls, samples, halo, mask_part, partials)
    got = lax.ppermute(send, "inner", [(b, b ^ 1) for b in range(INNER)])
    power = call(
        functools.partial(power_kernel, window),
        [VMEM, VMEM, AFTER],
        sds((blk_count, slab), F32),
        flops=4 * blk_count * channels * slab,
        bytes_accessed=channels * slab * 2,
    )(waveforms, mask, send)
    sums = call(
        functools.partial(add_kernel, tm_count),
        [VMEM] * 2,
        [sds((blk_count, slab + window), F32)] * half,
        bytes_accessed=blk_count * slab * 12 * half,
    )(keep, got)
    sums = [sums[0]] + [swap(sums[flip], flip) for flip in range(1, half)]
    return call(
        finish_kernel,
        [VMEM] * (half + 2),
        sds((blk_count, slab), F32),
        bytes_accessed=blk_count * slab * 4 * (half + 2),
    )(*sums, power, scale)


def solution(mesh):
    blk_count, tm_count = mesh.devices.shape
    shape = (blk_count // INNER, INNER, tm_count)
    mesh = jax.sharding.Mesh(mesh.devices.reshape(shape), ("outer", "inner", "tm"))
    blk, every = ("outer", "inner"), ("outer", "inner", "tm")
    placed = (P(None, every), P(blk, None, None), P(blk, None), P())
    return jax.shard_map(
        on_device, mesh=mesh, in_specs=placed, out_specs=P(None, every), check_vma=False
    )
```

```python
import functools

import jax
import jax.numpy as jnp
from jax import lax
from jax.experimental import pallas as pl
from jax.experimental.pallas import tpu as pltpu
from jax.sharding import PartitionSpec as P

EPSILON = 1e-05
LANES = 128
INNER = 4
FINE = 16
MIB = 1024 * 1024

BF16 = jnp.bfloat16
F32 = jnp.float32


HBM = pl.BlockSpec(memory_space=pltpu.HBM)
VMEM = pl.BlockSpec(memory_space=pltpu.VMEM)
AFTER = pl.BlockSpec(memory_space=pl.ANY)


def call(kernel, in_specs, out_shape, scratch=(), flops=0, bytes_accessed=0, vmem=24):
    return pl.pallas_call(
        kernel,
        in_specs=in_specs,
        out_specs=jax.tree.map(lambda _: VMEM, out_shape),
        out_shape=out_shape,
        scratch_shapes=list(scratch),
        compiler_params=pltpu.CompilerParams(vmem_limit_bytes=vmem * MIB),
        cost_estimate=pl.CostEstimate(
            flops=flops, bytes_accessed=bytes_accessed, transcendentals=0
        ),
    )


def one_hot(order_row, station_count):
    columns = order_row.shape[1]
    first = 3 * lax.broadcasted_iota(jnp.int32, (station_count, columns), 0)
    hit = (order_row >= first) & (order_row < first + 3)
    return jnp.where(hit, 1.0, 0.0).astype(BF16)


def side_major(inner):
    return lax.rem(inner, 2) * (INNER // 2) + lax.div(inner, 2)


def place_of(real, part):
    base = real // FINE * FINE
    return base, real - base


def regroup_rows(source, target, part):
    channels, width = source.shape
    groups = target.shape[0] // part
    real = channels // groups
    base, extra = place_of(real, part)
    rest = source[groups * base :, :].astype(F32)
    fill = jnp.zeros((part - real, width), F32)
    for group in range(groups):
        if base:
            run = source[group * base : (group + 1) * base, :]
            target[group * part : group * part + base, :] = run
        piece = [rest[group * extra : (group + 1) * extra], fill]
        target[group * part + base : (group + 1) * part, :] = jnp.concatenate(
            piece, axis=0
        ).astype(BF16)


def regroup(channels, padded, part):
    groups = padded // part
    real = channels // groups
    base, extra = place_of(real, part)
    channel = lax.broadcasted_iota(jnp.int32, (channels, padded), 0)
    place = lax.broadcasted_iota(jnp.int32, (1, padded), 1)
    group, within = place >> (part.bit_length() - 1), place & (part - 1)
    rest = groups * base + extra * group + within - base
    source = jnp.where(within < base, base * group + within, rest)
    source = jnp.where(within < real, source, -1)
    return jnp.where(channel == source, 1.0, 0.0).astype(BF16)


def spare_lanes(part, real):
    slots = LANES // part * (part - real)
    slot = lax.broadcasted_iota(jnp.int32, (8, LANES), 0)
    lane = lax.broadcasted_iota(jnp.int32, (8, LANES), 1)
    spare = part - real
    home = lax.div(slot, spare) * part + real + lax.rem(slot, spare)
    return jnp.where((lane == home) & (slot < slots), 1.0, 0.0).astype(BF16)


def prologue_kernel(tm_count, wave_hbm, tpl_hbm, flag_hbm, order_hbm, *refs):
    send_ref, samples_ref, *outs = refs[: INNER + 1]
    wave_ref, grouped, tpl_ref, tpl_grouped, flag_ref, order_ref, turned, sems = refs[INNER + 1 :]
    channels, window = tpl_hbm.shape[1:]
    copies = [
        pltpu.make_async_copy(flag_hbm, flag_ref, sems.at[0]),
        pltpu.make_async_copy(order_hbm, order_ref, sems.at[1]),
        pltpu.make_async_copy(tpl_hbm.at[0], tpl_ref, sems.at[2]),
        pltpu.make_async_copy(wave_hbm, wave_ref, sems.at[3]),
    ]
    for copy in copies:
        copy.start()
    stations = flag_ref.shape[1]
    padded = turned.shape[1]
    part = LANES // tm_count
    rows = outs[0].shape[0]
    groups = regroup(channels, padded, part)
    copies[0].wait()
    copies[1].wait()
    flags = jnp.broadcast_to(flag_ref[...].astype(F32), (8, stations))
    mask = jnp.dot(
        flags.astype(BF16), one_hot(order_ref[...], stations), preferred_element_type=F32
    )
    live = jnp.sum(mask[:1], keepdims=True)
    mask = jnp.dot(mask.astype(BF16), groups, preferred_element_type=F32)[:1]
    copies[2].wait()
    regroup_rows(tpl_ref, tpl_grouped, part)
    masked = tpl_grouped[...].T.astype(F32) * mask
    turned[...] = masked
    norm = jnp.sqrt(jnp.sum(masked * masked, keepdims=True) + EPSILON)
    rest = jnp.broadcast_to(jnp.sqrt(window * live) / norm, (1, rows))
    row = lax.broadcasted_iota(jnp.int32, (1, rows), 1)
    scale = jnp.zeros((1, rows), F32)
    for piece in range(3):
        now = rest.astype(BF16).astype(F32)
        scale = jnp.where(row == piece, now, scale)
        rest = rest - now
    slots = -(-stations // rows)
    wide = flags[:1]
    if stations % rows:
        wide = jnp.concatenate([wide, jnp.zeros((1, rows - stations % rows), F32)], axis=1)
    meta = [wide[:, slot * rows : (slot + 1) * rows] for slot in range(slots)] + [scale]
    meta = jnp.concatenate(meta + [jnp.zeros((8 - len(meta), rows), F32)], axis=0)
    meta = lax.dot_general(
        meta.astype(BF16),
        spare_lanes(part, part * channels // padded),
        (((0,), (0,)), ((), ())),
        preferred_element_type=F32,
    )
    my_tm = lax.axis_index("tm")
    my_inner = lax.axis_index("inner")
    my_core = lax.rem(my_inner, 2)
    first = send_ref.shape[0] - rows
    spot = lax.broadcasted_iota(jnp.int32, (FINE, LANES), 1) >> (part.bit_length() - 1)
    for flip in range(INNER):
        start = pl.multiple_of(side_major(my_inner ^ flip) * LANES, LANES)
        pieces = []
        for step in range(window // (FINE * tm_count)):
            tile = jnp.zeros((FINE, LANES), F32)
            for within in range(tm_count):
                row = FINE * (step * tm_count + within)
                chunk = turned[row : row + FINE, pl.ds(start, LANES)]
                turn = lax.rem(part * (within - my_tm) + LANES, LANES)
                tile = jnp.where(spot == within, pltpu.roll(chunk, turn, 1), tile)
            pieces.append(tile)
        payload = (jnp.concatenate(pieces, axis=0) + meta).astype(BF16)
        if flip == 1:
            send_ref[first:, :] = payload
        else:
            outs[flip - (flip > 1)][...] = payload

    copies[3].wait()
    regroup_rows(wave_ref, grouped, part)
    half = padded // 2
    samples_ref[...] = grouped[pl.ds(pl.multiple_of(my_core * half, half), half), :]
    theirs = pl.ds(pl.multiple_of((1 - my_core) * half, half), half)
    for tile in range(first // half):
        columns = slice(tile * LANES, (tile + 1) * LANES)
        send_ref[tile * half : (tile + 1) * half, :] = grouped[theirs, columns]


def pack_kernel(mine_ref, core_ref, y_ref, both_ref, out_ref):
    inner = lax.axis_index("inner")
    rows = mine_ref.shape[0]
    out_ref[inner] = mine_ref[...]
    out_ref[inner ^ 1] = core_ref[core_ref.shape[0] - rows :, :]
    out_ref[inner ^ 2] = y_ref[...]
    out_ref[inner ^ 3] = both_ref[...]


def split_kernel(tm_count, flips, keep_ref, got_ref, after, *outs):
    del after
    my_inner = lax.axis_index("inner")
    core = lax.rem(my_inner, 2)
    me = lax.div(my_inner, 2) * tm_count + lax.axis_index("tm")
    part = outs[0].shape[1]
    half, slab = keep_ref.shape
    for flip, out_ref in zip(flips, outs):
        start = (me ^ flip) * part
        out_ref[core] = keep_ref[pl.ds(pl.multiple_of(start, part), part), :]
        for tile in range(slab // LANES):
            rows = pl.ds(pl.multiple_of(tile * half + start, part), part)
            out_ref[1 - core, :, tile * LANES : (tile + 1) * LANES] = got_ref[rows, :]


def join_kernel(tm_count, *refs):
    parts, out_ref, head_ref = refs[:-2], refs[-2], refs[-1]
    me = lax.div(lax.axis_index("inner"), 2) * tm_count + lax.axis_index("tm")
    slab = parts[0].shape[2]
    for flip, part in enumerate(parts):
        other = me ^ flip
        y, tm = lax.div(other, tm_count), lax.rem(other, tm_count)
        for core in range(2):
            place = (y * 2 + core) * tm_count + tm
            out_ref[:, pl.ds(pl.multiple_of(place * slab, slab), slab)] = part[core]
    head_ref[...] = out_ref[:, : head_ref.shape[1]]


def arrival(template, count):
    inner = template & (INNER - 1)
    return ((lax.axis_index("outer") * INNER - (template - inner)) & (count - 1)) + inner


def correlate(tpls, samples, out_ref, first, left, shifts, products):
    slab = out_ref.shape[2]
    part, columns = samples.shape
    size, depth = left.shape
    copies = LANES // FINE
    usable = columns - 2 * LANES
    for copy in range(depth // part):
        tile, turn = copy // copies * LANES, copy % copies * FINE
        turned = samples if turn == 0 else pltpu.roll(samples, columns - turn, 1)
        shifts[copy * part : (copy + 1) * part, :] = turned[:, tile : tile + usable + LANES]
    count = len(tpls) * INNER
    row = lax.broadcasted_iota(jnp.int32, (size, size), 0)
    column = lax.broadcasted_iota(jnp.int32, (size, size), 1)
    shift = count.bit_length() - 1
    source = arrival(row & (count - 1), count) * FINE + (row >> shift)
    order = jnp.where(column == source, 1.0, 0.0).astype(BF16)
    for step in range(depth // LANES):
        rows = [
            pack[:, FINE * step : FINE * (step + 1), :].reshape(INNER * FINE, LANES)
            for pack in tpls
        ]
        left[:, step * LANES : (step + 1) * LANES] = jnp.dot(
            order, jnp.concatenate(rows, axis=0), preferred_element_type=F32
        ).astype(BF16)
    tiles = products.shape[2] // LANES
    span = (tiles - 1) * LANES
    per_block = span // slab
    blocks = usable // span

    def multiply(index, slot):
        start = pl.multiple_of(index * span, span)
        for tile in range(0, tiles, 2):
            width = min(2, tiles - tile) * LANES
            here = pl.ds(pl.multiple_of(start + tile * LANES, LANES), width)
            products[slot, :, tile * LANES : tile * LANES + width] = jnp.dot(
                left[...], shifts[:, here], preferred_element_type=F32
            )

    def gather(index, slot):
        def tree(first, number):
            if number == 1:
                return products[slot, first * count : (first + 1) * count, :]
            half = number // 2
            later = pltpu.roll(tree(first + half, half), span + LANES - half, 1)
            return tree(first, half) + later

        total = tree(0, FINE)
        for piece in range(per_block):
            out_ref[first + index * per_block + piece] = total[:, piece * slab : (piece + 1) * slab]

    multiply(0, 0)
    if blocks <= 4:
        for index in range(1, blocks):
            multiply(index, index % 2)
            gather(index - 1, (index - 1) % 2)
    else:

        def step(index, carry):
            multiply(index, lax.rem(index, 2))
            gather(index - 1, lax.rem(index + 1, 2))
            return carry

        lax.fori_loop(1, blocks, step, 0)
    gather(blocks - 1, (blocks - 1) % 2)


def first_dots_kernel(*refs):
    tpls, (samples_ref, out_ref, left, shifts, products) = refs[:-5], refs[-5:]
    columns = shifts.shape[1] + LANES
    correlate(tpls, samples_ref[:, :columns], out_ref, 0, left, shifts, products)


def last_dots_kernel(*refs):
    tpls, (samples_ref, halo_ref, mask_ref, done_ref) = refs[:-11], refs[-11:-7]
    (keep_ref, send_ref), (out_ref, edges, *scratch) = refs[-7:-5], refs[-5:]
    first, slab = done_ref.shape[0], done_ref.shape[2]
    group = edges.shape[0]
    window = halo_ref.shape[1]
    after = [samples_ref[:, (m + 1) * slab : (m + 1) * slab + window] for m in range(group - 1)]
    squares = masked_squares(mask_ref[...], jnp.concatenate(after + [halo_ref[...]], axis=1))
    column = lax.broadcasted_iota(jnp.int32, squares.shape, 1) & (window - 1)
    reach = 1
    while reach < window:
        earlier = pltpu.roll(squares, reach, 1)
        squares = squares + jnp.where(column >= reach, earlier, 0.0)
        reach *= 2
    squares = jnp.where(column >= 1, pltpu.roll(squares, 1, 1), 0.0)
    for member in range(group):
        edges[member] = squares[:, member * window : (member + 1) * window]
    rest = samples_ref.shape[1] + window - scratch[1].shape[1] - LANES
    samples = jnp.concatenate([samples_ref[:, rest:], halo_ref[...]], axis=1)
    out_ref[:first] = done_ref[...]
    correlate(tpls, samples, out_ref, first, *scratch)
    core = lax.rem(lax.axis_index("inner"), 2)
    run = keep_ref.shape[0] // 2
    for y in range(2):
        for tm in range(run):
            for ref, side in ((keep_ref, core), (send_ref, 1 - core)):
                member = (2 * y + side) * run + tm
                ref[y * run + tm, :, :slab] = out_ref[member]
                ref[y * run + tm, :, slab:] = edges[member]


def add_kernel(tm_count, keep_ref, got_ref, *outs):
    me = lax.div(lax.axis_index("inner"), 2) * tm_count + lax.axis_index("tm")
    for flip, out_ref in enumerate(outs):
        out_ref[...] = keep_ref[me ^ flip] + got_ref[me ^ flip]


def masked_squares(mask, wave):
    wave = wave.astype(F32)
    squares = wave * wave
    high = squares.astype(BF16)
    low = (squares - high.astype(F32)).astype(BF16)
    return jnp.dot(mask, high, preferred_element_type=F32) + jnp.dot(
        mask, low, preferred_element_type=F32
    )


def mask_kernel(stations, channels, tm_count, *refs):
    tpls, (order_ref, scale_ref, mask_ref, part_ref) = refs[:-4], refs[-4:]
    rows = tpls[0].shape[1]
    count = len(tpls) * INNER
    padded = INNER * LANES
    part = LANES // tm_count
    meta = lax.dot_general(
        spare_lanes(part, part * channels // padded),
        jnp.concatenate([pack[...].reshape(INNER * rows, LANES) for pack in tpls], axis=0),
        (((1,), (1,)), ((), ())),
        preferred_element_type=F32,
    )
    template = lax.broadcasted_iota(jnp.int32, (count, count), 0)
    place = lax.broadcasted_iota(jnp.int32, (count, count), 1)
    sort = jnp.where(place == arrival(template, count), 1.0, 0.0).astype(BF16)
    slots = -(-stations // rows)

    def read(slot):
        return jnp.concatenate(
            [meta[slot : slot + 1, t * rows : (t + 1) * rows] for t in range(count)], axis=0
        )

    values = jnp.concatenate([read(slot) for slot in range(slots + 1)], axis=1)
    values = jnp.dot(sort, values.astype(BF16), preferred_element_type=F32)
    start = slots * rows
    scale = jnp.sum(values[:, start : start + 3], axis=1, keepdims=True)
    scale_ref[...] = jnp.broadcast_to(scale, scale_ref.shape)
    mask = jnp.dot(
        values[:, :stations].astype(BF16),
        one_hot(order_ref[...], stations),
        preferred_element_type=F32,
    ).astype(BF16)
    mask_ref[...] = mask
    grouped = jnp.dot(mask, regroup(channels, padded, part), preferred_element_type=F32)
    mine = side_major(lax.axis_index("inner")) * LANES + lax.axis_index("tm") * part
    part_ref[...] = pltpu.roll(grouped, lax.rem(padded - mine, padded), 1)[:, :part].astype(BF16)


def power_kernel(window, wave_ref, mask_ref, after, out_ref):
    del after
    power = masked_squares(mask_ref[...], wave_ref[...])
    columns = power.shape[1]
    column = lax.broadcasted_iota(jnp.int32, power.shape, 1)
    reach = 1
    while reach < window:
        later = pltpu.roll(power, columns - reach, 1)
        power = power + jnp.where(column < columns - reach, later, 0.0)
        reach *= 2
    out_ref[...] = power


def finish_kernel(*refs):
    parts, (power_ref, scale_ref, out_ref) = refs[:-3], refs[-3:]
    slab = power_ref.shape[1]
    total = parts[0][...]
    for part in parts[1:]:
        total = total + part[...]
    dots, edge = total[:, :slab], total[:, slab:]
    inside = slab - edge.shape[1]
    energy = jnp.concatenate(
        [power_ref[:, :inside], power_ref[:, inside:] + edge], axis=1
    )
    out_ref[...] = dots * (scale_ref[:, :1] / jnp.sqrt(energy + EPSILON))


def on_device(waveforms, templates, station_mask, channel_order):
    channels, slab = waveforms.shape
    rows, _, window = templates.shape
    stations = station_mask.shape[1]
    outer_count, tm_count = lax.axis_size("outer"), lax.axis_size("tm")
    blk_count = outer_count * INNER
    assert rows == 1 and LANES % tm_count == 0
    group = INNER * tm_count
    padded = INNER * LANES
    part = padded // group
    chunk = group * slab
    span = 2 * slab
    total = blk_count * tm_count
    blk, every = ("outer", "inner"), ("outer", "inner", "tm")
    sds = jax.ShapeDtypeStruct
    order_row = channel_order[None, :]

    rows = window * part // LANES
    held = [
        pltpu.with_memory_space_constraint(x, pltpu.HBM)
        for x in (waveforms, templates, station_mask, order_row)
    ]
    send, keep, *pieces = call(
        functools.partial(prologue_kernel, tm_count),
        [HBM] * 4,
        [
            sds((padded // 2 * slab // LANES + rows, LANES), BF16),
            sds((padded // 2, slab), BF16),
            *[sds((rows, LANES), BF16)] * (INNER - 1),
        ],
        [
            pltpu.VMEM((channels, slab), BF16),
            pltpu.VMEM((padded, slab), BF16),
            pltpu.VMEM((channels, window), BF16),
            pltpu.VMEM((padded, window), BF16),
            pltpu.VMEM((1, stations), jnp.int32),
            pltpu.VMEM((1, channels), jnp.int32),
            pltpu.VMEM((window, padded), F32),
            pltpu.SemaphoreType.DMA((4,)),
        ],
        bytes_accessed=channels * (window + slab) * 2,
    )(*held)

    def plane(part, flip):
        return lax.ppermute(part, "inner", [(b, b ^ flip) for b in range(INNER)])

    got = plane(send, 1)
    others = [plane(pieces[1], 2), plane(pieces[2], 3)]
    pack = call(
        pack_kernel, [VMEM] * INNER, sds((INNER, rows, LANES), BF16), bytes_accessed=rows * LANES * 8
    )(pieces[0], got, *others)

    def shift(distance):
        return lax.ppermute(
            pack, "outer", [(b, (b + distance) % outer_count) for b in range(outer_count)]
        )

    tpls = [pack] + [shift(distance) for distance in range(1, outer_count)]

    half = group // 2
    def split(flips, after):
        return call(
            functools.partial(split_kernel, tm_count, flips),
            [VMEM, VMEM, AFTER],
            [sds((2, part, slab), BF16)] * len(flips),
            bytes_accessed=padded * slab * 2,
        )(keep, got, after)

    parts = split(range(tm_count), got) + split(range(tm_count, half), tpls[1])

    def swap(part, flip):
        y, tm = flip // tm_count, flip % tm_count
        route = [(i, i ^ (2 * tm_count * y + tm)) for i in range(total)]
        return lax.ppermute(part, every, route)

    waves = [parts[0]] + [swap(parts[flip], flip) for flip in range(1, half)]
    samples, head = call(
        functools.partial(join_kernel, tm_count),
        [VMEM] * half,
        [sds((part, chunk), BF16), sds((part, window), BF16)],
        bytes_accessed=part * chunk * 4,
    )(*waves)
    halo = lax.ppermute(head, "outer", [(b, b - 1) for b in range(1, outer_count)])

    scale, mask, mask_part = call(
        functools.partial(mask_kernel, stations, channels, tm_count),
        [VMEM] * (outer_count + 1),
        [
            sds((blk_count, LANES), F32),
            sds((blk_count, channels), BF16),
            sds((blk_count, part), BF16),
        ],
        bytes_accessed=blk_count * rows * LANES * 2,
    )(*tpls, order_row)

    depth = window // FINE * part

    def scratch(columns):
        return [
            pltpu.VMEM((blk_count * FINE, depth), BF16),
            pltpu.VMEM((depth, columns + LANES), BF16),
            pltpu.VMEM((2, blk_count * FINE, span + LANES), F32),
        ]

    blocks = group // 2
    work = 2 * blk_count * window * part * span
    partials = call(
        first_dots_kernel,
        [VMEM] * (outer_count + 1),
        sds((2 * (blocks - 1), blk_count, slab), F32),
        scratch((blocks - 1) * span),
        flops=work * (blocks - 1),
        bytes_accessed=part * chunk * 2,
    )(*tpls, samples)
    keep, send = call(
        last_dots_kernel,
        [VMEM] * (outer_count + 4),
        [sds((half, blk_count, slab + window), F32)] * 2,
        [
            pltpu.VMEM((group, blk_count, slab), F32),
            pltpu.VMEM((group, blk_count, window), F32),
        ]
        + scratch(span),
        flops=work,
        bytes_accessed=part * chunk * 2,
    )(*tpls, samples, halo, mask_part, partials)
    got = lax.ppermute(send, "inner", [(b, b ^ 1) for b in range(INNER)])
    power = call(
        functools.partial(power_kernel, window),
        [VMEM, VMEM, AFTER],
        sds((blk_count, slab), F32),
        flops=4 * blk_count * channels * slab,
        bytes_accessed=channels * slab * 2,
    )(waveforms, mask, send)
    sums = call(
        functools.partial(add_kernel, tm_count),
        [VMEM] * 2,
        [sds((blk_count, slab + window), F32)] * half,
        bytes_accessed=blk_count * slab * 12 * half,
    )(keep, got)
    sums = [sums[0]] + [swap(sums[flip], flip) for flip in range(1, half)]
    return call(
        finish_kernel,
        [VMEM] * (half + 2),
        sds((blk_count, slab), F32),
        bytes_accessed=blk_count * slab * 4 * (half + 2),
    )(*sums, power, scale)


def solution(mesh):
    blk_count, tm_count = mesh.devices.shape
    shape = (blk_count // INNER, INNER, tm_count)
    mesh = jax.sharding.Mesh(mesh.devices.reshape(shape), ("outer", "inner", "tm"))
    blk, every = ("outer", "inner"), ("outer", "inner", "tm")
    placed = (P(None, every), P(blk, None, None), P(blk, None), P())
    return jax.shard_map(
        on_device, mesh=mesh, in_specs=placed, out_specs=P(None, every), check_vma=False
    )
```

```python
import functools

import jax
import jax.numpy as jnp
from jax import lax
from jax.experimental import pallas as pl
from jax.experimental.pallas import tpu as pltpu
from jax.sharding import PartitionSpec as P

EPSILON = 1e-05
LANES = 128
INNER = 4
FINE = 16
MIB = 1024 * 1024

BF16 = jnp.bfloat16
F32 = jnp.float32


HBM = pl.BlockSpec(memory_space=pltpu.HBM)
VMEM = pl.BlockSpec(memory_space=pltpu.VMEM)
AFTER = pl.BlockSpec(memory_space=pl.ANY)


def call(kernel, in_specs, out_shape, scratch=(), flops=0, bytes_accessed=0, vmem=24):
    return pl.pallas_call(
        kernel,
        in_specs=in_specs,
        out_specs=jax.tree.map(lambda _: VMEM, out_shape),
        out_shape=out_shape,
        scratch_shapes=list(scratch),
        compiler_params=pltpu.CompilerParams(vmem_limit_bytes=vmem * MIB),
        cost_estimate=pl.CostEstimate(
            flops=flops, bytes_accessed=bytes_accessed, transcendentals=0
        ),
    )


def one_hot(order_row, station_count):
    columns = order_row.shape[1]
    first = 3 * lax.broadcasted_iota(jnp.int32, (station_count, columns), 0)
    hit = (order_row >= first) & (order_row < first + 3)
    return jnp.where(hit, 1.0, 0.0).astype(BF16)


def side_major(inner):
    return lax.rem(inner, 2) * (INNER // 2) + lax.div(inner, 2)


def place_of(real, part):
    base = real // FINE * FINE
    return base, real - base


def regroup_rows(source, target, part):
    channels, width = source.shape
    groups = target.shape[0] // part
    real = channels // groups
    base, extra = place_of(real, part)
    rest = source[groups * base :, :].astype(F32)
    fill = jnp.zeros((part - real, width), F32)
    for group in range(groups):
        if base:
            run = source[group * base : (group + 1) * base, :]
            target[group * part : group * part + base, :] = run
        piece = [rest[group * extra : (group + 1) * extra], fill]
        target[group * part + base : (group + 1) * part, :] = jnp.concatenate(
            piece, axis=0
        ).astype(BF16)


def regroup(channels, padded, part):
    groups = padded // part
    real = channels // groups
    base, extra = place_of(real, part)
    channel = lax.broadcasted_iota(jnp.int32, (channels, padded), 0)
    place = lax.broadcasted_iota(jnp.int32, (1, padded), 1)
    group, within = place >> (part.bit_length() - 1), place & (part - 1)
    rest = groups * base + extra * group + within - base
    source = jnp.where(within < base, base * group + within, rest)
    source = jnp.where(within < real, source, -1)
    return jnp.where(channel == source, 1.0, 0.0).astype(BF16)


def spare_lanes(part, real):
    slots = LANES // part * (part - real)
    slot = lax.broadcasted_iota(jnp.int32, (8, LANES), 0)
    lane = lax.broadcasted_iota(jnp.int32, (8, LANES), 1)
    spare = part - real
    home = lax.div(slot, spare) * part + real + lax.rem(slot, spare)
    return jnp.where((lane == home) & (slot < slots), 1.0, 0.0).astype(BF16)


def prologue_kernel(tm_count, wave_hbm, tpl_hbm, flag_hbm, order_hbm, *refs):
    send_ref, samples_ref, *outs = refs[: INNER + 1]
    wave_ref, grouped, tpl_ref, tpl_grouped, flag_ref, order_ref, turned, sems = refs[INNER + 1 :]
    channels, window = tpl_hbm.shape[1:]
    copies = [
        pltpu.make_async_copy(flag_hbm, flag_ref, sems.at[0]),
        pltpu.make_async_copy(order_hbm, order_ref, sems.at[1]),
        pltpu.make_async_copy(tpl_hbm.at[0], tpl_ref, sems.at[2]),
        pltpu.make_async_copy(wave_hbm, wave_ref, sems.at[3]),
    ]
    for copy in copies:
        copy.start()
    stations = flag_ref.shape[1]
    padded = turned.shape[1]
    part = LANES // tm_count
    rows = outs[0].shape[0]
    groups = regroup(channels, padded, part)
    copies[0].wait()
    copies[1].wait()
    flags = jnp.broadcast_to(flag_ref[...].astype(F32), (8, stations))
    mask = jnp.dot(
        flags.astype(BF16), one_hot(order_ref[...], stations), preferred_element_type=F32
    )
    live = jnp.sum(mask[:1], keepdims=True)
    mask = jnp.dot(mask.astype(BF16), groups, preferred_element_type=F32)[:1]
    copies[2].wait()
    regroup_rows(tpl_ref, tpl_grouped, part)
    masked = tpl_grouped[...].T.astype(F32) * mask
    turned[...] = masked
    norm = jnp.sqrt(jnp.sum(masked * masked, keepdims=True) + EPSILON)
    rest = jnp.broadcast_to(jnp.sqrt(window * live) / norm, (1, rows))
    row = lax.broadcasted_iota(jnp.int32, (1, rows), 1)
    scale = jnp.zeros((1, rows), F32)
    for piece in range(3):
        now = rest.astype(BF16).astype(F32)
        scale = jnp.where(row == piece, now, scale)
        rest = rest - now
    slots = -(-stations // rows)
    wide = flags[:1]
    if stations % rows:
        wide = jnp.concatenate([wide, jnp.zeros((1, rows - stations % rows), F32)], axis=1)
    meta = [wide[:, slot * rows : (slot + 1) * rows] for slot in range(slots)] + [scale]
    meta = jnp.concatenate(meta + [jnp.zeros((8 - len(meta), rows), F32)], axis=0)
    meta = lax.dot_general(
        meta.astype(BF16),
        spare_lanes(part, part * channels // padded),
        (((0,), (0,)), ((), ())),
        preferred_element_type=F32,
    )
    my_tm = lax.axis_index("tm")
    my_inner = lax.axis_index("inner")
    my_core = lax.rem(my_inner, 2)
    first = send_ref.shape[0] - rows
    spot = lax.broadcasted_iota(jnp.int32, (FINE, LANES), 1) >> (part.bit_length() - 1)
    for flip in range(INNER):
        start = pl.multiple_of(side_major(my_inner ^ flip) * LANES, LANES)
        pieces = []
        for step in range(window // (FINE * tm_count)):
            tile = jnp.zeros((FINE, LANES), F32)
            for within in range(tm_count):
                row = FINE * (step * tm_count + within)
                chunk = turned[row : row + FINE, pl.ds(start, LANES)]
                turn = lax.rem(part * (within - my_tm) + LANES, LANES)
                tile = jnp.where(spot == within, pltpu.roll(chunk, turn, 1), tile)
            pieces.append(tile)
        payload = (jnp.concatenate(pieces, axis=0) + meta).astype(BF16)
        if flip == 1:
            send_ref[first:, :] = payload
        else:
            outs[flip - (flip > 1)][...] = payload

    copies[3].wait()
    regroup_rows(wave_ref, grouped, part)
    half = padded // 2
    samples_ref[...] = grouped[pl.ds(pl.multiple_of(my_core * half, half), half), :]
    theirs = pl.ds(pl.multiple_of((1 - my_core) * half, half), half)
    for tile in range(first // half):
        columns = slice(tile * LANES, (tile + 1) * LANES)
        send_ref[tile * half : (tile + 1) * half, :] = grouped[theirs, columns]


def pack_kernel(mine_ref, core_ref, y_ref, both_ref, out_ref):
    inner = lax.axis_index("inner")
    rows = mine_ref.shape[0]
    out_ref[inner] = mine_ref[...]
    out_ref[inner ^ 1] = core_ref[core_ref.shape[0] - rows :, :]
    out_ref[inner ^ 2] = y_ref[...]
    out_ref[inner ^ 3] = both_ref[...]


def split_kernel(tm_count, flips, keep_ref, got_ref, after, *outs):
    del after
    my_inner = lax.axis_index("inner")
    core = lax.rem(my_inner, 2)
    me = lax.div(my_inner, 2) * tm_count + lax.axis_index("tm")
    part = outs[0].shape[1]
    half, slab = keep_ref.shape
    for flip, out_ref in zip(flips, outs):
        start = (me ^ flip) * part
        out_ref[core] = keep_ref[pl.ds(pl.multiple_of(start, part), part), :]
        for tile in range(slab // LANES):
            rows = pl.ds(pl.multiple_of(tile * half + start, part), part)
            out_ref[1 - core, :, tile * LANES : (tile + 1) * LANES] = got_ref[rows, :]


def join_kernel(tm_count, *refs):
    parts, out_ref, head_ref = refs[:-2], refs[-2], refs[-1]
    me = lax.div(lax.axis_index("inner"), 2) * tm_count + lax.axis_index("tm")
    slab = parts[0].shape[2]
    for flip, part in enumerate(parts):
        other = me ^ flip
        y, tm = lax.div(other, tm_count), lax.rem(other, tm_count)
        for core in range(2):
            place = (y * 2 + core) * tm_count + tm
            out_ref[:, pl.ds(pl.multiple_of(place * slab, slab), slab)] = part[core]
    head_ref[...] = out_ref[:, : head_ref.shape[1]]


def arrival(template, count):
    inner = template & (INNER - 1)
    return ((lax.axis_index("outer") * INNER - (template - inner)) & (count - 1)) + inner


def correlate(tpls, samples, out_ref, first, left, shifts, products):
    slab = out_ref.shape[2]
    part, columns = samples.shape
    size, depth = left.shape
    copies = LANES // FINE
    usable = columns - 2 * LANES
    for copy in range(depth // part):
        tile, turn = copy // copies * LANES, copy % copies * FINE
        turned = samples if turn == 0 else pltpu.roll(samples, columns - turn, 1)
        shifts[copy * part : (copy + 1) * part, :] = turned[:, tile : tile + usable + LANES]
    count = len(tpls) * INNER
    row = lax.broadcasted_iota(jnp.int32, (size, size), 0)
    column = lax.broadcasted_iota(jnp.int32, (size, size), 1)
    shift = count.bit_length() - 1
    source = arrival(row & (count - 1), count) * FINE + (row >> shift)
    order = jnp.where(column == source, 1.0, 0.0).astype(BF16)
    for step in range(depth // LANES):
        rows = [
            pack[:, FINE * step : FINE * (step + 1), :].reshape(INNER * FINE, LANES)
            for pack in tpls
        ]
        left[:, step * LANES : (step + 1) * LANES] = jnp.dot(
            order, jnp.concatenate(rows, axis=0), preferred_element_type=F32
        ).astype(BF16)
    tiles = products.shape[2] // LANES
    span = (tiles - 1) * LANES
    per_block = span // slab
    blocks = usable // span

    def multiply(index, slot):
        start = pl.multiple_of(index * span, span)
        for tile in range(0, tiles, 2):
            width = min(2, tiles - tile) * LANES
            here = pl.ds(pl.multiple_of(start + tile * LANES, LANES), width)
            products[slot, :, tile * LANES : tile * LANES + width] = jnp.dot(
                left[...], shifts[:, here], preferred_element_type=F32
            )

    def gather(index, slot):
        def tree(first, number):
            if number == 1:
                return products[slot, first * count : (first + 1) * count, :]
            half = number // 2
            later = pltpu.roll(tree(first + half, half), span + LANES - half, 1)
            return tree(first, half) + later

        total = tree(0, FINE)
        for piece in range(per_block):
            out_ref[first + index * per_block + piece] = total[:, piece * slab : (piece + 1) * slab]

    multiply(0, 0)
    if blocks <= 4:
        for index in range(1, blocks):
            multiply(index, index % 2)
            gather(index - 1, (index - 1) % 2)
    else:

        def step(index, carry):
            multiply(index, lax.rem(index, 2))
            gather(index - 1, lax.rem(index + 1, 2))
            return carry

        lax.fori_loop(1, blocks, step, 0)
    gather(blocks - 1, (blocks - 1) % 2)


def first_dots_kernel(*refs):
    tpls, (samples_ref, out_ref, left, shifts, products) = refs[:-5], refs[-5:]
    columns = shifts.shape[1] + LANES
    correlate(tpls, samples_ref[:, :columns], out_ref, 0, left, shifts, products)


def last_dots_kernel(*refs):
    tpls, (samples_ref, halo_ref, mask_ref, done_ref) = refs[:-11], refs[-11:-7]
    (keep_ref, send_ref), (out_ref, edges, *scratch) = refs[-7:-5], refs[-5:]
    first, slab = done_ref.shape[0], done_ref.shape[2]
    group = edges.shape[0]
    window = halo_ref.shape[1]
    after = [samples_ref[:, (m + 1) * slab : (m + 1) * slab + window] for m in range(group - 1)]
    squares = masked_squares(mask_ref[...], jnp.concatenate(after + [halo_ref[...]], axis=1))
    column = lax.broadcasted_iota(jnp.int32, squares.shape, 1) & (window - 1)
    reach = 1
    while reach < window:
        earlier = pltpu.roll(squares, reach, 1)
        squares = squares + jnp.where(column >= reach, earlier, 0.0)
        reach *= 2
    squares = jnp.where(column >= 1, pltpu.roll(squares, 1, 1), 0.0)
    for member in range(group):
        edges[member] = squares[:, member * window : (member + 1) * window]
    rest = samples_ref.shape[1] + window - scratch[1].shape[1] - LANES
    samples = jnp.concatenate([samples_ref[:, rest:], halo_ref[...]], axis=1)
    out_ref[:first] = done_ref[...]
    correlate(tpls, samples, out_ref, first, *scratch)
    core = lax.rem(lax.axis_index("inner"), 2)
    run = keep_ref.shape[0] // 2
    for y in range(2):
        for tm in range(run):
            for ref, side in ((keep_ref, core), (send_ref, 1 - core)):
                member = (2 * y + side) * run + tm
                ref[y * run + tm, :, :slab] = out_ref[member]
                ref[y * run + tm, :, slab:] = edges[member]


def add_kernel(tm_count, keep_ref, got_ref, *outs):
    me = lax.div(lax.axis_index("inner"), 2) * tm_count + lax.axis_index("tm")
    for flip, out_ref in enumerate(outs):
        out_ref[...] = keep_ref[me ^ flip] + got_ref[me ^ flip]


def masked_squares(mask, wave):
    wave = wave.astype(F32)
    squares = wave * wave
    high = squares.astype(BF16)
    low = (squares - high.astype(F32)).astype(BF16)
    return jnp.dot(mask, high, preferred_element_type=F32) + jnp.dot(
        mask, low, preferred_element_type=F32
    )


def mask_kernel(stations, channels, tm_count, *refs):
    tpls, (order_ref, scale_ref, mask_ref, part_ref) = refs[:-4], refs[-4:]
    rows = tpls[0].shape[1]
    count = len(tpls) * INNER
    padded = INNER * LANES
    part = LANES // tm_count
    meta = lax.dot_general(
        spare_lanes(part, part * channels // padded),
        jnp.concatenate([pack[...].reshape(INNER * rows, LANES) for pack in tpls], axis=0),
        (((1,), (1,)), ((), ())),
        preferred_element_type=F32,
    )
    template = lax.broadcasted_iota(jnp.int32, (count, count), 0)
    place = lax.broadcasted_iota(jnp.int32, (count, count), 1)
    sort = jnp.where(place == arrival(template, count), 1.0, 0.0).astype(BF16)
    slots = -(-stations // rows)

    def read(slot):
        return jnp.concatenate(
            [meta[slot : slot + 1, t * rows : (t + 1) * rows] for t in range(count)], axis=0
        )

    values = jnp.concatenate([read(slot) for slot in range(slots + 1)], axis=1)
    values = jnp.dot(sort, values.astype(BF16), preferred_element_type=F32)
    start = slots * rows
    scale = jnp.sum(values[:, start : start + 3], axis=1, keepdims=True)
    scale_ref[...] = jnp.broadcast_to(scale, scale_ref.shape)
    mask = jnp.dot(
        values[:, :stations].astype(BF16),
        one_hot(order_ref[...], stations),
        preferred_element_type=F32,
    ).astype(BF16)
    mask_ref[...] = mask
    grouped = jnp.dot(mask, regroup(channels, padded, part), preferred_element_type=F32)
    mine = side_major(lax.axis_index("inner")) * LANES + lax.axis_index("tm") * part
    part_ref[...] = pltpu.roll(grouped, lax.rem(padded - mine, padded), 1)[:, :part].astype(BF16)


def power_kernel(window, wave_ref, mask_ref, after, out_ref):
    del after
    power = masked_squares(mask_ref[...], wave_ref[...])
    columns = power.shape[1]
    column = lax.broadcasted_iota(jnp.int32, power.shape, 1)
    reach = 1
    while reach < window:
        later = pltpu.roll(power, columns - reach, 1)
        power = power + jnp.where(column < columns - reach, later, 0.0)
        reach *= 2
    out_ref[...] = power


def finish_kernel(*refs):
    parts, (power_ref, scale_ref, out_ref) = refs[:-3], refs[-3:]
    slab = power_ref.shape[1]
    total = parts[0][...]
    for part in parts[1:]:
        total = total + part[...]
    dots, edge = total[:, :slab], total[:, slab:]
    inside = slab - edge.shape[1]
    energy = jnp.concatenate(
        [power_ref[:, :inside], power_ref[:, inside:] + edge], axis=1
    )
    out_ref[...] = dots * (scale_ref[:, :1] / jnp.sqrt(energy + EPSILON))


def on_device(waveforms, templates, station_mask, channel_order):
    channels, slab = waveforms.shape
    rows, _, window = templates.shape
    stations = station_mask.shape[1]
    outer_count, tm_count = lax.axis_size("outer"), lax.axis_size("tm")
    blk_count = outer_count * INNER
    assert rows == 1 and LANES % tm_count == 0
    group = INNER * tm_count
    padded = INNER * LANES
    part = padded // group
    chunk = group * slab
    span = 2 * slab
    total = blk_count * tm_count
    blk, every = ("outer", "inner"), ("outer", "inner", "tm")
    sds = jax.ShapeDtypeStruct
    order_row = channel_order[None, :]

    rows = window * part // LANES
    held = [
        pltpu.with_memory_space_constraint(x, pltpu.HBM)
        for x in (waveforms, templates, station_mask, order_row)
    ]
    send, keep, *pieces = call(
        functools.partial(prologue_kernel, tm_count),
        [HBM] * 4,
        [
            sds((padded // 2 * slab // LANES + rows, LANES), BF16),
            sds((padded // 2, slab), BF16),
            *[sds((rows, LANES), BF16)] * (INNER - 1),
        ],
        [
            pltpu.VMEM((channels, slab), BF16),
            pltpu.VMEM((padded, slab), BF16),
            pltpu.VMEM((channels, window), BF16),
            pltpu.VMEM((padded, window), BF16),
            pltpu.VMEM((1, stations), jnp.int32),
            pltpu.VMEM((1, channels), jnp.int32),
            pltpu.VMEM((window, padded), F32),
            pltpu.SemaphoreType.DMA((4,)),
        ],
        bytes_accessed=channels * (window + slab) * 2,
    )(*held)

    def plane(part, flip):
        return lax.ppermute(part, "inner", [(b, b ^ flip) for b in range(INNER)])

    got = plane(send, 1)
    others = [plane(pieces[1], 2), plane(pieces[2], 3)]
    pack = call(
        pack_kernel, [VMEM] * INNER, sds((INNER, rows, LANES), BF16), bytes_accessed=rows * LANES * 8
    )(pieces[0], got, *others)

    def shift(distance):
        return lax.ppermute(
            pack, "outer", [(b, (b + distance) % outer_count) for b in range(outer_count)]
        )

    tpls = [pack] + [shift(distance) for distance in range(1, outer_count)]

    half = group // 2
    def split(flips, after):
        return call(
            functools.partial(split_kernel, tm_count, flips),
            [VMEM, VMEM, AFTER],
            [sds((2, part, slab), BF16)] * len(flips),
            bytes_accessed=padded * slab * 2,
        )(keep, got, after)

    def swap(part, flip):
        y, tm = flip // tm_count, flip % tm_count
        route = [(i, i ^ (2 * tm_count * y + tm)) for i in range(total)]
        return lax.ppermute(part, every, route)

    parts = split(range(tm_count), pack)
    waves = [parts[0]] + [swap(parts[flip], flip) for flip in range(1, tm_count)]
    parts += split(range(tm_count, half), waves[1])
    waves += [swap(parts[flip], flip) for flip in range(tm_count, half)]
    samples, head = call(
        functools.partial(join_kernel, tm_count),
        [VMEM] * half,
        [sds((part, chunk), BF16), sds((part, window), BF16)],
        bytes_accessed=part * chunk * 4,
    )(*waves)
    halo = lax.ppermute(head, "outer", [(b, b - 1) for b in range(1, outer_count)])

    scale, mask, mask_part = call(
        functools.partial(mask_kernel, stations, channels, tm_count),
        [VMEM] * (outer_count + 1),
        [
            sds((blk_count, LANES), F32),
            sds((blk_count, channels), BF16),
            sds((blk_count, part), BF16),
        ],
        bytes_accessed=blk_count * rows * LANES * 2,
    )(*tpls, order_row)

    depth = window // FINE * part

    def scratch(columns):
        return [
            pltpu.VMEM((blk_count * FINE, depth), BF16),
            pltpu.VMEM((depth, columns + LANES), BF16),
            pltpu.VMEM((2, blk_count * FINE, span + LANES), F32),
        ]

    blocks = group // 2
    work = 2 * blk_count * window * part * span
    partials = call(
        first_dots_kernel,
        [VMEM] * (outer_count + 1),
        sds((2 * (blocks - 1), blk_count, slab), F32),
        scratch((blocks - 1) * span),
        flops=work * (blocks - 1),
        bytes_accessed=part * chunk * 2,
    )(*tpls, samples)
    keep, send = call(
        last_dots_kernel,
        [VMEM] * (outer_count + 4),
        [sds((half, blk_count, slab + window), F32)] * 2,
        [
            pltpu.VMEM((group, blk_count, slab), F32),
            pltpu.VMEM((group, blk_count, window), F32),
        ]
        + scratch(span),
        flops=work,
        bytes_accessed=part * chunk * 2,
    )(*tpls, samples, halo, mask_part, partials)
    got = lax.ppermute(send, "inner", [(b, b ^ 1) for b in range(INNER)])
    power = call(
        functools.partial(power_kernel, window),
        [VMEM, VMEM, AFTER],
        sds((blk_count, slab), F32),
        flops=4 * blk_count * channels * slab,
        bytes_accessed=channels * slab * 2,
    )(waveforms, mask, send)
    sums = call(
        functools.partial(add_kernel, tm_count),
        [VMEM] * 2,
        [sds((blk_count, slab + window), F32)] * half,
        bytes_accessed=blk_count * slab * 12 * half,
    )(keep, got)
    sums = [sums[0]] + [swap(sums[flip], flip) for flip in range(1, half)]
    return call(
        finish_kernel,
        [VMEM] * (half + 2),
        sds((blk_count, slab), F32),
        bytes_accessed=blk_count * slab * 4 * (half + 2),
    )(*sums, power, scale)


def solution(mesh):
    blk_count, tm_count = mesh.devices.shape
    shape = (blk_count // INNER, INNER, tm_count)
    mesh = jax.sharding.Mesh(mesh.devices.reshape(shape), ("outer", "inner", "tm"))
    blk, every = ("outer", "inner"), ("outer", "inner", "tm")
    placed = (P(None, every), P(blk, None, None), P(blk, None), P())
    return jax.shard_map(
        on_device, mesh=mesh, in_specs=placed, out_specs=P(None, every), check_vma=False
    )
```

```python
import functools

import jax
import jax.numpy as jnp
from jax import lax
from jax.experimental import pallas as pl
from jax.experimental.pallas import tpu as pltpu
from jax.sharding import PartitionSpec as P

EPSILON = 1e-05
LANES = 128
INNER = 4
FINE = 16
MIB = 1024 * 1024

BF16 = jnp.bfloat16
F32 = jnp.float32


HBM = pl.BlockSpec(memory_space=pltpu.HBM)
VMEM = pl.BlockSpec(memory_space=pltpu.VMEM)
AFTER = pl.BlockSpec(memory_space=pl.ANY)


def call(kernel, in_specs, out_shape, scratch=(), flops=0, bytes_accessed=0, vmem=24):
    return pl.pallas_call(
        kernel,
        in_specs=in_specs,
        out_specs=jax.tree.map(lambda _: VMEM, out_shape),
        out_shape=out_shape,
        scratch_shapes=list(scratch),
        compiler_params=pltpu.CompilerParams(vmem_limit_bytes=vmem * MIB),
        cost_estimate=pl.CostEstimate(
            flops=flops, bytes_accessed=bytes_accessed, transcendentals=0
        ),
    )


def one_hot(order_row, station_count):
    columns = order_row.shape[1]
    first = 3 * lax.broadcasted_iota(jnp.int32, (station_count, columns), 0)
    hit = (order_row >= first) & (order_row < first + 3)
    return jnp.where(hit, 1.0, 0.0).astype(BF16)


def side_major(inner):
    return lax.rem(inner, 2) * (INNER // 2) + lax.div(inner, 2)


def place_of(real, part):
    base = real // FINE * FINE
    return base, real - base


def regroup_rows(source, target, part):
    channels, width = source.shape
    groups = target.shape[0] // part
    real = channels // groups
    base, extra = place_of(real, part)
    rest = source[groups * base :, :].astype(F32)
    fill = jnp.zeros((part - real, width), F32)
    for group in range(groups):
        if base:
            run = source[group * base : (group + 1) * base, :]
            target[group * part : group * part + base, :] = run
        piece = [rest[group * extra : (group + 1) * extra], fill]
        target[group * part + base : (group + 1) * part, :] = jnp.concatenate(
            piece, axis=0
        ).astype(BF16)


def regroup(channels, padded, part):
    groups = padded // part
    real = channels // groups
    base, extra = place_of(real, part)
    channel = lax.broadcasted_iota(jnp.int32, (channels, padded), 0)
    place = lax.broadcasted_iota(jnp.int32, (1, padded), 1)
    group, within = place >> (part.bit_length() - 1), place & (part - 1)
    rest = groups * base + extra * group + within - base
    source = jnp.where(within < base, base * group + within, rest)
    source = jnp.where(within < real, source, -1)
    return jnp.where(channel == source, 1.0, 0.0).astype(BF16)


def spare_lanes(part, real):
    slots = LANES // part * (part - real)
    slot = lax.broadcasted_iota(jnp.int32, (8, LANES), 0)
    lane = lax.broadcasted_iota(jnp.int32, (8, LANES), 1)
    spare = part - real
    home = lax.div(slot, spare) * part + real + lax.rem(slot, spare)
    return jnp.where((lane == home) & (slot < slots), 1.0, 0.0).astype(BF16)


def prologue_kernel(tm_count, wave_hbm, tpl_hbm, flag_hbm, order_hbm, *refs):
    send_ref, samples_ref, *outs = refs[: INNER + 1]
    wave_ref, grouped, tpl_ref, tpl_grouped, flag_ref, order_ref, turned, sems = refs[INNER + 1 :]
    channels, window = tpl_hbm.shape[1:]
    copies = [
        pltpu.make_async_copy(flag_hbm, flag_ref, sems.at[0]),
        pltpu.make_async_copy(order_hbm, order_ref, sems.at[1]),
        pltpu.make_async_copy(tpl_hbm.at[0], tpl_ref, sems.at[2]),
        pltpu.make_async_copy(wave_hbm, wave_ref, sems.at[3]),
    ]
    for copy in copies:
        copy.start()
    stations = flag_ref.shape[1]
    padded = turned.shape[1]
    part = LANES // tm_count
    rows = outs[0].shape[0]
    groups = regroup(channels, padded, part)
    copies[0].wait()
    copies[1].wait()
    flags = jnp.broadcast_to(flag_ref[...].astype(F32), (8, stations))
    mask = jnp.dot(
        flags.astype(BF16), one_hot(order_ref[...], stations), preferred_element_type=F32
    )
    live = jnp.sum(mask[:1], keepdims=True)
    mask = jnp.dot(mask.astype(BF16), groups, preferred_element_type=F32)[:1]
    copies[2].wait()
    regroup_rows(tpl_ref, tpl_grouped, part)
    masked = tpl_grouped[...].T.astype(F32) * mask
    turned[...] = masked
    norm = jnp.sqrt(jnp.sum(masked * masked, keepdims=True) + EPSILON)
    rest = jnp.broadcast_to(jnp.sqrt(window * live) / norm, (1, rows))
    row = lax.broadcasted_iota(jnp.int32, (1, rows), 1)
    scale = jnp.zeros((1, rows), F32)
    for piece in range(3):
        now = rest.astype(BF16).astype(F32)
        scale = jnp.where(row == piece, now, scale)
        rest = rest - now
    slots = -(-stations // rows)
    wide = flags[:1]
    if stations % rows:
        wide = jnp.concatenate([wide, jnp.zeros((1, rows - stations % rows), F32)], axis=1)
    meta = [wide[:, slot * rows : (slot + 1) * rows] for slot in range(slots)] + [scale]
    meta = jnp.concatenate(meta + [jnp.zeros((8 - len(meta), rows), F32)], axis=0)
    meta = lax.dot_general(
        meta.astype(BF16),
        spare_lanes(part, part * channels // padded),
        (((0,), (0,)), ((), ())),
        preferred_element_type=F32,
    )
    my_tm = lax.axis_index("tm")
    my_inner = lax.axis_index("inner")
    my_core = lax.rem(my_inner, 2)
    first = send_ref.shape[0] - rows
    spot = lax.broadcasted_iota(jnp.int32, (FINE, LANES), 1) >> (part.bit_length() - 1)
    for flip in range(INNER):
        start = pl.multiple_of(side_major(my_inner ^ flip) * LANES, LANES)
        pieces = []
        for step in range(window // (FINE * tm_count)):
            tile = jnp.zeros((FINE, LANES), F32)
            for within in range(tm_count):
                row = FINE * (step * tm_count + within)
                chunk = turned[row : row + FINE, pl.ds(start, LANES)]
                turn = lax.rem(part * (within - my_tm) + LANES, LANES)
                tile = jnp.where(spot == within, pltpu.roll(chunk, turn, 1), tile)
            pieces.append(tile)
        payload = (jnp.concatenate(pieces, axis=0) + meta).astype(BF16)
        if flip == 1:
            send_ref[first:, :] = payload
        else:
            outs[flip - (flip > 1)][...] = payload

    copies[3].wait()
    regroup_rows(wave_ref, grouped, part)
    half = padded // 2
    samples_ref[...] = grouped[pl.ds(pl.multiple_of(my_core * half, half), half), :]
    theirs = pl.ds(pl.multiple_of((1 - my_core) * half, half), half)
    for tile in range(first // half):
        columns = slice(tile * LANES, (tile + 1) * LANES)
        send_ref[tile * half : (tile + 1) * half, :] = grouped[theirs, columns]


def pack_kernel(mine_ref, core_ref, y_ref, both_ref, out_ref):
    inner = lax.axis_index("inner")
    rows = mine_ref.shape[0]
    out_ref[inner] = mine_ref[...]
    out_ref[inner ^ 1] = core_ref[core_ref.shape[0] - rows :, :]
    out_ref[inner ^ 2] = y_ref[...]
    out_ref[inner ^ 3] = both_ref[...]


def split_kernel(tm_count, flips, keep_ref, got_ref, after, *outs):
    del after
    my_inner = lax.axis_index("inner")
    core = lax.rem(my_inner, 2)
    me = lax.div(my_inner, 2) * tm_count + lax.axis_index("tm")
    part = outs[0].shape[1]
    half, slab = keep_ref.shape
    for flip, out_ref in zip(flips, outs):
        start = (me ^ flip) * part
        out_ref[core] = keep_ref[pl.ds(pl.multiple_of(start, part), part), :]
        for tile in range(slab // LANES):
            rows = pl.ds(pl.multiple_of(tile * half + start, part), part)
            out_ref[1 - core, :, tile * LANES : (tile + 1) * LANES] = got_ref[rows, :]


def join_kernel(tm_count, *refs):
    parts, out_ref, head_ref = refs[:-2], refs[-2], refs[-1]
    me = lax.div(lax.axis_index("inner"), 2) * tm_count + lax.axis_index("tm")
    slab = parts[0].shape[2]
    for flip, part in enumerate(parts):
        other = me ^ flip
        y, tm = lax.div(other, tm_count), lax.rem(other, tm_count)
        for core in range(2):
            place = (y * 2 + core) * tm_count + tm
            out_ref[:, pl.ds(pl.multiple_of(place * slab, slab), slab)] = part[core]
    head_ref[...] = out_ref[:, : head_ref.shape[1]]


def arrival(template):
    return template ^ (lax.axis_index("outer") * INNER)


def arrange(tpls, left):
    size, depth = left.shape
    count = len(tpls) * INNER
    row = lax.broadcasted_iota(jnp.int32, (size, size), 0)
    column = lax.broadcasted_iota(jnp.int32, (size, size), 1)
    shift = count.bit_length() - 1
    source = arrival(row & (count - 1)) * FINE + (row >> shift)
    order = jnp.where(column == source, 1.0, 0.0).astype(BF16)
    for step in range(depth // LANES):
        rows = [
            pack[:, FINE * step : FINE * (step + 1), :].reshape(INNER * FINE, LANES)
            for pack in tpls
        ]
        left[:, step * LANES : (step + 1) * LANES] = jnp.dot(
            order, jnp.concatenate(rows, axis=0), preferred_element_type=F32
        ).astype(BF16)


def correlate(left, full, out_ref, slab, side, shifts, products):
    part = full.shape[0]
    size, depth = left.shape
    count = size // FINE
    copies = LANES // FINE
    run = out_ref.shape[0] // 2
    width = run * slab
    for y in range(2):
        columns = width + 2 * LANES
        start = pl.multiple_of((2 * y + side) * width, width)
        samples = full[:, pl.ds(start, columns)]
        for copy in range(depth // part):
            tile, turn = copy // copies * LANES, copy % copies * FINE
            turned = samples if turn == 0 else pltpu.roll(samples, columns - turn, 1)
            shifts[y, copy * part : (copy + 1) * part, :] = turned[:, tile : tile + width + LANES]
    tiles = products.shape[2] // LANES
    span = (tiles - 1) * LANES
    per_block = span // slab
    blocks = [(y, index) for y in range(2) for index in range(width // span)]

    def multiply(place, slot):
        y, index = place
        for tile in range(0, tiles, 2):
            start = index * span + tile * LANES
            lanes = min(2, tiles - tile) * LANES
            products[slot, :, tile * LANES : tile * LANES + lanes] = jnp.dot(
                left[...], shifts[y, :, start : start + lanes], preferred_element_type=F32
            )

    def gather(place, slot):
        def tree(first, number):
            if number == 1:
                return products[slot, first * count : (first + 1) * count, :]
            half = number // 2
            later = pltpu.roll(tree(first + half, half), span + LANES - half, 1)
            return tree(first, half) + later

        total = tree(0, FINE)
        y, index = place
        for piece in range(per_block):
            out_ref[y * run + index * per_block + piece, :, :slab] = total[
                :, piece * slab : (piece + 1) * slab
            ]

    multiply(blocks[0], 0)
    for number in range(1, len(blocks)):
        multiply(blocks[number], number % 2)
        gather(blocks[number - 1], (number - 1) % 2)
    gather(blocks[-1], (len(blocks) - 1) % 2)


def first_dots_kernel(stations, channels, tm_count, *refs):
    tpls, (order_ref, samples_ref, halo_ref) = refs[:-12], refs[-12:-9]
    send_ref, edges_ref, left, scale_ref, mask_ref = refs[-9:-4]
    full, edges, shifts, products = refs[-4:]
    core = lax.rem(lax.axis_index("inner"), 2)
    group, _, window = edges.shape
    chunk = samples_ref.shape[1]
    slab = chunk // group
    full[:, :chunk] = samples_ref[...]
    full[:, chunk:] = halo_ref[...]
    arrange(tpls, left)
    correlate(left, full, send_ref, slab, 1 - core, shifts, products)
    part_mask = read_masks(stations, channels, tm_count, tpls, order_ref, scale_ref, mask_ref)
    after = [full[:, (m + 1) * slab : (m + 1) * slab + window] for m in range(group)]
    squares = masked_squares(part_mask, jnp.concatenate(after, axis=1))
    column = lax.broadcasted_iota(jnp.int32, squares.shape, 1) & (window - 1)
    reach = 1
    while reach < window:
        earlier = pltpu.roll(squares, reach, 1)
        squares = squares + jnp.where(column >= reach, earlier, 0.0)
        reach *= 2
    squares = jnp.where(column >= 1, pltpu.roll(squares, 1, 1), 0.0)
    for member in range(group):
        edges[member] = squares[:, member * window : (member + 1) * window]
    run = group // 4
    for y in range(2):
        for tm in range(run):
            send_ref[y * run + tm, :, slab:] = edges[(2 * y + 1 - core) * run + tm]
            edges_ref[y * run + tm] = edges[(2 * y + core) * run + tm]


def second_dots_kernel(left, samples_ref, halo_ref, edges_ref, after, keep_ref, *scratch):
    del after
    full, shifts, products = scratch
    chunk = samples_ref.shape[1]
    full[:, :chunk] = samples_ref[...]
    full[:, chunk:] = halo_ref[...]
    core = lax.rem(lax.axis_index("inner"), 2)
    slab = keep_ref.shape[2] - edges_ref.shape[2]
    correlate(left, full, keep_ref, slab, core, shifts, products)
    keep_ref[:, :, slab:] = edges_ref[...]


def add_kernel(tm_count, keep_ref, got_ref, *outs):
    me = lax.div(lax.axis_index("inner"), 2) * tm_count + lax.axis_index("tm")
    for flip, out_ref in enumerate(outs):
        out_ref[...] = keep_ref[me ^ flip] + got_ref[me ^ flip]


def masked_squares(mask, wave):
    wave = wave.astype(F32)
    squares = wave * wave
    high = squares.astype(BF16)
    low = (squares - high.astype(F32)).astype(BF16)
    return jnp.dot(mask, high, preferred_element_type=F32) + jnp.dot(
        mask, low, preferred_element_type=F32
    )


def read_masks(stations, channels, tm_count, tpls, order_ref, scale_ref, mask_ref):
    rows = tpls[0].shape[1]
    count = len(tpls) * INNER
    padded = INNER * LANES
    part = LANES // tm_count
    meta = lax.dot_general(
        spare_lanes(part, part * channels // padded),
        jnp.concatenate([pack[...].reshape(INNER * rows, LANES) for pack in tpls], axis=0),
        (((1,), (1,)), ((), ())),
        preferred_element_type=F32,
    )
    template = lax.broadcasted_iota(jnp.int32, (count, count), 0)
    place = lax.broadcasted_iota(jnp.int32, (count, count), 1)
    sort = jnp.where(place == arrival(template), 1.0, 0.0).astype(BF16)
    slots = -(-stations // rows)

    def read(slot):
        return jnp.concatenate(
            [meta[slot : slot + 1, t * rows : (t + 1) * rows] for t in range(count)], axis=0
        )

    values = jnp.concatenate([read(slot) for slot in range(slots + 1)], axis=1)
    values = jnp.dot(sort, values.astype(BF16), preferred_element_type=F32)
    start = slots * rows
    scale = jnp.sum(values[:, start : start + 3], axis=1, keepdims=True)
    scale_ref[...] = jnp.broadcast_to(scale, scale_ref.shape)
    mask = jnp.dot(
        values[:, :stations].astype(BF16),
        one_hot(order_ref[...], stations),
        preferred_element_type=F32,
    ).astype(BF16)
    mask_ref[...] = mask
    grouped = jnp.dot(mask, regroup(channels, padded, part), preferred_element_type=F32)
    mine = side_major(lax.axis_index("inner")) * LANES + lax.axis_index("tm") * part
    return pltpu.roll(grouped, lax.rem(padded - mine, padded), 1)[:, :part].astype(BF16)


def power_kernel(window, wave_ref, mask_ref, after, out_ref):
    del after
    power = masked_squares(mask_ref[...], wave_ref[...])
    columns = power.shape[1]
    column = lax.broadcasted_iota(jnp.int32, power.shape, 1)
    reach = 1
    while reach < window:
        later = pltpu.roll(power, columns - reach, 1)
        power = power + jnp.where(column < columns - reach, later, 0.0)
        reach *= 2
    out_ref[...] = power


def finish_kernel(*refs):
    parts, (power_ref, scale_ref, out_ref) = refs[:-3], refs[-3:]
    slab = power_ref.shape[1]
    total = parts[0][...]
    for part in parts[1:]:
        total = total + part[...]
    dots, edge = total[:, :slab], total[:, slab:]
    inside = slab - edge.shape[1]
    energy = jnp.concatenate(
        [power_ref[:, :inside], power_ref[:, inside:] + edge], axis=1
    )
    out_ref[...] = dots * (scale_ref[:, :1] / jnp.sqrt(energy + EPSILON))


def on_device(waveforms, templates, station_mask, channel_order):
    channels, slab = waveforms.shape
    rows, _, window = templates.shape
    stations = station_mask.shape[1]
    outer_count, tm_count = lax.axis_size("outer"), lax.axis_size("tm")
    blk_count = outer_count * INNER
    assert rows == 1 and LANES % tm_count == 0
    group = INNER * tm_count
    padded = INNER * LANES
    part = padded // group
    chunk = group * slab
    span = 2 * slab
    total = blk_count * tm_count
    blk, every = ("outer", "inner"), ("outer", "inner", "tm")
    sds = jax.ShapeDtypeStruct
    order_row = channel_order[None, :]

    rows = window * part // LANES
    held = [
        pltpu.with_memory_space_constraint(x, pltpu.HBM)
        for x in (waveforms, templates, station_mask, order_row)
    ]
    send, keep, *pieces = call(
        functools.partial(prologue_kernel, tm_count),
        [HBM] * 4,
        [
            sds((padded // 2 * slab // LANES + rows, LANES), BF16),
            sds((padded // 2, slab), BF16),
            *[sds((rows, LANES), BF16)] * (INNER - 1),
        ],
        [
            pltpu.VMEM((channels, slab), BF16),
            pltpu.VMEM((padded, slab), BF16),
            pltpu.VMEM((channels, window), BF16),
            pltpu.VMEM((padded, window), BF16),
            pltpu.VMEM((1, stations), jnp.int32),
            pltpu.VMEM((1, channels), jnp.int32),
            pltpu.VMEM((window, padded), F32),
            pltpu.SemaphoreType.DMA((4,)),
        ],
        bytes_accessed=channels * (window + slab) * 2,
    )(*held)

    def plane(part, flip):
        return lax.ppermute(part, "inner", [(b, b ^ flip) for b in range(INNER)])

    got = plane(send, 1)
    others = [plane(pieces[1], 2), plane(pieces[2], 3)]
    pack = call(
        pack_kernel, [VMEM] * INNER, sds((INNER, rows, LANES), BF16), bytes_accessed=rows * LANES * 8
    )(pieces[0], got, *others)

    tpls = [pack] + [
        lax.ppermute(pack, "outer", [(b, b ^ flip) for b in range(outer_count)])
        for flip in range(1, outer_count)
    ]

    half = group // 2
    def split(flips, after):
        return call(
            functools.partial(split_kernel, tm_count, flips),
            [VMEM, VMEM, AFTER],
            [sds((2, part, slab), BF16)] * len(flips),
            bytes_accessed=padded * slab * 2,
        )(keep, got, after)

    def swap(part, flip):
        y, tm = flip // tm_count, flip % tm_count
        route = [(i, i ^ (2 * tm_count * y + tm)) for i in range(total)]
        return lax.ppermute(part, every, route)

    parts = split(range(tm_count), pack)
    waves = [parts[0]] + [swap(parts[flip], flip) for flip in range(1, tm_count)]
    parts += split(range(tm_count, half), tpls[1])
    waves += [swap(parts[flip], flip) for flip in range(tm_count, half)]
    samples, head = call(
        functools.partial(join_kernel, tm_count),
        [VMEM] * half,
        [sds((part, chunk), BF16), sds((part, window), BF16)],
        bytes_accessed=part * chunk * 4,
    )(*waves)
    halo = lax.ppermute(head, "outer", [(b, b - 1) for b in range(1, outer_count)])

    depth = window // FINE * part
    count = blk_count
    work = 2 * count * window * part * chunk // 2

    def scratch():
        return [
            pltpu.VMEM((2, depth, chunk // 4 + LANES), BF16),
            pltpu.VMEM((2, count * FINE, span + LANES), F32),
        ]

    send, edges, left, scale, mask = call(
        functools.partial(first_dots_kernel, stations, channels, tm_count),
        [VMEM] * (outer_count + 3),
        [
            sds((half, count, slab + window), F32),
            sds((half, count, window), F32),
            sds((count * FINE, depth), BF16),
            sds((count, LANES), F32),
            sds((count, channels), BF16),
        ],
        [
            pltpu.VMEM((part, chunk + window), BF16),
            pltpu.VMEM((group, count, window), F32),
        ]
        + scratch(),
        flops=work,
        bytes_accessed=part * chunk * 2,
        vmem=36,
    )(*tpls, order_row, samples, halo)
    keep = call(
        second_dots_kernel,
        [VMEM] * 4 + [AFTER],
        sds((half, count, slab + window), F32),
        [pltpu.VMEM((part, chunk + window), BF16)] + scratch(),
        flops=work,
        bytes_accessed=part * chunk * 2,
        vmem=36,
    )(left, samples, halo, edges, send)
    got = lax.ppermute(send, "inner", [(b, b ^ 1) for b in range(INNER)])
    power = call(
        functools.partial(power_kernel, window),
        [VMEM, VMEM, AFTER],
        sds((blk_count, slab), F32),
        flops=4 * blk_count * channels * slab,
        bytes_accessed=channels * slab * 2,
    )(waveforms, mask, keep)
    sums = call(
        functools.partial(add_kernel, tm_count),
        [VMEM] * 2,
        [sds((blk_count, slab + window), F32)] * half,
        bytes_accessed=blk_count * slab * 12 * half,
    )(keep, got)
    sums = [sums[0]] + [swap(sums[flip], flip) for flip in range(1, half)]
    return call(
        finish_kernel,
        [VMEM] * (half + 2),
        sds((blk_count, slab), F32),
        bytes_accessed=blk_count * slab * 4 * (half + 2),
    )(*sums, power, scale)


def solution(mesh):
    blk_count, tm_count = mesh.devices.shape
    shape = (blk_count // INNER, INNER, tm_count)
    mesh = jax.sharding.Mesh(mesh.devices.reshape(shape), ("outer", "inner", "tm"))
    blk, every = ("outer", "inner"), ("outer", "inner", "tm")
    placed = (P(None, every), P(blk, None, None), P(blk, None), P())
    return jax.shard_map(
        on_device, mesh=mesh, in_specs=placed, out_specs=P(None, every), check_vma=False
    )
```

```python
import functools

import jax
import jax.numpy as jnp
from jax import lax
from jax.experimental import pallas as pl
from jax.experimental.pallas import tpu as pltpu
from jax.sharding import PartitionSpec as P

EPSILON = 1e-05
LANES = 128
INNER = 4
FINE = 16
MIB = 1024 * 1024

BF16 = jnp.bfloat16
F32 = jnp.float32


HBM = pl.BlockSpec(memory_space=pltpu.HBM)
VMEM = pl.BlockSpec(memory_space=pltpu.VMEM)
AFTER = pl.BlockSpec(memory_space=pl.ANY)


def call(kernel, in_specs, out_shape, scratch=(), flops=0, bytes_accessed=0, vmem=24):
    return pl.pallas_call(
        kernel,
        in_specs=in_specs,
        out_specs=jax.tree.map(lambda _: VMEM, out_shape),
        out_shape=out_shape,
        scratch_shapes=list(scratch),
        compiler_params=pltpu.CompilerParams(vmem_limit_bytes=vmem * MIB),
        cost_estimate=pl.CostEstimate(
            flops=flops, bytes_accessed=bytes_accessed, transcendentals=0
        ),
    )


def one_hot(order_row, station_count):
    columns = order_row.shape[1]
    first = 3 * lax.broadcasted_iota(jnp.int32, (station_count, columns), 0)
    hit = (order_row >= first) & (order_row < first + 3)
    return jnp.where(hit, 1.0, 0.0).astype(BF16)


def side_major(inner):
    return lax.rem(inner, 2) * (INNER // 2) + lax.div(inner, 2)


def place_of(real, part):
    base = real // FINE * FINE
    return base, real - base


def regroup_rows(source, target, part):
    channels, width = source.shape
    groups = target.shape[0] // part
    real = channels // groups
    base, extra = place_of(real, part)
    rest = source[groups * base :, :].astype(F32)
    fill = jnp.zeros((part - real, width), F32)
    for group in range(groups):
        if base:
            run = source[group * base : (group + 1) * base, :]
            target[group * part : group * part + base, :] = run
        piece = [rest[group * extra : (group + 1) * extra], fill]
        target[group * part + base : (group + 1) * part, :] = jnp.concatenate(
            piece, axis=0
        ).astype(BF16)


def regroup(channels, padded, part):
    groups = padded // part
    real = channels // groups
    base, extra = place_of(real, part)
    channel = lax.broadcasted_iota(jnp.int32, (channels, padded), 0)
    place = lax.broadcasted_iota(jnp.int32, (1, padded), 1)
    group, within = place >> (part.bit_length() - 1), place & (part - 1)
    rest = groups * base + extra * group + within - base
    source = jnp.where(within < base, base * group + within, rest)
    source = jnp.where(within < real, source, -1)
    return jnp.where(channel == source, 1.0, 0.0).astype(BF16)


def spare_lanes(part, real):
    slots = LANES // part * (part - real)
    slot = lax.broadcasted_iota(jnp.int32, (8, LANES), 0)
    lane = lax.broadcasted_iota(jnp.int32, (8, LANES), 1)
    spare = part - real
    home = lax.div(slot, spare) * part + real + lax.rem(slot, spare)
    return jnp.where((lane == home) & (slot < slots), 1.0, 0.0).astype(BF16)


def prologue_kernel(tm_count, wave_hbm, tpl_hbm, flag_hbm, order_hbm, *refs):
    send_ref, samples_ref, *outs = refs[: INNER + 1]
    wave_ref, grouped, tpl_ref, tpl_grouped, flag_ref, order_ref, turned, sems = refs[INNER + 1 :]
    channels, window = tpl_hbm.shape[1:]
    copies = [
        pltpu.make_async_copy(flag_hbm, flag_ref, sems.at[0]),
        pltpu.make_async_copy(order_hbm, order_ref, sems.at[1]),
        pltpu.make_async_copy(tpl_hbm.at[0], tpl_ref, sems.at[2]),
        pltpu.make_async_copy(wave_hbm, wave_ref, sems.at[3]),
    ]
    for copy in copies:
        copy.start()
    stations = flag_ref.shape[1]
    padded = turned.shape[1]
    part = LANES // tm_count
    rows = outs[0].shape[0]
    groups = regroup(channels, padded, part)
    copies[0].wait()
    copies[1].wait()
    flags = jnp.broadcast_to(flag_ref[...].astype(F32), (8, stations))
    mask = jnp.dot(
        flags.astype(BF16), one_hot(order_ref[...], stations), preferred_element_type=F32
    )
    live = jnp.sum(mask[:1], keepdims=True)
    mask = jnp.dot(mask.astype(BF16), groups, preferred_element_type=F32)[:1]
    copies[2].wait()
    regroup_rows(tpl_ref, tpl_grouped, part)
    masked = tpl_grouped[...].T.astype(F32) * mask
    turned[...] = masked
    norm = jnp.sqrt(jnp.sum(masked * masked, keepdims=True) + EPSILON)
    rest = jnp.broadcast_to(jnp.sqrt(window * live) / norm, (1, rows))
    row = lax.broadcasted_iota(jnp.int32, (1, rows), 1)
    scale = jnp.zeros((1, rows), F32)
    for piece in range(3):
        now = rest.astype(BF16).astype(F32)
        scale = jnp.where(row == piece, now, scale)
        rest = rest - now
    slots = -(-stations // rows)
    wide = flags[:1]
    if stations % rows:
        wide = jnp.concatenate([wide, jnp.zeros((1, rows - stations % rows), F32)], axis=1)
    meta = [wide[:, slot * rows : (slot + 1) * rows] for slot in range(slots)] + [scale]
    meta = jnp.concatenate(meta + [jnp.zeros((8 - len(meta), rows), F32)], axis=0)
    meta = lax.dot_general(
        meta.astype(BF16),
        spare_lanes(part, part * channels // padded),
        (((0,), (0,)), ((), ())),
        preferred_element_type=F32,
    )
    my_tm = lax.axis_index("tm")
    my_inner = lax.axis_index("inner")
    my_core = lax.rem(my_inner, 2)
    first = send_ref.shape[0] - rows
    spot = lax.broadcasted_iota(jnp.int32, (FINE, LANES), 1) >> (part.bit_length() - 1)
    for flip in range(INNER):
        start = pl.multiple_of(side_major(my_inner ^ flip) * LANES, LANES)
        pieces = []
        for step in range(window // (FINE * tm_count)):
            tile = jnp.zeros((FINE, LANES), F32)
            for within in range(tm_count):
                row = FINE * (step * tm_count + within)
                chunk = turned[row : row + FINE, pl.ds(start, LANES)]
                turn = lax.rem(part * (within - my_tm) + LANES, LANES)
                tile = jnp.where(spot == within, pltpu.roll(chunk, turn, 1), tile)
            pieces.append(tile)
        payload = (jnp.concatenate(pieces, axis=0) + meta).astype(BF16)
        if flip == 1:
            send_ref[first:, :] = payload
        else:
            outs[flip - (flip > 1)][...] = payload

    copies[3].wait()
    regroup_rows(wave_ref, grouped, part)
    half = padded // 2
    samples_ref[...] = grouped[pl.ds(pl.multiple_of(my_core * half, half), half), :]
    theirs = pl.ds(pl.multiple_of((1 - my_core) * half, half), half)
    for tile in range(first // half):
        columns = slice(tile * LANES, (tile + 1) * LANES)
        send_ref[tile * half : (tile + 1) * half, :] = grouped[theirs, columns]


def pack_kernel(mine_ref, core_ref, y_ref, both_ref, out_ref):
    inner = lax.axis_index("inner")
    rows = mine_ref.shape[0]
    out_ref[inner] = mine_ref[...]
    out_ref[inner ^ 1] = core_ref[core_ref.shape[0] - rows :, :]
    out_ref[inner ^ 2] = y_ref[...]
    out_ref[inner ^ 3] = both_ref[...]


def split_kernel(tm_count, keep_ref, got_ref, *outs):
    my_inner = lax.axis_index("inner")
    core = lax.rem(my_inner, 2)
    me = lax.div(my_inner, 2) * tm_count + lax.axis_index("tm")
    part = outs[0].shape[1]
    half, slab = keep_ref.shape
    for flip, out_ref in enumerate(outs):
        start = (me ^ flip) * part
        out_ref[core] = keep_ref[pl.ds(pl.multiple_of(start, part), part), :]
        for tile in range(slab // LANES):
            rows = pl.ds(pl.multiple_of(tile * half + start, part), part)
            out_ref[1 - core, :, tile * LANES : (tile + 1) * LANES] = got_ref[rows, :]


def join_kernel(tm_count, *refs):
    parts, out_ref, head_ref = refs[:-2], refs[-2], refs[-1]
    me = lax.div(lax.axis_index("inner"), 2) * tm_count + lax.axis_index("tm")
    slab = parts[0].shape[2]
    for flip, part in enumerate(parts):
        other = me ^ flip
        y, tm = lax.div(other, tm_count), lax.rem(other, tm_count)
        for core in range(2):
            place = (y * 2 + core) * tm_count + tm
            out_ref[:, pl.ds(pl.multiple_of(place * slab, slab), slab)] = part[core]
    head_ref[...] = out_ref[:, : head_ref.shape[1]]


def arrival(template):
    return template ^ (lax.axis_index("outer") * INNER)


def arrange(tpls, left):
    size, depth = left.shape
    count = len(tpls) * INNER
    row = lax.broadcasted_iota(jnp.int32, (size, size), 0)
    column = lax.broadcasted_iota(jnp.int32, (size, size), 1)
    shift = count.bit_length() - 1
    source = arrival(row & (count - 1)) * FINE + (row >> shift)
    order = jnp.where(column == source, 1.0, 0.0).astype(BF16)
    for step in range(depth // LANES):
        rows = [
            pack[:, FINE * step : FINE * (step + 1), :].reshape(INNER * FINE, LANES)
            for pack in tpls
        ]
        left[:, step * LANES : (step + 1) * LANES] = jnp.dot(
            order, jnp.concatenate(rows, axis=0), preferred_element_type=F32
        ).astype(BF16)


def correlate(left, full, out_ref, slab, side, shifts, products):
    part = full.shape[0]
    size, depth = left.shape
    count = size // FINE
    copies = LANES // FINE
    run = out_ref.shape[0] // 2
    width = run * slab
    for y in range(2):
        columns = width + 2 * LANES
        start = pl.multiple_of((2 * y + side) * width, width)
        samples = full[:, pl.ds(start, columns)]
        for copy in range(depth // part):
            tile, turn = copy // copies * LANES, copy % copies * FINE
            turned = samples if turn == 0 else pltpu.roll(samples, columns - turn, 1)
            shifts[y, copy * part : (copy + 1) * part, :] = turned[:, tile : tile + width + LANES]
    tiles = products.shape[2] // LANES
    span = (tiles - 1) * LANES
    per_block = span // slab
    blocks = [(y, index) for y in range(2) for index in range(width // span)]

    def multiply(place, slot):
        y, index = place
        for tile in range(0, tiles, 2):
            start = index * span + tile * LANES
            lanes = min(2, tiles - tile) * LANES
            products[slot, :, tile * LANES : tile * LANES + lanes] = jnp.dot(
                left[...], shifts[y, :, start : start + lanes], preferred_element_type=F32
            )

    def gather(place, slot):
        def tree(first, number):
            if number == 1:
                return products[slot, first * count : (first + 1) * count, :]
            half = number // 2
            later = pltpu.roll(tree(first + half, half), span + LANES - half, 1)
            return tree(first, half) + later

        total = tree(0, FINE)
        y, index = place
        for piece in range(per_block):
            out_ref[y * run + index * per_block + piece, :, :slab] = total[
                :, piece * slab : (piece + 1) * slab
            ]

    multiply(blocks[0], 0)
    for number in range(1, len(blocks)):
        multiply(blocks[number], number % 2)
        gather(blocks[number - 1], (number - 1) % 2)
    gather(blocks[-1], (len(blocks) - 1) % 2)


def first_dots_kernel(stations, channels, tm_count, *refs):
    tpls, (order_ref, samples_ref, halo_ref) = refs[:-12], refs[-12:-9]
    send_ref, edges_ref, left, scale_ref, mask_ref = refs[-9:-4]
    full, edges, shifts, products = refs[-4:]
    core = lax.rem(lax.axis_index("inner"), 2)
    group, _, window = edges.shape
    chunk = samples_ref.shape[1]
    slab = chunk // group
    full[:, :chunk] = samples_ref[...]
    full[:, chunk:] = halo_ref[...]
    arrange(tpls, left)
    correlate(left, full, send_ref, slab, 1 - core, shifts, products)
    part_mask = read_masks(stations, channels, tm_count, tpls, order_ref, scale_ref, mask_ref)
    after = [full[:, (m + 1) * slab : (m + 1) * slab + window] for m in range(group)]
    squares = masked_squares(part_mask, jnp.concatenate(after, axis=1))
    column = lax.broadcasted_iota(jnp.int32, squares.shape, 1) & (window - 1)
    reach = 1
    while reach < window:
        earlier = pltpu.roll(squares, reach, 1)
        squares = squares + jnp.where(column >= reach, earlier, 0.0)
        reach *= 2
    squares = jnp.where(column >= 1, pltpu.roll(squares, 1, 1), 0.0)
    for member in range(group):
        edges[member] = squares[:, member * window : (member + 1) * window]
    run = group // 4
    for y in range(2):
        for tm in range(run):
            send_ref[y * run + tm, :, slab:] = edges[(2 * y + 1 - core) * run + tm]
            edges_ref[y * run + tm] = edges[(2 * y + core) * run + tm]


def second_dots_kernel(left, samples_ref, halo_ref, edges_ref, after, keep_ref, *scratch):
    del after
    full, shifts, products = scratch
    chunk = samples_ref.shape[1]
    full[:, :chunk] = samples_ref[...]
    full[:, chunk:] = halo_ref[...]
    core = lax.rem(lax.axis_index("inner"), 2)
    slab = keep_ref.shape[2] - edges_ref.shape[2]
    correlate(left, full, keep_ref, slab, core, shifts, products)
    keep_ref[:, :, slab:] = edges_ref[...]


def add_kernel(tm_count, keep_ref, got_ref, *outs):
    me = lax.div(lax.axis_index("inner"), 2) * tm_count + lax.axis_index("tm")
    for flip, out_ref in enumerate(outs):
        out_ref[...] = keep_ref[me ^ flip] + got_ref[me ^ flip]


def masked_squares(mask, wave):
    wave = wave.astype(F32)
    squares = wave * wave
    high = squares.astype(BF16)
    low = (squares - high.astype(F32)).astype(BF16)
    return jnp.dot(mask, high, preferred_element_type=F32) + jnp.dot(
        mask, low, preferred_element_type=F32
    )


def read_masks(stations, channels, tm_count, tpls, order_ref, scale_ref, mask_ref):
    rows = tpls[0].shape[1]
    count = len(tpls) * INNER
    padded = INNER * LANES
    part = LANES // tm_count
    meta = lax.dot_general(
        spare_lanes(part, part * channels // padded),
        jnp.concatenate([pack[...].reshape(INNER * rows, LANES) for pack in tpls], axis=0),
        (((1,), (1,)), ((), ())),
        preferred_element_type=F32,
    )
    template = lax.broadcasted_iota(jnp.int32, (count, count), 0)
    place = lax.broadcasted_iota(jnp.int32, (count, count), 1)
    sort = jnp.where(place == arrival(template), 1.0, 0.0).astype(BF16)
    slots = -(-stations // rows)

    def read(slot):
        return jnp.concatenate(
            [meta[slot : slot + 1, t * rows : (t + 1) * rows] for t in range(count)], axis=0
        )

    values = jnp.concatenate([read(slot) for slot in range(slots + 1)], axis=1)
    values = jnp.dot(sort, values.astype(BF16), preferred_element_type=F32)
    start = slots * rows
    scale = jnp.sum(values[:, start : start + 3], axis=1, keepdims=True)
    scale_ref[...] = jnp.broadcast_to(scale, scale_ref.shape)
    mask = jnp.dot(
        values[:, :stations].astype(BF16),
        one_hot(order_ref[...], stations),
        preferred_element_type=F32,
    ).astype(BF16)
    mask_ref[...] = mask
    grouped = jnp.dot(mask, regroup(channels, padded, part), preferred_element_type=F32)
    mine = side_major(lax.axis_index("inner")) * LANES + lax.axis_index("tm") * part
    return pltpu.roll(grouped, lax.rem(padded - mine, padded), 1)[:, :part].astype(BF16)


def power_kernel(window, wave_ref, mask_ref, after, out_ref):
    del after
    power = masked_squares(mask_ref[...], wave_ref[...])
    columns = power.shape[1]
    column = lax.broadcasted_iota(jnp.int32, power.shape, 1)
    reach = 1
    while reach < window:
        later = pltpu.roll(power, columns - reach, 1)
        power = power + jnp.where(column < columns - reach, later, 0.0)
        reach *= 2
    out_ref[...] = power


def finish_kernel(*refs):
    parts, (power_ref, scale_ref, out_ref) = refs[:-3], refs[-3:]
    slab = power_ref.shape[1]
    total = parts[0][...]
    for part in parts[1:]:
        total = total + part[...]
    dots, edge = total[:, :slab], total[:, slab:]
    inside = slab - edge.shape[1]
    energy = jnp.concatenate(
        [power_ref[:, :inside], power_ref[:, inside:] + edge], axis=1
    )
    out_ref[...] = dots * (scale_ref[:, :1] / jnp.sqrt(energy + EPSILON))


def on_device(waveforms, templates, station_mask, channel_order):
    channels, slab = waveforms.shape
    rows, _, window = templates.shape
    stations = station_mask.shape[1]
    outer_count, tm_count = lax.axis_size("outer"), lax.axis_size("tm")
    blk_count = outer_count * INNER
    assert rows == 1 and LANES % tm_count == 0
    group = INNER * tm_count
    padded = INNER * LANES
    part = padded // group
    chunk = group * slab
    span = 2 * slab
    total = blk_count * tm_count
    blk, every = ("outer", "inner"), ("outer", "inner", "tm")
    sds = jax.ShapeDtypeStruct
    order_row = channel_order[None, :]

    rows = window * part // LANES
    held = [
        pltpu.with_memory_space_constraint(x, pltpu.HBM)
        for x in (waveforms, templates, station_mask, order_row)
    ]
    send, keep, *pieces = call(
        functools.partial(prologue_kernel, tm_count),
        [HBM] * 4,
        [
            sds((padded // 2 * slab // LANES + rows, LANES), BF16),
            sds((padded // 2, slab), BF16),
            *[sds((rows, LANES), BF16)] * (INNER - 1),
        ],
        [
            pltpu.VMEM((channels, slab), BF16),
            pltpu.VMEM((padded, slab), BF16),
            pltpu.VMEM((channels, window), BF16),
            pltpu.VMEM((padded, window), BF16),
            pltpu.VMEM((1, stations), jnp.int32),
            pltpu.VMEM((1, channels), jnp.int32),
            pltpu.VMEM((window, padded), F32),
            pltpu.SemaphoreType.DMA((4,)),
        ],
        bytes_accessed=channels * (window + slab) * 2,
    )(*held)

    def plane(part, flip):
        return lax.ppermute(part, "inner", [(b, b ^ flip) for b in range(INNER)])

    got = plane(send, 1)
    others = [plane(pieces[1], 2), plane(pieces[2], 3)]
    pack = call(
        pack_kernel, [VMEM] * INNER, sds((INNER, rows, LANES), BF16), bytes_accessed=rows * LANES * 8
    )(pieces[0], got, *others)

    tpls = [pack] + [
        lax.ppermute(pack, "outer", [(b, b ^ flip) for b in range(outer_count)])
        for flip in range(1, outer_count)
    ]

    half = group // 2

    def swap(part, flip):
        y, tm = flip // tm_count, flip % tm_count
        route = [(i, i ^ (2 * tm_count * y + tm)) for i in range(total)]
        return lax.ppermute(part, every, route)

    parts = call(
        functools.partial(split_kernel, tm_count),
        [VMEM] * 2,
        [sds((2, part, slab), BF16)] * half,
        bytes_accessed=padded * slab * 2,
    )(keep, got)
    waves = [parts[0]] + [swap(parts[flip], flip) for flip in range(1, half)]
    samples, head = call(
        functools.partial(join_kernel, tm_count),
        [VMEM] * half,
        [sds((part, chunk), BF16), sds((part, window), BF16)],
        bytes_accessed=part * chunk * 4,
    )(*waves)
    halo = lax.ppermute(head, "outer", [(b, b - 1) for b in range(1, outer_count)])

    depth = window // FINE * part
    count = blk_count
    work = 2 * count * window * part * chunk // 2

    def scratch():
        return [
            pltpu.VMEM((2, depth, chunk // 4 + LANES), BF16),
            pltpu.VMEM((2, count * FINE, span + LANES), F32),
        ]

    send, edges, left, scale, mask = call(
        functools.partial(first_dots_kernel, stations, channels, tm_count),
        [VMEM] * (outer_count + 3),
        [
            sds((half, count, slab + window), F32),
            sds((half, count, window), F32),
            sds((count * FINE, depth), BF16),
            sds((count, LANES), F32),
            sds((count, channels), BF16),
        ],
        [
            pltpu.VMEM((part, chunk + window), BF16),
            pltpu.VMEM((group, count, window), F32),
        ]
        + scratch(),
        flops=work,
        bytes_accessed=part * chunk * 2,
        vmem=36,
    )(*tpls, order_row, samples, halo)
    keep = call(
        second_dots_kernel,
        [VMEM] * 4 + [AFTER],
        sds((half, count, slab + window), F32),
        [pltpu.VMEM((part, chunk + window), BF16)] + scratch(),
        flops=work,
        bytes_accessed=part * chunk * 2,
        vmem=36,
    )(left, samples, halo, edges, send)
    got = lax.ppermute(send, "inner", [(b, b ^ 1) for b in range(INNER)])
    power = call(
        functools.partial(power_kernel, window),
        [VMEM, VMEM, AFTER],
        sds((blk_count, slab), F32),
        flops=4 * blk_count * channels * slab,
        bytes_accessed=channels * slab * 2,
    )(waveforms, mask, keep)
    sums = call(
        functools.partial(add_kernel, tm_count),
        [VMEM] * 2,
        [sds((blk_count, slab + window), F32)] * half,
        bytes_accessed=blk_count * slab * 12 * half,
    )(keep, got)
    sums = [sums[0]] + [swap(sums[flip], flip) for flip in range(1, half)]
    return call(
        finish_kernel,
        [VMEM] * (half + 2),
        sds((blk_count, slab), F32),
        bytes_accessed=blk_count * slab * 4 * (half + 2),
    )(*sums, power, scale)


def solution(mesh):
    blk_count, tm_count = mesh.devices.shape
    shape = (blk_count // INNER, INNER, tm_count)
    mesh = jax.sharding.Mesh(mesh.devices.reshape(shape), ("outer", "inner", "tm"))
    blk, every = ("outer", "inner"), ("outer", "inner", "tm")
    placed = (P(None, every), P(blk, None, None), P(blk, None), P())
    return jax.shard_map(
        on_device, mesh=mesh, in_specs=placed, out_specs=P(None, every), check_vma=False
    )
```

```python
import functools

import jax
import jax.numpy as jnp
from jax import lax
from jax.experimental import pallas as pl
from jax.experimental.pallas import tpu as pltpu
from jax.sharding import PartitionSpec as P

EPSILON = 1e-05
LANES = 128
INNER = 4
FINE = 16
MIB = 1024 * 1024

BF16 = jnp.bfloat16
F32 = jnp.float32


HBM = pl.BlockSpec(memory_space=pltpu.HBM)
VMEM = pl.BlockSpec(memory_space=pltpu.VMEM)
AFTER = pl.BlockSpec(memory_space=pl.ANY)


def call(kernel, in_specs, out_shape, scratch=(), flops=0, bytes_accessed=0, vmem=24):
    return pl.pallas_call(
        kernel,
        in_specs=in_specs,
        out_specs=jax.tree.map(lambda _: VMEM, out_shape),
        out_shape=out_shape,
        scratch_shapes=list(scratch),
        compiler_params=pltpu.CompilerParams(vmem_limit_bytes=vmem * MIB),
        cost_estimate=pl.CostEstimate(
            flops=flops, bytes_accessed=bytes_accessed, transcendentals=0
        ),
    )


def one_hot(order_row, station_count):
    columns = order_row.shape[1]
    first = 3 * lax.broadcasted_iota(jnp.int32, (station_count, columns), 0)
    hit = (order_row >= first) & (order_row < first + 3)
    return jnp.where(hit, 1.0, 0.0).astype(BF16)


def side_major(inner):
    return lax.rem(inner, 2) * (INNER // 2) + lax.div(inner, 2)


def place_of(real, part):
    base = real // FINE * FINE
    return base, real - base


def regroup_rows(source, target, part):
    channels, width = source.shape
    groups = target.shape[0] // part
    real = channels // groups
    base, extra = place_of(real, part)
    rest = source[groups * base :, :].astype(F32)
    fill = jnp.zeros((part - real, width), F32)
    for group in range(groups):
        if base:
            run = source[group * base : (group + 1) * base, :]
            target[group * part : group * part + base, :] = run
        piece = [rest[group * extra : (group + 1) * extra], fill]
        target[group * part + base : (group + 1) * part, :] = jnp.concatenate(
            piece, axis=0
        ).astype(BF16)


def regroup(channels, padded, part):
    groups = padded // part
    real = channels // groups
    base, extra = place_of(real, part)
    channel = lax.broadcasted_iota(jnp.int32, (channels, padded), 0)
    place = lax.broadcasted_iota(jnp.int32, (1, padded), 1)
    group, within = place >> (part.bit_length() - 1), place & (part - 1)
    rest = groups * base + extra * group + within - base
    source = jnp.where(within < base, base * group + within, rest)
    source = jnp.where(within < real, source, -1)
    return jnp.where(channel == source, 1.0, 0.0).astype(BF16)


def spare_lanes(part, real):
    slots = LANES // part * (part - real)
    slot = lax.broadcasted_iota(jnp.int32, (8, LANES), 0)
    lane = lax.broadcasted_iota(jnp.int32, (8, LANES), 1)
    spare = part - real
    home = lax.div(slot, spare) * part + real + lax.rem(slot, spare)
    return jnp.where((lane == home) & (slot < slots), 1.0, 0.0).astype(BF16)


def prologue_kernel(tm_count, wave_hbm, tpl_hbm, flag_hbm, order_hbm, *refs):
    send_ref, samples_ref, *outs = refs[: INNER + 1]
    wave_ref, grouped, tpl_ref, tpl_grouped, flag_ref, order_ref, turned, sems = refs[INNER + 1 :]
    channels, window = tpl_hbm.shape[1:]
    copies = [
        pltpu.make_async_copy(flag_hbm, flag_ref, sems.at[0]),
        pltpu.make_async_copy(order_hbm, order_ref, sems.at[1]),
        pltpu.make_async_copy(tpl_hbm.at[0], tpl_ref, sems.at[2]),
        pltpu.make_async_copy(wave_hbm, wave_ref, sems.at[3]),
    ]
    for copy in copies:
        copy.start()
    stations = flag_ref.shape[1]
    padded = turned.shape[1]
    part = LANES // tm_count
    rows = outs[0].shape[0]
    groups = regroup(channels, padded, part)
    copies[0].wait()
    copies[1].wait()
    flags = jnp.broadcast_to(flag_ref[...].astype(F32), (8, stations))
    mask = jnp.dot(
        flags.astype(BF16), one_hot(order_ref[...], stations), preferred_element_type=F32
    )
    live = jnp.sum(mask[:1], keepdims=True)
    mask = jnp.dot(mask.astype(BF16), groups, preferred_element_type=F32)[:1]
    copies[2].wait()
    regroup_rows(tpl_ref, tpl_grouped, part)
    masked = tpl_grouped[...].T.astype(F32) * mask
    turned[...] = masked
    norm = jnp.sqrt(jnp.sum(masked * masked, keepdims=True) + EPSILON)
    rest = jnp.broadcast_to(jnp.sqrt(window * live) / norm, (1, rows))
    row = lax.broadcasted_iota(jnp.int32, (1, rows), 1)
    scale = jnp.zeros((1, rows), F32)
    for piece in range(3):
        now = rest.astype(BF16).astype(F32)
        scale = jnp.where(row == piece, now, scale)
        rest = rest - now
    slots = -(-stations // rows)
    wide = flags[:1]
    if stations % rows:
        wide = jnp.concatenate([wide, jnp.zeros((1, rows - stations % rows), F32)], axis=1)
    meta = [wide[:, slot * rows : (slot + 1) * rows] for slot in range(slots)] + [scale]
    meta = jnp.concatenate(meta + [jnp.zeros((8 - len(meta), rows), F32)], axis=0)
    meta = lax.dot_general(
        meta.astype(BF16),
        spare_lanes(part, part * channels // padded),
        (((0,), (0,)), ((), ())),
        preferred_element_type=F32,
    )
    my_tm = lax.axis_index("tm")
    my_inner = lax.axis_index("inner")
    my_core = lax.rem(my_inner, 2)
    first = send_ref.shape[0] - rows
    spot = lax.broadcasted_iota(jnp.int32, (FINE, LANES), 1) >> (part.bit_length() - 1)
    for flip in range(INNER):
        start = pl.multiple_of(side_major(my_inner ^ flip) * LANES, LANES)
        pieces = []
        for step in range(window // (FINE * tm_count)):
            tile = jnp.zeros((FINE, LANES), F32)
            for within in range(tm_count):
                row = FINE * (step * tm_count + within)
                chunk = turned[row : row + FINE, pl.ds(start, LANES)]
                turn = lax.rem(part * (within - my_tm) + LANES, LANES)
                tile = jnp.where(spot == within, pltpu.roll(chunk, turn, 1), tile)
            pieces.append(tile)
        payload = (jnp.concatenate(pieces, axis=0) + meta).astype(BF16)
        if flip == 1:
            send_ref[first:, :] = payload
        else:
            outs[flip - (flip > 1)][...] = payload

    copies[3].wait()
    regroup_rows(wave_ref, grouped, part)
    half = padded // 2
    samples_ref[...] = grouped[pl.ds(pl.multiple_of(my_core * half, half), half), :]
    theirs = pl.ds(pl.multiple_of((1 - my_core) * half, half), half)
    for tile in range(first // half):
        columns = slice(tile * LANES, (tile + 1) * LANES)
        send_ref[tile * half : (tile + 1) * half, :] = grouped[theirs, columns]


def pack_kernel(mine_ref, core_ref, y_ref, both_ref, out_ref):
    inner = lax.axis_index("inner")
    rows = mine_ref.shape[0]
    out_ref[inner] = mine_ref[...]
    out_ref[inner ^ 1] = core_ref[core_ref.shape[0] - rows :, :]
    out_ref[inner ^ 2] = y_ref[...]
    out_ref[inner ^ 3] = both_ref[...]


def split_kernel(tm_count, keep_ref, got_ref, *outs):
    my_inner = lax.axis_index("inner")
    core = lax.rem(my_inner, 2)
    me = lax.div(my_inner, 2) * tm_count + lax.axis_index("tm")
    part = outs[0].shape[1]
    half, slab = keep_ref.shape
    for flip, out_ref in enumerate(outs):
        start = (me ^ flip) * part
        out_ref[core] = keep_ref[pl.ds(pl.multiple_of(start, part), part), :]
        for tile in range(slab // LANES):
            rows = pl.ds(pl.multiple_of(tile * half + start, part), part)
            out_ref[1 - core, :, tile * LANES : (tile + 1) * LANES] = got_ref[rows, :]


def join_kernel(tm_count, *refs):
    parts, out_ref, head_ref = refs[:-2], refs[-2], refs[-1]
    me = lax.div(lax.axis_index("inner"), 2) * tm_count + lax.axis_index("tm")
    slab = parts[0].shape[2]
    for flip, part in enumerate(parts):
        other = me ^ flip
        y, tm = lax.div(other, tm_count), lax.rem(other, tm_count)
        for core in range(2):
            place = (y * 2 + core) * tm_count + tm
            out_ref[:, pl.ds(pl.multiple_of(place * slab, slab), slab)] = part[core]
    head_ref[...] = out_ref[:, : head_ref.shape[1]]


def arrival(template):
    return template ^ (lax.axis_index("outer") * INNER)


def arrange(tpls, left):
    size, depth = left.shape
    count = len(tpls) * INNER
    row = lax.broadcasted_iota(jnp.int32, (size, size), 0)
    column = lax.broadcasted_iota(jnp.int32, (size, size), 1)
    shift = count.bit_length() - 1
    source = arrival(row & (count - 1)) * FINE + (row >> shift)
    order = jnp.where(column == source, 1.0, 0.0).astype(BF16)
    for step in range(depth // LANES):
        rows = [
            pack[:, FINE * step : FINE * (step + 1), :].reshape(INNER * FINE, LANES)
            for pack in tpls
        ]
        left[:, step * LANES : (step + 1) * LANES] = jnp.dot(
            order, jnp.concatenate(rows, axis=0), preferred_element_type=F32
        ).astype(BF16)


def correlate(left, full, out_ref, slab, side, shifts, products):
    part = full.shape[0]
    size, depth = left.shape
    count = size // FINE
    copies = LANES // FINE
    run = out_ref.shape[0] // 2
    width = run * slab
    for y in range(2):
        columns = width + 2 * LANES
        start = pl.multiple_of((2 * y + side) * width, width)
        samples = full[:, pl.ds(start, columns)]
        for copy in range(depth // part):
            tile, turn = copy // copies * LANES, copy % copies * FINE
            turned = samples if turn == 0 else pltpu.roll(samples, columns - turn, 1)
            shifts[y, copy * part : (copy + 1) * part, :] = turned[:, tile : tile + width + LANES]
    tiles = products.shape[2] // LANES
    span = (tiles - 1) * LANES
    per_block = span // slab
    blocks = [(y, index) for y in range(2) for index in range(width // span)]

    def multiply(place, slot):
        y, index = place
        for tile in range(0, tiles, 2):
            start = index * span + tile * LANES
            lanes = min(2, tiles - tile) * LANES
            products[slot, :, tile * LANES : tile * LANES + lanes] = jnp.dot(
                left[...], shifts[y, :, start : start + lanes], preferred_element_type=F32
            )

    def gather(place, slot):
        def tree(first, number):
            if number == 1:
                return products[slot, first * count : (first + 1) * count, :]
            half = number // 2
            later = pltpu.roll(tree(first + half, half), span + LANES - half, 1)
            return tree(first, half) + later

        total = tree(0, FINE)
        y, index = place
        for piece in range(per_block):
            out_ref[y * run + index * per_block + piece, :, :slab] = total[
                :, piece * slab : (piece + 1) * slab
            ]

    multiply(blocks[0], 0)
    for number in range(1, len(blocks)):
        multiply(blocks[number], number % 2)
        gather(blocks[number - 1], (number - 1) % 2)
    gather(blocks[-1], (len(blocks) - 1) % 2)


def first_dots_kernel(outer_count, stations, channels, tm_count, *refs):
    tpls, (order_ref, samples_ref, halo_ref) = refs[:-12], refs[-12:-9]
    send_ref, edges_ref, left, scale_ref, mask_ref = refs[-9:-4]
    full, edges, shifts, products = refs[-4:]
    core = lax.rem(lax.axis_index("inner"), 2)
    group, _, window = edges.shape
    chunk = samples_ref.shape[1]
    slab = chunk // group
    full[:, :chunk] = samples_ref[...]
    full[:, chunk:] = halo_ref[...]
    tpls = [pack[...] for pack in tpls]
    if len(tpls) > outer_count:
        tpls = tpls[:-2] + [tpls[-2] + tpls[-1]]
    arrange(tpls, left)
    correlate(left, full, send_ref, slab, 1 - core, shifts, products)
    part_mask = read_masks(stations, channels, tm_count, tpls, order_ref, scale_ref, mask_ref)
    after = [full[:, (m + 1) * slab : (m + 1) * slab + window] for m in range(group)]
    squares = masked_squares(part_mask, jnp.concatenate(after, axis=1))
    column = lax.broadcasted_iota(jnp.int32, squares.shape, 1) & (window - 1)
    reach = 1
    while reach < window:
        earlier = pltpu.roll(squares, reach, 1)
        squares = squares + jnp.where(column >= reach, earlier, 0.0)
        reach *= 2
    squares = jnp.where(column >= 1, pltpu.roll(squares, 1, 1), 0.0)
    for member in range(group):
        edges[member] = squares[:, member * window : (member + 1) * window]
    run = group // 4
    for y in range(2):
        for tm in range(run):
            send_ref[y * run + tm, :, slab:] = edges[(2 * y + 1 - core) * run + tm]
            edges_ref[y * run + tm] = edges[(2 * y + core) * run + tm]


def second_dots_kernel(left, samples_ref, halo_ref, edges_ref, after, keep_ref, *scratch):
    del after
    full, shifts, products = scratch
    chunk = samples_ref.shape[1]
    full[:, :chunk] = samples_ref[...]
    full[:, chunk:] = halo_ref[...]
    core = lax.rem(lax.axis_index("inner"), 2)
    slab = keep_ref.shape[2] - edges_ref.shape[2]
    correlate(left, full, keep_ref, slab, core, shifts, products)
    keep_ref[:, :, slab:] = edges_ref[...]


def add_kernel(tm_count, keep_ref, got_ref, *outs):
    me = lax.div(lax.axis_index("inner"), 2) * tm_count + lax.axis_index("tm")
    for flip, out_ref in enumerate(outs):
        out_ref[...] = keep_ref[me ^ flip] + got_ref[me ^ flip]


def masked_squares(mask, wave):
    wave = wave.astype(F32)
    squares = wave * wave
    high = squares.astype(BF16)
    low = (squares - high.astype(F32)).astype(BF16)
    return jnp.dot(mask, high, preferred_element_type=F32) + jnp.dot(
        mask, low, preferred_element_type=F32
    )


def read_masks(stations, channels, tm_count, tpls, order_ref, scale_ref, mask_ref):
    rows = tpls[0].shape[1]
    count = len(tpls) * INNER
    padded = INNER * LANES
    part = LANES // tm_count
    meta = lax.dot_general(
        spare_lanes(part, part * channels // padded),
        jnp.concatenate([pack.reshape(INNER * rows, LANES) for pack in tpls], axis=0),
        (((1,), (1,)), ((), ())),
        preferred_element_type=F32,
    )
    template = lax.broadcasted_iota(jnp.int32, (count, count), 0)
    place = lax.broadcasted_iota(jnp.int32, (count, count), 1)
    sort = jnp.where(place == arrival(template), 1.0, 0.0).astype(BF16)
    slots = -(-stations // rows)

    def read(slot):
        return jnp.concatenate(
            [meta[slot : slot + 1, t * rows : (t + 1) * rows] for t in range(count)], axis=0
        )

    values = jnp.concatenate([read(slot) for slot in range(slots + 1)], axis=1)
    values = jnp.dot(sort, values.astype(BF16), preferred_element_type=F32)
    start = slots * rows
    scale = jnp.sum(values[:, start : start + 3], axis=1, keepdims=True)
    scale_ref[...] = jnp.broadcast_to(scale, scale_ref.shape)
    mask = jnp.dot(
        values[:, :stations].astype(BF16),
        one_hot(order_ref[...], stations),
        preferred_element_type=F32,
    ).astype(BF16)
    mask_ref[...] = mask
    grouped = jnp.dot(mask, regroup(channels, padded, part), preferred_element_type=F32)
    mine = side_major(lax.axis_index("inner")) * LANES + lax.axis_index("tm") * part
    return pltpu.roll(grouped, lax.rem(padded - mine, padded), 1)[:, :part].astype(BF16)


def power_kernel(window, wave_ref, mask_ref, after, out_ref):
    del after
    power = masked_squares(mask_ref[...], wave_ref[...])
    columns = power.shape[1]
    column = lax.broadcasted_iota(jnp.int32, power.shape, 1)
    reach = 1
    while reach < window:
        later = pltpu.roll(power, columns - reach, 1)
        power = power + jnp.where(column < columns - reach, later, 0.0)
        reach *= 2
    out_ref[...] = power


def finish_kernel(*refs):
    parts, (power_ref, scale_ref, out_ref) = refs[:-3], refs[-3:]
    slab = power_ref.shape[1]
    total = parts[0][...]
    for part in parts[1:]:
        total = total + part[...]
    dots, edge = total[:, :slab], total[:, slab:]
    inside = slab - edge.shape[1]
    energy = jnp.concatenate(
        [power_ref[:, :inside], power_ref[:, inside:] + edge], axis=1
    )
    out_ref[...] = dots * (scale_ref[:, :1] / jnp.sqrt(energy + EPSILON))


def on_device(waveforms, templates, station_mask, channel_order):
    channels, slab = waveforms.shape
    rows, _, window = templates.shape
    stations = station_mask.shape[1]
    outer_count, tm_count = lax.axis_size("outer"), lax.axis_size("tm")
    blk_count = outer_count * INNER
    assert rows == 1 and LANES % tm_count == 0
    group = INNER * tm_count
    padded = INNER * LANES
    part = padded // group
    chunk = group * slab
    span = 2 * slab
    total = blk_count * tm_count
    blk, every = ("outer", "inner"), ("outer", "inner", "tm")
    sds = jax.ShapeDtypeStruct
    order_row = channel_order[None, :]

    rows = window * part // LANES
    held = [
        pltpu.with_memory_space_constraint(x, pltpu.HBM)
        for x in (waveforms, templates, station_mask, order_row)
    ]
    send, keep, *pieces = call(
        functools.partial(prologue_kernel, tm_count),
        [HBM] * 4,
        [
            sds((padded // 2 * slab // LANES + rows, LANES), BF16),
            sds((padded // 2, slab), BF16),
            *[sds((rows, LANES), BF16)] * (INNER - 1),
        ],
        [
            pltpu.VMEM((channels, slab), BF16),
            pltpu.VMEM((padded, slab), BF16),
            pltpu.VMEM((channels, window), BF16),
            pltpu.VMEM((padded, window), BF16),
            pltpu.VMEM((1, stations), jnp.int32),
            pltpu.VMEM((1, channels), jnp.int32),
            pltpu.VMEM((window, padded), F32),
            pltpu.SemaphoreType.DMA((4,)),
        ],
        bytes_accessed=channels * (window + slab) * 2,
    )(*held)

    def plane(part, flip):
        return lax.ppermute(part, "inner", [(b, b ^ flip) for b in range(INNER)])

    got = plane(send, 1)
    others = [plane(pieces[1], 2), plane(pieces[2], 3)]
    pack = call(
        pack_kernel, [VMEM] * INNER, sds((INNER, rows, LANES), BF16), bytes_accessed=rows * LANES * 8
    )(pieces[0], got, *others)

    def cross(part, route):
        return lax.ppermute(part, "outer", route)

    if outer_count == 4:
        near = cross(pack, [(0, 1), (1, 0), (2, 3), (3, 2)])
        far = cross(pack, [(0, 2), (2, 0), (1, 3), (3, 1)])
        middle = cross(pack, [(1, 2), (2, 1)])
        ends = cross(far, [(1, 0), (2, 3)])
        tpls = [pack, near, far, middle, ends]
    else:
        tpls = [pack] + [
            cross(pack, [(b, b ^ flip) for b in range(outer_count)])
            for flip in range(1, outer_count)
        ]

    half = group // 2

    def swap(part, flip):
        y, tm = flip // tm_count, flip % tm_count
        route = [(i, i ^ (2 * tm_count * y + tm)) for i in range(total)]
        return lax.ppermute(part, every, route)

    parts = call(
        functools.partial(split_kernel, tm_count),
        [VMEM] * 2,
        [sds((2, part, slab), BF16)] * half,
        bytes_accessed=padded * slab * 2,
    )(keep, got)
    waves = [parts[0]] + [swap(parts[flip], flip) for flip in range(1, half)]
    samples, head = call(
        functools.partial(join_kernel, tm_count),
        [VMEM] * half,
        [sds((part, chunk), BF16), sds((part, window), BF16)],
        bytes_accessed=part * chunk * 4,
    )(*waves)
    halo = lax.ppermute(head, "outer", [(b, b - 1) for b in range(1, outer_count)])

    depth = window // FINE * part
    count = blk_count
    work = 2 * count * window * part * chunk // 2

    def scratch():
        return [
            pltpu.VMEM((2, depth, chunk // 4 + LANES), BF16),
            pltpu.VMEM((2, count * FINE, span + LANES), F32),
        ]

    send, edges, left, scale, mask = call(
        functools.partial(first_dots_kernel, outer_count, stations, channels, tm_count),
        [VMEM] * (len(tpls) + 3),
        [
            sds((half, count, slab + window), F32),
            sds((half, count, window), F32),
            sds((count * FINE, depth), BF16),
            sds((count, LANES), F32),
            sds((count, channels), BF16),
        ],
        [
            pltpu.VMEM((part, chunk + window), BF16),
            pltpu.VMEM((group, count, window), F32),
        ]
        + scratch(),
        flops=work,
        bytes_accessed=part * chunk * 2,
        vmem=36,
    )(*tpls, order_row, samples, halo)
    keep = call(
        second_dots_kernel,
        [VMEM] * 4 + [AFTER],
        sds((half, count, slab + window), F32),
        [pltpu.VMEM((part, chunk + window), BF16)] + scratch(),
        flops=work,
        bytes_accessed=part * chunk * 2,
        vmem=36,
    )(left, samples, halo, edges, send)
    got = lax.ppermute(send, "inner", [(b, b ^ 1) for b in range(INNER)])
    power = call(
        functools.partial(power_kernel, window),
        [VMEM, VMEM, AFTER],
        sds((blk_count, slab), F32),
        flops=4 * blk_count * channels * slab,
        bytes_accessed=channels * slab * 2,
    )(waveforms, mask, keep)
    sums = call(
        functools.partial(add_kernel, tm_count),
        [VMEM] * 2,
        [sds((blk_count, slab + window), F32)] * half,
        bytes_accessed=blk_count * slab * 12 * half,
    )(keep, got)
    sums = [sums[0]] + [swap(sums[flip], flip) for flip in reversed(range(1, half))]
    return call(
        finish_kernel,
        [VMEM] * (half + 2),
        sds((blk_count, slab), F32),
        bytes_accessed=blk_count * slab * 4 * (half + 2),
    )(*sums, power, scale)


def solution(mesh):
    blk_count, tm_count = mesh.devices.shape
    shape = (blk_count // INNER, INNER, tm_count)
    mesh = jax.sharding.Mesh(mesh.devices.reshape(shape), ("outer", "inner", "tm"))
    blk, every = ("outer", "inner"), ("outer", "inner", "tm")
    placed = (P(None, every), P(blk, None, None), P(blk, None), P())
    return jax.shard_map(
        on_device, mesh=mesh, in_specs=placed, out_specs=P(None, every), check_vma=False
    )
```

```python
import functools

import jax
import jax.numpy as jnp
from jax import lax
from jax.experimental import pallas as pl
from jax.experimental.pallas import tpu as pltpu
from jax.sharding import PartitionSpec as P

EPSILON = 1e-05
LANES = 128
INNER = 4
FINE = 16
MIB = 1024 * 1024
RELAY_FLOPS = 6 * 10**9

BF16 = jnp.bfloat16
F32 = jnp.float32


HBM = pl.BlockSpec(memory_space=pltpu.HBM)
VMEM = pl.BlockSpec(memory_space=pltpu.VMEM)
AFTER = pl.BlockSpec(memory_space=pl.ANY)


def call(kernel, in_specs, out_shape, scratch=(), flops=0, bytes_accessed=0, vmem=24):
    return pl.pallas_call(
        kernel,
        in_specs=in_specs,
        out_specs=jax.tree.map(lambda _: VMEM, out_shape),
        out_shape=out_shape,
        scratch_shapes=list(scratch),
        compiler_params=pltpu.CompilerParams(vmem_limit_bytes=vmem * MIB),
        cost_estimate=pl.CostEstimate(
            flops=flops, bytes_accessed=bytes_accessed, transcendentals=0
        ),
    )


def one_hot(order_row, station_count):
    columns = order_row.shape[1]
    first = 3 * lax.broadcasted_iota(jnp.int32, (station_count, columns), 0)
    hit = (order_row >= first) & (order_row < first + 3)
    return jnp.where(hit, 1.0, 0.0).astype(BF16)


def side_major(inner):
    return lax.rem(inner, 2) * (INNER // 2) + lax.div(inner, 2)


def place_of(real, part):
    base = real // FINE * FINE
    return base, real - base


def regroup_rows(source, target, part):
    channels, width = source.shape
    groups = target.shape[0] // part
    real = channels // groups
    base, extra = place_of(real, part)
    rest = source[groups * base :, :].astype(F32)
    fill = jnp.zeros((part - real, width), F32)
    for group in range(groups):
        if base:
            run = source[group * base : (group + 1) * base, :]
            target[group * part : group * part + base, :] = run
        piece = [rest[group * extra : (group + 1) * extra], fill]
        target[group * part + base : (group + 1) * part, :] = jnp.concatenate(
            piece, axis=0
        ).astype(BF16)


def regroup(channels, padded, part):
    groups = padded // part
    real = channels // groups
    base, extra = place_of(real, part)
    channel = lax.broadcasted_iota(jnp.int32, (channels, padded), 0)
    place = lax.broadcasted_iota(jnp.int32, (1, padded), 1)
    group, within = place >> (part.bit_length() - 1), place & (part - 1)
    rest = groups * base + extra * group + within - base
    source = jnp.where(within < base, base * group + within, rest)
    source = jnp.where(within < real, source, -1)
    return jnp.where(channel == source, 1.0, 0.0).astype(BF16)


def spare_lanes(part, real):
    slots = LANES // part * (part - real)
    slot = lax.broadcasted_iota(jnp.int32, (8, LANES), 0)
    lane = lax.broadcasted_iota(jnp.int32, (8, LANES), 1)
    spare = part - real
    home = lax.div(slot, spare) * part + real + lax.rem(slot, spare)
    return jnp.where((lane == home) & (slot < slots), 1.0, 0.0).astype(BF16)


def prologue_kernel(tm_count, wave_hbm, tpl_hbm, flag_hbm, order_hbm, *refs):
    send_ref, samples_ref, *outs = refs[: INNER + 1]
    wave_ref, grouped, tpl_ref, tpl_grouped, flag_ref, order_ref, turned, sems = refs[INNER + 1 :]
    channels, window = tpl_hbm.shape[1:]
    copies = [
        pltpu.make_async_copy(flag_hbm, flag_ref, sems.at[0]),
        pltpu.make_async_copy(order_hbm, order_ref, sems.at[1]),
        pltpu.make_async_copy(tpl_hbm.at[0], tpl_ref, sems.at[2]),
        pltpu.make_async_copy(wave_hbm, wave_ref, sems.at[3]),
    ]
    for copy in copies:
        copy.start()
    stations = flag_ref.shape[1]
    padded = turned.shape[1]
    part = LANES // tm_count
    rows = outs[0].shape[0]
    groups = regroup(channels, padded, part)
    copies[0].wait()
    copies[1].wait()
    flags = jnp.broadcast_to(flag_ref[...].astype(F32), (8, stations))
    mask = jnp.dot(
        flags.astype(BF16), one_hot(order_ref[...], stations), preferred_element_type=F32
    )
    live = jnp.sum(mask[:1], keepdims=True)
    mask = jnp.dot(mask.astype(BF16), groups, preferred_element_type=F32)[:1]
    copies[2].wait()
    regroup_rows(tpl_ref, tpl_grouped, part)
    masked = tpl_grouped[...].T.astype(F32) * mask
    turned[...] = masked
    norm = jnp.sqrt(jnp.sum(masked * masked, keepdims=True) + EPSILON)
    rest = jnp.broadcast_to(jnp.sqrt(window * live) / norm, (1, rows))
    row = lax.broadcasted_iota(jnp.int32, (1, rows), 1)
    scale = jnp.zeros((1, rows), F32)
    for piece in range(3):
        now = rest.astype(BF16).astype(F32)
        scale = jnp.where(row == piece, now, scale)
        rest = rest - now
    slots = -(-stations // rows)
    wide = flags[:1]
    if stations % rows:
        wide = jnp.concatenate([wide, jnp.zeros((1, rows - stations % rows), F32)], axis=1)
    meta = [wide[:, slot * rows : (slot + 1) * rows] for slot in range(slots)] + [scale]
    meta = jnp.concatenate(meta + [jnp.zeros((8 - len(meta), rows), F32)], axis=0)
    meta = lax.dot_general(
        meta.astype(BF16),
        spare_lanes(part, part * channels // padded),
        (((0,), (0,)), ((), ())),
        preferred_element_type=F32,
    )
    my_tm = lax.axis_index("tm")
    my_inner = lax.axis_index("inner")
    my_core = lax.rem(my_inner, 2)
    first = send_ref.shape[0] - rows
    spot = lax.broadcasted_iota(jnp.int32, (FINE, LANES), 1) >> (part.bit_length() - 1)
    for flip in range(INNER):
        start = pl.multiple_of(side_major(my_inner ^ flip) * LANES, LANES)
        pieces = []
        for step in range(window // (FINE * tm_count)):
            tile = jnp.zeros((FINE, LANES), F32)
            for within in range(tm_count):
                row = FINE * (step * tm_count + within)
                chunk = turned[row : row + FINE, pl.ds(start, LANES)]
                turn = lax.rem(part * (within - my_tm) + LANES, LANES)
                tile = jnp.where(spot == within, pltpu.roll(chunk, turn, 1), tile)
            pieces.append(tile)
        payload = (jnp.concatenate(pieces, axis=0) + meta).astype(BF16)
        if flip == 1:
            send_ref[first:, :] = payload
        else:
            outs[flip - (flip > 1)][...] = payload

    copies[3].wait()
    regroup_rows(wave_ref, grouped, part)
    half = padded // 2
    samples_ref[...] = grouped[pl.ds(pl.multiple_of(my_core * half, half), half), :]
    theirs = pl.ds(pl.multiple_of((1 - my_core) * half, half), half)
    for tile in range(first // half):
        columns = slice(tile * LANES, (tile + 1) * LANES)
        send_ref[tile * half : (tile + 1) * half, :] = grouped[theirs, columns]


def relay_kernel(in_ref, out_ref):
    out_ref[...] = in_ref[...]


def pack_kernel(mine_ref, core_ref, y_ref, both_ref, out_ref):
    inner = lax.axis_index("inner")
    rows = mine_ref.shape[0]
    out_ref[inner] = mine_ref[...]
    out_ref[inner ^ 1] = core_ref[core_ref.shape[0] - rows :, :]
    out_ref[inner ^ 2] = y_ref[...]
    out_ref[inner ^ 3] = both_ref[...]


def head_kernel(keep_ref, got_ref, out_ref):
    core = lax.rem(lax.axis_index("inner"), 2)
    half, window = out_ref.shape

    @pl.when(core == 0)
    def _():
        out_ref[...] = keep_ref[:, :window]

    @pl.when(core == 1)
    def _():
        for tile in range(window // LANES):
            out_ref[:, tile * LANES : (tile + 1) * LANES] = got_ref[
                tile * half : (tile + 1) * half, :
            ]


def split_kernel(tm_count, keep_ref, got_ref, halo_ref, after, *outs):
    del after
    my_inner = lax.axis_index("inner")
    core = lax.rem(my_inner, 2)
    me = lax.div(my_inner, 2) * tm_count + lax.axis_index("tm")
    part = outs[0].shape[0]
    half, slab = keep_ref.shape
    for flip, out_ref in enumerate(outs):
        start = (me ^ flip) * part
        rows = pl.ds(pl.multiple_of(start, part), part)
        out_ref[:, pl.ds(pl.multiple_of(core * slab, slab), slab)] = keep_ref[rows, :]
        for tile in range(slab // LANES):
            theirs = pl.ds(pl.multiple_of(tile * half + start, part), part)
            lanes = pl.multiple_of((1 - core) * slab + tile * LANES, LANES)
            out_ref[:, pl.ds(lanes, LANES)] = got_ref[theirs, :]
        out_ref[:, 2 * slab :] = halo_ref[rows, :]


def join_kernel(tm_count, slab, *refs):
    parts, out_ref = refs[:-1], refs[-1]
    me = lax.div(lax.axis_index("inner"), 2) * tm_count + lax.axis_index("tm")
    count = len(parts)
    for flip, part in enumerate(parts):
        other = me ^ flip
        y, tm = lax.div(other, tm_count), lax.rem(other, tm_count)
        for core in range(2):
            place = (y * 2 + core) * tm_count + tm
            out_ref[:, pl.ds(pl.multiple_of(place * slab, slab), slab)] = part[
                :, core * slab : (core + 1) * slab
            ]

        @pl.when(other == 0)
        def _():
            out_ref[:, 2 * count * slab :] = part[:, 2 * slab :]


def arrival(template):
    return template ^ (lax.axis_index("outer") * INNER)


def arrange(tpls, left):
    size, depth = left.shape
    count = len(tpls) * INNER
    row = lax.broadcasted_iota(jnp.int32, (size, size), 0)
    column = lax.broadcasted_iota(jnp.int32, (size, size), 1)
    shift = count.bit_length() - 1
    source = arrival(row & (count - 1)) * FINE + (row >> shift)
    order = jnp.where(column == source, 1.0, 0.0).astype(BF16)
    for step in range(depth // LANES):
        rows = [
            pack[:, FINE * step : FINE * (step + 1), :].reshape(INNER * FINE, LANES)
            for pack in tpls
        ]
        left[:, step * LANES : (step + 1) * LANES] = jnp.dot(
            order, jnp.concatenate(rows, axis=0), preferred_element_type=F32
        ).astype(BF16)


def correlate(left, full, out_ref, slab, side, shifts, products):
    part = full.shape[0]
    size, depth = left.shape
    count = size // FINE
    copies = LANES // FINE
    run = out_ref.shape[0] // 2
    width = run * slab
    for y in range(2):
        columns = width + 2 * LANES
        start = pl.multiple_of((2 * y + side) * width, width)
        samples = full[:, pl.ds(start, columns)]
        for copy in range(depth // part):
            tile, turn = copy // copies * LANES, copy % copies * FINE
            turned = samples if turn == 0 else pltpu.roll(samples, columns - turn, 1)
            shifts[y, copy * part : (copy + 1) * part, :] = turned[:, tile : tile + width + LANES]
    tiles = products.shape[2] // LANES
    span = (tiles - 1) * LANES
    per_block = span // slab
    blocks = [(y, index) for y in range(2) for index in range(width // span)]

    def multiply(place, slot):
        y, index = place
        for tile in range(0, tiles, 2):
            start = index * span + tile * LANES
            lanes = min(2, tiles - tile) * LANES
            products[slot, :, tile * LANES : tile * LANES + lanes] = jnp.dot(
                left[...], shifts[y, :, start : start + lanes], preferred_element_type=F32
            )

    def gather(place, slot):
        def tree(first, number):
            if number == 1:
                return products[slot, first * count : (first + 1) * count, :]
            half = number // 2
            later = pltpu.roll(tree(first + half, half), span + LANES - half, 1)
            return tree(first, half) + later

        total = tree(0, FINE)
        y, index = place
        for piece in range(per_block):
            out_ref[y * run + index * per_block + piece, :, :slab] = total[
                :, piece * slab : (piece + 1) * slab
            ]

    multiply(blocks[0], 0)
    for number in range(1, len(blocks)):
        multiply(blocks[number], number % 2)
        gather(blocks[number - 1], (number - 1) % 2)
    gather(blocks[-1], (len(blocks) - 1) % 2)


def first_dots_kernel(outer_count, stations, channels, tm_count, *refs):
    tpls, (order_ref, full) = refs[:-10], refs[-10:-8]
    send_ref, edges_ref, left, scale_ref, mask_ref = refs[-8:-3]
    edges, shifts, products = refs[-3:]
    core = lax.rem(lax.axis_index("inner"), 2)
    group, _, window = edges.shape
    slab = (full.shape[1] - window) // group
    tpls = [pack[...] for pack in tpls]
    if len(tpls) > outer_count:
        tpls = tpls[:-2] + [tpls[-2] + tpls[-1]]
    arrange(tpls, left)
    correlate(left, full, send_ref, slab, 1 - core, shifts, products)
    part_mask = read_masks(stations, channels, tm_count, tpls, order_ref, scale_ref, mask_ref)
    after = [full[:, (m + 1) * slab : (m + 1) * slab + window] for m in range(group)]
    squares = masked_squares(part_mask, jnp.concatenate(after, axis=1))
    column = lax.broadcasted_iota(jnp.int32, squares.shape, 1) & (window - 1)
    reach = 1
    while reach < window:
        earlier = pltpu.roll(squares, reach, 1)
        squares = squares + jnp.where(column >= reach, earlier, 0.0)
        reach *= 2
    squares = jnp.where(column >= 1, pltpu.roll(squares, 1, 1), 0.0)
    for member in range(group):
        edges[member] = squares[:, member * window : (member + 1) * window]
    run = group // 4
    for y in range(2):
        for tm in range(run):
            send_ref[y * run + tm, :, slab:] = edges[(2 * y + 1 - core) * run + tm]
            edges_ref[y * run + tm] = edges[(2 * y + core) * run + tm]


def second_dots_kernel(left, full, edges_ref, after, keep_ref, shifts, products):
    del after
    core = lax.rem(lax.axis_index("inner"), 2)
    slab = keep_ref.shape[2] - edges_ref.shape[2]
    correlate(left, full, keep_ref, slab, core, shifts, products)
    keep_ref[:, :, slab:] = edges_ref[...]


def add_kernel(tm_count, keep_ref, got_ref, *outs):
    me = lax.div(lax.axis_index("inner"), 2) * tm_count + lax.axis_index("tm")
    for flip, out_ref in enumerate(outs):
        out_ref[...] = keep_ref[me ^ flip] + got_ref[me ^ flip]


def masked_squares(mask, wave):
    wave = wave.astype(F32)
    squares = wave * wave
    high = squares.astype(BF16)
    low = (squares - high.astype(F32)).astype(BF16)
    return jnp.dot(mask, high, preferred_element_type=F32) + jnp.dot(
        mask, low, preferred_element_type=F32
    )


def read_masks(stations, channels, tm_count, tpls, order_ref, scale_ref, mask_ref):
    rows = tpls[0].shape[1]
    count = len(tpls) * INNER
    padded = INNER * LANES
    part = LANES // tm_count
    meta = lax.dot_general(
        spare_lanes(part, part * channels // padded),
        jnp.concatenate([pack.reshape(INNER * rows, LANES) for pack in tpls], axis=0),
        (((1,), (1,)), ((), ())),
        preferred_element_type=F32,
    )
    template = lax.broadcasted_iota(jnp.int32, (count, count), 0)
    place = lax.broadcasted_iota(jnp.int32, (count, count), 1)
    sort = jnp.where(place == arrival(template), 1.0, 0.0).astype(BF16)
    slots = -(-stations // rows)

    def read(slot):
        return jnp.concatenate(
            [meta[slot : slot + 1, t * rows : (t + 1) * rows] for t in range(count)], axis=0
        )

    values = jnp.concatenate([read(slot) for slot in range(slots + 1)], axis=1)
    values = jnp.dot(sort, values.astype(BF16), preferred_element_type=F32)
    start = slots * rows
    scale = jnp.sum(values[:, start : start + 3], axis=1, keepdims=True)
    scale_ref[...] = jnp.broadcast_to(scale, scale_ref.shape)
    mask = jnp.dot(
        values[:, :stations].astype(BF16),
        one_hot(order_ref[...], stations),
        preferred_element_type=F32,
    ).astype(BF16)
    mask_ref[...] = mask
    grouped = jnp.dot(mask, regroup(channels, padded, part), preferred_element_type=F32)
    mine = side_major(lax.axis_index("inner")) * LANES + lax.axis_index("tm") * part
    return pltpu.roll(grouped, lax.rem(padded - mine, padded), 1)[:, :part].astype(BF16)


def power_kernel(window, wave_ref, mask_ref, after, out_ref):
    del after
    power = masked_squares(mask_ref[...], wave_ref[...])
    columns = power.shape[1]
    column = lax.broadcasted_iota(jnp.int32, power.shape, 1)
    reach = 1
    while reach < window:
        later = pltpu.roll(power, columns - reach, 1)
        power = power + jnp.where(column < columns - reach, later, 0.0)
        reach *= 2
    out_ref[...] = power


def finish_kernel(*refs):
    parts, (power_ref, scale_ref, out_ref) = refs[:-3], refs[-3:]
    slab = power_ref.shape[1]
    total = parts[0][...]
    for part in parts[1:]:
        total = total + part[...]
    dots, edge = total[:, :slab], total[:, slab:]
    inside = slab - edge.shape[1]
    energy = jnp.concatenate(
        [power_ref[:, :inside], power_ref[:, inside:] + edge], axis=1
    )
    out_ref[...] = dots * (scale_ref[:, :1] / jnp.sqrt(energy + EPSILON))


def on_device(waveforms, templates, station_mask, channel_order):
    channels, slab = waveforms.shape
    rows, _, window = templates.shape
    stations = station_mask.shape[1]
    outer_count, tm_count = lax.axis_size("outer"), lax.axis_size("tm")
    blk_count = outer_count * INNER
    assert rows == 1 and LANES % tm_count == 0
    group = INNER * tm_count
    padded = INNER * LANES
    part = padded // group
    chunk = group * slab
    span = 2 * slab
    total = blk_count * tm_count
    blk, every = ("outer", "inner"), ("outer", "inner", "tm")
    sds = jax.ShapeDtypeStruct
    order_row = channel_order[None, :]

    rows = window * part // LANES
    held = [
        pltpu.with_memory_space_constraint(x, pltpu.HBM)
        for x in (waveforms, templates, station_mask, order_row)
    ]
    send, keep, *pieces = call(
        functools.partial(prologue_kernel, tm_count),
        [HBM] * 4,
        [
            sds((padded // 2 * slab // LANES + rows, LANES), BF16),
            sds((padded // 2, slab), BF16),
            *[sds((rows, LANES), BF16)] * (INNER - 1),
        ],
        [
            pltpu.VMEM((channels, slab), BF16),
            pltpu.VMEM((padded, slab), BF16),
            pltpu.VMEM((channels, window), BF16),
            pltpu.VMEM((padded, window), BF16),
            pltpu.VMEM((1, stations), jnp.int32),
            pltpu.VMEM((1, channels), jnp.int32),
            pltpu.VMEM((window, padded), F32),
            pltpu.SemaphoreType.DMA((4,)),
        ],
        bytes_accessed=channels * (window + slab) * 2,
    )(*held)

    def plane(part, flip):
        return lax.ppermute(part, "inner", [(b, b ^ flip) for b in range(INNER)])

    got = plane(send, 1)
    others = [plane(pieces[1], 2), plane(pieces[2], 3)]
    pack = call(
        pack_kernel, [VMEM] * INNER, sds((INNER, rows, LANES), BF16), bytes_accessed=rows * LANES * 8
    )(pieces[0], got, *others)

    def cross(part, route):
        return lax.ppermute(part, "outer", route)

    if outer_count == 4:
        near = cross(pack, [(0, 1), (1, 0), (2, 3), (3, 2)])
        far = cross(pack, [(0, 2), (2, 0), (1, 3), (3, 1)])
        middle = cross(pack, [(1, 2), (2, 1)])
        relay = call(relay_kernel, [VMEM], sds(pack.shape, BF16), flops=RELAY_FLOPS)
        ends = cross(relay(far), [(1, 0), (2, 3)])
        tpls = [pack, near, far, middle, ends]
    else:
        tpls = [pack] + [
            cross(pack, [(b, b ^ flip) for b in range(outer_count)])
            for flip in range(1, outer_count)
        ]

    half = group // 2

    def swap(part, flip):
        y, tm = flip // tm_count, flip % tm_count
        route = [(i, i ^ (2 * tm_count * y + tm)) for i in range(total)]
        return lax.ppermute(part, every, route)

    head = call(
        head_kernel, [VMEM] * 2, sds((padded // 2, window), BF16), bytes_accessed=padded * window
    )(keep, got)
    from_first = [(o * INNER + core) * tm_count for o in range(1, outer_count) for core in range(2)]
    halo = lax.ppermute(head, every, [(i, i - INNER * tm_count) for i in from_first])
    parts = call(
        functools.partial(split_kernel, tm_count),
        [VMEM] * 3 + [AFTER],
        [sds((part, 2 * slab + window), BF16)] * half,
        bytes_accessed=padded * slab * 2,
    )(keep, got, halo, pack)
    waves = [parts[0]] + [swap(parts[flip], flip) for flip in range(1, half)]
    samples = call(
        functools.partial(join_kernel, tm_count, slab),
        [VMEM] * half,
        sds((part, chunk + window), BF16),
        bytes_accessed=part * chunk * 4,
    )(*waves)

    depth = window // FINE * part
    count = blk_count
    work = 2 * count * window * part * chunk // 2

    def scratch():
        return [
            pltpu.VMEM((2, depth, chunk // 4 + LANES), BF16),
            pltpu.VMEM((2, count * FINE, span + LANES), F32),
        ]

    send, edges, left, scale, mask = call(
        functools.partial(first_dots_kernel, outer_count, stations, channels, tm_count),
        [VMEM] * (len(tpls) + 2),
        [
            sds((half, count, slab + window), F32),
            sds((half, count, window), F32),
            sds((count * FINE, depth), BF16),
            sds((count, LANES), F32),
            sds((count, channels), BF16),
        ],
        [pltpu.VMEM((group, count, window), F32)] + scratch(),
        flops=work,
        bytes_accessed=part * chunk * 2,
        vmem=36,
    )(*tpls, order_row, samples)
    keep = call(
        second_dots_kernel,
        [VMEM] * 3 + [AFTER],
        sds((half, count, slab + window), F32),
        scratch(),
        flops=work,
        bytes_accessed=part * chunk * 2,
        vmem=36,
    )(left, samples, edges, send)
    got = lax.ppermute(send, "inner", [(b, b ^ 1) for b in range(INNER)])
    power = call(
        functools.partial(power_kernel, window),
        [VMEM, VMEM, AFTER],
        sds((blk_count, slab), F32),
        flops=4 * blk_count * channels * slab,
        bytes_accessed=channels * slab * 2,
    )(waveforms, mask, keep)
    sums = call(
        functools.partial(add_kernel, tm_count),
        [VMEM] * 2,
        [sds((blk_count, slab + window), F32)] * half,
        bytes_accessed=blk_count * slab * 12 * half,
    )(keep, got)
    sums = [sums[0]] + [swap(sums[flip], flip) for flip in reversed(range(1, half))]
    return call(
        finish_kernel,
        [VMEM] * (half + 2),
        sds((blk_count, slab), F32),
        bytes_accessed=blk_count * slab * 4 * (half + 2),
    )(*sums, power, scale)


def solution(mesh):
    blk_count, tm_count = mesh.devices.shape
    shape = (blk_count // INNER, INNER, tm_count)
    mesh = jax.sharding.Mesh(mesh.devices.reshape(shape), ("outer", "inner", "tm"))
    blk, every = ("outer", "inner"), ("outer", "inner", "tm")
    placed = (P(None, every), P(blk, None, None), P(blk, None), P())
    return jax.shard_map(
        on_device, mesh=mesh, in_specs=placed, out_specs=P(None, every), check_vma=False
    )
```

```python
import functools

import jax
import jax.numpy as jnp
from jax import lax
from jax.experimental import pallas as pl
from jax.experimental.pallas import tpu as pltpu
from jax.sharding import PartitionSpec as P

EPSILON = 1e-05
LANES = 128
INNER = 4
FINE = 16
MIB = 1024 * 1024

BF16 = jnp.bfloat16
F32 = jnp.float32


HBM = pl.BlockSpec(memory_space=pltpu.HBM)
VMEM = pl.BlockSpec(memory_space=pltpu.VMEM)
AFTER = pl.BlockSpec(memory_space=pl.ANY)


def call(kernel, in_specs, out_shape, scratch=(), flops=0, bytes_accessed=0, vmem=24):
    return pl.pallas_call(
        kernel,
        in_specs=in_specs,
        out_specs=jax.tree.map(lambda _: VMEM, out_shape),
        out_shape=out_shape,
        scratch_shapes=list(scratch),
        compiler_params=pltpu.CompilerParams(vmem_limit_bytes=vmem * MIB),
        cost_estimate=pl.CostEstimate(
            flops=flops, bytes_accessed=bytes_accessed, transcendentals=0
        ),
    )


def one_hot(order_row, station_count):
    columns = order_row.shape[1]
    first = 3 * lax.broadcasted_iota(jnp.int32, (station_count, columns), 0)
    hit = (order_row >= first) & (order_row < first + 3)
    return jnp.where(hit, 1.0, 0.0).astype(BF16)


def side_major(inner):
    return lax.rem(inner, 2) * (INNER // 2) + lax.div(inner, 2)


def place_of(real, part):
    base = real // FINE * FINE
    return base, real - base


def regroup_rows(source, target, part):
    channels, width = source.shape
    groups = target.shape[0] // part
    real = channels // groups
    base, extra = place_of(real, part)
    rest = source[groups * base :, :].astype(F32)
    fill = jnp.zeros((part - real, width), F32)
    for group in range(groups):
        if base:
            run = source[group * base : (group + 1) * base, :]
            target[group * part : group * part + base, :] = run
        piece = [rest[group * extra : (group + 1) * extra], fill]
        target[group * part + base : (group + 1) * part, :] = jnp.concatenate(
            piece, axis=0
        ).astype(BF16)


def regroup(channels, padded, part):
    groups = padded // part
    real = channels // groups
    base, extra = place_of(real, part)
    channel = lax.broadcasted_iota(jnp.int32, (channels, padded), 0)
    place = lax.broadcasted_iota(jnp.int32, (1, padded), 1)
    group, within = place >> (part.bit_length() - 1), place & (part - 1)
    rest = groups * base + extra * group + within - base
    source = jnp.where(within < base, base * group + within, rest)
    source = jnp.where(within < real, source, -1)
    return jnp.where(channel == source, 1.0, 0.0).astype(BF16)


def spare_lanes(part, real):
    slots = LANES // part * (part - real)
    slot = lax.broadcasted_iota(jnp.int32, (8, LANES), 0)
    lane = lax.broadcasted_iota(jnp.int32, (8, LANES), 1)
    spare = part - real
    home = lax.div(slot, spare) * part + real + lax.rem(slot, spare)
    return jnp.where((lane == home) & (slot < slots), 1.0, 0.0).astype(BF16)


def prologue_kernel(tm_count, wave_hbm, tpl_hbm, flag_hbm, order_hbm, *refs):
    send_ref, samples_ref, *outs = refs[: INNER + 1]
    wave_ref, grouped, tpl_ref, tpl_grouped, flag_ref, order_ref, turned, sems = refs[INNER + 1 :]
    channels, window = tpl_hbm.shape[1:]
    copies = [
        pltpu.make_async_copy(flag_hbm, flag_ref, sems.at[0]),
        pltpu.make_async_copy(order_hbm, order_ref, sems.at[1]),
        pltpu.make_async_copy(tpl_hbm.at[0], tpl_ref, sems.at[2]),
        pltpu.make_async_copy(wave_hbm, wave_ref, sems.at[3]),
    ]
    for copy in copies:
        copy.start()
    stations = flag_ref.shape[1]
    padded = turned.shape[1]
    part = LANES // tm_count
    rows = outs[0].shape[0]
    groups = regroup(channels, padded, part)
    copies[0].wait()
    copies[1].wait()
    flags = jnp.broadcast_to(flag_ref[...].astype(F32), (8, stations))
    mask = jnp.dot(
        flags.astype(BF16), one_hot(order_ref[...], stations), preferred_element_type=F32
    )
    live = jnp.sum(mask[:1], keepdims=True)
    mask = jnp.dot(mask.astype(BF16), groups, preferred_element_type=F32)[:1]
    copies[2].wait()
    regroup_rows(tpl_ref, tpl_grouped, part)
    masked = tpl_grouped[...].T.astype(F32) * mask
    turned[...] = masked
    norm = jnp.sqrt(jnp.sum(masked * masked, keepdims=True) + EPSILON)
    rest = jnp.broadcast_to(jnp.sqrt(window * live) / norm, (1, rows))
    row = lax.broadcasted_iota(jnp.int32, (1, rows), 1)
    scale = jnp.zeros((1, rows), F32)
    for piece in range(3):
        now = rest.astype(BF16).astype(F32)
        scale = jnp.where(row == piece, now, scale)
        rest = rest - now
    slots = -(-stations // rows)
    wide = flags[:1]
    if stations % rows:
        wide = jnp.concatenate([wide, jnp.zeros((1, rows - stations % rows), F32)], axis=1)
    meta = [wide[:, slot * rows : (slot + 1) * rows] for slot in range(slots)] + [scale]
    meta = jnp.concatenate(meta + [jnp.zeros((8 - len(meta), rows), F32)], axis=0)
    meta = lax.dot_general(
        meta.astype(BF16),
        spare_lanes(part, part * channels // padded),
        (((0,), (0,)), ((), ())),
        preferred_element_type=F32,
    )
    my_tm = lax.axis_index("tm")
    my_inner = lax.axis_index("inner")
    my_core = lax.rem(my_inner, 2)
    first = send_ref.shape[0] - rows
    spot = lax.broadcasted_iota(jnp.int32, (FINE, LANES), 1) >> (part.bit_length() - 1)
    for flip in range(INNER):
        start = pl.multiple_of(side_major(my_inner ^ flip) * LANES, LANES)
        pieces = []
        for step in range(window // (FINE * tm_count)):
            tile = jnp.zeros((FINE, LANES), F32)
            for within in range(tm_count):
                row = FINE * (step * tm_count + within)
                chunk = turned[row : row + FINE, pl.ds(start, LANES)]
                turn = lax.rem(part * (within - my_tm) + LANES, LANES)
                tile = jnp.where(spot == within, pltpu.roll(chunk, turn, 1), tile)
            pieces.append(tile)
        payload = (jnp.concatenate(pieces, axis=0) + meta).astype(BF16)
        if flip == 1:
            send_ref[first:, :] = payload
        else:
            outs[flip - (flip > 1)][...] = payload

    copies[3].wait()
    regroup_rows(wave_ref, grouped, part)
    half = padded // 2
    samples_ref[...] = grouped[pl.ds(pl.multiple_of(my_core * half, half), half), :]
    theirs = pl.ds(pl.multiple_of((1 - my_core) * half, half), half)
    for tile in range(first // half):
        columns = slice(tile * LANES, (tile + 1) * LANES)
        send_ref[tile * half : (tile + 1) * half, :] = grouped[theirs, columns]


def pack_kernel(mine_ref, core_ref, y_ref, both_ref, out_ref):
    inner = lax.axis_index("inner")
    rows = mine_ref.shape[0]
    out_ref[inner] = mine_ref[...]
    out_ref[inner ^ 1] = core_ref[core_ref.shape[0] - rows :, :]
    out_ref[inner ^ 2] = y_ref[...]
    out_ref[inner ^ 3] = both_ref[...]


def head_kernel(keep_ref, got_ref, out_ref):
    core = lax.rem(lax.axis_index("inner"), 2)
    half, window = out_ref.shape

    @pl.when(core == 0)
    def _():
        out_ref[...] = keep_ref[:, :window]

    @pl.when(core == 1)
    def _():
        for tile in range(window // LANES):
            out_ref[:, tile * LANES : (tile + 1) * LANES] = got_ref[
                tile * half : (tile + 1) * half, :
            ]


def split_kernel(tm_count, keep_ref, got_ref, halo_ref, after, *outs):
    del after
    my_inner = lax.axis_index("inner")
    core = lax.rem(my_inner, 2)
    me = lax.div(my_inner, 2) * tm_count + lax.axis_index("tm")
    part = outs[0].shape[0]
    half, slab = keep_ref.shape
    for flip, out_ref in enumerate(outs):
        start = (me ^ flip) * part
        rows = pl.ds(pl.multiple_of(start, part), part)
        out_ref[:, pl.ds(pl.multiple_of(core * slab, slab), slab)] = keep_ref[rows, :]
        for tile in range(slab // LANES):
            theirs = pl.ds(pl.multiple_of(tile * half + start, part), part)
            lanes = pl.multiple_of((1 - core) * slab + tile * LANES, LANES)
            out_ref[:, pl.ds(lanes, LANES)] = got_ref[theirs, :]
        out_ref[:, 2 * slab :] = halo_ref[rows, :]


def join_kernel(tm_count, slab, *refs):
    parts, out_ref = refs[:-1], refs[-1]
    me = lax.div(lax.axis_index("inner"), 2) * tm_count + lax.axis_index("tm")
    count = len(parts)
    for flip, part in enumerate(parts):
        other = me ^ flip
        y, tm = lax.div(other, tm_count), lax.rem(other, tm_count)
        for core in range(2):
            place = (y * 2 + core) * tm_count + tm
            out_ref[:, pl.ds(pl.multiple_of(place * slab, slab), slab)] = part[
                :, core * slab : (core + 1) * slab
            ]

        @pl.when(other == 0)
        def _():
            out_ref[:, 2 * count * slab :] = part[:, 2 * slab :]


def arrival(template):
    return template ^ (lax.axis_index("outer") * INNER)


def arrange(tpls, left):
    size, depth = left.shape
    count = len(tpls) * INNER
    row = lax.broadcasted_iota(jnp.int32, (size, size), 0)
    column = lax.broadcasted_iota(jnp.int32, (size, size), 1)
    shift = count.bit_length() - 1
    source = arrival(row & (count - 1)) * FINE + (row >> shift)
    order = jnp.where(column == source, 1.0, 0.0).astype(BF16)
    for step in range(depth // LANES):
        rows = [
            pack[:, FINE * step : FINE * (step + 1), :].reshape(INNER * FINE, LANES)
            for pack in tpls
        ]
        left[:, step * LANES : (step + 1) * LANES] = jnp.dot(
            order, jnp.concatenate(rows, axis=0), preferred_element_type=F32
        ).astype(BF16)


def correlate(left, full, out_ref, slab, side, shifts, products):
    part = full.shape[0]
    size, depth = left.shape
    count = size // FINE
    copies = LANES // FINE
    run = out_ref.shape[0] // 2
    width = run * slab
    for y in range(2):
        columns = width + 2 * LANES
        start = pl.multiple_of((2 * y + side) * width, width)
        samples = full[:, pl.ds(start, columns)]
        for copy in range(depth // part):
            tile, turn = copy // copies * LANES, copy % copies * FINE
            turned = samples if turn == 0 else pltpu.roll(samples, columns - turn, 1)
            shifts[y, copy * part : (copy + 1) * part, :] = turned[:, tile : tile + width + LANES]
    tiles = products.shape[2] // LANES
    span = (tiles - 1) * LANES
    per_block = span // slab
    blocks = [(y, index) for y in range(2) for index in range(width // span)]

    def multiply(place, slot):
        y, index = place
        for tile in range(0, tiles, 2):
            start = index * span + tile * LANES
            lanes = min(2, tiles - tile) * LANES
            products[slot, :, tile * LANES : tile * LANES + lanes] = jnp.dot(
                left[...], shifts[y, :, start : start + lanes], preferred_element_type=F32
            )

    def gather(place, slot):
        def tree(first, number):
            if number == 1:
                return products[slot, first * count : (first + 1) * count, :]
            half = number // 2
            later = pltpu.roll(tree(first + half, half), span + LANES - half, 1)
            return tree(first, half) + later

        total = tree(0, FINE)
        y, index = place
        for piece in range(per_block):
            out_ref[y * run + index * per_block + piece, :, :slab] = total[
                :, piece * slab : (piece + 1) * slab
            ]

    multiply(blocks[0], 0)
    for number in range(1, len(blocks)):
        multiply(blocks[number], number % 2)
        gather(blocks[number - 1], (number - 1) % 2)
    gather(blocks[-1], (len(blocks) - 1) % 2)


def first_dots_kernel(outer_count, stations, channels, tm_count, *refs):
    tpls, (order_ref, full) = refs[:-10], refs[-10:-8]
    send_ref, edges_ref, left, scale_ref, mask_ref = refs[-8:-3]
    edges, shifts, products = refs[-3:]
    core = lax.rem(lax.axis_index("inner"), 2)
    group, _, window = edges.shape
    slab = (full.shape[1] - window) // group
    tpls = [pack[...] for pack in tpls]
    if len(tpls) > outer_count:
        tpls = tpls[:-2] + [tpls[-2] + tpls[-1]]
    arrange(tpls, left)
    correlate(left, full, send_ref, slab, 1 - core, shifts, products)
    part_mask = read_masks(stations, channels, tm_count, tpls, order_ref, scale_ref, mask_ref)
    after = [full[:, (m + 1) * slab : (m + 1) * slab + window] for m in range(group)]
    squares = masked_squares(part_mask, jnp.concatenate(after, axis=1))
    column = lax.broadcasted_iota(jnp.int32, squares.shape, 1) & (window - 1)
    reach = 1
    while reach < window:
        earlier = pltpu.roll(squares, reach, 1)
        squares = squares + jnp.where(column >= reach, earlier, 0.0)
        reach *= 2
    squares = jnp.where(column >= 1, pltpu.roll(squares, 1, 1), 0.0)
    for member in range(group):
        edges[member] = squares[:, member * window : (member + 1) * window]
    run = group // 4
    for y in range(2):
        for tm in range(run):
            send_ref[y * run + tm, :, slab:] = edges[(2 * y + 1 - core) * run + tm]
            edges_ref[y * run + tm] = edges[(2 * y + core) * run + tm]


def second_dots_kernel(left, full, edges_ref, after, keep_ref, shifts, products):
    del after
    core = lax.rem(lax.axis_index("inner"), 2)
    slab = keep_ref.shape[2] - edges_ref.shape[2]
    correlate(left, full, keep_ref, slab, core, shifts, products)
    keep_ref[:, :, slab:] = edges_ref[...]


def add_kernel(tm_count, keep_ref, got_ref, *outs):
    me = lax.div(lax.axis_index("inner"), 2) * tm_count + lax.axis_index("tm")
    for flip, out_ref in enumerate(outs):
        out_ref[...] = keep_ref[me ^ flip] + got_ref[me ^ flip]


def masked_squares(mask, wave):
    wave = wave.astype(F32)
    squares = wave * wave
    high = squares.astype(BF16)
    low = (squares - high.astype(F32)).astype(BF16)
    return jnp.dot(mask, high, preferred_element_type=F32) + jnp.dot(
        mask, low, preferred_element_type=F32
    )


def read_masks(stations, channels, tm_count, tpls, order_ref, scale_ref, mask_ref):
    rows = tpls[0].shape[1]
    count = len(tpls) * INNER
    padded = INNER * LANES
    part = LANES // tm_count
    meta = lax.dot_general(
        spare_lanes(part, part * channels // padded),
        jnp.concatenate([pack.reshape(INNER * rows, LANES) for pack in tpls], axis=0),
        (((1,), (1,)), ((), ())),
        preferred_element_type=F32,
    )
    template = lax.broadcasted_iota(jnp.int32, (count, count), 0)
    place = lax.broadcasted_iota(jnp.int32, (count, count), 1)
    sort = jnp.where(place == arrival(template), 1.0, 0.0).astype(BF16)
    slots = -(-stations // rows)

    def read(slot):
        return jnp.concatenate(
            [meta[slot : slot + 1, t * rows : (t + 1) * rows] for t in range(count)], axis=0
        )

    values = jnp.concatenate([read(slot) for slot in range(slots + 1)], axis=1)
    values = jnp.dot(sort, values.astype(BF16), preferred_element_type=F32)
    start = slots * rows
    scale = jnp.sum(values[:, start : start + 3], axis=1, keepdims=True)
    scale_ref[...] = jnp.broadcast_to(scale, scale_ref.shape)
    mask = jnp.dot(
        values[:, :stations].astype(BF16),
        one_hot(order_ref[...], stations),
        preferred_element_type=F32,
    ).astype(BF16)
    mask_ref[...] = mask
    grouped = jnp.dot(mask, regroup(channels, padded, part), preferred_element_type=F32)
    mine = side_major(lax.axis_index("inner")) * LANES + lax.axis_index("tm") * part
    return pltpu.roll(grouped, lax.rem(padded - mine, padded), 1)[:, :part].astype(BF16)


def power_kernel(window, wave_ref, mask_ref, after, out_ref):
    del after
    power = masked_squares(mask_ref[...], wave_ref[...])
    columns = power.shape[1]
    column = lax.broadcasted_iota(jnp.int32, power.shape, 1)
    reach = 1
    while reach < window:
        later = pltpu.roll(power, columns - reach, 1)
        power = power + jnp.where(column < columns - reach, later, 0.0)
        reach *= 2
    out_ref[...] = power


def finish_kernel(*refs):
    parts, (power_ref, scale_ref, out_ref) = refs[:-3], refs[-3:]
    slab = power_ref.shape[1]
    total = parts[0][...]
    for part in parts[1:]:
        total = total + part[...]
    dots, edge = total[:, :slab], total[:, slab:]
    inside = slab - edge.shape[1]
    energy = jnp.concatenate(
        [power_ref[:, :inside], power_ref[:, inside:] + edge], axis=1
    )
    out_ref[...] = dots * (scale_ref[:, :1] / jnp.sqrt(energy + EPSILON))


def on_device(waveforms, templates, station_mask, channel_order):
    channels, slab = waveforms.shape
    rows, _, window = templates.shape
    stations = station_mask.shape[1]
    outer_count, tm_count = lax.axis_size("outer"), lax.axis_size("tm")
    blk_count = outer_count * INNER
    assert rows == 1 and LANES % tm_count == 0
    group = INNER * tm_count
    padded = INNER * LANES
    part = padded // group
    chunk = group * slab
    span = 2 * slab
    total = blk_count * tm_count
    blk, every = ("outer", "inner"), ("outer", "inner", "tm")
    sds = jax.ShapeDtypeStruct
    order_row = channel_order[None, :]

    rows = window * part // LANES
    held = [
        pltpu.with_memory_space_constraint(x, pltpu.HBM)
        for x in (waveforms, templates, station_mask, order_row)
    ]
    send, keep, *pieces = call(
        functools.partial(prologue_kernel, tm_count),
        [HBM] * 4,
        [
            sds((padded // 2 * slab // LANES + rows, LANES), BF16),
            sds((padded // 2, slab), BF16),
            *[sds((rows, LANES), BF16)] * (INNER - 1),
        ],
        [
            pltpu.VMEM((channels, slab), BF16),
            pltpu.VMEM((padded, slab), BF16),
            pltpu.VMEM((channels, window), BF16),
            pltpu.VMEM((padded, window), BF16),
            pltpu.VMEM((1, stations), jnp.int32),
            pltpu.VMEM((1, channels), jnp.int32),
            pltpu.VMEM((window, padded), F32),
            pltpu.SemaphoreType.DMA((4,)),
        ],
        bytes_accessed=channels * (window + slab) * 2,
    )(*held)

    def plane(part, flip):
        return lax.ppermute(part, "inner", [(b, b ^ flip) for b in range(INNER)])

    got = plane(send, 1)
    others = [plane(pieces[1], 2), plane(pieces[2], 3)]
    pack = call(
        pack_kernel, [VMEM] * INNER, sds((INNER, rows, LANES), BF16), bytes_accessed=rows * LANES * 8
    )(pieces[0], got, *others)

    def cross(part, route):
        return lax.ppermute(part, "outer", route)

    if outer_count == 4:
        near = cross(pack, [(0, 1), (1, 0), (2, 3), (3, 2)])
        far = cross(pack, [(0, 2), (2, 0), (1, 3), (3, 1)])
        middle = cross(pack, [(1, 2), (2, 1)])
        ends = cross(far, [(1, 0), (2, 3)])
        tpls = [pack, near, far, middle, ends]
    else:
        tpls = [pack] + [
            cross(pack, [(b, b ^ flip) for b in range(outer_count)])
            for flip in range(1, outer_count)
        ]

    half = group // 2

    def swap(part, flip):
        y, tm = flip // tm_count, flip % tm_count
        route = [(i, i ^ (2 * tm_count * y + tm)) for i in range(total)]
        return lax.ppermute(part, every, route)

    head = call(
        head_kernel, [VMEM] * 2, sds((padded // 2, window), BF16), bytes_accessed=padded * window
    )(keep, got)
    from_first = [(o * INNER + core) * tm_count for o in range(1, outer_count) for core in range(2)]
    halo = lax.ppermute(head, every, [(i, i - INNER * tm_count) for i in from_first])
    parts = call(
        functools.partial(split_kernel, tm_count),
        [VMEM] * 3 + [AFTER],
        [sds((part, 2 * slab + window), BF16)] * half,
        bytes_accessed=padded * slab * 2,
    )(keep, got, halo, pack)
    waves = [parts[0]] + [swap(parts[flip], flip) for flip in range(1, half)]
    samples = call(
        functools.partial(join_kernel, tm_count, slab),
        [VMEM] * half,
        sds((part, chunk + window), BF16),
        bytes_accessed=part * chunk * 4,
    )(*waves)

    depth = window // FINE * part
    count = blk_count
    work = 2 * count * window * part * chunk // 2

    def scratch():
        return [
            pltpu.VMEM((2, depth, chunk // 4 + LANES), BF16),
            pltpu.VMEM((2, count * FINE, span + LANES), F32),
        ]

    send, edges, left, scale, mask = call(
        functools.partial(first_dots_kernel, outer_count, stations, channels, tm_count),
        [VMEM] * (len(tpls) + 2),
        [
            sds((half, count, slab + window), F32),
            sds((half, count, window), F32),
            sds((count * FINE, depth), BF16),
            sds((count, LANES), F32),
            sds((count, channels), BF16),
        ],
        [pltpu.VMEM((group, count, window), F32)] + scratch(),
        flops=work,
        bytes_accessed=part * chunk * 2,
        vmem=36,
    )(*tpls, order_row, samples)
    keep = call(
        second_dots_kernel,
        [VMEM] * 3 + [AFTER],
        sds((half, count, slab + window), F32),
        scratch(),
        flops=work,
        bytes_accessed=part * chunk * 2,
        vmem=36,
    )(left, samples, edges, send)
    got = lax.ppermute(send, "inner", [(b, b ^ 1) for b in range(INNER)])
    power = call(
        functools.partial(power_kernel, window),
        [VMEM, VMEM, AFTER],
        sds((blk_count, slab), F32),
        flops=4 * blk_count * channels * slab,
        bytes_accessed=channels * slab * 2,
    )(waveforms, mask, keep)
    sums = call(
        functools.partial(add_kernel, tm_count),
        [VMEM] * 2,
        [sds((blk_count, slab + window), F32)] * half,
        bytes_accessed=blk_count * slab * 12 * half,
    )(keep, got)
    sums = [sums[0]] + [swap(sums[flip], flip) for flip in reversed(range(1, half))]
    return call(
        finish_kernel,
        [VMEM] * (half + 2),
        sds((blk_count, slab), F32),
        bytes_accessed=blk_count * slab * 4 * (half + 2),
    )(*sums, power, scale)


def solution(mesh):
    blk_count, tm_count = mesh.devices.shape
    shape = (blk_count // INNER, INNER, tm_count)
    mesh = jax.sharding.Mesh(mesh.devices.reshape(shape), ("outer", "inner", "tm"))
    blk, every = ("outer", "inner"), ("outer", "inner", "tm")
    placed = (P(None, every), P(blk, None, None), P(blk, None), P())
    return jax.shard_map(
        on_device, mesh=mesh, in_specs=placed, out_specs=P(None, every), check_vma=False
    )
```

```python
import functools

import jax
import jax.numpy as jnp
from jax import lax
from jax.experimental import pallas as pl
from jax.experimental.pallas import tpu as pltpu
from jax.sharding import PartitionSpec as P

EPSILON = 1e-05
LANES = 128
INNER = 4
FINE = 16
MIB = 1024 * 1024

BF16 = jnp.bfloat16
F32 = jnp.float32


HBM = pl.BlockSpec(memory_space=pltpu.HBM)
VMEM = pl.BlockSpec(memory_space=pltpu.VMEM)
AFTER = pl.BlockSpec(memory_space=pl.ANY)


def call(kernel, in_specs, out_shape, scratch=(), flops=0, bytes_accessed=0, vmem=24):
    return pl.pallas_call(
        kernel,
        in_specs=in_specs,
        out_specs=jax.tree.map(lambda _: VMEM, out_shape),
        out_shape=out_shape,
        scratch_shapes=list(scratch),
        compiler_params=pltpu.CompilerParams(vmem_limit_bytes=vmem * MIB),
        cost_estimate=pl.CostEstimate(
            flops=flops, bytes_accessed=bytes_accessed, transcendentals=0
        ),
    )


def one_hot(order_row, station_count):
    columns = order_row.shape[1]
    first = 3 * lax.broadcasted_iota(jnp.int32, (station_count, columns), 0)
    hit = (order_row >= first) & (order_row < first + 3)
    return jnp.where(hit, 1.0, 0.0).astype(BF16)


def side_major(inner):
    return lax.rem(inner, 2) * (INNER // 2) + lax.div(inner, 2)


def place_of(real, part):
    base = real // FINE * FINE
    return base, real - base


def regroup_rows(source, target, part):
    channels, width = source.shape
    groups = target.shape[0] // part
    real = channels // groups
    base, extra = place_of(real, part)
    rest = source[groups * base :, :].astype(F32)
    fill = jnp.zeros((part - real, width), F32)
    for group in range(groups):
        if base:
            run = source[group * base : (group + 1) * base, :]
            target[group * part : group * part + base, :] = run
        piece = [rest[group * extra : (group + 1) * extra], fill]
        target[group * part + base : (group + 1) * part, :] = jnp.concatenate(
            piece, axis=0
        ).astype(BF16)


def regroup(channels, padded, part):
    groups = padded // part
    real = channels // groups
    base, extra = place_of(real, part)
    channel = lax.broadcasted_iota(jnp.int32, (channels, padded), 0)
    place = lax.broadcasted_iota(jnp.int32, (1, padded), 1)
    group, within = place >> (part.bit_length() - 1), place & (part - 1)
    rest = groups * base + extra * group + within - base
    source = jnp.where(within < base, base * group + within, rest)
    source = jnp.where(within < real, source, -1)
    return jnp.where(channel == source, 1.0, 0.0).astype(BF16)


def spare_lanes(part, real):
    slots = LANES // part * (part - real)
    slot = lax.broadcasted_iota(jnp.int32, (8, LANES), 0)
    lane = lax.broadcasted_iota(jnp.int32, (8, LANES), 1)
    spare = part - real
    home = lax.div(slot, spare) * part + real + lax.rem(slot, spare)
    return jnp.where((lane == home) & (slot < slots), 1.0, 0.0).astype(BF16)


def prologue_kernel(tm_count, wave_hbm, tpl_hbm, flag_hbm, order_hbm, *refs):
    send_ref, samples_ref, *outs = refs[: INNER + 1]
    wave_ref, grouped, tpl_ref, tpl_grouped, flag_ref, order_ref, turned, sems = refs[INNER + 1 :]
    channels, window = tpl_hbm.shape[1:]
    copies = [
        pltpu.make_async_copy(flag_hbm, flag_ref, sems.at[0]),
        pltpu.make_async_copy(order_hbm, order_ref, sems.at[1]),
        pltpu.make_async_copy(tpl_hbm.at[0], tpl_ref, sems.at[2]),
        pltpu.make_async_copy(wave_hbm, wave_ref, sems.at[3]),
    ]
    for copy in copies:
        copy.start()
    stations = flag_ref.shape[1]
    padded = turned.shape[1]
    part = LANES // tm_count
    rows = outs[0].shape[0]
    groups = regroup(channels, padded, part)
    copies[0].wait()
    copies[1].wait()
    flags = jnp.broadcast_to(flag_ref[...].astype(F32), (8, stations))
    mask = jnp.dot(
        flags.astype(BF16), one_hot(order_ref[...], stations), preferred_element_type=F32
    )
    live = jnp.sum(mask[:1], keepdims=True)
    mask = jnp.dot(mask.astype(BF16), groups, preferred_element_type=F32)[:1]
    copies[2].wait()
    regroup_rows(tpl_ref, tpl_grouped, part)
    masked = tpl_grouped[...].T.astype(F32) * mask
    turned[...] = masked
    norm = jnp.sqrt(jnp.sum(masked * masked, keepdims=True) + EPSILON)
    rest = jnp.broadcast_to(jnp.sqrt(window * live) / norm, (1, rows))
    row = lax.broadcasted_iota(jnp.int32, (1, rows), 1)
    scale = jnp.zeros((1, rows), F32)
    for piece in range(3):
        now = rest.astype(BF16).astype(F32)
        scale = jnp.where(row == piece, now, scale)
        rest = rest - now
    slots = -(-stations // rows)
    wide = flags[:1]
    if stations % rows:
        wide = jnp.concatenate([wide, jnp.zeros((1, rows - stations % rows), F32)], axis=1)
    meta = [wide[:, slot * rows : (slot + 1) * rows] for slot in range(slots)] + [scale]
    meta = jnp.concatenate(meta + [jnp.zeros((8 - len(meta), rows), F32)], axis=0)
    meta = lax.dot_general(
        meta.astype(BF16),
        spare_lanes(part, part * channels // padded),
        (((0,), (0,)), ((), ())),
        preferred_element_type=F32,
    )
    my_tm = lax.axis_index("tm")
    my_inner = lax.axis_index("inner")
    my_core = lax.rem(my_inner, 2)
    first = send_ref.shape[0] - rows
    spot = lax.broadcasted_iota(jnp.int32, (FINE, LANES), 1) >> (part.bit_length() - 1)
    for flip in range(INNER):
        start = pl.multiple_of(side_major(my_inner ^ flip) * LANES, LANES)
        pieces = []
        for step in range(window // (FINE * tm_count)):
            tile = jnp.zeros((FINE, LANES), F32)
            for within in range(tm_count):
                row = FINE * (step * tm_count + within)
                chunk = turned[row : row + FINE, pl.ds(start, LANES)]
                turn = lax.rem(part * (within - my_tm) + LANES, LANES)
                tile = jnp.where(spot == within, pltpu.roll(chunk, turn, 1), tile)
            pieces.append(tile)
        payload = (jnp.concatenate(pieces, axis=0) + meta).astype(BF16)
        if flip == 1:
            send_ref[first:, :] = payload
        else:
            outs[flip - (flip > 1)][...] = payload

    copies[3].wait()
    regroup_rows(wave_ref, grouped, part)
    half = padded // 2
    samples_ref[...] = grouped[pl.ds(pl.multiple_of(my_core * half, half), half), :]
    theirs = pl.ds(pl.multiple_of((1 - my_core) * half, half), half)
    for tile in range(first // half):
        columns = slice(tile * LANES, (tile + 1) * LANES)
        send_ref[tile * half : (tile + 1) * half, :] = grouped[theirs, columns]


def pack_kernel(mine_ref, core_ref, y_ref, both_ref, out_ref):
    inner = lax.axis_index("inner")
    rows = mine_ref.shape[0]
    out_ref[inner] = mine_ref[...]
    out_ref[inner ^ 1] = core_ref[core_ref.shape[0] - rows :, :]
    out_ref[inner ^ 2] = y_ref[...]
    out_ref[inner ^ 3] = both_ref[...]


def split_kernel(tm_count, keep_ref, got_ref, *outs):
    my_inner = lax.axis_index("inner")
    core = lax.rem(my_inner, 2)
    me = lax.div(my_inner, 2) * tm_count + lax.axis_index("tm")
    part = outs[0].shape[1]
    half, slab = keep_ref.shape
    for flip, out_ref in enumerate(outs):
        start = (me ^ flip) * part
        out_ref[core] = keep_ref[pl.ds(pl.multiple_of(start, part), part), :]
        for tile in range(slab // LANES):
            rows = pl.ds(pl.multiple_of(tile * half + start, part), part)
            out_ref[1 - core, :, tile * LANES : (tile + 1) * LANES] = got_ref[rows, :]


def join_kernel(tm_count, *refs):
    parts, out_ref, head_ref = refs[:-2], refs[-2], refs[-1]
    me = lax.div(lax.axis_index("inner"), 2) * tm_count + lax.axis_index("tm")
    slab = parts[0].shape[2]
    for flip, part in enumerate(parts):
        other = me ^ flip
        y, tm = lax.div(other, tm_count), lax.rem(other, tm_count)
        for core in range(2):
            place = (y * 2 + core) * tm_count + tm
            out_ref[:, pl.ds(pl.multiple_of(place * slab, slab), slab)] = part[core]
    head_ref[...] = out_ref[:, : head_ref.shape[1]]


def arrange(tpls, left):
    for flip, pack in enumerate(tpls):
        for inner in range(INNER):
            row = (flip * INNER + inner) * FINE
            for step in range(left.shape[1] // LANES):
                left[row : row + FINE, step * LANES : (step + 1) * LANES] = pack[
                    inner, FINE * step : FINE * (step + 1), :
                ]


def correlate(left, full, slab, run, side, ys, store, shifts, products):
    part = full.shape[0]
    size, depth = left.shape
    count = size // FINE
    copies = LANES // FINE
    width = run * slab
    for y in ys:
        columns = width + 2 * LANES
        start = pl.multiple_of((2 * y + side) * width, width)
        samples = full[:, pl.ds(start, columns)]
        for copy in range(depth // part):
            tile, turn = copy // copies * LANES, copy % copies * FINE
            turned = samples if turn == 0 else pltpu.roll(samples, columns - turn, 1)
            shifts[y, copy * part : (copy + 1) * part, :] = turned[:, tile : tile + width + LANES]
    tiles = products.shape[1]
    span = (tiles - 1) * LANES
    per_block = span // slab
    blocks = [(y, index) for y in ys for index in range(width // span)]

    def multiply(place, slot):
        y, index = place
        for tile in range(0, tiles, 2):
            start = index * span + tile * LANES
            pieces = min(2, tiles - tile)
            product = jnp.dot(
                left[...],
                shifts[y, :, start : start + pieces * LANES],
                preferred_element_type=F32,
            )
            for piece in range(pieces):
                products[slot, tile + piece] = product[:, piece * LANES : (piece + 1) * LANES]

    def gather(place, slot):
        def tree(first, number):
            if number == 1:
                rows = pl.ds(first, count, stride=FINE)
                return jnp.concatenate(
                    [products[slot, tile, rows, :] for tile in range(tiles)], axis=1
                )
            half = number // 2
            later = pltpu.roll(tree(first + half, half), span + LANES - half, 1)
            return tree(first, half) + later

        total = tree(0, FINE)
        y, index = place
        for piece in range(per_block):
            store(y, index * per_block + piece, total[:, piece * slab : (piece + 1) * slab])

    multiply(blocks[0], 0)
    for number in range(1, len(blocks)):
        multiply(blocks[number], number % 2)
        gather(blocks[number - 1], (number - 1) % 2)
    gather(blocks[-1], (len(blocks) - 1) % 2)


def first_dots_kernel(outer_count, stations, channels, tm_count, *refs):
    tpls, (order_ref, samples_ref) = refs[:-9], refs[-9:-7]
    begun_ref, left, scale_ref, mask_ref, part_ref, shifts, products = refs[-7:]
    tpls = [pack[...] for pack in tpls]
    if len(tpls) > outer_count:
        tpls = tpls[:-2] + [tpls[-2] + tpls[-1]]
    arrange(tpls, left)
    core = lax.rem(lax.axis_index("inner"), 2)
    run, _, slab = begun_ref.shape

    def store(y, place, sums):
        begun_ref[place] = sums

    correlate(left, samples_ref, slab, run, 1 - core, [0], store, shifts, products)
    read_masks(stations, channels, tm_count, tpls, order_ref, scale_ref, mask_ref, part_ref)


def middle_dots_kernel(left, samples_ref, halo_ref, begun_ref, mask_ref, *refs):
    send_ref, edges_ref, full, edges, shifts, products = refs
    group, _, window = edges.shape
    chunk = samples_ref.shape[1]
    slab = chunk // group
    run = group // 4
    core = lax.rem(lax.axis_index("inner"), 2)
    full[:, :chunk] = samples_ref[...]
    full[:, chunk:] = halo_ref[...]

    def store(y, place, sums):
        send_ref[y * run + place, :, :slab] = sums

    correlate(left, full, slab, run, 1 - core, [1], store, shifts, products)
    after = [full[:, (m + 1) * slab : (m + 1) * slab + window] for m in range(group)]
    squares = masked_squares(mask_ref[...], jnp.concatenate(after, axis=1))
    column = lax.broadcasted_iota(jnp.int32, squares.shape, 1) & (window - 1)
    reach = 1
    while reach < window:
        earlier = pltpu.roll(squares, reach, 1)
        squares = squares + jnp.where(column >= reach, earlier, 0.0)
        reach *= 2
    squares = jnp.where(column >= 1, pltpu.roll(squares, 1, 1), 0.0)
    for member in range(group):
        edges[member] = squares[:, member * window : (member + 1) * window]
    for tm in range(run):
        send_ref[tm, :, :slab] = begun_ref[tm]
        for y in range(2):
            send_ref[y * run + tm, :, slab:] = edges[(2 * y + 1 - core) * run + tm]
            edges_ref[y * run + tm] = edges[(2 * y + core) * run + tm]


def last_dots_kernel(left, samples_ref, halo_ref, edges_ref, after, keep_ref, *scratch):
    del after
    full, shifts, products = scratch
    chunk = samples_ref.shape[1]
    full[:, :chunk] = samples_ref[...]
    full[:, chunk:] = halo_ref[...]
    core = lax.rem(lax.axis_index("inner"), 2)
    run = keep_ref.shape[0] // 2
    slab = keep_ref.shape[2] - edges_ref.shape[2]

    def store(y, place, sums):
        keep_ref[y * run + place, :, :slab] = sums

    correlate(left, full, slab, run, core, [0, 1], store, shifts, products)
    keep_ref[:, :, slab:] = edges_ref[...]


def add_kernel(tm_count, keep_ref, got_ref, *outs):
    me = lax.div(lax.axis_index("inner"), 2) * tm_count + lax.axis_index("tm")
    for flip, out_ref in enumerate(outs):
        out_ref[...] = keep_ref[me ^ flip] + got_ref[me ^ flip]


def masked_squares(mask, wave):
    wave = wave.astype(F32)
    squares = wave * wave
    high = squares.astype(BF16)
    low = (squares - high.astype(F32)).astype(BF16)
    return jnp.dot(mask, high, preferred_element_type=F32) + jnp.dot(
        mask, low, preferred_element_type=F32
    )


def read_masks(stations, channels, tm_count, tpls, order_ref, scale_ref, mask_ref, part_ref):
    rows = tpls[0].shape[1]
    count = len(tpls) * INNER
    padded = INNER * LANES
    part = LANES // tm_count
    meta = lax.dot_general(
        spare_lanes(part, part * channels // padded),
        jnp.concatenate([pack.reshape(INNER * rows, LANES) for pack in tpls], axis=0),
        (((1,), (1,)), ((), ())),
        preferred_element_type=F32,
    )
    slots = -(-stations // rows)

    def read(slot):
        return jnp.concatenate(
            [meta[slot : slot + 1, t * rows : (t + 1) * rows] for t in range(count)], axis=0
        )

    values = jnp.concatenate([read(slot) for slot in range(slots + 1)], axis=1)
    start = slots * rows
    scale = jnp.sum(values[:, start : start + 3], axis=1, keepdims=True)
    scale_ref[...] = jnp.broadcast_to(scale, scale_ref.shape)
    mask = jnp.dot(
        values[:, :stations].astype(BF16),
        one_hot(order_ref[...], stations),
        preferred_element_type=F32,
    ).astype(BF16)
    mask_ref[...] = mask
    grouped = jnp.dot(mask, regroup(channels, padded, part), preferred_element_type=F32)
    mine = side_major(lax.axis_index("inner")) * LANES + lax.axis_index("tm") * part
    part_ref[...] = pltpu.roll(grouped, lax.rem(padded - mine, padded), 1)[:, :part].astype(BF16)


def power_kernel(window, wave_ref, mask_ref, after, out_ref):
    del after
    power = masked_squares(mask_ref[...], wave_ref[...])
    columns = power.shape[1]
    column = lax.broadcasted_iota(jnp.int32, power.shape, 1)
    reach = 1
    while reach < window:
        later = pltpu.roll(power, columns - reach, 1)
        power = power + jnp.where(column < columns - reach, later, 0.0)
        reach *= 2
    out_ref[...] = power


def finish_kernel(*refs):
    parts, (power_ref, scale_ref, out_ref) = refs[:-3], refs[-3:]
    slab = power_ref.shape[1]
    total = parts[0][...]
    for part in parts[1:]:
        total = total + part[...]
    dots, edge = total[:, :slab], total[:, slab:]
    inside = slab - edge.shape[1]
    energy = jnp.concatenate(
        [power_ref[:, :inside], power_ref[:, inside:] + edge], axis=1
    )
    rows = dots * (scale_ref[:, :1] / jnp.sqrt(energy + EPSILON))
    outer = lax.axis_index("outer")
    step = INNER
    while step < rows.shape[0]:
        pairs = [rows[start : start + step] for start in range(0, rows.shape[0], step)]
        swapped = [pairs[index ^ 1] for index in range(len(pairs))]
        flipped = (outer & (step // INNER)) != 0
        rows = jnp.where(flipped, jnp.concatenate(swapped, axis=0), rows)
        step *= 2
    out_ref[...] = rows


def on_device(waveforms, templates, station_mask, channel_order):
    channels, slab = waveforms.shape
    rows, _, window = templates.shape
    stations = station_mask.shape[1]
    outer_count, tm_count = lax.axis_size("outer"), lax.axis_size("tm")
    blk_count = outer_count * INNER
    assert rows == 1 and LANES % tm_count == 0
    group = INNER * tm_count
    padded = INNER * LANES
    part = padded // group
    chunk = group * slab
    span = 2 * slab
    total = blk_count * tm_count
    blk, every = ("outer", "inner"), ("outer", "inner", "tm")
    sds = jax.ShapeDtypeStruct
    order_row = channel_order[None, :]

    rows = window * part // LANES
    held = [
        pltpu.with_memory_space_constraint(x, pltpu.HBM)
        for x in (waveforms, templates, station_mask, order_row)
    ]
    send, keep, *pieces = call(
        functools.partial(prologue_kernel, tm_count),
        [HBM] * 4,
        [
            sds((padded // 2 * slab // LANES + rows, LANES), BF16),
            sds((padded // 2, slab), BF16),
            *[sds((rows, LANES), BF16)] * (INNER - 1),
        ],
        [
            pltpu.VMEM((channels, slab), BF16),
            pltpu.VMEM((padded, slab), BF16),
            pltpu.VMEM((channels, window), BF16),
            pltpu.VMEM((padded, window), BF16),
            pltpu.VMEM((1, stations), jnp.int32),
            pltpu.VMEM((1, channels), jnp.int32),
            pltpu.VMEM((window, padded), F32),
            pltpu.SemaphoreType.DMA((4,)),
        ],
        bytes_accessed=channels * (window + slab) * 2,
    )(*held)

    def plane(part, flip):
        return lax.ppermute(part, "inner", [(b, b ^ flip) for b in range(INNER)])

    got = plane(send, 1)
    others = [plane(pieces[1], 2), plane(pieces[2], 3)]
    pack = call(
        pack_kernel, [VMEM] * INNER, sds((INNER, rows, LANES), BF16), bytes_accessed=rows * LANES * 8
    )(pieces[0], got, *others)

    def cross(part, route):
        return lax.ppermute(part, "outer", route)

    if outer_count == 4:
        near = cross(pack, [(0, 1), (1, 0), (2, 3), (3, 2)])
        far = cross(pack, [(0, 2), (2, 0), (1, 3), (3, 1)])
        middle = cross(pack, [(1, 2), (2, 1)])
        ends = cross(far, [(1, 0), (2, 3)])
        tpls = [pack, near, far, middle, ends]
    else:
        tpls = [pack] + [
            cross(pack, [(b, b ^ flip) for b in range(outer_count)])
            for flip in range(1, outer_count)
        ]

    half = group // 2

    def swap(part, flip):
        y, tm = flip // tm_count, flip % tm_count
        route = [(i, i ^ (2 * tm_count * y + tm)) for i in range(total)]
        return lax.ppermute(part, every, route)

    parts = call(
        functools.partial(split_kernel, tm_count),
        [VMEM] * 2,
        [sds((2, part, slab), BF16)] * half,
        bytes_accessed=padded * slab * 2,
    )(keep, got)
    waves = [parts[0]] + [swap(parts[flip], flip) for flip in range(1, half)]
    samples, head = call(
        functools.partial(join_kernel, tm_count),
        [VMEM] * half,
        [sds((part, chunk), BF16), sds((part, window), BF16)],
        bytes_accessed=part * chunk * 4,
    )(*waves)
    halo = lax.ppermute(head, "outer", [(b, b - 1) for b in range(1, outer_count)])

    depth = window // FINE * part
    count = blk_count
    work = 2 * count * window * part * chunk // 2

    def scratch():
        return [
            pltpu.VMEM((2, depth, chunk // 4 + LANES), BF16),
            pltpu.VMEM((2, span // LANES + 1, count * FINE, LANES), F32),
        ]

    begun, left, scale, mask, mask_part = call(
        functools.partial(first_dots_kernel, outer_count, stations, channels, tm_count),
        [VMEM] * (len(tpls) + 2),
        [
            sds((tm_count, count, slab), F32),
            sds((count * FINE, depth), BF16),
            sds((count, LANES), F32),
            sds((count, channels), BF16),
            sds((count, part), BF16),
        ],
        scratch(),
        flops=work // 2,
        bytes_accessed=part * chunk * 2,
        vmem=36,
    )(*tpls, order_row, samples)
    full = pltpu.VMEM((part, chunk + window), BF16)
    send, edges = call(
        middle_dots_kernel,
        [VMEM] * 5,
        [sds((half, count, slab + window), F32), sds((half, count, window), F32)],
        [full, pltpu.VMEM((group, count, window), F32)] + scratch(),
        flops=work // 2,
        bytes_accessed=part * chunk * 2,
        vmem=36,
    )(left, samples, halo, begun, mask_part)
    keep = call(
        last_dots_kernel,
        [VMEM] * 4 + [AFTER],
        sds((half, count, slab + window), F32),
        [full] + scratch(),
        flops=work,
        bytes_accessed=part * chunk * 2,
        vmem=36,
    )(left, samples, halo, edges, send)
    got = lax.ppermute(send, "inner", [(b, b ^ 1) for b in range(INNER)])
    power = call(
        functools.partial(power_kernel, window),
        [VMEM, VMEM, AFTER],
        sds((blk_count, slab), F32),
        flops=4 * blk_count * channels * slab,
        bytes_accessed=channels * slab * 2,
    )(waveforms, mask, keep)
    sums = call(
        functools.partial(add_kernel, tm_count),
        [VMEM] * 2,
        [sds((blk_count, slab + window), F32)] * half,
        bytes_accessed=blk_count * slab * 12 * half,
    )(keep, got)
    sums = [sums[0]] + [swap(sums[flip], flip) for flip in reversed(range(1, half))]
    return call(
        finish_kernel,
        [VMEM] * (half + 2),
        sds((blk_count, slab), F32),
        bytes_accessed=blk_count * slab * 4 * (half + 2),
    )(*sums, power, scale)


def solution(mesh):
    blk_count, tm_count = mesh.devices.shape
    shape = (blk_count // INNER, INNER, tm_count)
    mesh = jax.sharding.Mesh(mesh.devices.reshape(shape), ("outer", "inner", "tm"))
    blk, every = ("outer", "inner"), ("outer", "inner", "tm")
    placed = (P(None, every), P(blk, None, None), P(blk, None), P())
    return jax.shard_map(
        on_device, mesh=mesh, in_specs=placed, out_specs=P(None, every), check_vma=False
    )
```

```python
import functools

import jax
import jax.numpy as jnp
from jax import lax
from jax.experimental import pallas as pl
from jax.experimental.pallas import tpu as pltpu
from jax.sharding import PartitionSpec as P

EPSILON = 1e-05
LANES = 128
INNER = 4
FINE = 16
MIB = 1024 * 1024

BF16 = jnp.bfloat16
F32 = jnp.float32


HBM = pl.BlockSpec(memory_space=pltpu.HBM)
VMEM = pl.BlockSpec(memory_space=pltpu.VMEM)
AFTER = pl.BlockSpec(memory_space=pl.ANY)


def call(kernel, in_specs, out_shape, scratch=(), flops=0, bytes_accessed=0, vmem=24):
    return pl.pallas_call(
        kernel,
        in_specs=in_specs,
        out_specs=jax.tree.map(lambda _: VMEM, out_shape),
        out_shape=out_shape,
        scratch_shapes=list(scratch),
        compiler_params=pltpu.CompilerParams(vmem_limit_bytes=vmem * MIB),
        cost_estimate=pl.CostEstimate(
            flops=flops, bytes_accessed=bytes_accessed, transcendentals=0
        ),
    )


def one_hot(order_row, station_count):
    columns = order_row.shape[1]
    first = 3 * lax.broadcasted_iota(jnp.int32, (station_count, columns), 0)
    hit = (order_row >= first) & (order_row < first + 3)
    return jnp.where(hit, 1.0, 0.0).astype(BF16)


def side_major(inner):
    return lax.rem(inner, 2) * (INNER // 2) + lax.div(inner, 2)


def place_of(real, part):
    base = real // FINE * FINE
    return base, real - base


def regroup_rows(source, target, part):
    channels, width = source.shape
    groups = target.shape[0] // part
    real = channels // groups
    base, extra = place_of(real, part)
    rest = source[groups * base :, :].astype(F32)
    fill = jnp.zeros((part - real, width), F32)
    for group in range(groups):
        if base:
            run = source[group * base : (group + 1) * base, :]
            target[group * part : group * part + base, :] = run
        piece = [rest[group * extra : (group + 1) * extra], fill]
        target[group * part + base : (group + 1) * part, :] = jnp.concatenate(
            piece, axis=0
        ).astype(BF16)


def regroup(channels, padded, part):
    groups = padded // part
    real = channels // groups
    base, extra = place_of(real, part)
    channel = lax.broadcasted_iota(jnp.int32, (channels, padded), 0)
    place = lax.broadcasted_iota(jnp.int32, (1, padded), 1)
    group, within = place >> (part.bit_length() - 1), place & (part - 1)
    rest = groups * base + extra * group + within - base
    source = jnp.where(within < base, base * group + within, rest)
    source = jnp.where(within < real, source, -1)
    return jnp.where(channel == source, 1.0, 0.0).astype(BF16)


def spare_lanes(part, real):
    slots = LANES // part * (part - real)
    slot = lax.broadcasted_iota(jnp.int32, (8, LANES), 0)
    lane = lax.broadcasted_iota(jnp.int32, (8, LANES), 1)
    spare = part - real
    home = lax.div(slot, spare) * part + real + lax.rem(slot, spare)
    return jnp.where((lane == home) & (slot < slots), 1.0, 0.0).astype(BF16)


def prologue_kernel(tm_count, wave_hbm, tpl_hbm, flag_hbm, order_hbm, *refs):
    send_ref, samples_ref, *outs = refs[: INNER + 1]
    wave_ref, grouped, tpl_ref, tpl_grouped, flag_ref, order_ref, turned, sems = refs[INNER + 1 :]
    channels, window = tpl_hbm.shape[1:]
    copies = [
        pltpu.make_async_copy(flag_hbm, flag_ref, sems.at[0]),
        pltpu.make_async_copy(order_hbm, order_ref, sems.at[1]),
        pltpu.make_async_copy(tpl_hbm.at[0], tpl_ref, sems.at[2]),
        pltpu.make_async_copy(wave_hbm, wave_ref, sems.at[3]),
    ]
    for copy in copies:
        copy.start()
    stations = flag_ref.shape[1]
    padded = turned.shape[1]
    part = LANES // tm_count
    rows = outs[0].shape[0]
    groups = regroup(channels, padded, part)
    copies[0].wait()
    copies[1].wait()
    flags = jnp.broadcast_to(flag_ref[...].astype(F32), (8, stations))
    mask = jnp.dot(
        flags.astype(BF16), one_hot(order_ref[...], stations), preferred_element_type=F32
    )
    live = jnp.sum(mask[:1], keepdims=True)
    mask = jnp.dot(mask.astype(BF16), groups, preferred_element_type=F32)[:1]
    copies[2].wait()
    regroup_rows(tpl_ref, tpl_grouped, part)
    masked = tpl_grouped[...].T.astype(F32) * mask
    turned[...] = masked
    norm = jnp.sqrt(jnp.sum(masked * masked, keepdims=True) + EPSILON)
    rest = jnp.broadcast_to(jnp.sqrt(window * live) / norm, (1, rows))
    row = lax.broadcasted_iota(jnp.int32, (1, rows), 1)
    scale = jnp.zeros((1, rows), F32)
    for piece in range(3):
        now = rest.astype(BF16).astype(F32)
        scale = jnp.where(row == piece, now, scale)
        rest = rest - now
    slots = -(-stations // rows)
    wide = flags[:1]
    if stations % rows:
        wide = jnp.concatenate([wide, jnp.zeros((1, rows - stations % rows), F32)], axis=1)
    meta = [wide[:, slot * rows : (slot + 1) * rows] for slot in range(slots)] + [scale]
    meta = jnp.concatenate(meta + [jnp.zeros((8 - len(meta), rows), F32)], axis=0)
    meta = lax.dot_general(
        meta.astype(BF16),
        spare_lanes(part, part * channels // padded),
        (((0,), (0,)), ((), ())),
        preferred_element_type=F32,
    )
    my_tm = lax.axis_index("tm")
    my_inner = lax.axis_index("inner")
    my_core = lax.rem(my_inner, 2)
    first = send_ref.shape[0] - rows
    spot = lax.broadcasted_iota(jnp.int32, (FINE, LANES), 1) >> (part.bit_length() - 1)
    for flip in range(INNER):
        start = pl.multiple_of(side_major(my_inner ^ flip) * LANES, LANES)
        pieces = []
        for step in range(window // (FINE * tm_count)):
            tile = jnp.zeros((FINE, LANES), F32)
            for within in range(tm_count):
                row = FINE * (step * tm_count + within)
                chunk = turned[row : row + FINE, pl.ds(start, LANES)]
                turn = lax.rem(part * (within - my_tm) + LANES, LANES)
                tile = jnp.where(spot == within, pltpu.roll(chunk, turn, 1), tile)
            pieces.append(tile)
        payload = (jnp.concatenate(pieces, axis=0) + meta).astype(BF16)
        if flip == 1:
            send_ref[first:, :] = payload
        else:
            outs[flip - (flip > 1)][...] = payload

    copies[3].wait()
    regroup_rows(wave_ref, grouped, part)
    half = padded // 2
    samples_ref[...] = grouped[pl.ds(pl.multiple_of(my_core * half, half), half), :]
    theirs = pl.ds(pl.multiple_of((1 - my_core) * half, half), half)
    for tile in range(first // half):
        columns = slice(tile * LANES, (tile + 1) * LANES)
        send_ref[tile * half : (tile + 1) * half, :] = grouped[theirs, columns]


def pack_kernel(mine_ref, core_ref, y_ref, both_ref, out_ref):
    inner = lax.axis_index("inner")
    rows = mine_ref.shape[0]
    out_ref[inner] = mine_ref[...]
    out_ref[inner ^ 1] = core_ref[core_ref.shape[0] - rows :, :]
    out_ref[inner ^ 2] = y_ref[...]
    out_ref[inner ^ 3] = both_ref[...]


def split_kernel(tm_count, keep_ref, got_ref, *outs):
    my_inner = lax.axis_index("inner")
    core = lax.rem(my_inner, 2)
    me = lax.div(my_inner, 2) * tm_count + lax.axis_index("tm")
    part = outs[0].shape[1]
    half, slab = keep_ref.shape
    for flip, out_ref in enumerate(outs):
        start = (me ^ flip) * part
        out_ref[core] = keep_ref[pl.ds(pl.multiple_of(start, part), part), :]
        for tile in range(slab // LANES):
            rows = pl.ds(pl.multiple_of(tile * half + start, part), part)
            out_ref[1 - core, :, tile * LANES : (tile + 1) * LANES] = got_ref[rows, :]


def join_kernel(tm_count, *refs):
    parts, out_ref, head_ref = refs[:-2], refs[-2], refs[-1]
    me = lax.div(lax.axis_index("inner"), 2) * tm_count + lax.axis_index("tm")
    slab = parts[0].shape[2]
    for flip, part in enumerate(parts):
        other = me ^ flip
        y, tm = lax.div(other, tm_count), lax.rem(other, tm_count)
        for core in range(2):
            place = (y * 2 + core) * tm_count + tm
            out_ref[:, pl.ds(pl.multiple_of(place * slab, slab), slab)] = part[core]
    head_ref[...] = out_ref[:, : head_ref.shape[1]]


def arrange(tpls, left):
    for flip, pack in enumerate(tpls):
        for inner in range(INNER):
            row = (flip * INNER + inner) * FINE
            for step in range(left.shape[1] // LANES):
                left[row : row + FINE, step * LANES : (step + 1) * LANES] = pack[
                    inner, FINE * step : FINE * (step + 1), :
                ]


def correlate(left, full, slab, run, side, ys, store, shifts, products):
    part = full.shape[0]
    size, depth = left.shape
    count = size // FINE
    copies = LANES // FINE
    width = run * slab
    for slot, y in enumerate(ys):
        columns = width + 2 * LANES
        start = pl.multiple_of((2 * y + side) * width, width)
        samples = full[:, pl.ds(start, columns)]
        for copy in range(depth // part):
            tile, turn = copy // copies * LANES, copy % copies * FINE
            turned = samples if turn == 0 else pltpu.roll(samples, columns - turn, 1)
            shifts[slot, copy * part : (copy + 1) * part, :] = turned[:, tile : tile + width + LANES]
    tiles = products.shape[1]
    span = (tiles - 1) * LANES
    per_block = span // slab
    blocks = [(y, index) for y in range(len(ys)) for index in range(width // span)]

    def multiply(place, slot):
        y, index = place
        for tile in range(0, tiles, 2):
            start = index * span + tile * LANES
            pieces = min(2, tiles - tile)
            product = jnp.dot(
                left[...],
                shifts[y, :, start : start + pieces * LANES],
                preferred_element_type=F32,
            )
            for piece in range(pieces):
                products[slot, tile + piece] = product[:, piece * LANES : (piece + 1) * LANES]

    def gather(place, slot):
        def tree(first, number):
            if number == 1:
                rows = pl.ds(first, count, stride=FINE)
                return jnp.concatenate(
                    [products[slot, tile, rows, :] for tile in range(tiles)], axis=1
                )
            half = number // 2
            later = pltpu.roll(tree(first + half, half), span + LANES - half, 1)
            return tree(first, half) + later

        total = tree(0, FINE)
        _, index = place
        for piece in range(per_block):
            store(index * per_block + piece, total[:, piece * slab : (piece + 1) * slab])

    multiply(blocks[0], 0)
    for number in range(1, len(blocks)):
        multiply(blocks[number], number % 2)
        gather(blocks[number - 1], (number - 1) % 2)
    gather(blocks[-1], (len(blocks) - 1) % 2)


def first_dots_kernel(outer_count, stations, channels, tm_count, *refs):
    tpls, (order_ref, samples_ref) = refs[:-9], refs[-9:-7]
    begun_ref, left, scale_ref, mask_ref, part_ref, shifts, products = refs[-7:]
    tpls = [pack[...] for pack in tpls]
    if len(tpls) > outer_count:
        tpls = tpls[:-2] + [tpls[-2] + tpls[-1]]
    arrange(tpls, left)
    core = lax.rem(lax.axis_index("inner"), 2)
    run, _, slab = begun_ref.shape

    def store(place, sums):
        begun_ref[place] = sums

    correlate(left, samples_ref, slab, run, 1 - core, [0], store, shifts, products)
    read_masks(stations, channels, tm_count, tpls, order_ref, scale_ref, mask_ref, part_ref)


def middle_dots_kernel(left, samples_ref, halo_ref, begun_ref, mask_ref, *refs):
    send_ref, edges_ref, full, edges, shifts, products = refs
    group, _, window = edges.shape
    chunk = samples_ref.shape[1]
    slab = chunk // group
    run = group // 4
    core = lax.rem(lax.axis_index("inner"), 2)
    full[:, :chunk] = samples_ref[...]
    full[:, chunk:] = halo_ref[...]

    def store(place, sums):
        send_ref[run + place, :, :slab] = sums

    correlate(left, full, slab, run, 1 - core, [1], store, shifts, products)
    after = [full[:, (m + 1) * slab : (m + 1) * slab + window] for m in range(group)]
    squares = masked_squares(mask_ref[...], jnp.concatenate(after, axis=1))
    column = lax.broadcasted_iota(jnp.int32, squares.shape, 1) & (window - 1)
    reach = 1
    while reach < window:
        earlier = pltpu.roll(squares, reach, 1)
        squares = squares + jnp.where(column >= reach, earlier, 0.0)
        reach *= 2
    squares = jnp.where(column >= 1, pltpu.roll(squares, 1, 1), 0.0)
    for member in range(group):
        edges[member] = squares[:, member * window : (member + 1) * window]
    for tm in range(run):
        send_ref[tm, :, :slab] = begun_ref[tm]
        for y in range(2):
            send_ref[y * run + tm, :, slab:] = edges[(2 * y + 1 - core) * run + tm]
            edges_ref[y * run + tm] = edges[(2 * y + core) * run + tm]


def own_dots_kernel(far, left, samples_ref, halo_ref, edges_ref, after, keep_ref, *scratch):
    del after
    full, shifts, products = scratch
    chunk = samples_ref.shape[1]
    full[:, :chunk] = samples_ref[...]
    full[:, chunk:] = halo_ref[...]
    core = lax.rem(lax.axis_index("inner"), 2)
    y = lax.div(lax.axis_index("inner"), 2) ^ far
    run = keep_ref.shape[0]
    slab = keep_ref.shape[2] - edges_ref.shape[2]

    def store(place, sums):
        keep_ref[place, :, :slab] = sums

    correlate(left, full, slab, run, core, [y], store, shifts, products)
    for tm in range(run):
        keep_ref[tm, :, slab:] = edges_ref[y * run + tm]


def add_kernel(far, keep_ref, got_ref, *outs):
    y = lax.div(lax.axis_index("inner"), 2) ^ far
    my_tm = lax.axis_index("tm")
    run = keep_ref.shape[0]
    for flip, out_ref in enumerate(outs):
        tm = my_tm ^ flip
        out_ref[...] = keep_ref[tm] + got_ref[y * run + tm]


def masked_squares(mask, wave):
    wave = wave.astype(F32)
    squares = wave * wave
    high = squares.astype(BF16)
    low = (squares - high.astype(F32)).astype(BF16)
    return jnp.dot(mask, high, preferred_element_type=F32) + jnp.dot(
        mask, low, preferred_element_type=F32
    )


def read_masks(stations, channels, tm_count, tpls, order_ref, scale_ref, mask_ref, part_ref):
    rows = tpls[0].shape[1]
    count = len(tpls) * INNER
    padded = INNER * LANES
    part = LANES // tm_count
    meta = lax.dot_general(
        spare_lanes(part, part * channels // padded),
        jnp.concatenate([pack.reshape(INNER * rows, LANES) for pack in tpls], axis=0),
        (((1,), (1,)), ((), ())),
        preferred_element_type=F32,
    )
    slots = -(-stations // rows)

    def read(slot):
        return jnp.concatenate(
            [meta[slot : slot + 1, t * rows : (t + 1) * rows] for t in range(count)], axis=0
        )

    values = jnp.concatenate([read(slot) for slot in range(slots + 1)], axis=1)
    start = slots * rows
    scale = jnp.sum(values[:, start : start + 3], axis=1, keepdims=True)
    scale_ref[...] = jnp.broadcast_to(scale, scale_ref.shape)
    mask = jnp.dot(
        values[:, :stations].astype(BF16),
        one_hot(order_ref[...], stations),
        preferred_element_type=F32,
    ).astype(BF16)
    mask_ref[...] = mask
    grouped = jnp.dot(mask, regroup(channels, padded, part), preferred_element_type=F32)
    mine = side_major(lax.axis_index("inner")) * LANES + lax.axis_index("tm") * part
    part_ref[...] = pltpu.roll(grouped, lax.rem(padded - mine, padded), 1)[:, :part].astype(BF16)


def power_kernel(window, wave_ref, mask_ref, after, out_ref):
    del after
    power = masked_squares(mask_ref[...], wave_ref[...])
    columns = power.shape[1]
    column = lax.broadcasted_iota(jnp.int32, power.shape, 1)
    reach = 1
    while reach < window:
        later = pltpu.roll(power, columns - reach, 1)
        power = power + jnp.where(column < columns - reach, later, 0.0)
        reach *= 2
    out_ref[...] = power


def finish_kernel(*refs):
    parts, (power_ref, scale_ref, out_ref) = refs[:-3], refs[-3:]
    slab = power_ref.shape[1]
    total = parts[0][...]
    for part in parts[1:]:
        total = total + part[...]
    dots, edge = total[:, :slab], total[:, slab:]
    inside = slab - edge.shape[1]
    energy = jnp.concatenate(
        [power_ref[:, :inside], power_ref[:, inside:] + edge], axis=1
    )
    rows = dots * (scale_ref[:, :1] / jnp.sqrt(energy + EPSILON))
    outer = lax.axis_index("outer")
    step = INNER
    while step < rows.shape[0]:
        pairs = [rows[start : start + step] for start in range(0, rows.shape[0], step)]
        swapped = [pairs[index ^ 1] for index in range(len(pairs))]
        flipped = (outer & (step // INNER)) != 0
        rows = jnp.where(flipped, jnp.concatenate(swapped, axis=0), rows)
        step *= 2
    out_ref[...] = rows


def on_device(waveforms, templates, station_mask, channel_order):
    channels, slab = waveforms.shape
    rows, _, window = templates.shape
    stations = station_mask.shape[1]
    outer_count, tm_count = lax.axis_size("outer"), lax.axis_size("tm")
    blk_count = outer_count * INNER
    assert rows == 1 and LANES % tm_count == 0
    group = INNER * tm_count
    padded = INNER * LANES
    part = padded // group
    chunk = group * slab
    span = 2 * slab
    total = blk_count * tm_count
    blk, every = ("outer", "inner"), ("outer", "inner", "tm")
    sds = jax.ShapeDtypeStruct
    order_row = channel_order[None, :]

    rows = window * part // LANES
    held = [
        pltpu.with_memory_space_constraint(x, pltpu.HBM)
        for x in (waveforms, templates, station_mask, order_row)
    ]
    send, keep, *pieces = call(
        functools.partial(prologue_kernel, tm_count),
        [HBM] * 4,
        [
            sds((padded // 2 * slab // LANES + rows, LANES), BF16),
            sds((padded // 2, slab), BF16),
            *[sds((rows, LANES), BF16)] * (INNER - 1),
        ],
        [
            pltpu.VMEM((channels, slab), BF16),
            pltpu.VMEM((padded, slab), BF16),
            pltpu.VMEM((channels, window), BF16),
            pltpu.VMEM((padded, window), BF16),
            pltpu.VMEM((1, stations), jnp.int32),
            pltpu.VMEM((1, channels), jnp.int32),
            pltpu.VMEM((window, padded), F32),
            pltpu.SemaphoreType.DMA((4,)),
        ],
        bytes_accessed=channels * (window + slab) * 2,
    )(*held)

    def plane(part, flip):
        return lax.ppermute(part, "inner", [(b, b ^ flip) for b in range(INNER)])

    got = plane(send, 1)
    others = [plane(pieces[1], 2), plane(pieces[2], 3)]
    pack = call(
        pack_kernel, [VMEM] * INNER, sds((INNER, rows, LANES), BF16), bytes_accessed=rows * LANES * 8
    )(pieces[0], got, *others)

    def cross(part, route):
        return lax.ppermute(part, "outer", route)

    if outer_count == 4:
        near = cross(pack, [(0, 1), (1, 0), (2, 3), (3, 2)])
        far = cross(pack, [(0, 2), (2, 0), (1, 3), (3, 1)])
        middle = cross(pack, [(1, 2), (2, 1)])
        ends = cross(far, [(1, 0), (2, 3)])
        tpls = [pack, near, far, middle, ends]
    else:
        tpls = [pack] + [
            cross(pack, [(b, b ^ flip) for b in range(outer_count)])
            for flip in range(1, outer_count)
        ]

    half = group // 2

    def swap(part, flip):
        y, tm = flip // tm_count, flip % tm_count
        route = [(i, i ^ (2 * tm_count * y + tm)) for i in range(total)]
        return lax.ppermute(part, every, route)

    parts = call(
        functools.partial(split_kernel, tm_count),
        [VMEM] * 2,
        [sds((2, part, slab), BF16)] * half,
        bytes_accessed=padded * slab * 2,
    )(keep, got)
    waves = [parts[0]] + [swap(parts[flip], flip) for flip in range(1, half)]
    samples, head = call(
        functools.partial(join_kernel, tm_count),
        [VMEM] * half,
        [sds((part, chunk), BF16), sds((part, window), BF16)],
        bytes_accessed=part * chunk * 4,
    )(*waves)
    halo = lax.ppermute(head, "outer", [(b, b - 1) for b in range(1, outer_count)])

    depth = window // FINE * part
    count = blk_count
    work = 2 * count * window * part * chunk // 2

    def scratch():
        return [
            pltpu.VMEM((2, depth, chunk // 4 + LANES), BF16),
            pltpu.VMEM((2, span // LANES + 1, count * FINE, LANES), F32),
        ]

    begun, left, scale, mask, mask_part = call(
        functools.partial(first_dots_kernel, outer_count, stations, channels, tm_count),
        [VMEM] * (len(tpls) + 2),
        [
            sds((tm_count, count, slab), F32),
            sds((count * FINE, depth), BF16),
            sds((count, LANES), F32),
            sds((count, channels), BF16),
            sds((count, part), BF16),
        ],
        scratch(),
        flops=work // 2,
        bytes_accessed=part * chunk * 2,
        vmem=36,
    )(*tpls, order_row, samples)
    full = pltpu.VMEM((part, chunk + window), BF16)
    send, edges = call(
        middle_dots_kernel,
        [VMEM] * 5,
        [sds((half, count, slab + window), F32), sds((half, count, window), F32)],
        [full, pltpu.VMEM((group, count, window), F32)] + scratch(),
        flops=work // 2,
        bytes_accessed=part * chunk * 2,
        vmem=36,
    )(left, samples, halo, begun, mask_part)
    got = lax.ppermute(send, "inner", [(b, b ^ 1) for b in range(INNER)])

    def own(far, after):
        keep = call(
            functools.partial(own_dots_kernel, far),
            [VMEM] * 4 + [AFTER],
            sds((tm_count, count, slab + window), F32),
            [full] + scratch(),
            flops=work // 2,
            bytes_accessed=part * chunk * 2,
            vmem=36,
        )(left, samples, halo, edges, after)
        return call(
            functools.partial(add_kernel, far),
            [VMEM] * 2,
            [sds((count, slab + window), F32)] * tm_count,
            bytes_accessed=count * slab * 12 * tm_count,
        )(keep, got)

    theirs = own(1, send)
    ours = own(0, theirs[0])
    power = call(
        functools.partial(power_kernel, window),
        [VMEM, VMEM, AFTER],
        sds((blk_count, slab), F32),
        flops=4 * blk_count * channels * slab,
        bytes_accessed=channels * slab * 2,
    )(waveforms, mask, ours[0])
    far = [swap(theirs[tm], tm_count + tm) for tm in reversed(range(tm_count))]
    sums = [functools.reduce(jnp.add, far)]
    sums += [swap(ours[tm], tm) for tm in range(1, tm_count)] + [ours[0]]
    return call(
        finish_kernel,
        [VMEM] * (len(sums) + 2),
        sds((blk_count, slab), F32),
        bytes_accessed=blk_count * slab * 4 * (half + 2),
    )(*sums, power, scale)


def solution(mesh):
    blk_count, tm_count = mesh.devices.shape
    shape = (blk_count // INNER, INNER, tm_count)
    mesh = jax.sharding.Mesh(mesh.devices.reshape(shape), ("outer", "inner", "tm"))
    blk, every = ("outer", "inner"), ("outer", "inner", "tm")
    placed = (P(None, every), P(blk, None, None), P(blk, None), P())
    return jax.shard_map(
        on_device, mesh=mesh, in_specs=placed, out_specs=P(None, every), check_vma=False
    )
```

```python
import functools

import jax
import jax.numpy as jnp
from jax import lax
from jax.experimental import pallas as pl
from jax.experimental.pallas import tpu as pltpu
from jax.sharding import PartitionSpec as P

EPSILON = 1e-05
LANES = 128
INNER = 4
ROWS = 16
FINE = 32
MIB = 1024 * 1024

BF16 = jnp.bfloat16
F32 = jnp.float32


HBM = pl.BlockSpec(memory_space=pltpu.HBM)
VMEM = pl.BlockSpec(memory_space=pltpu.VMEM)
AFTER = pl.BlockSpec(memory_space=pl.ANY)


def call(kernel, in_specs, out_shape, scratch=(), flops=0, bytes_accessed=0, vmem=24):
    return pl.pallas_call(
        kernel,
        in_specs=in_specs,
        out_specs=jax.tree.map(lambda _: VMEM, out_shape),
        out_shape=out_shape,
        scratch_shapes=list(scratch),
        compiler_params=pltpu.CompilerParams(vmem_limit_bytes=vmem * MIB),
        cost_estimate=pl.CostEstimate(
            flops=flops, bytes_accessed=bytes_accessed, transcendentals=0
        ),
    )


def one_hot(order_row, station_count):
    columns = order_row.shape[1]
    first = 3 * lax.broadcasted_iota(jnp.int32, (station_count, columns), 0)
    hit = (order_row >= first) & (order_row < first + 3)
    return jnp.where(hit, 1.0, 0.0).astype(BF16)


def side_major(inner):
    return lax.rem(inner, 2) * (INNER // 2) + lax.div(inner, 2)


def place_of(real, part):
    base = real // ROWS * ROWS
    return base, real - base


def regroup_rows(source, target, part):
    channels, width = source.shape
    groups = target.shape[0] // part
    real = channels // groups
    base, extra = place_of(real, part)
    rest = source[groups * base :, :].astype(F32)
    fill = jnp.zeros((part - real, width), F32)
    for group in range(groups):
        if base:
            run = source[group * base : (group + 1) * base, :]
            target[group * part : group * part + base, :] = run
        piece = [rest[group * extra : (group + 1) * extra], fill]
        target[group * part + base : (group + 1) * part, :] = jnp.concatenate(
            piece, axis=0
        ).astype(BF16)


def regroup(channels, padded, part):
    groups = padded // part
    real = channels // groups
    base, extra = place_of(real, part)
    channel = lax.broadcasted_iota(jnp.int32, (channels, padded), 0)
    place = lax.broadcasted_iota(jnp.int32, (1, padded), 1)
    group, within = place >> (part.bit_length() - 1), place & (part - 1)
    rest = groups * base + extra * group + within - base
    source = jnp.where(within < base, base * group + within, rest)
    source = jnp.where(within < real, source, -1)
    return jnp.where(channel == source, 1.0, 0.0).astype(BF16)


def spare_lanes(part, real):
    slots = LANES // part * (part - real)
    slot = lax.broadcasted_iota(jnp.int32, (8, LANES), 0)
    lane = lax.broadcasted_iota(jnp.int32, (8, LANES), 1)
    spare = part - real
    home = lax.div(slot, spare) * part + real + lax.rem(slot, spare)
    return jnp.where((lane == home) & (slot < slots), 1.0, 0.0).astype(BF16)


def prologue_kernel(tm_count, wave_hbm, tpl_hbm, flag_hbm, order_hbm, *refs):
    send_ref, samples_ref, *outs = refs[: INNER + 1]
    wave_ref, grouped, tpl_ref, tpl_grouped, flag_ref, order_ref, turned, sems = refs[INNER + 1 :]
    channels, window = tpl_hbm.shape[1:]
    copies = [
        pltpu.make_async_copy(flag_hbm, flag_ref, sems.at[0]),
        pltpu.make_async_copy(order_hbm, order_ref, sems.at[1]),
        pltpu.make_async_copy(tpl_hbm.at[0], tpl_ref, sems.at[2]),
        pltpu.make_async_copy(wave_hbm, wave_ref, sems.at[3]),
    ]
    for copy in copies:
        copy.start()
    stations = flag_ref.shape[1]
    padded = turned.shape[1]
    part = LANES // tm_count
    rows = outs[0].shape[0]
    groups = regroup(channels, padded, part)
    copies[0].wait()
    copies[1].wait()
    flags = jnp.broadcast_to(flag_ref[...].astype(F32), (8, stations))
    mask = jnp.dot(
        flags.astype(BF16), one_hot(order_ref[...], stations), preferred_element_type=F32
    )
    live = jnp.sum(mask[:1], keepdims=True)
    mask = jnp.dot(mask.astype(BF16), groups, preferred_element_type=F32)[:1]
    copies[2].wait()
    regroup_rows(tpl_ref, tpl_grouped, part)
    masked = tpl_grouped[...].T.astype(F32) * mask
    turned[...] = masked
    norm = jnp.sqrt(jnp.sum(masked * masked, keepdims=True) + EPSILON)
    rest = jnp.broadcast_to(jnp.sqrt(window * live) / norm, (1, rows))
    row = lax.broadcasted_iota(jnp.int32, (1, rows), 1)
    scale = jnp.zeros((1, rows), F32)
    for piece in range(3):
        now = rest.astype(BF16).astype(F32)
        scale = jnp.where(row == piece, now, scale)
        rest = rest - now
    slots = -(-stations // rows)
    wide = flags[:1]
    if stations % rows:
        wide = jnp.concatenate([wide, jnp.zeros((1, rows - stations % rows), F32)], axis=1)
    meta = [wide[:, slot * rows : (slot + 1) * rows] for slot in range(slots)] + [scale]
    meta = jnp.concatenate(meta + [jnp.zeros((8 - len(meta), rows), F32)], axis=0)
    meta = lax.dot_general(
        meta.astype(BF16),
        spare_lanes(part, part * channels // padded),
        (((0,), (0,)), ((), ())),
        preferred_element_type=F32,
    )
    my_tm = lax.axis_index("tm")
    my_inner = lax.axis_index("inner")
    my_core = lax.rem(my_inner, 2)
    first = send_ref.shape[0] - rows
    spot = lax.broadcasted_iota(jnp.int32, (FINE, LANES), 1) >> (part.bit_length() - 1)
    for flip in range(INNER):
        start = pl.multiple_of(side_major(my_inner ^ flip) * LANES, LANES)
        pieces = []
        for step in range(window // (FINE * tm_count)):
            tile = jnp.zeros((FINE, LANES), F32)
            for within in range(tm_count):
                row = FINE * (step * tm_count + within)
                chunk = turned[row : row + FINE, pl.ds(start, LANES)]
                turn = lax.rem(part * (within - my_tm) + LANES, LANES)
                tile = jnp.where(spot == within, pltpu.roll(chunk, turn, 1), tile)
            pieces.append(tile)
        payload = (jnp.concatenate(pieces, axis=0) + meta).astype(BF16)
        if flip == 1:
            send_ref[first:, :] = payload
        else:
            outs[flip - (flip > 1)][...] = payload

    copies[3].wait()
    regroup_rows(wave_ref, grouped, part)
    half = padded // 2
    samples_ref[...] = grouped[pl.ds(pl.multiple_of(my_core * half, half), half), :]
    theirs = pl.ds(pl.multiple_of((1 - my_core) * half, half), half)
    for tile in range(first // half):
        columns = slice(tile * LANES, (tile + 1) * LANES)
        send_ref[tile * half : (tile + 1) * half, :] = grouped[theirs, columns]


def pack_kernel(mine_ref, core_ref, y_ref, both_ref, out_ref):
    inner = lax.axis_index("inner")
    rows = mine_ref.shape[0]
    out_ref[inner] = mine_ref[...]
    out_ref[inner ^ 1] = core_ref[core_ref.shape[0] - rows :, :]
    out_ref[inner ^ 2] = y_ref[...]
    out_ref[inner ^ 3] = both_ref[...]


def split_kernel(tm_count, keep_ref, got_ref, *outs):
    my_inner = lax.axis_index("inner")
    core = lax.rem(my_inner, 2)
    me = lax.div(my_inner, 2) * tm_count + lax.axis_index("tm")
    part = outs[0].shape[1]
    half, slab = keep_ref.shape
    for flip, out_ref in enumerate(outs):
        start = (me ^ flip) * part
        out_ref[core] = keep_ref[pl.ds(pl.multiple_of(start, part), part), :]
        for tile in range(slab // LANES):
            rows = pl.ds(pl.multiple_of(tile * half + start, part), part)
            out_ref[1 - core, :, tile * LANES : (tile + 1) * LANES] = got_ref[rows, :]


def join_kernel(tm_count, *refs):
    parts, out_ref, head_ref = refs[:-2], refs[-2], refs[-1]
    me = lax.div(lax.axis_index("inner"), 2) * tm_count + lax.axis_index("tm")
    slab = parts[0].shape[2]
    for flip, part in enumerate(parts):
        other = me ^ flip
        y, tm = lax.div(other, tm_count), lax.rem(other, tm_count)
        for core in range(2):
            place = (y * 2 + core) * tm_count + tm
            out_ref[:, pl.ds(pl.multiple_of(place * slab, slab), slab)] = part[core]
    head_ref[...] = out_ref[:, : head_ref.shape[1]]


def arrange(tpls, left):
    for flip, pack in enumerate(tpls):
        for inner in range(INNER):
            row = (flip * INNER + inner) * FINE
            for step in range(left.shape[1] // LANES):
                left[row : row + FINE, step * LANES : (step + 1) * LANES] = pack[
                    inner, FINE * step : FINE * (step + 1), :
                ]


def correlate(left, full, slab, run, side, ys, store, shifts, products):
    part = full.shape[0]
    size, depth = left.shape
    count = size // FINE
    copies = LANES // FINE
    width = run * slab
    for y in ys:
        columns = width + 2 * LANES
        start = pl.multiple_of((2 * y + side) * width, width)
        samples = full[:, pl.ds(start, columns)]
        for copy in range(depth // part):
            tile, turn = copy // copies * LANES, copy % copies * FINE
            turned = samples if turn == 0 else pltpu.roll(samples, columns - turn, 1)
            shifts[y, copy * part : (copy + 1) * part, :] = turned[:, tile : tile + width + LANES]
    tiles = products.shape[1]
    span = (tiles - 1) * LANES
    per_block = span // slab
    blocks = [(y, index) for y in ys for index in range(width // span)]

    def multiply(place, slot):
        y, index = place
        for tile in range(0, tiles, 2):
            start = index * span + tile * LANES
            pieces = min(2, tiles - tile)
            product = jnp.dot(
                left[...],
                shifts[y, :, start : start + pieces * LANES],
                preferred_element_type=F32,
            )
            for piece in range(pieces):
                products[slot, tile + piece] = product[:, piece * LANES : (piece + 1) * LANES]

    def gather(place, slot):
        def tree(first, number):
            if number == 1:
                rows = pl.ds(first, count, stride=FINE)
                return jnp.concatenate(
                    [products[slot, tile, rows, :] for tile in range(tiles)], axis=1
                )
            half = number // 2
            later = pltpu.roll(tree(first + half, half), span + LANES - half, 1)
            return tree(first, half) + later

        total = tree(0, FINE)
        y, index = place
        for piece in range(per_block):
            store(y, index * per_block + piece, total[:, piece * slab : (piece + 1) * slab])

    multiply(blocks[0], 0)
    for number in range(1, len(blocks)):
        multiply(blocks[number], number % 2)
        gather(blocks[number - 1], (number - 1) % 2)
    gather(blocks[-1], (len(blocks) - 1) % 2)


def first_dots_kernel(outer_count, stations, channels, tm_count, *refs):
    tpls, (order_ref, samples_ref) = refs[:-9], refs[-9:-7]
    begun_ref, left, scale_ref, mask_ref, part_ref, shifts, products = refs[-7:]
    tpls = [pack[...] for pack in tpls]
    if len(tpls) > outer_count:
        tpls = tpls[:-2] + [tpls[-2] + tpls[-1]]
    arrange(tpls, left)
    core = lax.rem(lax.axis_index("inner"), 2)
    run, _, slab = begun_ref.shape

    def store(y, place, sums):
        begun_ref[place] = sums

    correlate(left, samples_ref, slab, run, 1 - core, [0], store, shifts, products)
    read_masks(stations, channels, tm_count, tpls, order_ref, scale_ref, mask_ref, part_ref)


def middle_dots_kernel(left, samples_ref, halo_ref, begun_ref, mask_ref, *refs):
    send_ref, edges_ref, full, edges, shifts, products = refs
    group, _, window = edges.shape
    chunk = samples_ref.shape[1]
    slab = chunk // group
    run = group // 4
    core = lax.rem(lax.axis_index("inner"), 2)
    full[:, :chunk] = samples_ref[...]
    full[:, chunk:] = halo_ref[...]

    def store(y, place, sums):
        send_ref[y * run + place, :, :slab] = sums

    correlate(left, full, slab, run, 1 - core, [1], store, shifts, products)
    after = [full[:, (m + 1) * slab : (m + 1) * slab + window] for m in range(group)]
    squares = masked_squares(mask_ref[...], jnp.concatenate(after, axis=1))
    column = lax.broadcasted_iota(jnp.int32, squares.shape, 1) & (window - 1)
    reach = 1
    while reach < window:
        earlier = pltpu.roll(squares, reach, 1)
        squares = squares + jnp.where(column >= reach, earlier, 0.0)
        reach *= 2
    squares = jnp.where(column >= 1, pltpu.roll(squares, 1, 1), 0.0)
    for member in range(group):
        edges[member] = squares[:, member * window : (member + 1) * window]
    for tm in range(run):
        send_ref[tm, :, :slab] = begun_ref[tm]
        for y in range(2):
            send_ref[y * run + tm, :, slab:] = edges[(2 * y + 1 - core) * run + tm]
            edges_ref[y * run + tm] = edges[(2 * y + core) * run + tm]


def last_dots_kernel(left, samples_ref, halo_ref, edges_ref, after, keep_ref, *scratch):
    del after
    full, shifts, products = scratch
    chunk = samples_ref.shape[1]
    full[:, :chunk] = samples_ref[...]
    full[:, chunk:] = halo_ref[...]
    core = lax.rem(lax.axis_index("inner"), 2)
    run = keep_ref.shape[0] // 2
    slab = keep_ref.shape[2] - edges_ref.shape[2]

    def store(y, place, sums):
        keep_ref[y * run + place, :, :slab] = sums

    correlate(left, full, slab, run, core, [0, 1], store, shifts, products)
    keep_ref[:, :, slab:] = edges_ref[...]


def add_kernel(tm_count, keep_ref, got_ref, *outs):
    me = lax.div(lax.axis_index("inner"), 2) * tm_count + lax.axis_index("tm")
    for flip, out_ref in enumerate(outs):
        out_ref[...] = keep_ref[me ^ flip] + got_ref[me ^ flip]


def masked_squares(mask, wave):
    wave = wave.astype(F32)
    squares = wave * wave
    high = squares.astype(BF16)
    low = (squares - high.astype(F32)).astype(BF16)
    return jnp.dot(mask, high, preferred_element_type=F32) + jnp.dot(
        mask, low, preferred_element_type=F32
    )


def read_masks(stations, channels, tm_count, tpls, order_ref, scale_ref, mask_ref, part_ref):
    rows = tpls[0].shape[1]
    count = len(tpls) * INNER
    padded = INNER * LANES
    part = LANES // tm_count
    meta = lax.dot_general(
        spare_lanes(part, part * channels // padded),
        jnp.concatenate([pack.reshape(INNER * rows, LANES) for pack in tpls], axis=0),
        (((1,), (1,)), ((), ())),
        preferred_element_type=F32,
    )
    slots = -(-stations // rows)

    def read(slot):
        return jnp.concatenate(
            [meta[slot : slot + 1, t * rows : (t + 1) * rows] for t in range(count)], axis=0
        )

    values = jnp.concatenate([read(slot) for slot in range(slots + 1)], axis=1)
    start = slots * rows
    scale = jnp.sum(values[:, start : start + 3], axis=1, keepdims=True)
    scale_ref[...] = jnp.broadcast_to(scale, scale_ref.shape)
    mask = jnp.dot(
        values[:, :stations].astype(BF16),
        one_hot(order_ref[...], stations),
        preferred_element_type=F32,
    ).astype(BF16)
    mask_ref[...] = mask
    grouped = jnp.dot(mask, regroup(channels, padded, part), preferred_element_type=F32)
    mine = side_major(lax.axis_index("inner")) * LANES + lax.axis_index("tm") * part
    part_ref[...] = pltpu.roll(grouped, lax.rem(padded - mine, padded), 1)[:, :part].astype(BF16)


def power_kernel(window, wave_ref, mask_ref, after, out_ref):
    del after
    power = masked_squares(mask_ref[...], wave_ref[...])
    columns = power.shape[1]
    column = lax.broadcasted_iota(jnp.int32, power.shape, 1)
    reach = 1
    while reach < window:
        later = pltpu.roll(power, columns - reach, 1)
        power = power + jnp.where(column < columns - reach, later, 0.0)
        reach *= 2
    out_ref[...] = power


def finish_kernel(*refs):
    parts, (power_ref, scale_ref, out_ref) = refs[:-3], refs[-3:]
    slab = power_ref.shape[1]
    total = parts[0][...]
    for part in parts[1:]:
        total = total + part[...]
    dots, edge = total[:, :slab], total[:, slab:]
    inside = slab - edge.shape[1]
    energy = jnp.concatenate(
        [power_ref[:, :inside], power_ref[:, inside:] + edge], axis=1
    )
    rows = dots * (scale_ref[:, :1] / jnp.sqrt(energy + EPSILON))
    outer = lax.axis_index("outer")
    step = INNER
    while step < rows.shape[0]:
        pairs = [rows[start : start + step] for start in range(0, rows.shape[0], step)]
        swapped = [pairs[index ^ 1] for index in range(len(pairs))]
        flipped = (outer & (step // INNER)) != 0
        rows = jnp.where(flipped, jnp.concatenate(swapped, axis=0), rows)
        step *= 2
    out_ref[...] = rows


def on_device(waveforms, templates, station_mask, channel_order):
    channels, slab = waveforms.shape
    rows, _, window = templates.shape
    stations = station_mask.shape[1]
    outer_count, tm_count = lax.axis_size("outer"), lax.axis_size("tm")
    blk_count = outer_count * INNER
    assert rows == 1 and LANES % tm_count == 0
    group = INNER * tm_count
    padded = INNER * LANES
    part = padded // group
    chunk = group * slab
    span = 2 * slab
    total = blk_count * tm_count
    blk, every = ("outer", "inner"), ("outer", "inner", "tm")
    sds = jax.ShapeDtypeStruct
    order_row = channel_order[None, :]

    rows = window * part // LANES
    held = [
        pltpu.with_memory_space_constraint(x, pltpu.HBM)
        for x in (waveforms, templates, station_mask, order_row)
    ]
    send, keep, *pieces = call(
        functools.partial(prologue_kernel, tm_count),
        [HBM] * 4,
        [
            sds((padded // 2 * slab // LANES + rows, LANES), BF16),
            sds((padded // 2, slab), BF16),
            *[sds((rows, LANES), BF16)] * (INNER - 1),
        ],
        [
            pltpu.VMEM((channels, slab), BF16),
            pltpu.VMEM((padded, slab), BF16),
            pltpu.VMEM((channels, window), BF16),
            pltpu.VMEM((padded, window), BF16),
            pltpu.VMEM((1, stations), jnp.int32),
            pltpu.VMEM((1, channels), jnp.int32),
            pltpu.VMEM((window, padded), F32),
            pltpu.SemaphoreType.DMA((4,)),
        ],
        bytes_accessed=channels * (window + slab) * 2,
    )(*held)

    def plane(part, flip):
        return lax.ppermute(part, "inner", [(b, b ^ flip) for b in range(INNER)])

    got = plane(send, 1)
    others = [plane(pieces[1], 2), plane(pieces[2], 3)]
    pack = call(
        pack_kernel, [VMEM] * INNER, sds((INNER, rows, LANES), BF16), bytes_accessed=rows * LANES * 8
    )(pieces[0], got, *others)

    def cross(part, route):
        return lax.ppermute(part, "outer", route)

    if outer_count == 4:
        near = cross(pack, [(0, 1), (1, 0), (2, 3), (3, 2)])
        far = cross(pack, [(0, 2), (2, 0), (1, 3), (3, 1)])
        middle = cross(pack, [(1, 2), (2, 1)])
        ends = cross(far, [(1, 0), (2, 3)])
        tpls = [pack, near, far, middle, ends]
    else:
        tpls = [pack] + [
            cross(pack, [(b, b ^ flip) for b in range(outer_count)])
            for flip in range(1, outer_count)
        ]

    half = group // 2

    def swap(part, flip):
        y, tm = flip // tm_count, flip % tm_count
        route = [(i, i ^ (2 * tm_count * y + tm)) for i in range(total)]
        return lax.ppermute(part, every, route)

    parts = call(
        functools.partial(split_kernel, tm_count),
        [VMEM] * 2,
        [sds((2, part, slab), BF16)] * half,
        bytes_accessed=padded * slab * 2,
    )(keep, got)
    waves = [parts[0]] + [swap(parts[flip], flip) for flip in range(1, half)]
    samples, head = call(
        functools.partial(join_kernel, tm_count),
        [VMEM] * half,
        [sds((part, chunk), BF16), sds((part, window), BF16)],
        bytes_accessed=part * chunk * 4,
    )(*waves)
    halo = lax.ppermute(head, "outer", [(b, b - 1) for b in range(1, outer_count)])

    depth = window // FINE * part
    count = blk_count
    work = 2 * count * window * part * chunk // 2

    def scratch():
        return [
            pltpu.VMEM((2, depth, chunk // 4 + LANES), BF16),
            pltpu.VMEM((2, span // LANES + 1, count * FINE, LANES), F32),
        ]

    begun, left, scale, mask, mask_part = call(
        functools.partial(first_dots_kernel, outer_count, stations, channels, tm_count),
        [VMEM] * (len(tpls) + 2),
        [
            sds((tm_count, count, slab), F32),
            sds((count * FINE, depth), BF16),
            sds((count, LANES), F32),
            sds((count, channels), BF16),
            sds((count, part), BF16),
        ],
        scratch(),
        flops=work // 2,
        bytes_accessed=part * chunk * 2,
        vmem=36,
    )(*tpls, order_row, samples)
    full = pltpu.VMEM((part, chunk + window), BF16)
    send, edges = call(
        middle_dots_kernel,
        [VMEM] * 5,
        [sds((half, count, slab + window), F32), sds((half, count, window), F32)],
        [full, pltpu.VMEM((group, count, window), F32)] + scratch(),
        flops=work // 2,
        bytes_accessed=part * chunk * 2,
        vmem=36,
    )(left, samples, halo, begun, mask_part)
    keep = call(
        last_dots_kernel,
        [VMEM] * 4 + [AFTER],
        sds((half, count, slab + window), F32),
        [full] + scratch(),
        flops=work,
        bytes_accessed=part * chunk * 2,
        vmem=36,
    )(left, samples, halo, edges, send)
    got = lax.ppermute(send, "inner", [(b, b ^ 1) for b in range(INNER)])
    power = call(
        functools.partial(power_kernel, window),
        [VMEM, VMEM, AFTER],
        sds((blk_count, slab), F32),
        flops=4 * blk_count * channels * slab,
        bytes_accessed=channels * slab * 2,
    )(waveforms, mask, keep)
    sums = call(
        functools.partial(add_kernel, tm_count),
        [VMEM] * 2,
        [sds((blk_count, slab + window), F32)] * half,
        bytes_accessed=blk_count * slab * 12 * half,
    )(keep, got)
    sums = [sums[0]] + [swap(sums[flip], flip) for flip in reversed(range(1, half))]
    return call(
        finish_kernel,
        [VMEM] * (half + 2),
        sds((blk_count, slab), F32),
        bytes_accessed=blk_count * slab * 4 * (half + 2),
    )(*sums, power, scale)


def solution(mesh):
    blk_count, tm_count = mesh.devices.shape
    shape = (blk_count // INNER, INNER, tm_count)
    mesh = jax.sharding.Mesh(mesh.devices.reshape(shape), ("outer", "inner", "tm"))
    blk, every = ("outer", "inner"), ("outer", "inner", "tm")
    placed = (P(None, every), P(blk, None, None), P(blk, None), P())
    return jax.shard_map(
        on_device, mesh=mesh, in_specs=placed, out_specs=P(None, every), check_vma=False
    )
```

```python
import functools

import jax
import jax.numpy as jnp
from jax import lax
from jax.experimental import pallas as pl
from jax.experimental.pallas import tpu as pltpu
from jax.sharding import PartitionSpec as P

EPSILON = 1e-05
LANES = 128
INNER = 4
FINE = 16
MIB = 1024 * 1024

BF16 = jnp.bfloat16
F32 = jnp.float32


HBM = pl.BlockSpec(memory_space=pltpu.HBM)
VMEM = pl.BlockSpec(memory_space=pltpu.VMEM)
AFTER = pl.BlockSpec(memory_space=pl.ANY)


def call(kernel, in_specs, out_shape, scratch=(), flops=0, bytes_accessed=0, vmem=24):
    return pl.pallas_call(
        kernel,
        in_specs=in_specs,
        out_specs=jax.tree.map(lambda _: VMEM, out_shape),
        out_shape=out_shape,
        scratch_shapes=list(scratch),
        compiler_params=pltpu.CompilerParams(vmem_limit_bytes=vmem * MIB),
        cost_estimate=pl.CostEstimate(
            flops=flops, bytes_accessed=bytes_accessed, transcendentals=0
        ),
    )


def one_hot(order_row, station_count):
    columns = order_row.shape[1]
    first = 3 * lax.broadcasted_iota(jnp.int32, (station_count, columns), 0)
    hit = (order_row >= first) & (order_row < first + 3)
    return jnp.where(hit, 1.0, 0.0).astype(BF16)


def side_major(inner):
    return lax.rem(inner, 2) * (INNER // 2) + lax.div(inner, 2)


def place_of(real, part):
    base = real // FINE * FINE
    return base, real - base


def regroup_rows(source, target, part):
    channels, width = source.shape
    groups = target.shape[0] // part
    real = channels // groups
    base, extra = place_of(real, part)
    rest = source[groups * base :, :].astype(F32)
    fill = jnp.zeros((part - real, width), F32)
    for group in range(groups):
        if base:
            run = source[group * base : (group + 1) * base, :]
            target[group * part : group * part + base, :] = run
        piece = [rest[group * extra : (group + 1) * extra], fill]
        target[group * part + base : (group + 1) * part, :] = jnp.concatenate(
            piece, axis=0
        ).astype(BF16)


def regroup(channels, padded, part):
    groups = padded // part
    real = channels // groups
    base, extra = place_of(real, part)
    channel = lax.broadcasted_iota(jnp.int32, (channels, padded), 0)
    place = lax.broadcasted_iota(jnp.int32, (1, padded), 1)
    group, within = place >> (part.bit_length() - 1), place & (part - 1)
    rest = groups * base + extra * group + within - base
    source = jnp.where(within < base, base * group + within, rest)
    source = jnp.where(within < real, source, -1)
    return jnp.where(channel == source, 1.0, 0.0).astype(BF16)


def spare_lanes(part, real):
    slots = LANES // part * (part - real)
    slot = lax.broadcasted_iota(jnp.int32, (8, LANES), 0)
    lane = lax.broadcasted_iota(jnp.int32, (8, LANES), 1)
    spare = part - real
    home = lax.div(slot, spare) * part + real + lax.rem(slot, spare)
    return jnp.where((lane == home) & (slot < slots), 1.0, 0.0).astype(BF16)


def prologue_kernel(tm_count, wave_hbm, tpl_hbm, flag_hbm, order_hbm, *refs):
    send_ref, samples_ref, *outs = refs[: INNER + 1]
    wave_ref, grouped, tpl_ref, tpl_grouped, flag_ref, order_ref, turned, sems = refs[INNER + 1 :]
    channels, window = tpl_hbm.shape[1:]
    copies = [
        pltpu.make_async_copy(flag_hbm, flag_ref, sems.at[0]),
        pltpu.make_async_copy(order_hbm, order_ref, sems.at[1]),
        pltpu.make_async_copy(tpl_hbm.at[0], tpl_ref, sems.at[2]),
        pltpu.make_async_copy(wave_hbm, wave_ref, sems.at[3]),
    ]
    for copy in copies:
        copy.start()
    stations = flag_ref.shape[1]
    padded = turned.shape[1]
    part = LANES // tm_count
    rows = outs[0].shape[0]
    groups = regroup(channels, padded, part)
    copies[0].wait()
    copies[1].wait()
    flags = jnp.broadcast_to(flag_ref[...].astype(F32), (8, stations))
    mask = jnp.dot(
        flags.astype(BF16), one_hot(order_ref[...], stations), preferred_element_type=F32
    )
    live = jnp.sum(mask[:1], keepdims=True)
    mask = jnp.dot(mask.astype(BF16), groups, preferred_element_type=F32)[:1]
    copies[2].wait()
    regroup_rows(tpl_ref, tpl_grouped, part)
    masked = tpl_grouped[...].T.astype(F32) * mask
    turned[...] = masked
    norm = jnp.sqrt(jnp.sum(masked * masked, keepdims=True) + EPSILON)
    rest = jnp.broadcast_to(jnp.sqrt(window * live) / norm, (1, rows))
    row = lax.broadcasted_iota(jnp.int32, (1, rows), 1)
    scale = jnp.zeros((1, rows), F32)
    for piece in range(3):
        now = rest.astype(BF16).astype(F32)
        scale = jnp.where(row == piece, now, scale)
        rest = rest - now
    slots = -(-stations // rows)
    wide = flags[:1]
    if stations % rows:
        wide = jnp.concatenate([wide, jnp.zeros((1, rows - stations % rows), F32)], axis=1)
    meta = [wide[:, slot * rows : (slot + 1) * rows] for slot in range(slots)] + [scale]
    meta = jnp.concatenate(meta + [jnp.zeros((8 - len(meta), rows), F32)], axis=0)
    meta = lax.dot_general(
        meta.astype(BF16),
        spare_lanes(part, part * channels // padded),
        (((0,), (0,)), ((), ())),
        preferred_element_type=F32,
    )
    my_tm = lax.axis_index("tm")
    my_inner = lax.axis_index("inner")
    my_core = lax.rem(my_inner, 2)
    first = send_ref.shape[0] - rows
    spot = lax.broadcasted_iota(jnp.int32, (FINE, LANES), 1) >> (part.bit_length() - 1)
    for flip in range(INNER):
        start = pl.multiple_of(side_major(my_inner ^ flip) * LANES, LANES)
        pieces = []
        for step in range(window // (FINE * tm_count)):
            tile = jnp.zeros((FINE, LANES), F32)
            for within in range(tm_count):
                row = FINE * (step * tm_count + within)
                chunk = turned[row : row + FINE, pl.ds(start, LANES)]
                turn = lax.rem(part * (within - my_tm) + LANES, LANES)
                tile = jnp.where(spot == within, pltpu.roll(chunk, turn, 1), tile)
            pieces.append(tile)
        payload = (jnp.concatenate(pieces, axis=0) + meta).astype(BF16)
        if flip == 1:
            send_ref[first:, :] = payload
        else:
            outs[flip - (flip > 1)][...] = payload

    copies[3].wait()
    regroup_rows(wave_ref, grouped, part)
    half = padded // 2
    samples_ref[...] = grouped[pl.ds(pl.multiple_of(my_core * half, half), half), :]
    theirs = pl.ds(pl.multiple_of((1 - my_core) * half, half), half)
    for tile in range(first // half):
        columns = slice(tile * LANES, (tile + 1) * LANES)
        send_ref[tile * half : (tile + 1) * half, :] = grouped[theirs, columns]


def pack_kernel(mine_ref, core_ref, y_ref, both_ref, out_ref):
    inner = lax.axis_index("inner")
    rows = mine_ref.shape[0]
    out_ref[inner] = mine_ref[...]
    out_ref[inner ^ 1] = core_ref[core_ref.shape[0] - rows :, :]
    out_ref[inner ^ 2] = y_ref[...]
    out_ref[inner ^ 3] = both_ref[...]


def split_kernel(tm_count, keep_ref, got_ref, *outs):
    my_inner = lax.axis_index("inner")
    core = lax.rem(my_inner, 2)
    me = lax.div(my_inner, 2) * tm_count + lax.axis_index("tm")
    part = outs[0].shape[1]
    half, slab = keep_ref.shape
    for flip, out_ref in enumerate(outs):
        start = (me ^ flip) * part
        out_ref[core] = keep_ref[pl.ds(pl.multiple_of(start, part), part), :]
        for tile in range(slab // LANES):
            rows = pl.ds(pl.multiple_of(tile * half + start, part), part)
            out_ref[1 - core, :, tile * LANES : (tile + 1) * LANES] = got_ref[rows, :]


def join_kernel(tm_count, *refs):
    parts, out_ref, head_ref = refs[:-2], refs[-2], refs[-1]
    me = lax.div(lax.axis_index("inner"), 2) * tm_count + lax.axis_index("tm")
    slab = parts[0].shape[2]
    for flip, part in enumerate(parts):
        other = me ^ flip
        y, tm = lax.div(other, tm_count), lax.rem(other, tm_count)
        for core in range(2):
            place = (y * 2 + core) * tm_count + tm
            out_ref[:, pl.ds(pl.multiple_of(place * slab, slab), slab)] = part[core]
    head_ref[...] = out_ref[:, : head_ref.shape[1]]


def arrange(tpls, left):
    for flip, pack in enumerate(tpls):
        for inner in range(INNER):
            row = (flip * INNER + inner) * FINE
            for step in range(left.shape[1] // LANES):
                left[row : row + FINE, step * LANES : (step + 1) * LANES] = pack[
                    inner, FINE * step : FINE * (step + 1), :
                ]


def correlate(left, full, slab, run, side, ys, store, shifts, products):
    part = full.shape[0]
    size, depth = left.shape
    count = size // FINE
    copies = LANES // FINE
    width = run * slab
    for y in ys:
        columns = width + 2 * LANES
        start = pl.multiple_of((2 * y + side) * width, width)
        samples = full[:, pl.ds(start, columns)]
        for copy in range(depth // part):
            tile, turn = copy // copies * LANES, copy % copies * FINE
            turned = samples if turn == 0 else pltpu.roll(samples, columns - turn, 1)
            shifts[y, copy * part : (copy + 1) * part, :] = turned[:, tile : tile + width + LANES]
    tiles = products.shape[1]
    span = (tiles - 1) * LANES
    per_block = span // slab
    blocks = [(y, index) for y in ys for index in range(width // span)]

    def multiply(place, slot):
        y, index = place
        for tile in range(0, tiles, 2):
            start = index * span + tile * LANES
            pieces = min(2, tiles - tile)
            product = jnp.dot(
                left[...],
                shifts[y, :, start : start + pieces * LANES],
                preferred_element_type=F32,
            )
            for piece in range(pieces):
                products[slot, tile + piece] = product[:, piece * LANES : (piece + 1) * LANES]

    def gather(place, slot):
        def tree(first, number):
            if number == 1:
                rows = pl.ds(first, count, stride=FINE)
                return jnp.concatenate(
                    [products[slot, tile, rows, :] for tile in range(tiles)], axis=1
                )
            half = number // 2
            later = pltpu.roll(tree(first + half, half), span + LANES - half, 1)
            return tree(first, half) + later

        total = tree(0, FINE)
        y, index = place
        for piece in range(per_block):
            store(y, index * per_block + piece, total[:, piece * slab : (piece + 1) * slab])

    multiply(blocks[0], 0)
    for number in range(1, len(blocks)):
        multiply(blocks[number], number % 2)
        gather(blocks[number - 1], (number - 1) % 2)
    gather(blocks[-1], (len(blocks) - 1) % 2)


def first_dots_kernel(outer_count, stations, channels, tm_count, *refs):
    tpls, (order_ref, samples_ref) = refs[:-9], refs[-9:-7]
    begun_ref, left, scale_ref, mask_ref, part_ref, shifts, products = refs[-7:]
    tpls = [pack[...] for pack in tpls]
    if len(tpls) > outer_count:
        tpls = tpls[:2] + [tpls[2] + tpls[3], tpls[4] + tpls[5]]
    arrange(tpls, left)
    core = lax.rem(lax.axis_index("inner"), 2)
    run, _, slab = begun_ref.shape

    def store(y, place, sums):
        begun_ref[place] = sums

    correlate(left, samples_ref, slab, run, 1 - core, [0], store, shifts, products)
    read_masks(stations, channels, tm_count, tpls, order_ref, scale_ref, mask_ref, part_ref)


def middle_dots_kernel(left, samples_ref, halo_ref, begun_ref, mask_ref, *refs):
    send_ref, edges_ref, full, edges, shifts, products = refs
    group, _, window = edges.shape
    chunk = samples_ref.shape[1]
    slab = chunk // group
    run = group // 4
    core = lax.rem(lax.axis_index("inner"), 2)
    full[:, :chunk] = samples_ref[...]
    full[:, chunk:] = halo_ref[...]

    def store(y, place, sums):
        send_ref[y * run + place, :, :slab] = sums

    correlate(left, full, slab, run, 1 - core, [1], store, shifts, products)
    after = [full[:, (m + 1) * slab : (m + 1) * slab + window] for m in range(group)]
    squares = masked_squares(mask_ref[...], jnp.concatenate(after, axis=1))
    column = lax.broadcasted_iota(jnp.int32, squares.shape, 1) & (window - 1)
    reach = 1
    while reach < window:
        earlier = pltpu.roll(squares, reach, 1)
        squares = squares + jnp.where(column >= reach, earlier, 0.0)
        reach *= 2
    squares = jnp.where(column >= 1, pltpu.roll(squares, 1, 1), 0.0)
    for member in range(group):
        edges[member] = squares[:, member * window : (member + 1) * window]
    for tm in range(run):
        send_ref[tm, :, :slab] = begun_ref[tm]
        for y in range(2):
            send_ref[y * run + tm, :, slab:] = edges[(2 * y + 1 - core) * run + tm]
            edges_ref[y * run + tm] = edges[(2 * y + core) * run + tm]


def last_dots_kernel(left, samples_ref, halo_ref, edges_ref, after, keep_ref, *scratch):
    del after
    full, shifts, products = scratch
    chunk = samples_ref.shape[1]
    full[:, :chunk] = samples_ref[...]
    full[:, chunk:] = halo_ref[...]
    core = lax.rem(lax.axis_index("inner"), 2)
    run = keep_ref.shape[0] // 2
    slab = keep_ref.shape[2] - edges_ref.shape[2]

    def store(y, place, sums):
        keep_ref[y * run + place, :, :slab] = sums

    correlate(left, full, slab, run, core, [0, 1], store, shifts, products)
    keep_ref[:, :, slab:] = edges_ref[...]


def add_kernel(tm_count, keep_ref, got_ref, *outs):
    me = lax.div(lax.axis_index("inner"), 2) * tm_count + lax.axis_index("tm")
    for flip, out_ref in enumerate(outs):
        out_ref[...] = keep_ref[me ^ flip] + got_ref[me ^ flip]


def masked_squares(mask, wave):
    wave = wave.astype(F32)
    squares = wave * wave
    high = squares.astype(BF16)
    low = (squares - high.astype(F32)).astype(BF16)
    return jnp.dot(mask, high, preferred_element_type=F32) + jnp.dot(
        mask, low, preferred_element_type=F32
    )


def read_masks(stations, channels, tm_count, tpls, order_ref, scale_ref, mask_ref, part_ref):
    rows = tpls[0].shape[1]
    count = len(tpls) * INNER
    padded = INNER * LANES
    part = LANES // tm_count
    meta = lax.dot_general(
        spare_lanes(part, part * channels // padded),
        jnp.concatenate([pack.reshape(INNER * rows, LANES) for pack in tpls], axis=0),
        (((1,), (1,)), ((), ())),
        preferred_element_type=F32,
    )
    slots = -(-stations // rows)

    def read(slot):
        return jnp.concatenate(
            [meta[slot : slot + 1, t * rows : (t + 1) * rows] for t in range(count)], axis=0
        )

    values = jnp.concatenate([read(slot) for slot in range(slots + 1)], axis=1)
    start = slots * rows
    scale = jnp.sum(values[:, start : start + 3], axis=1, keepdims=True)
    scale_ref[...] = jnp.broadcast_to(scale, scale_ref.shape)
    mask = jnp.dot(
        values[:, :stations].astype(BF16),
        one_hot(order_ref[...], stations),
        preferred_element_type=F32,
    ).astype(BF16)
    mask_ref[...] = mask
    grouped = jnp.dot(mask, regroup(channels, padded, part), preferred_element_type=F32)
    mine = side_major(lax.axis_index("inner")) * LANES + lax.axis_index("tm") * part
    part_ref[...] = pltpu.roll(grouped, lax.rem(padded - mine, padded), 1)[:, :part].astype(BF16)


def power_kernel(window, wave_ref, mask_ref, after, out_ref):
    del after
    power = masked_squares(mask_ref[...], wave_ref[...])
    columns = power.shape[1]
    column = lax.broadcasted_iota(jnp.int32, power.shape, 1)
    reach = 1
    while reach < window:
        later = pltpu.roll(power, columns - reach, 1)
        power = power + jnp.where(column < columns - reach, later, 0.0)
        reach *= 2
    out_ref[...] = power


def finish_kernel(*refs):
    parts, (power_ref, scale_ref, out_ref) = refs[:-3], refs[-3:]
    slab = power_ref.shape[1]
    total = parts[0][...]
    for part in parts[1:]:
        total = total + part[...]
    dots, edge = total[:, :slab], total[:, slab:]
    inside = slab - edge.shape[1]
    energy = jnp.concatenate(
        [power_ref[:, :inside], power_ref[:, inside:] + edge], axis=1
    )
    rows = dots * (scale_ref[:, :1] / jnp.sqrt(energy + EPSILON))
    outer = lax.axis_index("outer")
    step = INNER
    while step < rows.shape[0]:
        pairs = [rows[start : start + step] for start in range(0, rows.shape[0], step)]
        swapped = [pairs[index ^ 1] for index in range(len(pairs))]
        flipped = (outer & (step // INNER)) != 0
        rows = jnp.where(flipped, jnp.concatenate(swapped, axis=0), rows)
        step *= 2
    out_ref[...] = rows


def on_device(waveforms, templates, station_mask, channel_order):
    channels, slab = waveforms.shape
    rows, _, window = templates.shape
    stations = station_mask.shape[1]
    outer_count, tm_count = lax.axis_size("outer"), lax.axis_size("tm")
    blk_count = outer_count * INNER
    assert rows == 1 and LANES % tm_count == 0
    group = INNER * tm_count
    padded = INNER * LANES
    part = padded // group
    chunk = group * slab
    span = 2 * slab
    total = blk_count * tm_count
    blk, every = ("outer", "inner"), ("outer", "inner", "tm")
    sds = jax.ShapeDtypeStruct
    order_row = channel_order[None, :]

    rows = window * part // LANES
    held = [
        pltpu.with_memory_space_constraint(x, pltpu.HBM)
        for x in (waveforms, templates, station_mask, order_row)
    ]
    send, keep, *pieces = call(
        functools.partial(prologue_kernel, tm_count),
        [HBM] * 4,
        [
            sds((padded // 2 * slab // LANES + rows, LANES), BF16),
            sds((padded // 2, slab), BF16),
            *[sds((rows, LANES), BF16)] * (INNER - 1),
        ],
        [
            pltpu.VMEM((channels, slab), BF16),
            pltpu.VMEM((padded, slab), BF16),
            pltpu.VMEM((channels, window), BF16),
            pltpu.VMEM((padded, window), BF16),
            pltpu.VMEM((1, stations), jnp.int32),
            pltpu.VMEM((1, channels), jnp.int32),
            pltpu.VMEM((window, padded), F32),
            pltpu.SemaphoreType.DMA((4,)),
        ],
        bytes_accessed=channels * (window + slab) * 2,
    )(*held)

    def plane(part, flip):
        return lax.ppermute(part, "inner", [(b, b ^ flip) for b in range(INNER)])

    got = plane(send, 1)
    others = [plane(pieces[1], 2), plane(pieces[2], 3)]
    pack = call(
        pack_kernel, [VMEM] * INNER, sds((INNER, rows, LANES), BF16), bytes_accessed=rows * LANES * 8
    )(pieces[0], got, *others)

    def cross(part, route):
        return lax.ppermute(part, "outer", route)

    if outer_count == 4:
        near = cross(pack, [(0, 1), (1, 0), (2, 3), (3, 2)])
        middle = cross(pack, [(1, 2), (2, 1)])
        inward = cross(near, [(1, 2), (2, 1)])
        outward = cross(middle, [(1, 0), (2, 3)])
        ends = cross(inward, [(1, 0), (2, 3)])
        tpls = [pack, near, inward, outward, middle, ends]
    else:
        tpls = [pack] + [
            cross(pack, [(b, b ^ flip) for b in range(outer_count)])
            for flip in range(1, outer_count)
        ]

    half = group // 2

    def swap(part, flip):
        y, tm = flip // tm_count, flip % tm_count
        route = [(i, i ^ (2 * tm_count * y + tm)) for i in range(total)]
        return lax.ppermute(part, every, route)

    parts = call(
        functools.partial(split_kernel, tm_count),
        [VMEM] * 2,
        [sds((2, part, slab), BF16)] * half,
        bytes_accessed=padded * slab * 2,
    )(keep, got)
    waves = [parts[0]] + [swap(parts[flip], flip) for flip in range(1, half)]
    samples, head = call(
        functools.partial(join_kernel, tm_count),
        [VMEM] * half,
        [sds((part, chunk), BF16), sds((part, window), BF16)],
        bytes_accessed=part * chunk * 4,
    )(*waves)
    halo = lax.ppermute(head, "outer", [(b, b - 1) for b in range(1, outer_count)])

    depth = window // FINE * part
    count = blk_count
    work = 2 * count * window * part * chunk // 2

    def scratch():
        return [
            pltpu.VMEM((2, depth, chunk // 4 + LANES), BF16),
            pltpu.VMEM((2, span // LANES + 1, count * FINE, LANES), F32),
        ]

    begun, left, scale, mask, mask_part = call(
        functools.partial(first_dots_kernel, outer_count, stations, channels, tm_count),
        [VMEM] * (len(tpls) + 2),
        [
            sds((tm_count, count, slab), F32),
            sds((count * FINE, depth), BF16),
            sds((count, LANES), F32),
            sds((count, channels), BF16),
            sds((count, part), BF16),
        ],
        scratch(),
        flops=work // 2,
        bytes_accessed=part * chunk * 2,
        vmem=36,
    )(*tpls, order_row, samples)
    full = pltpu.VMEM((part, chunk + window), BF16)
    send, edges = call(
        middle_dots_kernel,
        [VMEM] * 5,
        [sds((half, count, slab + window), F32), sds((half, count, window), F32)],
        [full, pltpu.VMEM((group, count, window), F32)] + scratch(),
        flops=work // 2,
        bytes_accessed=part * chunk * 2,
        vmem=36,
    )(left, samples, halo, begun, mask_part)
    keep = call(
        last_dots_kernel,
        [VMEM] * 4 + [AFTER],
        sds((half, count, slab + window), F32),
        [full] + scratch(),
        flops=work,
        bytes_accessed=part * chunk * 2,
        vmem=36,
    )(left, samples, halo, edges, send)
    got = lax.ppermute(send, "inner", [(b, b ^ 1) for b in range(INNER)])
    power = call(
        functools.partial(power_kernel, window),
        [VMEM, VMEM, AFTER],
        sds((blk_count, slab), F32),
        flops=4 * blk_count * channels * slab,
        bytes_accessed=channels * slab * 2,
    )(waveforms, mask, keep)
    sums = call(
        functools.partial(add_kernel, tm_count),
        [VMEM] * 2,
        [sds((blk_count, slab + window), F32)] * half,
        bytes_accessed=blk_count * slab * 12 * half,
    )(keep, got)
    sums = [sums[0]] + [swap(sums[flip], flip) for flip in reversed(range(1, half))]
    return call(
        finish_kernel,
        [VMEM] * (half + 2),
        sds((blk_count, slab), F32),
        bytes_accessed=blk_count * slab * 4 * (half + 2),
    )(*sums, power, scale)


def solution(mesh):
    blk_count, tm_count = mesh.devices.shape
    shape = (blk_count // INNER, INNER, tm_count)
    mesh = jax.sharding.Mesh(mesh.devices.reshape(shape), ("outer", "inner", "tm"))
    blk, every = ("outer", "inner"), ("outer", "inner", "tm")
    placed = (P(None, every), P(blk, None, None), P(blk, None), P())
    return jax.shard_map(
        on_device, mesh=mesh, in_specs=placed, out_specs=P(None, every), check_vma=False
    )
```

```python
import functools

import jax
import jax.numpy as jnp
from jax import lax
from jax.experimental import pallas as pl
from jax.experimental.pallas import tpu as pltpu
from jax.sharding import PartitionSpec as P

EPSILON = 1e-05
LANES = 128
INNER = 4
FINE = 16
MIB = 1024 * 1024

BF16 = jnp.bfloat16
F32 = jnp.float32


HBM = pl.BlockSpec(memory_space=pltpu.HBM)
VMEM = pl.BlockSpec(memory_space=pltpu.VMEM)
AFTER = pl.BlockSpec(memory_space=pl.ANY)


def call(kernel, in_specs, out_shape, scratch=(), flops=0, bytes_accessed=0, vmem=24):
    return pl.pallas_call(
        kernel,
        in_specs=in_specs,
        out_specs=jax.tree.map(lambda _: VMEM, out_shape),
        out_shape=out_shape,
        scratch_shapes=list(scratch),
        compiler_params=pltpu.CompilerParams(vmem_limit_bytes=vmem * MIB),
        cost_estimate=pl.CostEstimate(
            flops=flops, bytes_accessed=bytes_accessed, transcendentals=0
        ),
    )


def one_hot(order_row, station_count):
    columns = order_row.shape[1]
    first = 3 * lax.broadcasted_iota(jnp.int32, (station_count, columns), 0)
    hit = (order_row >= first) & (order_row < first + 3)
    return jnp.where(hit, 1.0, 0.0).astype(BF16)


def side_major(inner):
    return lax.rem(inner, 2) * (INNER // 2) + lax.div(inner, 2)


def place_of(real, part):
    base = real // FINE * FINE
    return base, real - base


def regroup_rows(source, target, part):
    channels, width = source.shape
    groups = target.shape[0] // part
    real = channels // groups
    base, extra = place_of(real, part)
    rest = source[groups * base :, :].astype(F32)
    fill = jnp.zeros((part - real, width), F32)
    for group in range(groups):
        if base:
            run = source[group * base : (group + 1) * base, :]
            target[group * part : group * part + base, :] = run
        piece = [rest[group * extra : (group + 1) * extra], fill]
        target[group * part + base : (group + 1) * part, :] = jnp.concatenate(
            piece, axis=0
        ).astype(BF16)


def regroup(channels, padded, part):
    groups = padded // part
    real = channels // groups
    base, extra = place_of(real, part)
    channel = lax.broadcasted_iota(jnp.int32, (channels, padded), 0)
    place = lax.broadcasted_iota(jnp.int32, (1, padded), 1)
    group, within = place >> (part.bit_length() - 1), place & (part - 1)
    rest = groups * base + extra * group + within - base
    source = jnp.where(within < base, base * group + within, rest)
    source = jnp.where(within < real, source, -1)
    return jnp.where(channel == source, 1.0, 0.0).astype(BF16)


def spare_lanes(part, real):
    slots = LANES // part * (part - real)
    slot = lax.broadcasted_iota(jnp.int32, (8, LANES), 0)
    lane = lax.broadcasted_iota(jnp.int32, (8, LANES), 1)
    spare = part - real
    home = lax.div(slot, spare) * part + real + lax.rem(slot, spare)
    return jnp.where((lane == home) & (slot < slots), 1.0, 0.0).astype(BF16)


def prologue_kernel(tm_count, wave_hbm, tpl_hbm, flag_hbm, order_hbm, *refs):
    send_ref, samples_ref, *outs = refs[: INNER + 1]
    wave_ref, grouped, tpl_ref, tpl_grouped, flag_ref, order_ref, turned, sems = refs[INNER + 1 :]
    channels, window = tpl_hbm.shape[1:]
    copies = [
        pltpu.make_async_copy(flag_hbm, flag_ref, sems.at[0]),
        pltpu.make_async_copy(order_hbm, order_ref, sems.at[1]),
        pltpu.make_async_copy(tpl_hbm.at[0], tpl_ref, sems.at[2]),
        pltpu.make_async_copy(wave_hbm, wave_ref, sems.at[3]),
    ]
    for copy in copies:
        copy.start()
    stations = flag_ref.shape[1]
    padded = turned.shape[1]
    part = LANES // tm_count
    rows = outs[0].shape[0]
    groups = regroup(channels, padded, part)
    copies[0].wait()
    copies[1].wait()
    flags = jnp.broadcast_to(flag_ref[...].astype(F32), (8, stations))
    mask = jnp.dot(
        flags.astype(BF16), one_hot(order_ref[...], stations), preferred_element_type=F32
    )
    live = jnp.sum(mask[:1], keepdims=True)
    mask = jnp.dot(mask.astype(BF16), groups, preferred_element_type=F32)[:1]
    copies[2].wait()
    regroup_rows(tpl_ref, tpl_grouped, part)
    masked = tpl_grouped[...].T.astype(F32) * mask
    turned[...] = masked
    norm = jnp.sqrt(jnp.sum(masked * masked, keepdims=True) + EPSILON)
    rest = jnp.broadcast_to(jnp.sqrt(window * live) / norm, (1, rows))
    row = lax.broadcasted_iota(jnp.int32, (1, rows), 1)
    scale = jnp.zeros((1, rows), F32)
    for piece in range(3):
        now = rest.astype(BF16).astype(F32)
        scale = jnp.where(row == piece, now, scale)
        rest = rest - now
    slots = -(-stations // rows)
    wide = flags[:1]
    if stations % rows:
        wide = jnp.concatenate([wide, jnp.zeros((1, rows - stations % rows), F32)], axis=1)
    meta = [wide[:, slot * rows : (slot + 1) * rows] for slot in range(slots)] + [scale]
    meta = jnp.concatenate(meta + [jnp.zeros((8 - len(meta), rows), F32)], axis=0)
    meta = lax.dot_general(
        meta.astype(BF16),
        spare_lanes(part, part * channels // padded),
        (((0,), (0,)), ((), ())),
        preferred_element_type=F32,
    )
    my_tm = lax.axis_index("tm")
    my_inner = lax.axis_index("inner")
    my_core = lax.rem(my_inner, 2)
    first = send_ref.shape[0] - rows
    spot = lax.broadcasted_iota(jnp.int32, (FINE, LANES), 1) >> (part.bit_length() - 1)
    for flip in range(INNER):
        start = pl.multiple_of(side_major(my_inner ^ flip) * LANES, LANES)
        pieces = []
        for step in range(window // (FINE * tm_count)):
            tile = jnp.zeros((FINE, LANES), F32)
            for within in range(tm_count):
                row = FINE * (step * tm_count + within)
                chunk = turned[row : row + FINE, pl.ds(start, LANES)]
                turn = lax.rem(part * (within - my_tm) + LANES, LANES)
                tile = jnp.where(spot == within, pltpu.roll(chunk, turn, 1), tile)
            pieces.append(tile)
        payload = (jnp.concatenate(pieces, axis=0) + meta).astype(BF16)
        if flip == 1:
            send_ref[first:, :] = payload
        else:
            outs[flip - (flip > 1)][...] = payload

    copies[3].wait()
    regroup_rows(wave_ref, grouped, part)
    half = padded // 2
    samples_ref[...] = grouped[pl.ds(pl.multiple_of(my_core * half, half), half), :]
    theirs = pl.ds(pl.multiple_of((1 - my_core) * half, half), half)
    for tile in range(first // half):
        columns = slice(tile * LANES, (tile + 1) * LANES)
        send_ref[tile * half : (tile + 1) * half, :] = grouped[theirs, columns]


def pack_kernel(mine_ref, core_ref, y_ref, both_ref, out_ref):
    inner = lax.axis_index("inner")
    rows = mine_ref.shape[0]
    out_ref[inner] = mine_ref[...]
    out_ref[inner ^ 1] = core_ref[core_ref.shape[0] - rows :, :]
    out_ref[inner ^ 2] = y_ref[...]
    out_ref[inner ^ 3] = both_ref[...]


def split_kernel(tm_count, keep_ref, got_ref, *outs):
    my_inner = lax.axis_index("inner")
    core = lax.rem(my_inner, 2)
    me = lax.div(my_inner, 2) * tm_count + lax.axis_index("tm")
    part = outs[0].shape[1]
    half, slab = keep_ref.shape
    for flip, out_ref in enumerate(outs):
        start = (me ^ flip) * part
        out_ref[core] = keep_ref[pl.ds(pl.multiple_of(start, part), part), :]
        for tile in range(slab // LANES):
            rows = pl.ds(pl.multiple_of(tile * half + start, part), part)
            out_ref[1 - core, :, tile * LANES : (tile + 1) * LANES] = got_ref[rows, :]


def join_kernel(tm_count, *refs):
    parts, out_ref, head_ref = refs[:-2], refs[-2], refs[-1]
    me = lax.div(lax.axis_index("inner"), 2) * tm_count + lax.axis_index("tm")
    slab = parts[0].shape[2]
    for flip, part in enumerate(parts):
        other = me ^ flip
        y, tm = lax.div(other, tm_count), lax.rem(other, tm_count)
        for core in range(2):
            place = (y * 2 + core) * tm_count + tm
            out_ref[:, pl.ds(pl.multiple_of(place * slab, slab), slab)] = part[core]
    head_ref[...] = out_ref[:, : head_ref.shape[1]]


def arrange(tpls, left):
    for flip, pack in enumerate(tpls):
        for inner in range(INNER):
            row = (flip * INNER + inner) * FINE
            for step in range(left.shape[1] // LANES):
                left[row : row + FINE, step * LANES : (step + 1) * LANES] = pack[
                    inner, FINE * step : FINE * (step + 1), :
                ]


def correlate(left, full, slab, run, side, ys, store, shifts, products):
    part = full.shape[0]
    size, depth = left.shape
    count = size // FINE
    copies = LANES // FINE
    width = run * slab
    for y in ys:
        columns = width + 2 * LANES
        start = pl.multiple_of((2 * y + side) * width, width)
        samples = full[:, pl.ds(start, columns)]
        for copy in range(copies):
            turned = samples if copy == 0 else pltpu.roll(samples, columns - copy * FINE, 1)
            shifts[y, copy * part : (copy + 1) * part, :] = turned
    tiles = products.shape[1]
    span = (tiles - 1) * LANES
    per_block = span // slab
    blocks = [(y, index) for y in ys for index in range(width // span)]

    def multiply(place, slot):
        y, index = place
        for tile in range(0, tiles, 2):
            start = index * span + tile * LANES
            pieces = min(2, tiles - tile)
            starts = range(start, start + depth // (copies * part) * LANES, LANES)
            right = [shifts[y, :, first : first + pieces * LANES] for first in starts]
            product = jnp.dot(
                left[...], jnp.concatenate(right, axis=0), preferred_element_type=F32
            )
            for piece in range(pieces):
                products[slot, tile + piece] = product[:, piece * LANES : (piece + 1) * LANES]

    def gather(place, slot):
        def tree(first, number):
            if number == 1:
                rows = pl.ds(first, count, stride=FINE)
                return jnp.concatenate(
                    [products[slot, tile, rows, :] for tile in range(tiles)], axis=1
                )
            half = number // 2
            later = pltpu.roll(tree(first + half, half), span + LANES - half, 1)
            return tree(first, half) + later

        total = tree(0, FINE)
        y, index = place
        for piece in range(per_block):
            store(y, index * per_block + piece, total[:, piece * slab : (piece + 1) * slab])

    multiply(blocks[0], 0)
    for number in range(1, len(blocks)):
        multiply(blocks[number], number % 2)
        gather(blocks[number - 1], (number - 1) % 2)
    gather(blocks[-1], (len(blocks) - 1) % 2)


def first_dots_kernel(outer_count, stations, channels, tm_count, *refs):
    tpls, (order_ref, samples_ref) = refs[:-9], refs[-9:-7]
    begun_ref, left, scale_ref, mask_ref, part_ref, shifts, products = refs[-7:]
    tpls = [pack[...] for pack in tpls]
    if len(tpls) > outer_count:
        tpls = tpls[:-2] + [tpls[-2] + tpls[-1]]
    arrange(tpls, left)
    core = lax.rem(lax.axis_index("inner"), 2)
    run, _, slab = begun_ref.shape

    def store(y, place, sums):
        begun_ref[place] = sums

    correlate(left, samples_ref, slab, run, 1 - core, [0], store, shifts, products)
    read_masks(stations, channels, tm_count, tpls, order_ref, scale_ref, mask_ref, part_ref)


def middle_dots_kernel(left, samples_ref, halo_ref, begun_ref, mask_ref, *refs):
    send_ref, edges_ref, full, edges, shifts, products = refs
    group, _, window = edges.shape
    chunk = samples_ref.shape[1]
    slab = chunk // group
    run = group // 4
    core = lax.rem(lax.axis_index("inner"), 2)
    full[:, :chunk] = samples_ref[...]
    full[:, chunk:] = halo_ref[...]

    def store(y, place, sums):
        send_ref[y * run + place, :, :slab] = sums

    correlate(left, full, slab, run, 1 - core, [1], store, shifts, products)
    after = [full[:, (m + 1) * slab : (m + 1) * slab + window] for m in range(group)]
    squares = masked_squares(mask_ref[...], jnp.concatenate(after, axis=1))
    column = lax.broadcasted_iota(jnp.int32, squares.shape, 1) & (window - 1)
    reach = 1
    while reach < window:
        earlier = pltpu.roll(squares, reach, 1)
        squares = squares + jnp.where(column >= reach, earlier, 0.0)
        reach *= 2
    squares = jnp.where(column >= 1, pltpu.roll(squares, 1, 1), 0.0)
    for member in range(group):
        edges[member] = squares[:, member * window : (member + 1) * window]
    for tm in range(run):
        send_ref[tm, :, :slab] = begun_ref[tm]
        for y in range(2):
            send_ref[y * run + tm, :, slab:] = edges[(2 * y + 1 - core) * run + tm]
            edges_ref[y * run + tm] = edges[(2 * y + core) * run + tm]


def last_dots_kernel(left, samples_ref, halo_ref, edges_ref, after, keep_ref, *scratch):
    del after
    full, shifts, products = scratch
    chunk = samples_ref.shape[1]
    full[:, :chunk] = samples_ref[...]
    full[:, chunk:] = halo_ref[...]
    core = lax.rem(lax.axis_index("inner"), 2)
    run = keep_ref.shape[0] // 2
    slab = keep_ref.shape[2] - edges_ref.shape[2]

    def store(y, place, sums):
        keep_ref[y * run + place, :, :slab] = sums

    correlate(left, full, slab, run, core, [0, 1], store, shifts, products)
    keep_ref[:, :, slab:] = edges_ref[...]


def add_kernel(tm_count, keep_ref, got_ref, *outs):
    me = lax.div(lax.axis_index("inner"), 2) * tm_count + lax.axis_index("tm")
    for flip, out_ref in enumerate(outs):
        out_ref[...] = keep_ref[me ^ flip] + got_ref[me ^ flip]


def masked_squares(mask, wave):
    wave = wave.astype(F32)
    squares = wave * wave
    high = squares.astype(BF16)
    low = (squares - high.astype(F32)).astype(BF16)
    return jnp.dot(mask, high, preferred_element_type=F32) + jnp.dot(
        mask, low, preferred_element_type=F32
    )


def read_masks(stations, channels, tm_count, tpls, order_ref, scale_ref, mask_ref, part_ref):
    rows = tpls[0].shape[1]
    count = len(tpls) * INNER
    padded = INNER * LANES
    part = LANES // tm_count
    meta = lax.dot_general(
        spare_lanes(part, part * channels // padded),
        jnp.concatenate([pack.reshape(INNER * rows, LANES) for pack in tpls], axis=0),
        (((1,), (1,)), ((), ())),
        preferred_element_type=F32,
    )
    slots = -(-stations // rows)

    def read(slot):
        return jnp.concatenate(
            [meta[slot : slot + 1, t * rows : (t + 1) * rows] for t in range(count)], axis=0
        )

    values = jnp.concatenate([read(slot) for slot in range(slots + 1)], axis=1)
    start = slots * rows
    scale = jnp.sum(values[:, start : start + 3], axis=1, keepdims=True)
    scale_ref[...] = jnp.broadcast_to(scale, scale_ref.shape)
    mask = jnp.dot(
        values[:, :stations].astype(BF16),
        one_hot(order_ref[...], stations),
        preferred_element_type=F32,
    ).astype(BF16)
    mask_ref[...] = mask
    grouped = jnp.dot(mask, regroup(channels, padded, part), preferred_element_type=F32)
    mine = side_major(lax.axis_index("inner")) * LANES + lax.axis_index("tm") * part
    part_ref[...] = pltpu.roll(grouped, lax.rem(padded - mine, padded), 1)[:, :part].astype(BF16)


def power_kernel(window, wave_ref, mask_ref, after, out_ref):
    del after
    power = masked_squares(mask_ref[...], wave_ref[...])
    columns = power.shape[1]
    column = lax.broadcasted_iota(jnp.int32, power.shape, 1)
    reach = 1
    while reach < window:
        later = pltpu.roll(power, columns - reach, 1)
        power = power + jnp.where(column < columns - reach, later, 0.0)
        reach *= 2
    out_ref[...] = power


def finish_kernel(*refs):
    parts, (power_ref, scale_ref, out_ref) = refs[:-3], refs[-3:]
    slab = power_ref.shape[1]
    total = parts[0][...]
    for part in parts[1:]:
        total = total + part[...]
    dots, edge = total[:, :slab], total[:, slab:]
    inside = slab - edge.shape[1]
    energy = jnp.concatenate(
        [power_ref[:, :inside], power_ref[:, inside:] + edge], axis=1
    )
    rows = dots * (scale_ref[:, :1] / jnp.sqrt(energy + EPSILON))
    outer = lax.axis_index("outer")
    step = INNER
    while step < rows.shape[0]:
        pairs = [rows[start : start + step] for start in range(0, rows.shape[0], step)]
        swapped = [pairs[index ^ 1] for index in range(len(pairs))]
        flipped = (outer & (step // INNER)) != 0
        rows = jnp.where(flipped, jnp.concatenate(swapped, axis=0), rows)
        step *= 2
    out_ref[...] = rows


def on_device(waveforms, templates, station_mask, channel_order):
    channels, slab = waveforms.shape
    rows, _, window = templates.shape
    stations = station_mask.shape[1]
    outer_count, tm_count = lax.axis_size("outer"), lax.axis_size("tm")
    blk_count = outer_count * INNER
    assert rows == 1 and LANES % tm_count == 0
    group = INNER * tm_count
    padded = INNER * LANES
    part = padded // group
    chunk = group * slab
    span = 2 * slab
    total = blk_count * tm_count
    blk, every = ("outer", "inner"), ("outer", "inner", "tm")
    sds = jax.ShapeDtypeStruct
    order_row = channel_order[None, :]

    rows = window * part // LANES
    held = [
        pltpu.with_memory_space_constraint(x, pltpu.HBM)
        for x in (waveforms, templates, station_mask, order_row)
    ]
    send, keep, *pieces = call(
        functools.partial(prologue_kernel, tm_count),
        [HBM] * 4,
        [
            sds((padded // 2 * slab // LANES + rows, LANES), BF16),
            sds((padded // 2, slab), BF16),
            *[sds((rows, LANES), BF16)] * (INNER - 1),
        ],
        [
            pltpu.VMEM((channels, slab), BF16),
            pltpu.VMEM((padded, slab), BF16),
            pltpu.VMEM((channels, window), BF16),
            pltpu.VMEM((padded, window), BF16),
            pltpu.VMEM((1, stations), jnp.int32),
            pltpu.VMEM((1, channels), jnp.int32),
            pltpu.VMEM((window, padded), F32),
            pltpu.SemaphoreType.DMA((4,)),
        ],
        bytes_accessed=channels * (window + slab) * 2,
    )(*held)

    def plane(part, flip):
        return lax.ppermute(part, "inner", [(b, b ^ flip) for b in range(INNER)])

    got = plane(send, 1)
    others = [plane(pieces[1], 2), plane(pieces[2], 3)]
    pack = call(
        pack_kernel, [VMEM] * INNER, sds((INNER, rows, LANES), BF16), bytes_accessed=rows * LANES * 8
    )(pieces[0], got, *others)

    def cross(part, route):
        return lax.ppermute(part, "outer", route)

    if outer_count == 4:
        near = cross(pack, [(0, 1), (1, 0), (2, 3), (3, 2)])
        far = cross(pack, [(0, 2), (2, 0), (1, 3), (3, 1)])
        middle = cross(pack, [(1, 2), (2, 1)])
        ends = cross(far, [(1, 0), (2, 3)])
        tpls = [pack, near, far, middle, ends]
    else:
        tpls = [pack] + [
            cross(pack, [(b, b ^ flip) for b in range(outer_count)])
            for flip in range(1, outer_count)
        ]

    half = group // 2

    def swap(part, flip):
        y, tm = flip // tm_count, flip % tm_count
        route = [(i, i ^ (2 * tm_count * y + tm)) for i in range(total)]
        return lax.ppermute(part, every, route)

    parts = call(
        functools.partial(split_kernel, tm_count),
        [VMEM] * 2,
        [sds((2, part, slab), BF16)] * half,
        bytes_accessed=padded * slab * 2,
    )(keep, got)
    waves = [parts[0]] + [swap(parts[flip], flip) for flip in range(1, half)]
    samples, head = call(
        functools.partial(join_kernel, tm_count),
        [VMEM] * half,
        [sds((part, chunk), BF16), sds((part, window), BF16)],
        bytes_accessed=part * chunk * 4,
    )(*waves)
    halo = lax.ppermute(head, "outer", [(b, b - 1) for b in range(1, outer_count)])

    depth = window // FINE * part
    count = blk_count
    work = 2 * count * window * part * chunk // 2

    def scratch():
        return [
            pltpu.VMEM((2, LANES // FINE * part, chunk // 4 + 2 * LANES), BF16),
            pltpu.VMEM((2, span // LANES + 1, count * FINE, LANES), F32),
        ]

    begun, left, scale, mask, mask_part = call(
        functools.partial(first_dots_kernel, outer_count, stations, channels, tm_count),
        [VMEM] * (len(tpls) + 2),
        [
            sds((tm_count, count, slab), F32),
            sds((count * FINE, depth), BF16),
            sds((count, LANES), F32),
            sds((count, channels), BF16),
            sds((count, part), BF16),
        ],
        scratch(),
        flops=work // 2,
        bytes_accessed=part * chunk * 2,
        vmem=36,
    )(*tpls, order_row, samples)
    full = pltpu.VMEM((part, chunk + window), BF16)
    send, edges = call(
        middle_dots_kernel,
        [VMEM] * 5,
        [sds((half, count, slab + window), F32), sds((half, count, window), F32)],
        [full, pltpu.VMEM((group, count, window), F32)] + scratch(),
        flops=work // 2,
        bytes_accessed=part * chunk * 2,
        vmem=36,
    )(left, samples, halo, begun, mask_part)
    keep = call(
        last_dots_kernel,
        [VMEM] * 4 + [AFTER],
        sds((half, count, slab + window), F32),
        [full] + scratch(),
        flops=work,
        bytes_accessed=part * chunk * 2,
        vmem=36,
    )(left, samples, halo, edges, send)
    got = lax.ppermute(send, "inner", [(b, b ^ 1) for b in range(INNER)])
    power = call(
        functools.partial(power_kernel, window),
        [VMEM, VMEM, AFTER],
        sds((blk_count, slab), F32),
        flops=4 * blk_count * channels * slab,
        bytes_accessed=channels * slab * 2,
    )(waveforms, mask, keep)
    sums = call(
        functools.partial(add_kernel, tm_count),
        [VMEM] * 2,
        [sds((blk_count, slab + window), F32)] * half,
        bytes_accessed=blk_count * slab * 12 * half,
    )(keep, got)
    sums = [sums[0]] + [swap(sums[flip], flip) for flip in reversed(range(1, half))]
    return call(
        finish_kernel,
        [VMEM] * (half + 2),
        sds((blk_count, slab), F32),
        bytes_accessed=blk_count * slab * 4 * (half + 2),
    )(*sums, power, scale)


def solution(mesh):
    blk_count, tm_count = mesh.devices.shape
    shape = (blk_count // INNER, INNER, tm_count)
    mesh = jax.sharding.Mesh(mesh.devices.reshape(shape), ("outer", "inner", "tm"))
    blk, every = ("outer", "inner"), ("outer", "inner", "tm")
    placed = (P(None, every), P(blk, None, None), P(blk, None), P())
    return jax.shard_map(
        on_device, mesh=mesh, in_specs=placed, out_specs=P(None, every), check_vma=False
    )
```

```python
import functools

import jax
import jax.numpy as jnp
from jax import lax
from jax.experimental import pallas as pl
from jax.experimental.pallas import tpu as pltpu
from jax.sharding import PartitionSpec as P

EPSILON = 1e-05
LANES = 128
INNER = 4
FINE = 16
MIB = 1024 * 1024

BF16 = jnp.bfloat16
F32 = jnp.float32


HBM = pl.BlockSpec(memory_space=pltpu.HBM)
VMEM = pl.BlockSpec(memory_space=pltpu.VMEM)
AFTER = pl.BlockSpec(memory_space=pl.ANY)


def call(kernel, in_specs, out_shape, scratch=(), flops=0, bytes_accessed=0, vmem=24):
    return pl.pallas_call(
        kernel,
        in_specs=in_specs,
        out_specs=jax.tree.map(lambda _: VMEM, out_shape),
        out_shape=out_shape,
        scratch_shapes=list(scratch),
        compiler_params=pltpu.CompilerParams(vmem_limit_bytes=vmem * MIB),
        cost_estimate=pl.CostEstimate(
            flops=flops, bytes_accessed=bytes_accessed, transcendentals=0
        ),
    )


def one_hot(order_row, station_count):
    columns = order_row.shape[1]
    first = 3 * lax.broadcasted_iota(jnp.int32, (station_count, columns), 0)
    hit = (order_row >= first) & (order_row < first + 3)
    return jnp.where(hit, 1.0, 0.0).astype(BF16)


def side_major(inner):
    return lax.rem(inner, 2) * (INNER // 2) + lax.div(inner, 2)


def place_of(real, part):
    base = real // FINE * FINE
    return base, real - base


def regroup_rows(source, target, part):
    channels, width = source.shape
    groups = target.shape[0] // part
    real = channels // groups
    base, extra = place_of(real, part)
    rest = source[groups * base :, :].astype(F32)
    fill = jnp.zeros((part - real, width), F32)
    for group in range(groups):
        if base:
            run = source[group * base : (group + 1) * base, :]
            target[group * part : group * part + base, :] = run
        piece = [rest[group * extra : (group + 1) * extra], fill]
        target[group * part + base : (group + 1) * part, :] = jnp.concatenate(
            piece, axis=0
        ).astype(BF16)


def regroup(channels, padded, part):
    groups = padded // part
    real = channels // groups
    base, extra = place_of(real, part)
    channel = lax.broadcasted_iota(jnp.int32, (channels, padded), 0)
    place = lax.broadcasted_iota(jnp.int32, (1, padded), 1)
    group, within = place >> (part.bit_length() - 1), place & (part - 1)
    rest = groups * base + extra * group + within - base
    source = jnp.where(within < base, base * group + within, rest)
    source = jnp.where(within < real, source, -1)
    return jnp.where(channel == source, 1.0, 0.0).astype(BF16)


def spare_lanes(part, real):
    slots = LANES // part * (part - real)
    slot = lax.broadcasted_iota(jnp.int32, (8, LANES), 0)
    lane = lax.broadcasted_iota(jnp.int32, (8, LANES), 1)
    spare = part - real
    home = lax.div(slot, spare) * part + real + lax.rem(slot, spare)
    return jnp.where((lane == home) & (slot < slots), 1.0, 0.0).astype(BF16)


def prologue_kernel(tm_count, wave_hbm, tpl_hbm, flag_hbm, order_hbm, *refs):
    send_ref, samples_ref, *outs = refs[: INNER + 1]
    wave_ref, grouped, tpl_ref, tpl_grouped, flag_ref, order_ref, turned, sems = refs[INNER + 1 :]
    channels, window = tpl_hbm.shape[1:]
    copies = [
        pltpu.make_async_copy(flag_hbm, flag_ref, sems.at[0]),
        pltpu.make_async_copy(order_hbm, order_ref, sems.at[1]),
        pltpu.make_async_copy(tpl_hbm.at[0], tpl_ref, sems.at[2]),
        pltpu.make_async_copy(wave_hbm, wave_ref, sems.at[3]),
    ]
    for copy in copies:
        copy.start()
    stations = flag_ref.shape[1]
    padded = turned.shape[1]
    part = LANES // tm_count
    rows = outs[0].shape[0]
    groups = regroup(channels, padded, part)
    copies[0].wait()
    copies[1].wait()
    flags = jnp.broadcast_to(flag_ref[...].astype(F32), (8, stations))
    mask = jnp.dot(
        flags.astype(BF16), one_hot(order_ref[...], stations), preferred_element_type=F32
    )
    live = jnp.sum(mask[:1], keepdims=True)
    mask = jnp.dot(mask.astype(BF16), groups, preferred_element_type=F32)[:1]
    copies[2].wait()
    regroup_rows(tpl_ref, tpl_grouped, part)
    masked = tpl_grouped[...].T.astype(F32) * mask
    turned[...] = masked
    norm = jnp.sqrt(jnp.sum(masked * masked, keepdims=True) + EPSILON)
    rest = jnp.broadcast_to(jnp.sqrt(window * live) / norm, (1, rows))
    row = lax.broadcasted_iota(jnp.int32, (1, rows), 1)
    scale = jnp.zeros((1, rows), F32)
    for piece in range(3):
        now = rest.astype(BF16).astype(F32)
        scale = jnp.where(row == piece, now, scale)
        rest = rest - now
    slots = -(-stations // rows)
    wide = flags[:1]
    if stations % rows:
        wide = jnp.concatenate([wide, jnp.zeros((1, rows - stations % rows), F32)], axis=1)
    meta = [wide[:, slot * rows : (slot + 1) * rows] for slot in range(slots)] + [scale]
    meta = jnp.concatenate(meta + [jnp.zeros((8 - len(meta), rows), F32)], axis=0)
    meta = lax.dot_general(
        meta.astype(BF16),
        spare_lanes(part, part * channels // padded),
        (((0,), (0,)), ((), ())),
        preferred_element_type=F32,
    )
    my_tm = lax.axis_index("tm")
    my_inner = lax.axis_index("inner")
    my_core = lax.rem(my_inner, 2)
    first = send_ref.shape[0] - rows
    spot = lax.broadcasted_iota(jnp.int32, (FINE, LANES), 1) >> (part.bit_length() - 1)
    for flip in range(INNER):
        start = pl.multiple_of(side_major(my_inner ^ flip) * LANES, LANES)
        pieces = []
        for step in range(window // (FINE * tm_count)):
            tile = jnp.zeros((FINE, LANES), F32)
            for within in range(tm_count):
                row = FINE * (step * tm_count + within)
                chunk = turned[row : row + FINE, pl.ds(start, LANES)]
                turn = lax.rem(part * (within - my_tm) + LANES, LANES)
                tile = jnp.where(spot == within, pltpu.roll(chunk, turn, 1), tile)
            pieces.append(tile)
        payload = (jnp.concatenate(pieces, axis=0) + meta).astype(BF16)
        if flip == 1:
            send_ref[first:, :] = payload
        else:
            outs[flip - (flip > 1)][...] = payload

    copies[3].wait()
    regroup_rows(wave_ref, grouped, part)
    half = padded // 2
    samples_ref[...] = grouped[pl.ds(pl.multiple_of(my_core * half, half), half), :]
    theirs = pl.ds(pl.multiple_of((1 - my_core) * half, half), half)
    for tile in range(first // half):
        columns = slice(tile * LANES, (tile + 1) * LANES)
        send_ref[tile * half : (tile + 1) * half, :] = grouped[theirs, columns]


def pack_kernel(mine_ref, core_ref, y_ref, both_ref, out_ref):
    inner = lax.axis_index("inner")
    rows = mine_ref.shape[0]
    out_ref[inner] = mine_ref[...]
    out_ref[inner ^ 1] = core_ref[core_ref.shape[0] - rows :, :]
    out_ref[inner ^ 2] = y_ref[...]
    out_ref[inner ^ 3] = both_ref[...]


def split_kernel(tm_count, keep_ref, got_ref, *outs):
    my_inner = lax.axis_index("inner")
    core = lax.rem(my_inner, 2)
    me = lax.div(my_inner, 2) * tm_count + lax.axis_index("tm")
    part = outs[0].shape[1]
    half, slab = keep_ref.shape
    for flip, out_ref in enumerate(outs):
        start = (me ^ flip) * part
        out_ref[core] = keep_ref[pl.ds(pl.multiple_of(start, part), part), :]
        for tile in range(slab // LANES):
            rows = pl.ds(pl.multiple_of(tile * half + start, part), part)
            out_ref[1 - core, :, tile * LANES : (tile + 1) * LANES] = got_ref[rows, :]


def join_kernel(tm_count, *refs):
    parts, out_ref, head_ref = refs[:-2], refs[-2], refs[-1]
    me = lax.div(lax.axis_index("inner"), 2) * tm_count + lax.axis_index("tm")
    slab = parts[0].shape[2]
    for flip, part in enumerate(parts):
        other = me ^ flip
        y, tm = lax.div(other, tm_count), lax.rem(other, tm_count)
        for core in range(2):
            place = (y * 2 + core) * tm_count + tm
            out_ref[:, pl.ds(pl.multiple_of(place * slab, slab), slab)] = part[core]
    head_ref[...] = out_ref[:, : head_ref.shape[1]]


def arrange(tpls, left):
    for flip, pack in enumerate(tpls):
        for inner in range(INNER):
            row = (flip * INNER + inner) * FINE
            for step in range(left.shape[1] // LANES):
                left[row : row + FINE, step * LANES : (step + 1) * LANES] = pack[
                    inner, FINE * step : FINE * (step + 1), :
                ]


def correlate(left, full, slab, run, side, ys, store, shifts, products):
    part = full.shape[0]
    size, depth = left.shape
    count = size // FINE
    copies = LANES // FINE
    width = run * slab
    for y in ys:
        columns = width + 2 * LANES
        start = pl.multiple_of((2 * y + side) * width, width)
        samples = full[:, pl.ds(start, columns)]
        for copy in range(copies):
            turned = samples if copy == 0 else pltpu.roll(samples, columns - copy * FINE, 1)
            shifts[y, copy * part : (copy + 1) * part, :] = turned
    tiles = products.shape[1]
    span = (tiles - 1) * LANES
    per_block = span // slab
    blocks = [(y, index) for y in ys for index in range(width // span)]

    def multiply(place, slot):
        y, index = place
        for tile in range(0, tiles, 2):
            start = index * span + tile * LANES
            pieces = min(2, tiles - tile)
            starts = range(start, start + depth // (copies * part) * LANES, LANES)
            right = [shifts[y, :, first : first + pieces * LANES] for first in starts]
            product = jnp.dot(
                left[...], jnp.concatenate(right, axis=0), preferred_element_type=F32
            )
            for piece in range(pieces):
                products[slot, tile + piece] = product[:, piece * LANES : (piece + 1) * LANES]

    def gather(place, slot):
        def tree(first, number, here):
            if number == 1:
                rows = pl.ds(first, count, stride=FINE)
                return jnp.concatenate([products[slot, tile, rows, :] for tile in here], axis=1)
            half = number // 2
            later = pltpu.roll(tree(first + half, half, here), len(here) * LANES - half, 1)
            return tree(first, half, here) + later

        y, index = place
        cut = tiles // 3
        for low, high in ((0, cut), (cut, tiles - 1)):
            total = tree(0, FINE, range(low, high + 1))
            for tile in range(low, high):
                member, lane = divmod(tile * LANES, slab)
                columns = total[:, (tile - low) * LANES : (tile - low + 1) * LANES]
                store(y, index * per_block + member, lane, columns)

    multiply(blocks[0], 0)
    for number in range(1, len(blocks)):
        multiply(blocks[number], number % 2)
        gather(blocks[number - 1], (number - 1) % 2)
    gather(blocks[-1], (len(blocks) - 1) % 2)


def first_dots_kernel(outer_count, stations, channels, tm_count, *refs):
    tpls, (order_ref, samples_ref) = refs[:-9], refs[-9:-7]
    begun_ref, left, scale_ref, mask_ref, part_ref, shifts, products = refs[-7:]
    tpls = [pack[...] for pack in tpls]
    if len(tpls) > outer_count:
        tpls = tpls[:-2] + [tpls[-2] + tpls[-1]]
    arrange(tpls, left)
    core = lax.rem(lax.axis_index("inner"), 2)
    run, _, slab = begun_ref.shape

    def store(y, place, lane, sums):
        begun_ref[place, :, lane : lane + LANES] = sums

    correlate(left, samples_ref, slab, run, 1 - core, [0], store, shifts, products)
    read_masks(stations, channels, tm_count, tpls, order_ref, scale_ref, mask_ref, part_ref)


def middle_dots_kernel(left, samples_ref, halo_ref, begun_ref, mask_ref, *refs):
    send_ref, edges_ref, full, edges, shifts, products = refs
    group, _, window = edges.shape
    chunk = samples_ref.shape[1]
    slab = chunk // group
    run = group // 4
    core = lax.rem(lax.axis_index("inner"), 2)
    full[:, :chunk] = samples_ref[...]
    full[:, chunk:] = halo_ref[...]

    def store(y, place, lane, sums):
        send_ref[run + place, :, lane : lane + LANES] = sums

    correlate(left, full, slab, run, 1 - core, [1], store, shifts, products)
    after = [full[:, (m + 1) * slab : (m + 1) * slab + window] for m in range(group)]
    squares = masked_squares(mask_ref[...], jnp.concatenate(after, axis=1))
    column = lax.broadcasted_iota(jnp.int32, squares.shape, 1) & (window - 1)
    reach = 1
    while reach < window:
        earlier = pltpu.roll(squares, reach, 1)
        squares = squares + jnp.where(column >= reach, earlier, 0.0)
        reach *= 2
    squares = jnp.where(column >= 1, pltpu.roll(squares, 1, 1), 0.0)
    for member in range(group):
        edges[member] = squares[:, member * window : (member + 1) * window]
    for tm in range(run):
        send_ref[tm, :, :slab] = begun_ref[tm]
        for y in range(2):
            send_ref[y * run + tm, :, slab:] = edges[(2 * y + 1 - core) * run + tm]
            edges_ref[y * run + tm] = edges[(2 * y + core) * run + tm]


def last_dots_kernel(left, samples_ref, halo_ref, edges_ref, after, keep_ref, *scratch):
    del after
    full, shifts, products = scratch
    chunk = samples_ref.shape[1]
    full[:, :chunk] = samples_ref[...]
    full[:, chunk:] = halo_ref[...]
    core = lax.rem(lax.axis_index("inner"), 2)
    run = keep_ref.shape[0] // 2
    slab = keep_ref.shape[2] - edges_ref.shape[2]

    def store(y, place, lane, sums):
        keep_ref[y * run + place, :, lane : lane + LANES] = sums

    correlate(left, full, slab, run, core, [0, 1], store, shifts, products)
    keep_ref[:, :, slab:] = edges_ref[...]


def add_kernel(tm_count, keep_ref, got_ref, *outs):
    me = lax.div(lax.axis_index("inner"), 2) * tm_count + lax.axis_index("tm")
    for flip, out_ref in enumerate(outs):
        out_ref[...] = keep_ref[me ^ flip] + got_ref[me ^ flip]


def masked_squares(mask, wave):
    wave = wave.astype(F32)
    squares = wave * wave
    high = squares.astype(BF16)
    low = (squares - high.astype(F32)).astype(BF16)
    return jnp.dot(mask, high, preferred_element_type=F32) + jnp.dot(
        mask, low, preferred_element_type=F32
    )


def read_masks(stations, channels, tm_count, tpls, order_ref, scale_ref, mask_ref, part_ref):
    rows = tpls[0].shape[1]
    count = len(tpls) * INNER
    padded = INNER * LANES
    part = LANES // tm_count
    meta = lax.dot_general(
        spare_lanes(part, part * channels // padded),
        jnp.concatenate([pack.reshape(INNER * rows, LANES) for pack in tpls], axis=0),
        (((1,), (1,)), ((), ())),
        preferred_element_type=F32,
    )
    slots = -(-stations // rows)

    def read(slot):
        return jnp.concatenate(
            [meta[slot : slot + 1, t * rows : (t + 1) * rows] for t in range(count)], axis=0
        )

    values = jnp.concatenate([read(slot) for slot in range(slots + 1)], axis=1)
    start = slots * rows
    scale = jnp.sum(values[:, start : start + 3], axis=1, keepdims=True)
    scale_ref[...] = jnp.broadcast_to(scale, scale_ref.shape)
    mask = jnp.dot(
        values[:, :stations].astype(BF16),
        one_hot(order_ref[...], stations),
        preferred_element_type=F32,
    ).astype(BF16)
    mask_ref[...] = mask
    grouped = jnp.dot(mask, regroup(channels, padded, part), preferred_element_type=F32)
    mine = side_major(lax.axis_index("inner")) * LANES + lax.axis_index("tm") * part
    part_ref[...] = pltpu.roll(grouped, lax.rem(padded - mine, padded), 1)[:, :part].astype(BF16)


def power_kernel(window, wave_ref, mask_ref, after, out_ref):
    del after
    power = masked_squares(mask_ref[...], wave_ref[...])
    columns = power.shape[1]
    column = lax.broadcasted_iota(jnp.int32, power.shape, 1)
    reach = 1
    while reach < window:
        later = pltpu.roll(power, columns - reach, 1)
        power = power + jnp.where(column < columns - reach, later, 0.0)
        reach *= 2
    out_ref[...] = power


def finish_kernel(*refs):
    parts, (power_ref, scale_ref, out_ref) = refs[:-3], refs[-3:]
    slab = power_ref.shape[1]
    total = parts[0][...]
    for part in parts[1:]:
        total = total + part[...]
    dots, edge = total[:, :slab], total[:, slab:]
    inside = slab - edge.shape[1]
    energy = jnp.concatenate(
        [power_ref[:, :inside], power_ref[:, inside:] + edge], axis=1
    )
    rows = dots * (scale_ref[:, :1] / jnp.sqrt(energy + EPSILON))
    outer = lax.axis_index("outer")
    step = INNER
    while step < rows.shape[0]:
        pairs = [rows[start : start + step] for start in range(0, rows.shape[0], step)]
        swapped = [pairs[index ^ 1] for index in range(len(pairs))]
        flipped = (outer & (step // INNER)) != 0
        rows = jnp.where(flipped, jnp.concatenate(swapped, axis=0), rows)
        step *= 2
    out_ref[...] = rows


def on_device(waveforms, templates, station_mask, channel_order):
    channels, slab = waveforms.shape
    rows, _, window = templates.shape
    stations = station_mask.shape[1]
    outer_count, tm_count = lax.axis_size("outer"), lax.axis_size("tm")
    blk_count = outer_count * INNER
    assert rows == 1 and LANES % tm_count == 0
    group = INNER * tm_count
    padded = INNER * LANES
    part = padded // group
    chunk = group * slab
    span = 2 * slab
    total = blk_count * tm_count
    blk, every = ("outer", "inner"), ("outer", "inner", "tm")
    sds = jax.ShapeDtypeStruct
    order_row = channel_order[None, :]

    rows = window * part // LANES
    held = [
        pltpu.with_memory_space_constraint(x, pltpu.HBM)
        for x in (waveforms, templates, station_mask, order_row)
    ]
    send, keep, *pieces = call(
        functools.partial(prologue_kernel, tm_count),
        [HBM] * 4,
        [
            sds((padded // 2 * slab // LANES + rows, LANES), BF16),
            sds((padded // 2, slab), BF16),
            *[sds((rows, LANES), BF16)] * (INNER - 1),
        ],
        [
            pltpu.VMEM((channels, slab), BF16),
            pltpu.VMEM((padded, slab), BF16),
            pltpu.VMEM((channels, window), BF16),
            pltpu.VMEM((padded, window), BF16),
            pltpu.VMEM((1, stations), jnp.int32),
            pltpu.VMEM((1, channels), jnp.int32),
            pltpu.VMEM((window, padded), F32),
            pltpu.SemaphoreType.DMA((4,)),
        ],
        bytes_accessed=channels * (window + slab) * 2,
    )(*held)

    def plane(part, flip):
        return lax.ppermute(part, "inner", [(b, b ^ flip) for b in range(INNER)])

    got = plane(send, 1)
    others = [plane(pieces[1], 2), plane(pieces[2], 3)]
    pack = call(
        pack_kernel, [VMEM] * INNER, sds((INNER, rows, LANES), BF16), bytes_accessed=rows * LANES * 8
    )(pieces[0], got, *others)

    def cross(part, route):
        return lax.ppermute(part, "outer", route)

    if outer_count == 4:
        near = cross(pack, [(0, 1), (1, 0), (2, 3), (3, 2)])
        far = cross(pack, [(0, 2), (2, 0), (1, 3), (3, 1)])
        middle = cross(pack, [(1, 2), (2, 1)])
        ends = cross(far, [(1, 0), (2, 3)])
        tpls = [pack, near, far, middle, ends]
    else:
        tpls = [pack] + [
            cross(pack, [(b, b ^ flip) for b in range(outer_count)])
            for flip in range(1, outer_count)
        ]

    half = group // 2

    def swap(part, flip):
        y, tm = flip // tm_count, flip % tm_count
        route = [(i, i ^ (2 * tm_count * y + tm)) for i in range(total)]
        return lax.ppermute(part, every, route)

    parts = call(
        functools.partial(split_kernel, tm_count),
        [VMEM] * 2,
        [sds((2, part, slab), BF16)] * half,
        bytes_accessed=padded * slab * 2,
    )(keep, got)
    waves = [parts[0]] + [swap(parts[flip], flip) for flip in range(1, half)]
    samples, head = call(
        functools.partial(join_kernel, tm_count),
        [VMEM] * half,
        [sds((part, chunk), BF16), sds((part, window), BF16)],
        bytes_accessed=part * chunk * 4,
    )(*waves)
    halo = lax.ppermute(head, "outer", [(b, b - 1) for b in range(1, outer_count)])

    depth = window // FINE * part
    count = blk_count
    work = 2 * count * window * part * chunk // 2

    def scratch():
        return [
            pltpu.VMEM((2, LANES // FINE * part, chunk // 4 + 2 * LANES), BF16),
            pltpu.VMEM((2, span // LANES + 1, count * FINE, LANES), F32),
        ]

    begun, left, scale, mask, mask_part = call(
        functools.partial(first_dots_kernel, outer_count, stations, channels, tm_count),
        [VMEM] * (len(tpls) + 2),
        [
            sds((tm_count, count, slab), F32),
            sds((count * FINE, depth), BF16),
            sds((count, LANES), F32),
            sds((count, channels), BF16),
            sds((count, part), BF16),
        ],
        scratch(),
        flops=work // 2,
        bytes_accessed=part * chunk * 2,
        vmem=36,
    )(*tpls, order_row, samples)
    full = pltpu.VMEM((part, chunk + window), BF16)
    send, edges = call(
        middle_dots_kernel,
        [VMEM] * 5,
        [sds((half, count, slab + window), F32), sds((half, count, window), F32)],
        [full, pltpu.VMEM((group, count, window), F32)] + scratch(),
        flops=work // 2,
        bytes_accessed=part * chunk * 2,
        vmem=36,
    )(left, samples, halo, begun, mask_part)
    keep = call(
        last_dots_kernel,
        [VMEM] * 4 + [AFTER],
        sds((half, count, slab + window), F32),
        [full] + scratch(),
        flops=work,
        bytes_accessed=part * chunk * 2,
        vmem=36,
    )(left, samples, halo, edges, send)
    got = lax.ppermute(send, "inner", [(b, b ^ 1) for b in range(INNER)])
    power = call(
        functools.partial(power_kernel, window),
        [VMEM, VMEM, AFTER],
        sds((blk_count, slab), F32),
        flops=4 * blk_count * channels * slab,
        bytes_accessed=channels * slab * 2,
    )(waveforms, mask, keep)
    sums = call(
        functools.partial(add_kernel, tm_count),
        [VMEM] * 2,
        [sds((blk_count, slab + window), F32)] * half,
        bytes_accessed=blk_count * slab * 12 * half,
    )(keep, got)
    sums = [sums[0]] + [swap(sums[flip], flip) for flip in reversed(range(1, half))]
    return call(
        finish_kernel,
        [VMEM] * (half + 2),
        sds((blk_count, slab), F32),
        bytes_accessed=blk_count * slab * 4 * (half + 2),
    )(*sums, power, scale)


def solution(mesh):
    blk_count, tm_count = mesh.devices.shape
    shape = (blk_count // INNER, INNER, tm_count)
    mesh = jax.sharding.Mesh(mesh.devices.reshape(shape), ("outer", "inner", "tm"))
    blk, every = ("outer", "inner"), ("outer", "inner", "tm")
    placed = (P(None, every), P(blk, None, None), P(blk, None), P())
    return jax.shard_map(
        on_device, mesh=mesh, in_specs=placed, out_specs=P(None, every), check_vma=False
    )
```

```python
import functools

import jax
import jax.numpy as jnp
from jax import lax
from jax.experimental import pallas as pl
from jax.experimental.pallas import tpu as pltpu
from jax.sharding import PartitionSpec as P

EPSILON = 1e-05
LANES = 128
INNER = 4
FINE = 16
MIB = 1024 * 1024

BF16 = jnp.bfloat16
F32 = jnp.float32


HBM = pl.BlockSpec(memory_space=pltpu.HBM)
VMEM = pl.BlockSpec(memory_space=pltpu.VMEM)
AFTER = pl.BlockSpec(memory_space=pl.ANY)


def call(kernel, in_specs, out_shape, scratch=(), flops=0, bytes_accessed=0, vmem=24):
    return pl.pallas_call(
        kernel,
        in_specs=in_specs,
        out_specs=jax.tree.map(lambda _: VMEM, out_shape),
        out_shape=out_shape,
        scratch_shapes=list(scratch),
        compiler_params=pltpu.CompilerParams(vmem_limit_bytes=vmem * MIB),
        cost_estimate=pl.CostEstimate(
            flops=flops, bytes_accessed=bytes_accessed, transcendentals=0
        ),
    )


def one_hot(order_row, station_count):
    columns = order_row.shape[1]
    first = 3 * lax.broadcasted_iota(jnp.int32, (station_count, columns), 0)
    hit = (order_row >= first) & (order_row < first + 3)
    return jnp.where(hit, 1.0, 0.0).astype(BF16)


def side_major(inner):
    return lax.rem(inner, 2) * (INNER // 2) + lax.div(inner, 2)


def place_of(real, part):
    base = real // FINE * FINE
    return base, real - base


def regroup_rows(source, target, part):
    channels, width = source.shape
    groups = target.shape[0] // part
    real = channels // groups
    base, extra = place_of(real, part)
    rest = source[groups * base :, :].astype(F32)
    fill = jnp.zeros((part - real, width), F32)
    for group in range(groups):
        if base:
            run = source[group * base : (group + 1) * base, :]
            target[group * part : group * part + base, :] = run
        piece = [rest[group * extra : (group + 1) * extra], fill]
        target[group * part + base : (group + 1) * part, :] = jnp.concatenate(
            piece, axis=0
        ).astype(BF16)


def regroup(channels, padded, part):
    groups = padded // part
    real = channels // groups
    base, extra = place_of(real, part)
    channel = lax.broadcasted_iota(jnp.int32, (channels, padded), 0)
    place = lax.broadcasted_iota(jnp.int32, (1, padded), 1)
    group, within = place >> (part.bit_length() - 1), place & (part - 1)
    rest = groups * base + extra * group + within - base
    source = jnp.where(within < base, base * group + within, rest)
    source = jnp.where(within < real, source, -1)
    return jnp.where(channel == source, 1.0, 0.0).astype(BF16)


def spare_lanes(part, real):
    slots = LANES // part * (part - real)
    slot = lax.broadcasted_iota(jnp.int32, (8, LANES), 0)
    lane = lax.broadcasted_iota(jnp.int32, (8, LANES), 1)
    spare = part - real
    home = lax.div(slot, spare) * part + real + lax.rem(slot, spare)
    return jnp.where((lane == home) & (slot < slots), 1.0, 0.0).astype(BF16)


def prologue_kernel(tm_count, wave_hbm, tpl_hbm, flag_hbm, order_hbm, *refs):
    send_ref, samples_ref, *outs = refs[: INNER + 1]
    wave_ref, grouped, tpl_ref, tpl_grouped, flag_ref, order_ref, turned, sems = refs[INNER + 1 :]
    channels, window = tpl_hbm.shape[1:]
    copies = [
        pltpu.make_async_copy(flag_hbm, flag_ref, sems.at[0]),
        pltpu.make_async_copy(order_hbm, order_ref, sems.at[1]),
        pltpu.make_async_copy(tpl_hbm.at[0], tpl_ref, sems.at[2]),
        pltpu.make_async_copy(wave_hbm, wave_ref, sems.at[3]),
    ]
    for copy in copies:
        copy.start()
    stations = flag_ref.shape[1]
    padded = turned.shape[1]
    part = LANES // tm_count
    rows = outs[0].shape[0]
    groups = regroup(channels, padded, part)
    copies[0].wait()
    copies[1].wait()
    flags = jnp.broadcast_to(flag_ref[...].astype(F32), (8, stations))
    mask = jnp.dot(
        flags.astype(BF16), one_hot(order_ref[...], stations), preferred_element_type=F32
    )
    live = jnp.sum(mask[:1], keepdims=True)
    mask = jnp.dot(mask.astype(BF16), groups, preferred_element_type=F32)[:1]
    copies[2].wait()
    regroup_rows(tpl_ref, tpl_grouped, part)
    masked = tpl_grouped[...].T.astype(F32) * mask
    turned[...] = masked
    norm = jnp.sqrt(jnp.sum(masked * masked, keepdims=True) + EPSILON)
    rest = jnp.broadcast_to(jnp.sqrt(window * live) / norm, (1, rows))
    row = lax.broadcasted_iota(jnp.int32, (1, rows), 1)
    scale = jnp.zeros((1, rows), F32)
    for piece in range(3):
        now = rest.astype(BF16).astype(F32)
        scale = jnp.where(row == piece, now, scale)
        rest = rest - now
    slots = -(-stations // rows)
    wide = flags[:1]
    if stations % rows:
        wide = jnp.concatenate([wide, jnp.zeros((1, rows - stations % rows), F32)], axis=1)
    meta = [wide[:, slot * rows : (slot + 1) * rows] for slot in range(slots)] + [scale]
    meta = jnp.concatenate(meta + [jnp.zeros((8 - len(meta), rows), F32)], axis=0)
    meta = lax.dot_general(
        meta.astype(BF16),
        spare_lanes(part, part * channels // padded),
        (((0,), (0,)), ((), ())),
        preferred_element_type=F32,
    )
    my_tm = lax.axis_index("tm")
    my_inner = lax.axis_index("inner")
    my_core = lax.rem(my_inner, 2)
    first = send_ref.shape[0] - rows
    spot = lax.broadcasted_iota(jnp.int32, (FINE, LANES), 1) >> (part.bit_length() - 1)
    for flip in range(INNER):
        start = pl.multiple_of(side_major(my_inner ^ flip) * LANES, LANES)
        pieces = []
        for step in range(window // (FINE * tm_count)):
            tile = jnp.zeros((FINE, LANES), F32)
            for within in range(tm_count):
                row = FINE * (step * tm_count + within)
                chunk = turned[row : row + FINE, pl.ds(start, LANES)]
                turn = lax.rem(part * (within - my_tm) + LANES, LANES)
                tile = jnp.where(spot == within, pltpu.roll(chunk, turn, 1), tile)
            pieces.append(tile)
        payload = (jnp.concatenate(pieces, axis=0) + meta).astype(BF16)
        if flip == 1:
            send_ref[first:, :] = payload
        else:
            outs[flip - (flip > 1)][...] = payload

    copies[3].wait()
    regroup_rows(wave_ref, grouped, part)
    half = padded // 2
    samples_ref[...] = grouped[pl.ds(pl.multiple_of(my_core * half, half), half), :]
    theirs = pl.ds(pl.multiple_of((1 - my_core) * half, half), half)
    for tile in range(first // half):
        columns = slice(tile * LANES, (tile + 1) * LANES)
        send_ref[tile * half : (tile + 1) * half, :] = grouped[theirs, columns]


def pack_kernel(mine_ref, core_ref, y_ref, both_ref, out_ref):
    inner = lax.axis_index("inner")
    rows = mine_ref.shape[0]
    out_ref[inner] = mine_ref[...]
    out_ref[inner ^ 1] = core_ref[core_ref.shape[0] - rows :, :]
    out_ref[inner ^ 2] = y_ref[...]
    out_ref[inner ^ 3] = both_ref[...]


def split_kernel(tm_count, keep_ref, got_ref, *outs):
    my_inner = lax.axis_index("inner")
    core = lax.rem(my_inner, 2)
    me = lax.div(my_inner, 2) * tm_count + lax.axis_index("tm")
    part = outs[0].shape[1]
    half, slab = keep_ref.shape
    for flip, out_ref in enumerate(outs):
        start = (me ^ flip) * part
        out_ref[core] = keep_ref[pl.ds(pl.multiple_of(start, part), part), :]
        for tile in range(slab // LANES):
            rows = pl.ds(pl.multiple_of(tile * half + start, part), part)
            out_ref[1 - core, :, tile * LANES : (tile + 1) * LANES] = got_ref[rows, :]


def join_kernel(tm_count, *refs):
    parts, out_ref, head_ref = refs[:-2], refs[-2], refs[-1]
    me = lax.div(lax.axis_index("inner"), 2) * tm_count + lax.axis_index("tm")
    slab = parts[0].shape[2]
    for flip, part in enumerate(parts):
        other = me ^ flip
        y, tm = lax.div(other, tm_count), lax.rem(other, tm_count)
        for core in range(2):
            place = (y * 2 + core) * tm_count + tm
            out_ref[:, pl.ds(pl.multiple_of(place * slab, slab), slab)] = part[core]
    head_ref[...] = out_ref[:, : head_ref.shape[1]]


def arrange(tpls, left):
    for flip, pack in enumerate(tpls):
        for inner in range(INNER):
            row = (flip * INNER + inner) * FINE
            for step in range(left.shape[1] // LANES):
                left[row : row + FINE, step * LANES : (step + 1) * LANES] = pack[
                    inner, FINE * step : FINE * (step + 1), :
                ]


def correlate(left, full, slab, run, side, ys, store, shifts, products):
    part = full.shape[0]
    size, depth = left.shape
    count = size // FINE
    copies = LANES // FINE
    width = run * slab
    for y in ys:
        columns = width + 2 * LANES
        start = pl.multiple_of((2 * y + side) * width, width)
        samples = full[:, pl.ds(start, columns)]
        for copy in range(copies):
            turned = samples if copy == 0 else pltpu.roll(samples, columns - copy * FINE, 1)
            shifts[y, copy * part : (copy + 1) * part, :] = turned
    tiles = products.shape[1]
    span = (tiles - 1) * LANES
    per_block = span // slab
    blocks = [(y, index) for y in ys for index in range(width // span)]

    def multiply(place, slot):
        y, index = place
        for tile in range(0, tiles, 2):
            start = index * span + tile * LANES
            pieces = min(2, tiles - tile)
            starts = range(start, start + depth // (copies * part) * LANES, LANES)
            right = [shifts[y, :, first : first + pieces * LANES] for first in starts]
            product = jnp.dot(
                left[...], jnp.concatenate(right, axis=0), preferred_element_type=F32
            )
            for piece in range(pieces):
                products[slot, tile + piece] = product[:, piece * LANES : (piece + 1) * LANES]

    def gather(place, slot):
        def tree(first, number):
            if number == 1:
                rows = pl.ds(first, count, stride=FINE)
                return jnp.concatenate(
                    [products[slot, tile, rows, :] for tile in range(tiles)], axis=1
                )
            half = number // 2
            later = pltpu.roll(tree(first + half, half), span + LANES - half, 1)
            return tree(first, half) + later

        total = tree(0, FINE)
        y, index = place
        for piece in range(per_block):
            store(y, index * per_block + piece, total[:, piece * slab : (piece + 1) * slab])

    multiply(blocks[0], 0)
    for number in range(1, len(blocks)):
        multiply(blocks[number], number % 2)
        gather(blocks[number - 1], (number - 1) % 2)
    gather(blocks[-1], (len(blocks) - 1) % 2)


def first_dots_kernel(outer_count, stations, channels, tm_count, *refs):
    tpls, (order_ref, samples_ref) = refs[:-9], refs[-9:-7]
    begun_ref, left, scale_ref, mask_ref, part_ref, shifts, products = refs[-7:]
    tpls = [pack[...] for pack in tpls]
    if len(tpls) > outer_count:
        tpls = tpls[:-2] + [tpls[-2] + tpls[-1]]
    arrange(tpls, left)
    core = lax.rem(lax.axis_index("inner"), 2)
    run, _, slab = begun_ref.shape

    def store(y, place, sums):
        begun_ref[place] = sums

    correlate(left, samples_ref, slab, run, 1 - core, [0], store, shifts, products)
    read_masks(stations, channels, tm_count, tpls, order_ref, scale_ref, mask_ref, part_ref)


def middle_dots_kernel(left, samples_ref, halo_ref, begun_ref, mask_ref, *refs):
    send_ref, edges_ref, full, edges, shifts, products = refs
    group, _, window = edges.shape
    chunk = samples_ref.shape[1]
    slab = chunk // group
    run = group // 4
    core = lax.rem(lax.axis_index("inner"), 2)
    full[:, :chunk] = samples_ref[...]
    full[:, chunk:] = halo_ref[...]

    def store(y, place, sums):
        send_ref[y * run + place, :, :slab] = sums

    correlate(left, full, slab, run, 1 - core, [1], store, shifts, products)
    after = [full[:, (m + 1) * slab : (m + 1) * slab + window] for m in range(group)]
    squares = masked_squares(mask_ref[...], jnp.concatenate(after, axis=1))
    column = lax.broadcasted_iota(jnp.int32, squares.shape, 1) & (window - 1)
    reach = 1
    while reach < window:
        earlier = pltpu.roll(squares, reach, 1)
        squares = squares + jnp.where(column >= reach, earlier, 0.0)
        reach *= 2
    squares = jnp.where(column >= 1, pltpu.roll(squares, 1, 1), 0.0)
    for member in range(group):
        edges[member] = squares[:, member * window : (member + 1) * window]
    for tm in range(run):
        send_ref[tm, :, :slab] = begun_ref[tm]
        for y in range(2):
            send_ref[y * run + tm, :, slab:] = edges[(2 * y + 1 - core) * run + tm]
            edges_ref[y * run + tm] = edges[(2 * y + core) * run + tm]


def last_dots_kernel(left, full, edges_ref, after, keep_ref, shifts, products):
    del after
    core = lax.rem(lax.axis_index("inner"), 2)
    run = keep_ref.shape[0] // 2
    slab = keep_ref.shape[2] - edges_ref.shape[2]

    def store(y, place, sums):
        keep_ref[y * run + place, :, :slab] = sums

    correlate(left, full, slab, run, core, [0, 1], store, shifts, products)
    keep_ref[:, :, slab:] = edges_ref[...]


def add_kernel(tm_count, keep_ref, got_ref, *outs):
    me = lax.div(lax.axis_index("inner"), 2) * tm_count + lax.axis_index("tm")
    for flip, out_ref in enumerate(outs):
        out_ref[...] = keep_ref[me ^ flip] + got_ref[me ^ flip]


def masked_squares(mask, wave):
    wave = wave.astype(F32)
    squares = wave * wave
    high = squares.astype(BF16)
    low = (squares - high.astype(F32)).astype(BF16)
    return jnp.dot(mask, high, preferred_element_type=F32) + jnp.dot(
        mask, low, preferred_element_type=F32
    )


def read_masks(stations, channels, tm_count, tpls, order_ref, scale_ref, mask_ref, part_ref):
    rows = tpls[0].shape[1]
    count = len(tpls) * INNER
    padded = INNER * LANES
    part = LANES // tm_count
    meta = lax.dot_general(
        spare_lanes(part, part * channels // padded),
        jnp.concatenate([pack.reshape(INNER * rows, LANES) for pack in tpls], axis=0),
        (((1,), (1,)), ((), ())),
        preferred_element_type=F32,
    )
    slots = -(-stations // rows)

    def read(slot):
        return jnp.concatenate(
            [meta[slot : slot + 1, t * rows : (t + 1) * rows] for t in range(count)], axis=0
        )

    values = jnp.concatenate([read(slot) for slot in range(slots + 1)], axis=1)
    start = slots * rows
    scale = jnp.sum(values[:, start : start + 3], axis=1, keepdims=True)
    scale_ref[...] = jnp.broadcast_to(scale, scale_ref.shape)
    mask = jnp.dot(
        values[:, :stations].astype(BF16),
        one_hot(order_ref[...], stations),
        preferred_element_type=F32,
    ).astype(BF16)
    mask_ref[...] = mask
    grouped = jnp.dot(mask, regroup(channels, padded, part), preferred_element_type=F32)
    mine = side_major(lax.axis_index("inner")) * LANES + lax.axis_index("tm") * part
    part_ref[...] = pltpu.roll(grouped, lax.rem(padded - mine, padded), 1)[:, :part].astype(BF16)


def power_kernel(window, wave_ref, mask_ref, after, out_ref):
    del after
    power = masked_squares(mask_ref[...], wave_ref[...])
    columns = power.shape[1]
    column = lax.broadcasted_iota(jnp.int32, power.shape, 1)
    reach = 1
    while reach < window:
        later = pltpu.roll(power, columns - reach, 1)
        power = power + jnp.where(column < columns - reach, later, 0.0)
        reach *= 2
    out_ref[...] = power


def finish_kernel(*refs):
    parts, (power_ref, scale_ref, out_ref) = refs[:-3], refs[-3:]
    slab = power_ref.shape[1]
    total = parts[0][...]
    for part in parts[1:]:
        total = total + part[...]
    dots, edge = total[:, :slab], total[:, slab:]
    inside = slab - edge.shape[1]
    energy = jnp.concatenate(
        [power_ref[:, :inside], power_ref[:, inside:] + edge], axis=1
    )
    rows = dots * (scale_ref[:, :1] / jnp.sqrt(energy + EPSILON))
    outer = lax.axis_index("outer")
    step = INNER
    while step < rows.shape[0]:
        pairs = [rows[start : start + step] for start in range(0, rows.shape[0], step)]
        swapped = [pairs[index ^ 1] for index in range(len(pairs))]
        flipped = (outer & (step // INNER)) != 0
        rows = jnp.where(flipped, jnp.concatenate(swapped, axis=0), rows)
        step *= 2
    out_ref[...] = rows


def on_device(waveforms, templates, station_mask, channel_order):
    channels, slab = waveforms.shape
    rows, _, window = templates.shape
    stations = station_mask.shape[1]
    outer_count, tm_count = lax.axis_size("outer"), lax.axis_size("tm")
    blk_count = outer_count * INNER
    assert rows == 1 and LANES % tm_count == 0
    group = INNER * tm_count
    padded = INNER * LANES
    part = padded // group
    chunk = group * slab
    span = 2 * slab
    total = blk_count * tm_count
    blk, every = ("outer", "inner"), ("outer", "inner", "tm")
    sds = jax.ShapeDtypeStruct
    order_row = channel_order[None, :]

    rows = window * part // LANES
    held = [
        pltpu.with_memory_space_constraint(x, pltpu.HBM)
        for x in (waveforms, templates, station_mask, order_row)
    ]
    send, keep, *pieces = call(
        functools.partial(prologue_kernel, tm_count),
        [HBM] * 4,
        [
            sds((padded // 2 * slab // LANES + rows, LANES), BF16),
            sds((padded // 2, slab), BF16),
            *[sds((rows, LANES), BF16)] * (INNER - 1),
        ],
        [
            pltpu.VMEM((channels, slab), BF16),
            pltpu.VMEM((padded, slab), BF16),
            pltpu.VMEM((channels, window), BF16),
            pltpu.VMEM((padded, window), BF16),
            pltpu.VMEM((1, stations), jnp.int32),
            pltpu.VMEM((1, channels), jnp.int32),
            pltpu.VMEM((window, padded), F32),
            pltpu.SemaphoreType.DMA((4,)),
        ],
        bytes_accessed=channels * (window + slab) * 2,
    )(*held)

    def plane(part, flip):
        return lax.ppermute(part, "inner", [(b, b ^ flip) for b in range(INNER)])

    got = plane(send, 1)
    others = [plane(pieces[1], 2), plane(pieces[2], 3)]
    pack = call(
        pack_kernel, [VMEM] * INNER, sds((INNER, rows, LANES), BF16), bytes_accessed=rows * LANES * 8
    )(pieces[0], got, *others)

    def cross(part, route):
        return lax.ppermute(part, "outer", route)

    if outer_count == 4:
        near = cross(pack, [(0, 1), (1, 0), (2, 3), (3, 2)])
        far = cross(pack, [(0, 2), (2, 0), (1, 3), (3, 1)])
        middle = cross(pack, [(1, 2), (2, 1)])
        ends = cross(far, [(1, 0), (2, 3)])
        tpls = [pack, near, far, middle, ends]
    else:
        tpls = [pack] + [
            cross(pack, [(b, b ^ flip) for b in range(outer_count)])
            for flip in range(1, outer_count)
        ]

    half = group // 2

    def swap(part, flip):
        y, tm = flip // tm_count, flip % tm_count
        route = [(i, i ^ (2 * tm_count * y + tm)) for i in range(total)]
        return lax.ppermute(part, every, route)

    parts = call(
        functools.partial(split_kernel, tm_count),
        [VMEM] * 2,
        [sds((2, part, slab), BF16)] * half,
        bytes_accessed=padded * slab * 2,
    )(keep, got)
    waves = [parts[0]] + [swap(parts[flip], flip) for flip in range(1, half)]
    samples, head = call(
        functools.partial(join_kernel, tm_count),
        [VMEM] * half,
        [sds((part, chunk), BF16), sds((part, window), BF16)],
        bytes_accessed=part * chunk * 4,
    )(*waves)
    halo = lax.ppermute(head, "outer", [(b, b - 1) for b in range(1, outer_count)])

    depth = window // FINE * part
    count = blk_count
    work = 2 * count * window * part * chunk // 2

    def scratch():
        return [
            pltpu.VMEM((2, LANES // FINE * part, chunk // 4 + 2 * LANES), BF16),
            pltpu.VMEM((2, span // LANES + 1, count * FINE, LANES), F32),
        ]

    begun, left, scale, mask, mask_part = call(
        functools.partial(first_dots_kernel, outer_count, stations, channels, tm_count),
        [VMEM] * (len(tpls) + 2),
        [
            sds((tm_count, count, slab), F32),
            sds((count * FINE, depth), BF16),
            sds((count, LANES), F32),
            sds((count, channels), BF16),
            sds((count, part), BF16),
        ],
        scratch(),
        flops=work // 2,
        bytes_accessed=part * chunk * 2,
        vmem=36,
    )(*tpls, order_row, samples)
    send, edges, full = call(
        middle_dots_kernel,
        [VMEM] * 5,
        [
            sds((half, count, slab + window), F32),
            sds((half, count, window), F32),
            sds((part, chunk + window), BF16),
        ],
        [pltpu.VMEM((group, count, window), F32)] + scratch(),
        flops=work // 2,
        bytes_accessed=part * chunk * 2,
        vmem=36,
    )(left, samples, halo, begun, mask_part)
    keep = call(
        last_dots_kernel,
        [VMEM] * 3 + [AFTER],
        sds((half, count, slab + window), F32),
        scratch(),
        flops=work,
        bytes_accessed=part * chunk * 2,
        vmem=36,
    )(left, full, edges, send)
    got = lax.ppermute(send, "inner", [(b, b ^ 1) for b in range(INNER)])
    power = call(
        functools.partial(power_kernel, window),
        [VMEM, VMEM, AFTER],
        sds((blk_count, slab), F32),
        flops=4 * blk_count * channels * slab,
        bytes_accessed=channels * slab * 2,
    )(waveforms, mask, keep)
    sums = call(
        functools.partial(add_kernel, tm_count),
        [VMEM] * 2,
        [sds((blk_count, slab + window), F32)] * half,
        bytes_accessed=blk_count * slab * 12 * half,
    )(keep, got)
    sums = [sums[0]] + [swap(sums[flip], flip) for flip in reversed(range(1, half))]
    return call(
        finish_kernel,
        [VMEM] * (half + 2),
        sds((blk_count, slab), F32),
        bytes_accessed=blk_count * slab * 4 * (half + 2),
    )(*sums, power, scale)


def solution(mesh):
    blk_count, tm_count = mesh.devices.shape
    shape = (blk_count // INNER, INNER, tm_count)
    mesh = jax.sharding.Mesh(mesh.devices.reshape(shape), ("outer", "inner", "tm"))
    blk, every = ("outer", "inner"), ("outer", "inner", "tm")
    placed = (P(None, every), P(blk, None, None), P(blk, None), P())
    return jax.shard_map(
        on_device, mesh=mesh, in_specs=placed, out_specs=P(None, every), check_vma=False
    )
```
